32 devices in a mesh: blk: 16 (over z, y, core), head: 2 (over x).
Axes of the slice: x: 2, y: 2, z: 4, core: 2. Of those that a mesh axis runs over, the one named last changes fastest.
Arguments:
- hidden_in: bfloat16 [2, 4096, 768], P(None, ('blk', 'head')), may hold values from -6 to 6
- segment_ids: int32 [2, 4096], P(None, ('blk', 'head')), may hold values from 0 to 4, never falling along the last dimension, each value on 1 to 2000 neighbouring positions
- neighbour_valid: int32 [2, 64], P(None, ('blk', 'head')), may hold values 0 or 1
- neighbours: bfloat16 [2, 64, 2, 128, 768], P(None, ('blk', 'head')), may hold values from -6 to 6
- out_grad: bfloat16 [2, 4096, 768], P(None, ('blk', 'head')), may hold values from -6 to 6
- norm_attn: bfloat16 [768], P(('blk', 'head')), may hold values from 0.099609375 to 1.8984375
- w_qkv: bfloat16 [768, 2304], P(('blk', 'head')), may hold values from -0.21875 to 0.21875
- w_attn_out: bfloat16 [768, 768], P(('blk', 'head')), may hold values from -1.5 to 1.5
- norm_cross: bfloat16 [768], P(('blk', 'head')), may hold values from 0.099609375 to 1.8984375
- w_cross_q: bfloat16 [768, 768], P(('blk', 'head')), may hold values from -0.21875 to 0.21875
- w_cross_kv: bfloat16 [768, 1536], P(('blk', 'head')), may hold values from -0.21875 to 0.21875
- w_cross_out: bfloat16 [768, 768], P(('blk', 'head')), may hold values from -2 to 2
- norm_mlp: bfloat16 [768], P(('blk', 'head')), may hold values from 0.099609375 to 1.8984375
- w_up: bfloat16 [768, 3072], P(('blk', 'head')), may hold values from -0.21875 to 0.21875
- w_down: bfloat16 [3072, 768], P(('blk', 'head')), may hold values from -0.109375 to 0.109375
Outputs:
- output: bfloat16 [2, 4096, 768], P(None, ('blk', 'head'))
- grad_in: bfloat16 [2, 4096, 768], P(None, ('blk', 'head'))
- grad_neighbours: bfloat16 [2, 64, 2, 128, 768], P(None, ('blk', 'head'))
- grad_norm_attn: float32 [768], P(('blk', 'head'))
- grad_qkv: float32 [768, 2304], P(('blk', 'head'))
- grad_attn_out: float32 [768, 768], P(('blk', 'head'))
- grad_norm_cross: float32 [768], P(('blk', 'head'))
- grad_cross_q: float32 [768, 768], P(('blk', 'head'))
- grad_cross_kv: float32 [768, 1536], P(('blk', 'head'))
- grad_cross_out: float32 [768, 768], P(('blk', 'head'))
- grad_norm_mlp: float32 [768], P(('blk', 'head'))
- grad_up: float32 [768, 3072], P(('blk', 'head'))
- grad_down: float32 [3072, 768], P(('blk', 'head'))
The draws below stay inside these ranges and needn't reach their ends.
Inputs may be any that keep to these rules, and one draw needn't show every extreme that they name: `segment_ids`: along each micro-batch's sequence the numbers never fall and count documents from 0; each document has 1 to 2000 tokens, and one has exactly 2000.
All inputs are finite; a program needn't handle non-finite values. No bound on the sum of `neighbour_valid` on one device may be relied on, other than what follows from the above.
Results may differ from the reference program's by a relative error of at most 0.024.
Values may be sent and summed in bfloat16 or wider, within the bound.
A program may use at most 256 MiB of HBM per device.

```python
import math
import jax
import jax.numpy as jnp
import numpy as np
from jax import lax

D = 768
HEADS = 12
HEAD_DIM = 64
FF = 3072
SPAN = 64
NEIGHBOURS = 2
NEIGH_LEN = 128
DOC_MAX = 2000
MICRO = 2
SEQ = 4096
SPANS = 64
DOCS = 5
QROWS = 512


def touch_ends(drawn, own_key, least, largest):
    longest = drawn.shape.index(max(drawn.shape))
    spots = []
    for shift in (0, 1):
        where = [jax.random.randint(jax.random.fold_in(own_key, axis), (), 0, length) for axis, length in enumerate(drawn.shape)]
        where[longest] = (where[longest] + shift) % drawn.shape[longest]
        spots.append(tuple(where))
    return drawn.at[spots[0]].set(least).at[spots[1]].set(largest)


def levels(own_key, dims, split, least, top_value):
    def one(axis_at, shards_of):
        draws = jax.random.uniform(jax.random.fold_in(jax.random.fold_in(own_key, 6), axis_at), (shards_of,), jnp.float32, least / len(split), top_value / len(split))
        return jnp.repeat(jnp.exp(draws), dims[axis_at] // shards_of).reshape((-1,) + (1,) * (len(dims) - axis_at - 1))

    factor_of = one(*split[0])
    for cut in split[1:]:
        factor_of = factor_of * one(*cut)
    return factor_of


def length_profile(number_of, total, most, lean):
    portions = [(1 << 20) // math.isqrt(standing ** lean) + 1 for standing in range(2, number_of + 1)]
    surplus, holding = total - most - (number_of - 1), [1] * (number_of - 1)
    while surplus > 0:
        movable = [i for i in range(number_of - 1) if holding[i] < most]
        mass, budget = sum([portions[i] for i in movable]), surplus
        for i in movable:
            addition = min(most - holding[i], max(1, budget * portions[i] // mass), surplus)
            holding[i] = holding[i] + addition
            surplus = surplus - addition
    return np.array([most] + holding)


def ragged_sizes(stream_key, count, total, bound, slope):
    if count == 2:
        one = jax.random.randint(stream_key, (), max(1, total - bound), min(bound, total - 1) + 1)
        return jnp.stack([one, total - one])
    tallies = jnp.asarray(length_profile(count, total, bound, slope), jnp.int32)
    couples = (count - 1) // 2
    source_of, receiver = tallies[1:1 + 2 * couples:2], tallies[2:2 + 2 * couples:2]
    margin = jnp.minimum(source_of - 1, bound - receiver)
    moved = jax.random.randint(jax.random.fold_in(stream_key, 1), (couples,), 0, 1 << 20) % (margin + 1)
    tallies = tallies.at[1:1 + 2 * couples:2].set(source_of - moved).at[2:2 + 2 * couples:2].set(receiver + moved)
    return tallies[jax.random.permutation(jax.random.fold_in(stream_key, 2), count)]


def gaussian(key, shape, scale, limit, split=(), kind=jnp.bfloat16):
    drawn = jax.random.normal(key, shape, jnp.float32) * scale
    if len(split) > 0:
        drawn = levels(key, shape, split, -0.22, 0.18) * drawn
    return jnp.clip(drawn, min=-limit, max=limit).astype(kind)


def setup_inputs(seed: int = 0) -> dict:
    streams_of = jax.random.split(jax.random.key(seed), 16)
    hidden_in = gaussian(streams_of[0], (MICRO, SEQ, D), 1.0, 6.0, ((1, 32),))
    segment_ids = jax.vmap(lambda own: jnp.searchsorted(jnp.cumsum(ragged_sizes(own, DOCS, SEQ, DOC_MAX, 1)), jnp.arange(SEQ), side="right"))(jax.random.split(streams_of[1], MICRO)).reshape((MICRO, SEQ)).astype(jnp.int32)
    neighbour_valid = touch_ends((jax.random.randint(streams_of[2], (MICRO, SPANS), 0, 4) < 3).astype(jnp.int32), jax.random.fold_in(streams_of[2], 1), 0, 1)
    neighbours = gaussian(streams_of[3], (MICRO, SPANS, NEIGHBOURS, NEIGH_LEN, D), 1.0, 6.0, ((1, 32),))
    out_grad = gaussian(streams_of[4], (MICRO, SEQ, D), 1.0, 6.0, ((1, 32),))
    norm_attn = jnp.clip(1.0 + 0.18 * jax.random.normal(streams_of[5], (D,), jnp.float32), 0.099609375, 1.8984375).astype(jnp.bfloat16)
    w_qkv = gaussian(streams_of[6], (D, 3 * D), D ** -0.5, 0.21875, ((0, 32),))
    w_attn_out = gaussian(streams_of[7], (D, D), (D // 48) ** -0.5, 1.5, ((0, 32),))
    norm_cross = jnp.clip(1.0 + 0.18 * jax.random.normal(streams_of[8], (D,), jnp.float32), 0.099609375, 1.8984375).astype(jnp.bfloat16)
    w_cross_q = gaussian(streams_of[9], (D, D), D ** -0.5, 0.21875, ((0, 32),))
    w_cross_kv = gaussian(streams_of[10], (D, 2 * D), D ** -0.5, 0.21875, ((0, 32),))
    w_cross_out = gaussian(streams_of[11], (D, D), (D // 96) ** -0.5, 2.0, ((0, 32),))
    norm_mlp = jnp.clip(1.0 + 0.18 * jax.random.normal(streams_of[12], (D,), jnp.float32), 0.099609375, 1.8984375).astype(jnp.bfloat16)
    w_up = gaussian(streams_of[13], (D, FF), D ** -0.5, 0.21875, ((0, 32),))
    w_down = gaussian(streams_of[14], (FF, D), FF ** -0.5, 0.109375, ((0, 32),))
    return {"hidden_in": hidden_in, "segment_ids": segment_ids, "neighbour_valid": neighbour_valid, "neighbours": neighbours, "out_grad": out_grad, "norm_attn": norm_attn, "w_qkv": w_qkv, "w_attn_out": w_attn_out, "norm_cross": norm_cross, "w_cross_q": w_cross_q, "w_cross_kv": w_cross_kv, "w_cross_out": w_cross_out, "norm_mlp": norm_mlp, "w_up": w_up, "w_down": w_down}


@jax.custom_vjp
def low(v):
    return lax.optimization_barrier(v.astype(jnp.bfloat16)).astype(jnp.float32)

@jax.custom_vjp
def low_back(v):
    return v

def low_keep(v):
    return (low(v), None)

def low_pass(kept, grad):
    return (grad,)

def back_keep(v):
    return (v, None)

def back_low(kept, grad):
    return (low(grad),)
low.defvjp(low_keep, low_pass)
low_back.defvjp(back_keep, back_low)

def matmul(left, right):
    return jnp.dot(left, right, precision=lax.Precision.HIGHEST)

def layer_norm(values, norm_gain):
    centred = values - lax.optimization_barrier(jnp.mean(values, axis=-1, keepdims=True))
    spread = lax.optimization_barrier(jnp.mean(centred * centred, axis=-1, keepdims=True))
    return centred * lax.rsqrt(spread + 1e-05) * norm_gain

def doc_positions(seg_ids):
    length = seg_ids.shape[0]
    token_index = jnp.arange(length, dtype=jnp.int32)
    starts = jnp.concatenate([jnp.ones((1,), jnp.bool_), seg_ids[1:] != seg_ids[:-1]])
    first_index = lax.cummax(jnp.where(starts, token_index, 0), axis=0)
    return token_index - first_index

def rotary(values, positions):
    half_dim = values.shape[-1] // 2
    frequency = jnp.exp(jnp.arange(half_dim, dtype=jnp.float32) * (-2.0 * math.log(10000.0) / values.shape[-1]))
    angles = positions.astype(jnp.float32)[:, None] * frequency[None, :]
    cosine = jnp.cos(angles)[:, None, :]
    sine_part = jnp.sin(angles)[:, None, :]
    first_half = values[..., :half_dim]
    second_half = values[..., half_dim:]
    return jnp.concatenate([first_half * cosine - second_half * sine_part, second_half * cosine + first_half * sine_part], axis=-1)

def self_attention(queries, key_rows, value_rows, seg_ids):
    score_scale = 1.0 / math.sqrt(HEAD_DIM)
    key_pad = (DOC_MAX + QROWS - 2) // QROWS * QROWS
    window = key_pad + QROWS
    keys_padded = jnp.concatenate([jnp.zeros((key_pad, HEADS, HEAD_DIM), key_rows.dtype), key_rows], axis=0)
    values_padded = jnp.concatenate([jnp.zeros((key_pad, HEADS, HEAD_DIM), value_rows.dtype), value_rows], axis=0)
    segs_padded = jnp.concatenate([jnp.full((key_pad,), -1, jnp.int32), seg_ids], axis=0)

    def one_block(block_number):
        start = (block_number * QROWS).astype(jnp.int32)
        query_block = lax.dynamic_slice_in_dim(queries, start, QROWS, 0)
        key_block = lax.dynamic_slice_in_dim(keys_padded, start, window, 0)
        value_block = lax.dynamic_slice_in_dim(values_padded, start, window, 0)
        query_segs = lax.dynamic_slice_in_dim(seg_ids, start, QROWS, 0)
        key_segs = lax.dynamic_slice_in_dim(segs_padded, start, window, 0)
        scores = low_back(jnp.einsum('qhd,khd->hqk', query_block, key_block, precision=lax.Precision.HIGHEST) * score_scale)
        query_place = jnp.arange(QROWS, dtype=jnp.int32)[:, None] + key_pad
        key_place = jnp.arange(window, dtype=jnp.int32)[None, :]
        allowed = (query_segs[:, None] == key_segs[None, :]) & (key_place <= query_place)
        scores = jnp.where(allowed[None], scores, -1e+30)
        attn_probs = jax.nn.softmax(scores, axis=-1)
        return jnp.einsum('hqk,khd->qhd', low(attn_probs), value_block, precision=lax.Precision.HIGHEST)
    blocks = lax.map(jax.checkpoint(one_block), jnp.arange(SEQ // QROWS, dtype=jnp.int32))
    return blocks.reshape(SEQ, HEADS, HEAD_DIM)

def cross_attention(queries, neigh_rows, span_flags, w_cross_kv):
    score_scale = 1.0 / math.sqrt(HEAD_DIM)
    per_block = QROWS // SPAN
    pair_rows = NEIGHBOURS * NEIGH_LEN
    shifted = jnp.concatenate([queries[SPAN - 1:], jnp.zeros((SPAN - 1, D), queries.dtype)], axis=0)
    grouped = shifted.reshape(SEQ // QROWS, per_block, SPAN, HEADS, HEAD_DIM)
    neigh_grouped = neigh_rows.reshape(SEQ // QROWS, per_block, pair_rows, D)
    flag_grouped = span_flags.reshape(SEQ // QROWS, per_block)

    def one_group(pieces):
        query_block, neigh_block, flag_block = pieces
        pairs = low_back(low(jnp.einsum('cnd,de->cne', neigh_block, w_cross_kv, precision=lax.Precision.HIGHEST)))
        key_block = pairs[..., :D].reshape(per_block, pair_rows, HEADS, HEAD_DIM)
        value_block = pairs[..., D:].reshape(per_block, pair_rows, HEADS, HEAD_DIM)
        scores = low_back(jnp.einsum('cqhd,ckhd->chqk', query_block, key_block, precision=lax.Precision.HIGHEST) * score_scale)
        attn_probs = jax.nn.softmax(scores, axis=-1)
        mixed_rows = jnp.einsum('chqk,ckhd->cqhd', low(attn_probs), value_block, precision=lax.Precision.HIGHEST)
        return mixed_rows * flag_block[:, None, None, None]
    result = lax.map(jax.checkpoint(one_group), (grouped, neigh_grouped, flag_grouped))
    result = result.reshape(SEQ, D)
    return jnp.concatenate([jnp.zeros((SPAN - 1, D), result.dtype), result[:SEQ - SPAN + 1]], axis=0)

def decoder_layer(hidden, neigh_rows, weight_list, seg_ids, span_flags):
    norm_attn, w_qkv, w_attn_out, norm_cross, w_cross_q, w_cross_kv, w_cross_out, norm_mlp, w_up, w_down = weight_list
    positions = doc_positions(seg_ids)
    normed = low(layer_norm(hidden, norm_attn))
    raw_qkv = low_back(matmul(normed, w_qkv)).reshape(SEQ, 3, HEADS, HEAD_DIM)
    rotated = jnp.stack([rotary(raw_qkv[:, 0], positions), rotary(raw_qkv[:, 1], positions), raw_qkv[:, 2]], axis=1)
    sent = low_back(low(rotated))
    attended = low_back(low(self_attention(sent[:, 0], sent[:, 1], sent[:, 2], seg_ids)))
    after_attn = hidden + low_back(matmul(attended.reshape(SEQ, D), w_attn_out))
    normed_cross = low(layer_norm(after_attn, norm_cross))
    cross_query = low_back(low(matmul(normed_cross, w_cross_q)))
    cross_mixed = low_back(low(cross_attention(cross_query, neigh_rows, span_flags, w_cross_kv)))
    after_cross = after_attn + low_back(matmul(cross_mixed, w_cross_out))
    normed_mlp = low(layer_norm(after_cross, norm_mlp))
    mlp_upper = low_back(matmul(normed_mlp, w_up))
    activated = low(jax.nn.gelu(mlp_upper, approximate=True))
    return after_cross + low_back(matmul(activated, w_down))

def reference(hidden_in, segment_ids, neighbour_valid, neighbours, out_grad, norm_attn, w_qkv, w_attn_out, norm_cross, w_cross_q, w_cross_kv, w_cross_out, norm_mlp, w_up, w_down):
    weight_list = tuple((weight.astype(jnp.float32) for weight in (norm_attn, w_qkv, w_attn_out, norm_cross, w_cross_q, w_cross_kv, w_cross_out, norm_mlp, w_up, w_down)))
    outputs = []
    input_grads = []
    neigh_grads = []
    grad_totals = None
    for micro_index in range(MICRO):
        hidden = hidden_in[micro_index].astype(jnp.float32)
        neigh_rows = neighbours[micro_index].astype(jnp.float32).reshape(SPANS, NEIGHBOURS * NEIGH_LEN, D)
        span_flags = neighbour_valid[micro_index].astype(jnp.float32)
        seg_ids = segment_ids[micro_index]

        def forward(hidden_value, neigh_value, weight_value):
            return decoder_layer(hidden_value, neigh_value, weight_value, seg_ids, span_flags)
        result, pullback = jax.vjp(forward, hidden, neigh_rows, weight_list)
        grad_hidden, grad_neigh, grad_weights = pullback(out_grad[micro_index].astype(jnp.float32))
        outputs.append(result.astype(jnp.bfloat16))
        input_grads.append(grad_hidden.astype(jnp.bfloat16))
        neigh_grads.append(grad_neigh.reshape(SPANS, NEIGHBOURS, NEIGH_LEN, D).astype(jnp.bfloat16))
        if grad_totals is None:
            grad_totals = grad_weights
        else:
            grad_totals = jax.tree.map(lambda running, addend: running + addend, grad_totals, grad_weights)
    return (jnp.stack(outputs), jnp.stack(input_grads), jnp.stack(neigh_grads), grad_totals[0], grad_totals[1], grad_totals[2], grad_totals[3], grad_totals[4], grad_totals[5], grad_totals[6], grad_totals[7], grad_totals[8], grad_totals[9])
```

```python
import functools
import math

import jax
import jax.numpy as jnp
from jax import lax
from jax.experimental import pallas as pl
from jax.experimental.pallas import tpu as pltpu
from jax.sharding import PartitionSpec as P

MESH = pl.DeviceIdType.MESH
ANY = pl.BlockSpec(memory_space=pl.ANY)


def coords():
    blk = lax.axis_index("blk")
    return blk // 4, (blk // 2) % 2, blk % 2, lax.axis_index("head")


def place(z, y, c, x):
    return (z * 4 + y * 2 + c, x)


def loop(count, body):
    if count <= 8:
        for step in range(count):
            body(step)
    else:
        lax.fori_loop(0, count, lambda step, carry: (body(step), carry)[1], 0)


def all_barrier(total, me):
    barrier = pltpu.get_barrier_semaphore()

    def greet(step, carry):
        peer = lax.rem(me + step, total)
        pl.semaphore_signal(
            barrier, inc=1, device_id=(peer // 2, lax.rem(peer, 2)), device_id_type=MESH
        )
        return carry

    lax.fori_loop(1, total, greet, 0)
    pl.semaphore_wait(barrier, total - 1)


def remote(src, dst, send, recv, where):
    return pltpu.make_async_remote_copy(
        src_ref=src, dst_ref=dst, send_sem=send, recv_sem=recv, device_id=where, device_id_type=MESH
    )


def gather_kernel(depth, items, *refs):
    count = len(items)
    w_refs = refs[:5]
    small_ref, hid_ref, grad_ref = refs[5:8]
    out_refs = refs[8:11]
    small_out, lead_hid, lead_grad = refs[11:14]
    own_sem, send_sem, recv_sem, misc_sem, lead_send, lead_recv = refs[14:]
    z, y, c, x = coords()
    total = depth * 8
    me = lax.axis_index("blk") * 2 + lax.axis_index("head")
    rows_per = w_refs[0].shape[0]

    def view(item, zs, ys, cs, xs):
        buffer, first, last, kind = item
        return out_refs[buffer].at[pl.ds(first, last - first), zs, ys, cs, xs]

    all_barrier(total, me)
    own_small = pltpu.make_async_copy(small_ref, small_out.at[me], misc_sem.at[1])
    own_small.start()

    def send_small(step, carry):
        peer = lax.rem(me + step, total)
        remote(
            small_ref, small_out.at[me], misc_sem.at[0], misc_sem.at[1], (peer // 2, lax.rem(peer, 2))
        ).start()
        return carry

    own = []
    for index, item in enumerate(items):
        buffer, first, last, kind = item
        width = out_refs[buffer].shape[-1]
        copies = []
        for block in range(first, last):
            if buffer == 1:
                src = w_refs[1 + block]
            else:
                src = w_refs[2 * buffer].at[:, pl.ds(block * width, width)]
            copies.append((src, out_refs[buffer].at[block, z, y, c, x]))
        for src, dst in copies:
            copy = pltpu.make_async_copy(src, dst, own_sem.at[index])
            copy.start()
        own.append(pltpu.make_async_copy(view(item, z, y, c, x), view(item, z, y, c, x), own_sem.at[index]))
    lax.fori_loop(1, total, send_small, 0)
    prev = lax.rem(me + total - 1, total)
    prev_at = (prev // 2, lax.rem(prev, 2))
    leads = [
        remote(hid_ref.at[:, pl.ds(0, 64)], lead_hid, lead_send.at[0], lead_recv.at[0], prev_at),
        remote(grad_ref.at[:, pl.ds(0, 64)], lead_grad, lead_send.at[1], lead_recv.at[1], prev_at),
    ]

    whole = slice(None)

    def phase_one(index):
        own[index].wait()
        item = items[index]

        def send(step):
            other = lax.rem(z + step + 1, depth)
            remote(
                view(item, z, y, c, x), view(item, z, y, c, x),
                send_sem.at[index, 0], recv_sem.at[index, 0], place(other, y, c, x),
            ).start()

        loop(depth - 1, send)

    def bulk(index, phase):
        item = items[index]
        first_x = item[3] == 0
        if phase == 1:
            ref = view(item, whole, y, c, x)
            where = place(z, y, c, 1 - x) if first_x else place(z, 1 - y, c, x)
        elif phase == 2:
            ref = view(item, whole, y, c, whole) if first_x else view(item, whole, whole, c, x)
            where = place(z, 1 - y, c, x) if first_x else place(z, y, c, 1 - x)
        else:
            ref = view(item, whole, whole, c, whole)
            where = place(z, y, 1 - c, x)
        return remote(ref, ref, send_sem.at[index, phase], recv_sem.at[index, phase], where)

    def arrived(index, phase):
        item = items[index]
        if phase == 0:
            ref = view(item, pl.ds(0, depth - 1), y, c, x)
            pltpu.make_async_copy(ref, ref, recv_sem.at[index, 0]).wait()
        else:
            bulk(index, phase).wait_recv()

    def sent(index, phase):
        item = items[index]
        if phase == 0:
            ref = view(item, pl.ds(0, depth - 1), y, c, x)
            pltpu.make_async_copy(ref, ref, send_sem.at[index, 0]).wait()
        else:
            bulk(index, phase).wait_send()

    pairs = (count + 1) // 2
    for step in range(pairs + 2 * 4):
        for phase in range(4, -1, -1):
            pair = step - 2 * phase
            if not 0 <= pair < pairs:
                continue
            for index in range(2 * pair, min(2 * pair + 2, count)):
                if phase == 0:
                    phase_one(index)
                else:
                    arrived(index, phase - 1)
                    if phase < 4:
                        bulk(index, phase).start()
        if step == 0:
            for lead in leads:
                lead.start()
    for index in range(count):
        for phase in range(4):
            sent(index, phase)
    for lead in leads:
        lead.wait()
    pltpu.make_async_copy(small_out, small_out, misc_sem.at[1]).wait()
    rest = small_out.at[pl.ds(0, total - 1)]
    pltpu.make_async_copy(rest, rest, misc_sem.at[0]).wait()


def gather_all(depth, w_qkv, w_attn_out, w_cross_q, w_cross_out, w_kv, small, hidden, grads):
    total = depth * 8
    rows = w_qkv.shape[0]
    items = [
        (0, 0, 3, 0), (0, 3, 6, 1),
        (2, 0, 1, 0), (2, 1, 2, 1),
        (1, 0, 1, 0), (1, 1, 2, 1),
        (1, 2, 3, 0),
    ]
    shapes = [
        (6, depth, 2, 2, 2, rows, w_qkv.shape[1] // 6),
        (3, depth, 2, 2, 2, rows, w_attn_out.shape[1]),
        (2, depth, 2, 2, 2, rows, w_kv.shape[1] // 2),
    ]
    lead_shape = (hidden.shape[0], 64, hidden.shape[2])
    outs = [jax.ShapeDtypeStruct(shape, jnp.bfloat16) for shape in shapes]
    outs += [jax.ShapeDtypeStruct((total,) + small.shape, small.dtype)]
    outs += [jax.ShapeDtypeStruct(lead_shape, jnp.bfloat16)] * 2
    count = len(items)
    return pl.pallas_call(
        functools.partial(gather_kernel, depth, items),
        out_shape=outs,
        in_specs=[ANY] * 8,
        out_specs=[ANY] * 6,
        scratch_shapes=[
            pltpu.SemaphoreType.DMA((count,)),
            pltpu.SemaphoreType.DMA((count, 4)),
            pltpu.SemaphoreType.DMA((count, 4)),
            pltpu.SemaphoreType.DMA((2,)),
            pltpu.SemaphoreType.DMA((2,)),
            pltpu.SemaphoreType.DMA((2,)),
        ],
        compiler_params=pltpu.CompilerParams(collective_id=0, has_side_effects=True),
    )(w_qkv, w_attn_out, w_cross_q, w_cross_out, w_kv, small, hidden, grads)


def unit_of(device, total):
    if total == 32:
        depth = device // 8
        middle = (depth == 1) | (depth == 2)
        end = 16 + (depth // 3) * 4 + (lax.rem(device, 8) // 4) * 2 + lax.rem(device, 2)
        unit = jnp.where(middle, device - 8, end)
        return unit, middle | (lax.rem(device // 2, 2) == 0)
    stride = total // UNITS
    return jnp.minimum(device // stride, UNITS - 1), (lax.rem(device, stride) == 0) & (device // stride < UNITS)


def to_units_kernel(total, src, dst, send_sem, recv_sem):
    me = lax.axis_index("blk") * 2 + lax.axis_index("head")
    mine, holder = unit_of(me, total)
    all_barrier(total, me)
    lanes = src.shape[-1]

    def slot(device):
        return dst.at[:, :, pl.ds(pl.multiple_of(device * lanes, 128), lanes)]

    @pl.when(holder)
    def _():
        pltpu.make_async_copy(src.at[mine], slot(me), recv_sem).start()

    def send(step, carry):
        peer = lax.rem(me + step, total)
        unit, held = unit_of(peer, total)

        @pl.when(held)
        def _():
            remote(src.at[unit], slot(me), send_sem, recv_sem, (peer // 2, lax.rem(peer, 2))).start()

        return carry

    lax.fori_loop(1, total, send, 0)

    @pl.when(holder)
    def _():
        part = src.at[pl.ds(0, UNITS - 1)]
        pltpu.make_async_copy(dst, dst, recv_sem).wait()
        pltpu.make_async_copy(part, part, send_sem).wait()

    @pl.when(jnp.logical_not(holder))
    def _():
        pltpu.make_async_copy(src, src, send_sem).wait()


def to_units(total, message, collective):
    units, parts, width, lanes = message.shape
    return pl.pallas_call(
        functools.partial(to_units_kernel, total),
        out_shape=jax.ShapeDtypeStruct((parts, width, lanes * total), message.dtype),
        in_specs=[ANY],
        out_specs=ANY,
        scratch_shapes=[pltpu.SemaphoreType.DMA, pltpu.SemaphoreType.DMA],
        compiler_params=pltpu.CompilerParams(collective_id=collective, has_side_effects=True),
    )(message)


def to_tokens_kernel(total, extras, *refs):
    src = refs[0]
    extra_in = refs[1 : 1 + extras]
    dst = refs[1 + extras]
    extra_out = refs[2 + extras : 2 + 2 * extras]
    send_sem, recv_sem, extra_send, extra_recv = refs[2 + 2 * extras :]
    me = lax.axis_index("blk") * 2 + lax.axis_index("head")
    mine, holder = unit_of(me, total)
    all_barrier(total, me)
    lanes = dst.shape[-1]
    after = lax.rem(me + 1, total)
    moves = [
        remote(
            extra_in[index], extra_out[index], extra_send.at[index], extra_recv.at[index],
            (after // 2, lax.rem(after, 2)),
        )
        for index in range(extras)
    ]
    for move in moves:
        move.start()

    def slot(device):
        return src.at[:, :, pl.ds(pl.multiple_of(device * lanes, 128), lanes)]

    @pl.when(holder)
    def _():
        pltpu.make_async_copy(slot(me), dst.at[mine], recv_sem).start()

        def send(step, carry):
            peer = lax.rem(me + step, total)
            remote(
                slot(peer), dst.at[mine], send_sem, recv_sem, (peer // 2, lax.rem(peer, 2))
            ).start()
            return carry

        lax.fori_loop(1, total, send, 0)

    pltpu.make_async_copy(dst, dst, recv_sem).wait()

    @pl.when(holder)
    def _():
        part = src.at[:, :, pl.ds(0, lanes * (total - 1))]
        pltpu.make_async_copy(part, part, send_sem).wait()

    for move in moves:
        move.wait()


def to_tokens(total, units, extra, collective):
    parts, width, length = units.shape
    count = len(extra)
    result = jax.ShapeDtypeStruct((UNITS, parts, width, length // total), units.dtype)
    return pl.pallas_call(
        functools.partial(to_tokens_kernel, total, count),
        out_shape=[result] + [jax.ShapeDtypeStruct(e.shape, e.dtype) for e in extra],
        in_specs=[ANY] * (1 + count),
        out_specs=[ANY] * (1 + count),
        scratch_shapes=[
            pltpu.SemaphoreType.DMA,
            pltpu.SemaphoreType.DMA,
            pltpu.SemaphoreType.DMA((max(count, 1),)),
            pltpu.SemaphoreType.DMA((max(count, 1),)),
        ],
        compiler_params=pltpu.CompilerParams(collective_id=collective, has_side_effects=True),
    )(units, *extra)


def scatter_kernel(depth, items, *refs):
    count = len(items)
    total = depth * 8
    d_refs = refs[:3]
    gain_ref = refs[3]
    out_refs = refs[4:7]
    gain_out = refs[7]
    own = refs[8 : 8 + count]
    got_core = refs[8 + count : 8 + 2 * count]
    got_one = refs[8 + 2 * count : 8 + 3 * count]
    got_two = refs[8 + 3 * count : 8 + 4 * count]
    got_z = refs[8 + 4 * count : 8 + 5 * count]
    gains, local_sem, send_sem, recv_sem, gain_sem = refs[8 + 5 * count :]
    z, y, c, x = coords()
    me = lax.axis_index("blk") * 2 + lax.axis_index("head")
    all_barrier(total, me)
    whole = slice(None)

    pltpu.make_async_copy(gain_ref.at[me], gains.at[me], gain_sem.at[1]).start()

    def send_gain(step, carry):
        peer = lax.rem(me + step, total)
        remote(
            gain_ref.at[peer], gains.at[me], gain_sem.at[0], gain_sem.at[1], (peer // 2, lax.rem(peer, 2))
        ).start()
        return carry

    def local(index):
        buffer, first, last, kind = items[index]
        src = d_refs[buffer].at[pl.ds(first, last - first), whole, whole, c]
        return pltpu.make_async_copy(src, own[index], local_sem.at[index])

    def core(index):
        buffer, first, last, kind = items[index]
        src = d_refs[buffer].at[pl.ds(first, last - first), whole, whole, 1 - c]
        return remote(
            src, got_core[index], send_sem.at[index, 0], recv_sem.at[index, 0], place(z, y, 1 - c, x)
        )

    def one(index):
        if items[index][3] == 0:
            src, where = own[index].at[whole, whole, 1 - y], place(z, 1 - y, c, x)
        else:
            src, where = own[index].at[whole, whole, whole, 1 - x], place(z, y, c, 1 - x)
        return remote(src, got_one[index], send_sem.at[index, 1], recv_sem.at[index, 1], where)

    def two(index):
        if items[index][3] == 0:
            src, where = own[index].at[whole, whole, y, 1 - x], place(z, y, c, 1 - x)
        else:
            src, where = own[index].at[whole, whole, 1 - y, x], place(z, 1 - y, c, x)
        return remote(src, got_two[index], send_sem.at[index, 2], recv_sem.at[index, 2], where)

    def send_z(index):
        def send(step):
            other = lax.rem(z + step + 1, depth)
            remote(
                own[index].at[whole, other, y, x], got_z[index].at[z],
                send_sem.at[index, 3], recv_sem.at[index, 3], place(other, y, c, x),
            ).start()

        loop(depth - 1, send)

    def add_into(target, source):
        target[...] = (target[...].astype(jnp.float32) + source[...].astype(jnp.float32)).astype(
            jnp.bfloat16
        )

    def sum_core(index):
        blocks = own[index].shape[0]

        def body(step):
            block, level = step // depth, lax.rem(step, depth)
            for row in range(2):
                for col in range(2):
                    add_into(own[index].at[block, level, row, col], got_core[index].at[block, level, row, col])

        lax.fori_loop(0, blocks * depth, lambda step, carry: (body(step), carry)[1], 0)

    def sum_one(index):
        blocks = own[index].shape[0]

        def body(step):
            block, level = step // depth, lax.rem(step, depth)
            for side in range(2):
                if items[index][3] == 0:
                    target = own[index].at[block, level, y, side]
                else:
                    target = own[index].at[block, level, side, x]
                add_into(target, got_one[index].at[block, level, side])

        lax.fori_loop(0, blocks * depth, lambda step, carry: (body(step), carry)[1], 0)

    def sum_two(index):
        blocks = own[index].shape[0]

        def body(step):
            block, level = step // depth, lax.rem(step, depth)
            add_into(own[index].at[block, level, y, x], got_two[index].at[block, level])

        lax.fori_loop(0, blocks * depth, lambda step, carry: (body(step), carry)[1], 0)

    def sum_z(index):
        buffer, first, last, kind = items[index]
        for block in range(last - first):
            running = own[index][block, z, y, x].astype(jnp.float32)

            def body(step, value):
                other = lax.rem(z + step, depth)
                return value + got_z[index][other, block].astype(jnp.float32)

            out_refs[buffer][first + block] = lax.fori_loop(1, depth, body, running)

    for index in range(count):
        local(index).start()
    pairs = (count + 1) // 2
    for step in range(pairs + 4):
        for phase in range(4, -1, -1):
            pair = step - phase
            if not 0 <= pair < pairs:
                continue
            for index in range(2 * pair, min(2 * pair + 2, count)):
                if phase == 0:
                    core(index).start()
                elif phase == 1:
                    local(index).wait()
                    core(index).wait_recv()
                    sum_core(index)
                    one(index).start()
                elif phase == 2:
                    one(index).wait_recv()
                    sum_one(index)
                    two(index).start()
                elif phase == 3:
                    two(index).wait_recv()
                    sum_two(index)
                    send_z(index)
                else:
                    landed = got_z[index].at[pl.ds(0, depth - 1)]
                    pltpu.make_async_copy(landed, landed, recv_sem.at[index, 3]).wait()
                    sum_z(index)
        if step == 0:
            lax.fori_loop(1, total, send_gain, 0)
    pltpu.make_async_copy(gains, gains, gain_sem.at[1]).wait()
    gain_out[...] = jnp.sum(gains[...], axis=0)
    for index in range(count):
        core(index).wait_send()
        one(index).wait_send()
        two(index).wait_send()
        gone = got_z[index].at[pl.ds(0, depth - 1)]
        pltpu.make_async_copy(gone, gone, send_sem.at[index, 3]).wait()
    rest = gains.at[pl.ds(0, total - 1)]
    pltpu.make_async_copy(rest, rest, gain_sem.at[0]).wait()


def scatter_all(depth, d_qkv, d_squares, d_kv, d_gains, collective):
    items = [
        (0, 0, 3, 0), (0, 3, 6, 1),
        (2, 0, 1, 0), (2, 1, 2, 1),
        (1, 0, 1, 0), (1, 1, 2, 1),
        (1, 2, 3, 0),
    ]
    count = len(items)
    parts = (d_qkv, d_squares, d_kv)
    own, core, one, two, along = [], [], [], [], []
    for buffer, first, last, kind in items:
        rows, width = parts[buffer].shape[-2:]
        blocks = last - first
        own.append(pltpu.VMEM((blocks, depth, 2, 2, rows, width), jnp.bfloat16))
        core.append(pltpu.VMEM((blocks, depth, 2, 2, rows, width), jnp.bfloat16))
        one.append(pltpu.VMEM((blocks, depth, 2, rows, width), jnp.bfloat16))
        two.append(pltpu.VMEM((blocks, depth, rows, width), jnp.bfloat16))
        along.append(pltpu.VMEM((depth, blocks, rows, width), jnp.bfloat16))
    outs = [jax.ShapeDtypeStruct((p.shape[0],) + p.shape[-2:], jnp.float32) for p in parts]
    outs.append(jax.ShapeDtypeStruct(d_gains.shape[1:], jnp.float32))
    vmem = pl.BlockSpec(memory_space=pltpu.VMEM)
    return pl.pallas_call(
        functools.partial(scatter_kernel, depth, items),
        out_shape=outs,
        in_specs=[ANY] * 4,
        out_specs=[vmem] * 4,
        scratch_shapes=own + core + one + two + along + [
            pltpu.VMEM(d_gains.shape, jnp.float32),
            pltpu.SemaphoreType.DMA((count,)),
            pltpu.SemaphoreType.DMA((count, 4)),
            pltpu.SemaphoreType.DMA((count, 4)),
            pltpu.SemaphoreType.DMA((2,)),
        ],
        compiler_params=pltpu.CompilerParams(
            collective_id=collective, has_side_effects=True, vmem_limit_bytes=60 * 2**20
        ),
    )(d_qkv, d_squares, d_kv, d_gains)


HEADS = 12
HEAD_DIM = 64
SPAN = 64
NEIGHBOURS = 2
NEIGH_LEN = 128
MICRO = 2
UNITS = MICRO * HEADS
AXES = ("blk", "head")
TILE = 256
LEAD = SPAN - 1
SCORE_SCALE = 1.0 / math.sqrt(HEAD_DIM)
LOG2E = math.log2(math.e)


def tile_at(ref, index, row):
    return ref[row, :, pl.ds(pl.multiple_of(index * TILE, TILE), TILE)]


def row_at(ref, index):
    return ref[:, pl.ds(pl.multiple_of(index * TILE, TILE), TILE)]


def tile_mask(key_tile, query_tile, first_row):
    key_place = key_tile * TILE + lax.broadcasted_iota(jnp.int32, (TILE, TILE), 0)
    query_place = query_tile * TILE + lax.broadcasted_iota(jnp.int32, (TILE, TILE), 1)
    return (key_place <= query_place) & (key_place >= first_row)


def attn_forward_kernel(low_ref, first_ref, qkv_ref, shifted_ref, mixed_ref, total_ref):
    tiles = qkv_ref.shape[-1] // TILE

    def one_query(query_tile, carry):
        query_t = tile_at(qkv_ref, query_tile, 0)
        first_row = row_at(first_ref, query_tile)

        def one_key(step, state):
            peak, weight, mixed = state
            key_tile = query_tile - step
            keys = tile_at(qkv_ref, key_tile, 1).T
            scores = jnp.dot(keys, query_t, preferred_element_type=jnp.float32) * (SCORE_SCALE * LOG2E)
            scores = jnp.where(tile_mask(key_tile, query_tile, first_row), scores, -1e30)
            new_peak = jnp.maximum(peak, jnp.max(scores, axis=0, keepdims=True))
            probs = jnp.exp2(scores - new_peak)
            fade = jnp.exp2(peak - new_peak)
            weight = weight * fade + jnp.sum(probs, axis=0, keepdims=True)
            mixed = mixed * fade + jnp.dot(
                tile_at(qkv_ref, key_tile, 2), probs.astype(jnp.bfloat16), preferred_element_type=jnp.float32
            )
            return new_peak, weight, mixed

        start = (
            jnp.full((1, TILE), -1e30, jnp.float32),
            jnp.zeros((1, TILE), jnp.float32),
            jnp.zeros((HEAD_DIM, TILE), jnp.float32),
        )
        steps = query_tile + 1 - low_ref[query_tile]
        peak, weight, mixed = lax.fori_loop(0, steps, one_key, start)
        columns = pl.ds(pl.multiple_of(query_tile * TILE, TILE), TILE)
        mixed_ref[:, columns] = mixed / weight
        total_ref[:, columns] = peak + jnp.log2(weight)
        return carry

    lax.fori_loop(0, tiles, one_query, 0)
    length = qkv_ref.shape[-1]

    def turn(step, carry):
        rows = pl.ds(pl.multiple_of(step * 16, 16), 16)
        shifted_ref[rows, :] = pltpu.roll(mixed_ref[rows, :], length - LEAD, 1).astype(jnp.bfloat16)
        return carry

    lax.fori_loop(0, HEAD_DIM // 16, turn, 0)


def attn_backward_kernel(
    low_ref, high_ref, first_ref, qkv_ref, shifted_ref, mixed_ref, total_ref, out_ref, grad_ref, dq_ref, delta_ref
):
    length = qkv_ref.shape[-1]
    tiles = length // TILE
    delta_ref[...] = jnp.zeros_like(delta_ref)

    def turn(step, carry):
        rows = pl.ds(pl.multiple_of(step * 16, 16), 16)
        grad = pltpu.roll(shifted_ref[rows, :].astype(jnp.float32), LEAD, 1)
        grad_ref[rows, :] = grad.astype(jnp.bfloat16)
        delta_ref[...] += jnp.sum(grad * mixed_ref[rows, :], axis=0, keepdims=True)
        dq_ref[rows, :] = jnp.zeros((16, length), jnp.float32)
        return carry

    lax.fori_loop(0, HEAD_DIM // 16, turn, 0)

    def one_key(key_tile, carry):
        key_t = tile_at(qkv_ref, key_tile, 1)
        keys = key_t.T
        values = tile_at(qkv_ref, key_tile, 2).T

        def one_query(query_tile, state):
            d_key, d_value = state
            query_t = tile_at(qkv_ref, query_tile, 0)
            grad_t = row_at(grad_ref, query_tile)
            scores = jnp.dot(keys, query_t, preferred_element_type=jnp.float32) * (SCORE_SCALE * LOG2E)
            allowed = tile_mask(key_tile, query_tile, row_at(first_ref, query_tile))
            probs = jnp.where(allowed, jnp.exp2(scores - row_at(total_ref, query_tile)), 0.0)
            d_probs = jnp.dot(values, grad_t, preferred_element_type=jnp.float32)
            d_scores = (probs * (d_probs - row_at(delta_ref, query_tile))).astype(jnp.bfloat16)
            d_value = d_value + jnp.dot(
                probs.astype(jnp.bfloat16), grad_t.T, preferred_element_type=jnp.float32
            )
            d_key = d_key + jnp.dot(d_scores, query_t.T, preferred_element_type=jnp.float32)
            columns = pl.ds(pl.multiple_of(query_tile * TILE, TILE), TILE)
            dq_ref[:, columns] += jnp.dot(key_t, d_scores, preferred_element_type=jnp.float32)
            return d_key, d_value

        zeros = jnp.zeros((TILE, HEAD_DIM), jnp.float32)
        d_key, d_value = lax.fori_loop(key_tile, high_ref[key_tile], one_query, (zeros, zeros))
        columns = pl.ds(pl.multiple_of(key_tile * TILE, TILE), TILE)
        out_ref[1, :, columns] = (d_key * SCORE_SCALE).T.astype(jnp.bfloat16)
        out_ref[2, :, columns] = d_value.T.astype(jnp.bfloat16)
        return carry

    lax.fori_loop(0, tiles, one_key, 0)

    def finish(step, carry):
        rows = pl.ds(pl.multiple_of(step * 16, 16), 16)
        out_ref[0, rows, :] = (dq_ref[rows, :] * SCORE_SCALE).astype(jnp.bfloat16)
        return carry

    lax.fori_loop(0, HEAD_DIM // 16, finish, 0)


SMEM = pl.BlockSpec(memory_space=pltpu.SMEM)
VMEM = pl.BlockSpec(memory_space=pltpu.VMEM)


def local_params():
    return pltpu.CompilerParams(vmem_limit_bytes=60 * 2**20)


def attn_forward(low, first, qkv):
    width, length = qkv.shape[1:]
    return pl.pallas_call(
        attn_forward_kernel,
        out_shape=[
            jax.ShapeDtypeStruct((width, length), jnp.bfloat16),
            jax.ShapeDtypeStruct((width, length), jnp.float32),
            jax.ShapeDtypeStruct((1, length), jnp.float32),
        ],
        in_specs=[SMEM, VMEM, VMEM],
        out_specs=[VMEM] * 3,
        compiler_params=local_params(),
        cost_estimate=pl.CostEstimate(flops=10**9, bytes_accessed=4 * 10**6, transcendentals=4 * 10**6),
    )(low, first, qkv)


def attn_backward(low, high, first, qkv, shifted, mixed, totals):
    width, length = qkv.shape[1:]
    return pl.pallas_call(
        attn_backward_kernel,
        out_shape=jax.ShapeDtypeStruct((3, width, length), jnp.bfloat16),
        in_specs=[SMEM, SMEM] + [VMEM] * 5,
        out_specs=VMEM,
        scratch_shapes=[
            pltpu.VMEM((width, length), jnp.bfloat16),
            pltpu.VMEM((width, length), jnp.float32),
            pltpu.VMEM((1, length), jnp.float32),
        ],
        compiler_params=local_params(),
        cost_estimate=pl.CostEstimate(flops=3 * 10**9, bytes_accessed=4 * 10**6, transcendentals=4 * 10**6),
    )(low, high, first, qkv, shifted, mixed, totals)


def layer_norm(values, norm_gain):
    centred = values - jnp.mean(values, axis=-1, keepdims=True)
    spread = jnp.mean(centred * centred, axis=-1, keepdims=True)
    return centred * lax.rsqrt(spread + 1e-05) * norm_gain


def norm_backward(values, norm_gain, grad_out):
    result, pullback = jax.vjp(layer_norm, values, norm_gain)
    return pullback(grad_out)


def gelu_tanh(values):
    return jax.nn.gelu(values, approximate=True)


def soft_forward(scores):
    maximum = jnp.max(scores, axis=-1, keepdims=True)
    exp_rows = jnp.exp(scores - maximum)
    row_total = jnp.sum(exp_rows, axis=-1, keepdims=True)
    return (exp_rows / row_total, maximum + jnp.log(row_total))


def soft_backward(scores, log_total, grad_probs):
    attn_probs = jnp.exp(scores - log_total)
    row_delta = jnp.sum(attn_probs * grad_probs, axis=-1, keepdims=True)
    return (attn_probs, (attn_probs * (grad_probs - row_delta)).astype(jnp.bfloat16))


def split_cross(query_groups, pair_groups):
    group_count, span_rows, model_width = query_groups.shape
    pair_rows = pair_groups.shape[1]
    query_rows = query_groups.reshape(group_count, span_rows, HEADS, HEAD_DIM)
    key_rows = pair_groups[..., :model_width].reshape(group_count, pair_rows, HEADS, HEAD_DIM)
    value_rows = pair_groups[..., model_width:].reshape(group_count, pair_rows, HEADS, HEAD_DIM)
    return (query_rows, key_rows, value_rows)


def cross_forward(query_groups, pair_groups, score_scale):
    group_count, span_rows, model_width = query_groups.shape
    query_rows, key_rows, value_rows = split_cross(query_groups, pair_groups)
    scores = (
        jnp.einsum("cqhd,ckhd->chqk", query_rows, key_rows, preferred_element_type=jnp.float32)
        * score_scale
    )
    attn_probs, log_total = soft_forward(scores)
    mixed_rows = jnp.einsum(
        "chqk,ckhd->cqhd",
        attn_probs.astype(jnp.bfloat16),
        value_rows,
        preferred_element_type=jnp.float32,
    )
    return (mixed_rows.reshape(group_count, span_rows, model_width), log_total)


def cross_backward(query_groups, pair_groups, log_total, grad_groups, score_scale):
    group_count, span_rows, model_width = query_groups.shape
    pair_rows = pair_groups.shape[1]
    query_rows, key_rows, value_rows = split_cross(query_groups, pair_groups)
    grad_rows = grad_groups.reshape(group_count, span_rows, HEADS, HEAD_DIM)
    scores = (
        jnp.einsum("cqhd,ckhd->chqk", query_rows, key_rows, preferred_element_type=jnp.float32)
        * score_scale
    )
    grad_probs = jnp.einsum(
        "cqhd,ckhd->chqk", grad_rows, value_rows, preferred_element_type=jnp.float32
    )
    attn_probs, grad_scores = soft_backward(scores, log_total, grad_probs)
    grad_query = (
        jnp.einsum("chqk,ckhd->cqhd", grad_scores, key_rows, preferred_element_type=jnp.float32)
        * score_scale
    )
    grad_key = (
        jnp.einsum("chqk,cqhd->ckhd", grad_scores, query_rows, preferred_element_type=jnp.float32)
        * score_scale
    )
    grad_value = jnp.einsum(
        "chqk,cqhd->ckhd",
        attn_probs.astype(jnp.bfloat16),
        grad_rows,
        preferred_element_type=jnp.float32,
    )
    grad_pairs = jnp.concatenate(
        [
            grad_key.reshape(group_count, pair_rows, model_width),
            grad_value.reshape(group_count, pair_rows, model_width),
        ],
        axis=-1,
    )
    return (grad_query.reshape(group_count, span_rows, model_width), grad_pairs)


def dot32(left, right):
    return jnp.dot(left, right, preferred_element_type=jnp.float32)


def outer(left, right):
    return jnp.einsum("td,te->de", left, right, preferred_element_type=jnp.float32)


def turn_heads(values, cosine, sine):
    first_half, second_half = values[:, :32], values[:, 32:]
    return jnp.concatenate(
        [first_half * cosine - second_half * sine, second_half * cosine + first_half * sine], axis=1
    )


def on_device(
    hidden_in,
    segment_ids,
    neighbour_valid,
    neighbours,
    out_grad,
    norm_attn,
    w_qkv,
    w_attn_out,
    norm_cross,
    w_cross_q,
    w_cross_kv,
    w_cross_out,
    norm_mlp,
    w_up,
    w_down,
):
    micro, tok_count, model_width = hidden_in.shape
    blk_count = lax.axis_size("blk")
    depth = blk_count // 4
    total = blk_count * 2
    length = tok_count * total
    row_count = micro * tok_count
    gain_rows = norm_attn.shape[0]
    span_count = tok_count // SPAN
    pair_rows = NEIGHBOURS * NEIGH_LEN
    device = lax.axis_index(AXES)

    up_full = lax.all_gather(w_up, AXES, axis=0, tiled=True)
    down_full = lax.all_gather(w_down, AXES, axis=0, tiled=True)

    small = jnp.zeros((16, 128), jnp.bfloat16)
    for row, gain in enumerate((norm_attn, norm_cross, norm_mlp)):
        small = small.at[row, :gain_rows].set(gain)
    small = small.at[3 : 3 + micro, :tok_count].set(segment_ids.astype(jnp.bfloat16))
    got_qkv, got_sq, got_kv, got_small, lead_hid, lead_grad = gather_all(
        depth, w_qkv, w_attn_out, w_cross_q, w_cross_out, w_cross_kv, small, hidden_in, out_grad
    )
    gains = got_small[:, :3, :gain_rows].astype(jnp.float32).transpose(1, 0, 2).reshape(3, model_width)
    gain_attn, gain_cross, gain_mlp = gains[0], gains[1], gains[2]
    seg_full = got_small[:, 3 : 3 + micro, :tok_count].transpose(1, 0, 2).reshape(micro, length)
    seg_full = seg_full.astype(jnp.int32)
    qkv_blocks = got_qkv.reshape(6, model_width, model_width // 2)
    squares = got_sq.reshape(3, model_width, model_width)
    attn_out_full, cross_q_full, cross_out_full = squares[0], squares[1], squares[2]
    kv_blocks = got_kv.reshape(2, model_width, model_width)

    token_index = device * tok_count + jnp.arange(tok_count, dtype=jnp.int32)
    first_of = jnp.sum(
        (seg_full[:, None, :] < segment_ids[:, :, None]).astype(jnp.int32), axis=-1
    )
    local_pos = token_index[None] - first_of
    frequency = jnp.exp(
        jnp.arange(HEAD_DIM // 2, dtype=jnp.float32) * (-2.0 * math.log(10000.0) / HEAD_DIM)
    )
    angles = frequency[:, None, None] * local_pos.astype(jnp.float32)[None]
    cosine, sine = jnp.cos(angles), jnp.sin(angles)

    unit, holder = unit_of(device, total)
    seg_unit = lax.dynamic_index_in_dim(seg_full, unit // HEADS, 0, keepdims=False)
    seg_tiles = seg_unit.reshape(length // TILE, TILE)
    tile_first = jnp.sum((seg_unit[None] < seg_tiles[:, :1]).astype(jnp.int32), axis=-1)
    inside = jnp.sum((seg_tiles[:, None, :] < seg_tiles[:, :, None]).astype(jnp.int32), axis=-1)
    tile_index = jnp.arange(length // TILE, dtype=jnp.int32)
    first_row = jnp.where(
        seg_tiles == seg_tiles[:, :1], tile_first[:, None], tile_index[:, None] * TILE + inside
    ).reshape(1, length)
    low = tile_first // TILE
    high = jnp.sum((low[None] <= tile_index[:, None]).astype(jnp.int32), axis=-1)
    low = jnp.where(holder, low, tile_index + 1)
    high = jnp.where(holder, high, 0)

    hidden = hidden_in.astype(jnp.float32)
    normed_attn = layer_norm(hidden, gain_attn).astype(jnp.bfloat16).reshape(row_count, model_width)
    raw = jnp.einsum("bde,td->bet", qkv_blocks, normed_attn, preferred_element_type=jnp.float32)
    raw = raw.reshape(3, HEADS, HEAD_DIM, micro, tok_count)
    rotated = jnp.stack(
        [turn_heads(raw[0], cosine, sine), turn_heads(raw[1], cosine, sine), raw[2]]
    ).astype(jnp.bfloat16)
    message = rotated.transpose(3, 1, 0, 2, 4).reshape(UNITS, 3, HEAD_DIM, tok_count)
    unit_qkv = to_units(total, message, 1)
    shifted, mixed, totals = attn_forward(low, first_row, unit_qkv)
    (attended_t,) = to_tokens(total, shifted[None], (), 2)
    attended_t = attended_t.reshape(micro, model_width, tok_count)

    def shift(rows, lead):
        return jnp.concatenate([rows[:, LEAD:], lead[:, :LEAD]], axis=1).reshape(row_count, model_width)

    hidden_s = shift(hidden_in, lead_hid).astype(jnp.float32)
    grad_low = shift(out_grad, lead_grad)
    cotangent = grad_low.astype(jnp.float32)
    after_attn = hidden_s + jnp.einsum(
        "mdt,de->mte", attended_t, attn_out_full, preferred_element_type=jnp.float32
    ).reshape(row_count, model_width)
    normed_cross = layer_norm(after_attn, gain_cross).astype(jnp.bfloat16)
    cross_query = dot32(normed_cross, cross_q_full).astype(jnp.bfloat16)
    neigh_rows = neighbours.reshape(micro * span_count * pair_rows, model_width)
    groups = micro * span_count
    pairs_local = jnp.concatenate(
        [dot32(neigh_rows, kv_blocks[0]).astype(jnp.bfloat16), dot32(neigh_rows, kv_blocks[1]).astype(jnp.bfloat16)],
        axis=1,
    ).reshape(groups, pair_rows, 2 * model_width)
    shifted_index = token_index + LEAD
    used = jnp.where(
        shifted_index[None] < length, jnp.repeat(neighbour_valid, SPAN, axis=1).astype(jnp.float32), 0.0
    ).reshape(row_count, 1)
    query_groups = cross_query.reshape(groups, SPAN, model_width)
    cross_rows, cross_total = cross_forward(query_groups, pairs_local, SCORE_SCALE)
    cross_mixed = (cross_rows.reshape(row_count, model_width) * used).astype(jnp.bfloat16)
    after_cross = after_attn + dot32(cross_mixed, cross_out_full)
    normed_mlp = layer_norm(after_cross, gain_mlp).astype(jnp.bfloat16)
    mlp_upper = dot32(normed_mlp, up_full)
    activated, gelu_pull = jax.vjp(gelu_tanh, mlp_upper)
    activated = activated.astype(jnp.bfloat16)
    result_rows = (after_cross + dot32(activated, down_full)).astype(jnp.bfloat16)
    result_rows = result_rows.reshape(micro, tok_count, model_width)
    d_activated = dot32(grad_low, down_full.T)
    d_upper = gelu_pull(d_activated)[0].astype(jnp.bfloat16)
    d_normed_mlp = dot32(d_upper, up_full.T)

    up_share = lax.psum_scatter(
        outer(normed_mlp, d_upper).astype(jnp.bfloat16), AXES, scatter_dimension=0, tiled=True
    ).astype(jnp.float32)
    down_share = lax.psum_scatter(
        outer(activated, grad_low).astype(jnp.bfloat16), AXES, scatter_dimension=0, tiled=True
    ).astype(jnp.float32)

    d_second_in, d_gain_mlp = norm_backward(after_cross, gain_mlp, d_normed_mlp)
    d_second = cotangent + d_second_in
    d_second_low = d_second.astype(jnp.bfloat16)
    d_mixed = dot32(d_second_low, cross_out_full.T).astype(jnp.bfloat16)
    d_groups = (d_mixed.astype(jnp.float32) * used).astype(jnp.bfloat16).reshape(groups, SPAN, model_width)
    grad_query_groups, d_pairs = cross_backward(
        query_groups, pairs_local, cross_total, d_groups, SCORE_SCALE
    )
    d_cross_query = grad_query_groups.reshape(row_count, model_width).astype(jnp.bfloat16)
    d_normed_cross = dot32(d_cross_query, cross_q_full.T)
    d_first_in, d_gain_cross = norm_backward(after_attn, gain_cross, d_normed_cross)
    d_first = d_second + d_first_in
    d_first_low = d_first.astype(jnp.bfloat16).reshape(micro, tok_count, model_width)
    d_attended_t = jnp.einsum(
        "de,mte->mdt", attn_out_full, d_first_low, preferred_element_type=jnp.float32
    ).astype(jnp.bfloat16)
    unit_grad = to_units(total, d_attended_t.reshape(UNITS, 1, HEAD_DIM, tok_count), 3)
    unit_back = attn_backward(low, high, first_row, unit_qkv, unit_grad[0], mixed, totals)
    d_first = d_first.reshape(micro, tok_count, model_width)
    sent_t, tail_first, tail_result = to_tokens(
        total, unit_back, (d_first[:, tok_count - 64 :], result_rows[:, tok_count - 64 :]), 4
    )

    def unshift(rows, tail):
        return jnp.concatenate([tail[:, 1:], rows[:, : tok_count - LEAD]], axis=1)

    output = unshift(result_rows, tail_result)
    d_first_home = unshift(d_first, tail_first)
    sent_t = sent_t.reshape(micro, HEADS, 3, HEAD_DIM, tok_count).transpose(2, 1, 3, 0, 4)
    sent_t = sent_t.astype(jnp.float32)
    raw_t = jnp.stack(
        [turn_heads(sent_t[0], cosine, -sine), turn_heads(sent_t[1], cosine, -sine), sent_t[2]]
    ).astype(jnp.bfloat16).reshape(6, model_width // 2, row_count)
    d_normed_attn = jnp.einsum("bet,bde->td", raw_t, qkv_blocks, preferred_element_type=jnp.float32)
    d_hidden_in, d_gain_attn = norm_backward(
        hidden, gain_attn, d_normed_attn.reshape(micro, tok_count, model_width)
    )
    grad_in = (d_first_home + d_hidden_in).astype(jnp.bfloat16)

    d_pairs_low = d_pairs.astype(jnp.bfloat16).reshape(groups * pair_rows, 2 * model_width)
    d_keys, d_values = d_pairs_low[:, :model_width], d_pairs_low[:, model_width:]
    d_neigh = (
        jnp.einsum("te,de->td", d_keys, kv_blocks[0], preferred_element_type=jnp.float32)
        + jnp.einsum("te,de->td", d_values, kv_blocks[1], preferred_element_type=jnp.float32)
    ).astype(jnp.bfloat16)
    grad_neighbours = d_neigh.reshape(neighbours.shape)

    def blocks_of(array):
        return array.astype(jnp.bfloat16).reshape(
            array.shape[0], depth, 2, 2, 2, gain_rows, array.shape[-1]
        )

    d_qkv = jnp.einsum("td,bet->bde", normed_attn, raw_t, preferred_element_type=jnp.float32)
    d_sq = jnp.stack(
        [
            jnp.einsum("mdt,mte->de", attended_t, d_first_low, preferred_element_type=jnp.float32),
            outer(normed_cross, d_cross_query),
            outer(cross_mixed, d_second_low),
        ]
    )
    d_kv = jnp.stack([outer(neigh_rows, d_keys), outer(neigh_rows, d_values)])
    d_gains = jnp.stack([d_gain_attn, d_gain_cross, d_gain_mlp]).reshape(3, total, gain_rows)
    d_gains = jnp.zeros((total, 8, 128), jnp.float32).at[:, :3, :gain_rows].set(d_gains.transpose(1, 0, 2))
    s_qkv, s_sq, s_kv, s_gain = scatter_all(
        depth, blocks_of(d_qkv), blocks_of(d_sq), blocks_of(d_kv), d_gains, 5
    )
    return (
        output,
        grad_in,
        grad_neighbours,
        s_gain[0, :gain_rows],
        s_qkv.transpose(1, 0, 2).reshape(gain_rows, 3 * model_width),
        s_sq[0],
        s_gain[1, :gain_rows],
        s_sq[1],
        s_kv.transpose(1, 0, 2).reshape(gain_rows, 2 * model_width),
        s_sq[2],
        s_gain[2, :gain_rows],
        up_share,
        down_share,
    )


def solution(mesh):
    placed = (
        P(None, ("blk", "head"), None),
        P(None, ("blk", "head")),
        P(None, ("blk", "head")),
        P(None, ("blk", "head"), None, None, None),
        P(None, ("blk", "head"), None),
        P(("blk", "head")),
        P(("blk", "head"), None),
        P(("blk", "head"), None),
        P(("blk", "head")),
        P(("blk", "head"), None),
        P(("blk", "head"), None),
        P(("blk", "head"), None),
        P(("blk", "head")),
        P(("blk", "head"), None),
        P(("blk", "head"), None),
    )
    return jax.shard_map(
        on_device,
        mesh=mesh,
        in_specs=placed,
        out_specs=(
            P(None, ("blk", "head"), None),
            P(None, ("blk", "head"), None),
            P(None, ("blk", "head"), None, None, None),
            P(("blk", "head")),
            P(("blk", "head"), None),
            P(("blk", "head"), None),
            P(("blk", "head")),
            P(("blk", "head"), None),
            P(("blk", "head"), None),
            P(("blk", "head"), None),
            P(("blk", "head")),
            P(("blk", "head"), None),
            P(("blk", "head"), None),
        ),
        check_vma=False,
    )
```

```python
import functools
import math

import jax
import jax.numpy as jnp
from jax import lax
from jax.experimental import pallas as pl
from jax.experimental.pallas import tpu as pltpu
from jax.sharding import PartitionSpec as P

MESH = pl.DeviceIdType.MESH
ANY = pl.BlockSpec(memory_space=pl.ANY)


def coords():
    blk = lax.axis_index("blk")
    return blk // 4, (blk // 2) % 2, blk % 2, lax.axis_index("head")


def place(z, y, c, x):
    return (z * 4 + y * 2 + c, x)


def loop(count, body):
    if count <= 8:
        for step in range(count):
            body(step)
    else:
        lax.fori_loop(0, count, lambda step, carry: (body(step), carry)[1], 0)


def all_barrier(total, me):
    barrier = pltpu.get_barrier_semaphore()

    def greet(step, carry):
        peer = lax.rem(me + step, total)
        pl.semaphore_signal(
            barrier, inc=1, device_id=(peer // 2, lax.rem(peer, 2)), device_id_type=MESH
        )
        return carry

    lax.fori_loop(1, total, greet, 0)
    pl.semaphore_wait(barrier, total - 1)


def remote(src, dst, send, recv, where):
    return pltpu.make_async_remote_copy(
        src_ref=src, dst_ref=dst, send_sem=send, recv_sem=recv, device_id=where, device_id_type=MESH
    )


def gather_kernel(depth, items, *refs):
    count = len(items)
    w_refs = refs[:5]
    small_ref, hid_ref, grad_ref = refs[5:8]
    out_refs = refs[8:11]
    small_out, lead_hid, lead_grad = refs[11:14]
    own_sem, send_sem, recv_sem, misc_sem, lead_send, lead_recv = refs[14:]
    z, y, c, x = coords()
    total = depth * 8
    me = lax.axis_index("blk") * 2 + lax.axis_index("head")
    rows_per = w_refs[0].shape[0]

    def view(item, zs, ys, cs, xs):
        buffer, first, last, kind = item
        return out_refs[buffer].at[pl.ds(first, last - first), zs, ys, cs, xs]

    all_barrier(total, me)
    own_small = pltpu.make_async_copy(small_ref, small_out.at[me], misc_sem.at[1])
    own_small.start()

    def send_small(step, carry):
        peer = lax.rem(me + step, total)
        remote(
            small_ref, small_out.at[me], misc_sem.at[0], misc_sem.at[1], (peer // 2, lax.rem(peer, 2))
        ).start()
        return carry

    own = []
    for index, item in enumerate(items):
        buffer, first, last, kind = item
        width = out_refs[buffer].shape[-1]
        copies = []
        for block in range(first, last):
            if buffer == 1:
                src = w_refs[1 + block]
            else:
                src = w_refs[2 * buffer].at[:, pl.ds(block * width, width)]
            copies.append((src, out_refs[buffer].at[block, z, y, c, x]))
        for src, dst in copies:
            copy = pltpu.make_async_copy(src, dst, own_sem.at[index])
            copy.start()
        own.append(pltpu.make_async_copy(view(item, z, y, c, x), view(item, z, y, c, x), own_sem.at[index]))
    lax.fori_loop(1, total, send_small, 0)
    prev = lax.rem(me + total - 1, total)
    prev_at = (prev // 2, lax.rem(prev, 2))
    leads = [
        remote(hid_ref.at[:, pl.ds(0, 64)], lead_hid, lead_send.at[0], lead_recv.at[0], prev_at),
        remote(grad_ref.at[:, pl.ds(0, 64)], lead_grad, lead_send.at[1], lead_recv.at[1], prev_at),
    ]

    whole = slice(None)

    def phase_one(index):
        own[index].wait()
        item = items[index]

        def send(step):
            other = lax.rem(z + step + 1, depth)
            remote(
                view(item, z, y, c, x), view(item, z, y, c, x),
                send_sem.at[index, 0], recv_sem.at[index, 0], place(other, y, c, x),
            ).start()

        loop(depth - 1, send)

    def bulk(index, phase):
        item = items[index]
        first_x = item[3] == 0
        if phase == 1:
            ref = view(item, whole, y, c, x)
            where = place(z, y, c, 1 - x) if first_x else place(z, 1 - y, c, x)
        elif phase == 2:
            ref = view(item, whole, y, c, whole) if first_x else view(item, whole, whole, c, x)
            where = place(z, 1 - y, c, x) if first_x else place(z, y, c, 1 - x)
        else:
            ref = view(item, whole, whole, c, whole)
            where = place(z, y, 1 - c, x)
        return remote(ref, ref, send_sem.at[index, phase], recv_sem.at[index, phase], where)

    def arrived(index, phase):
        item = items[index]
        if phase == 0:
            ref = view(item, pl.ds(0, depth - 1), y, c, x)
            pltpu.make_async_copy(ref, ref, recv_sem.at[index, 0]).wait()
        else:
            bulk(index, phase).wait_recv()

    def sent(index, phase):
        item = items[index]
        if phase == 0:
            ref = view(item, pl.ds(0, depth - 1), y, c, x)
            pltpu.make_async_copy(ref, ref, send_sem.at[index, 0]).wait()
        else:
            bulk(index, phase).wait_send()

    pairs = (count + 1) // 2
    for step in range(pairs + 2 * 4):
        for phase in range(4, -1, -1):
            pair = step - 2 * phase
            if not 0 <= pair < pairs:
                continue
            for index in range(2 * pair, min(2 * pair + 2, count)):
                if phase == 0:
                    phase_one(index)
                else:
                    arrived(index, phase - 1)
                    if phase < 4:
                        bulk(index, phase).start()
        if step == 0:
            for lead in leads:
                lead.start()
    for index in range(count):
        for phase in range(4):
            sent(index, phase)
    for lead in leads:
        lead.wait()
    pltpu.make_async_copy(small_out, small_out, misc_sem.at[1]).wait()
    rest = small_out.at[pl.ds(0, total - 1)]
    pltpu.make_async_copy(rest, rest, misc_sem.at[0]).wait()


def gather_all(depth, w_qkv, w_attn_out, w_cross_q, w_cross_out, w_kv, small, hidden, grads):
    total = depth * 8
    rows = w_qkv.shape[0]
    items = [
        (0, 0, 3, 0), (0, 3, 6, 1),
        (2, 0, 1, 0), (2, 1, 2, 1),
        (1, 0, 1, 0), (1, 1, 2, 1),
        (1, 2, 3, 0),
    ]
    shapes = [
        (6, depth, 2, 2, 2, rows, w_qkv.shape[1] // 6),
        (3, depth, 2, 2, 2, rows, w_attn_out.shape[1]),
        (2, depth, 2, 2, 2, rows, w_kv.shape[1] // 2),
    ]
    lead_shape = (hidden.shape[0], 64, hidden.shape[2])
    outs = [jax.ShapeDtypeStruct(shape, jnp.bfloat16) for shape in shapes]
    outs += [jax.ShapeDtypeStruct((total,) + small.shape, small.dtype)]
    outs += [jax.ShapeDtypeStruct(lead_shape, jnp.bfloat16)] * 2
    count = len(items)
    return pl.pallas_call(
        functools.partial(gather_kernel, depth, items),
        out_shape=outs,
        in_specs=[ANY] * 8,
        out_specs=[ANY] * 6,
        scratch_shapes=[
            pltpu.SemaphoreType.DMA((count,)),
            pltpu.SemaphoreType.DMA((count, 4)),
            pltpu.SemaphoreType.DMA((count, 4)),
            pltpu.SemaphoreType.DMA((2,)),
            pltpu.SemaphoreType.DMA((2,)),
            pltpu.SemaphoreType.DMA((2,)),
        ],
        compiler_params=pltpu.CompilerParams(collective_id=0, has_side_effects=True),
    )(w_qkv, w_attn_out, w_cross_q, w_cross_out, w_kv, small, hidden, grads)


def unit_of(device, total):
    if total == 32:
        depth = device // 8
        middle = (depth == 1) | (depth == 2)
        end = 16 + (depth // 3) * 4 + (lax.rem(device, 8) // 4) * 2 + lax.rem(device, 2)
        unit = jnp.where(middle, device - 8, end)
        return unit, middle | (lax.rem(device // 2, 2) == 0)
    stride = total // UNITS
    return jnp.minimum(device // stride, UNITS - 1), (lax.rem(device, stride) == 0) & (device // stride < UNITS)


def to_units_kernel(total, src, dst, send_sem, recv_sem):
    me = lax.axis_index("blk") * 2 + lax.axis_index("head")
    mine, holder = unit_of(me, total)
    all_barrier(total, me)
    lanes = src.shape[-1]

    def slot(device):
        return dst.at[:, :, pl.ds(pl.multiple_of(device * lanes, 128), lanes)]

    @pl.when(holder)
    def _():
        pltpu.make_async_copy(src.at[mine], slot(me), recv_sem).start()

    def send(step, carry):
        peer = lax.rem(me + step, total)
        unit, held = unit_of(peer, total)

        @pl.when(held)
        def _():
            remote(src.at[unit], slot(me), send_sem, recv_sem, (peer // 2, lax.rem(peer, 2))).start()

        return carry

    lax.fori_loop(1, total, send, 0)

    @pl.when(holder)
    def _():
        part = src.at[pl.ds(0, UNITS - 1)]
        pltpu.make_async_copy(dst, dst, recv_sem).wait()
        pltpu.make_async_copy(part, part, send_sem).wait()

    @pl.when(jnp.logical_not(holder))
    def _():
        pltpu.make_async_copy(src, src, send_sem).wait()


def to_units(total, message, collective):
    units, parts, width, lanes = message.shape
    return pl.pallas_call(
        functools.partial(to_units_kernel, total),
        out_shape=jax.ShapeDtypeStruct((parts, width, lanes * total), message.dtype),
        in_specs=[ANY],
        out_specs=ANY,
        scratch_shapes=[pltpu.SemaphoreType.DMA, pltpu.SemaphoreType.DMA],
        compiler_params=pltpu.CompilerParams(collective_id=collective, has_side_effects=True),
    )(message)


def to_tokens_kernel(total, extras, *refs):
    src = refs[0]
    extra_in = refs[1 : 1 + extras]
    dst = refs[1 + extras]
    extra_out = refs[2 + extras : 2 + 2 * extras]
    send_sem, recv_sem, extra_send, extra_recv = refs[2 + 2 * extras :]
    me = lax.axis_index("blk") * 2 + lax.axis_index("head")
    mine, holder = unit_of(me, total)
    all_barrier(total, me)
    lanes = dst.shape[-1]
    after = lax.rem(me + 1, total)
    moves = [
        remote(
            extra_in[index], extra_out[index], extra_send.at[index], extra_recv.at[index],
            (after // 2, lax.rem(after, 2)),
        )
        for index in range(extras)
    ]
    for move in moves:
        move.start()

    def slot(device):
        return src.at[:, :, pl.ds(pl.multiple_of(device * lanes, 128), lanes)]

    @pl.when(holder)
    def _():
        pltpu.make_async_copy(slot(me), dst.at[mine], recv_sem).start()

        def send(step, carry):
            peer = lax.rem(me + step, total)
            remote(
                slot(peer), dst.at[mine], send_sem, recv_sem, (peer // 2, lax.rem(peer, 2))
            ).start()
            return carry

        lax.fori_loop(1, total, send, 0)

    pltpu.make_async_copy(dst, dst, recv_sem).wait()

    @pl.when(holder)
    def _():
        part = src.at[:, :, pl.ds(0, lanes * (total - 1))]
        pltpu.make_async_copy(part, part, send_sem).wait()

    for move in moves:
        move.wait()


def to_tokens(total, units, extra, collective):
    parts, width, length = units.shape
    count = len(extra)
    result = jax.ShapeDtypeStruct((UNITS, parts, width, length // total), units.dtype)
    return pl.pallas_call(
        functools.partial(to_tokens_kernel, total, count),
        out_shape=[result] + [jax.ShapeDtypeStruct(e.shape, e.dtype) for e in extra],
        in_specs=[ANY] * (1 + count),
        out_specs=[ANY] * (1 + count),
        scratch_shapes=[
            pltpu.SemaphoreType.DMA,
            pltpu.SemaphoreType.DMA,
            pltpu.SemaphoreType.DMA((max(count, 1),)),
            pltpu.SemaphoreType.DMA((max(count, 1),)),
        ],
        compiler_params=pltpu.CompilerParams(collective_id=collective, has_side_effects=True),
    )(units, *extra)


def scatter_kernel(depth, items, *refs):
    count = len(items)
    total = depth * 8
    d_refs = refs[:3]
    gain_ref = refs[3]
    out_refs = refs[4:7]
    gain_out = refs[7]
    own = refs[8 : 8 + count]
    got_core = refs[8 + count : 8 + 2 * count]
    got_one = refs[8 + 2 * count : 8 + 3 * count]
    got_two = refs[8 + 3 * count : 8 + 4 * count]
    got_z = refs[8 + 4 * count : 8 + 5 * count]
    gains, local_sem, send_sem, recv_sem, gain_sem = refs[8 + 5 * count :]
    z, y, c, x = coords()
    me = lax.axis_index("blk") * 2 + lax.axis_index("head")
    all_barrier(total, me)
    whole = slice(None)

    pltpu.make_async_copy(gain_ref.at[me], gains.at[me], gain_sem.at[1]).start()

    def send_gain(step, carry):
        peer = lax.rem(me + step, total)
        remote(
            gain_ref.at[peer], gains.at[me], gain_sem.at[0], gain_sem.at[1], (peer // 2, lax.rem(peer, 2))
        ).start()
        return carry

    def local(index):
        buffer, first, last, kind = items[index]
        src = d_refs[buffer].at[pl.ds(first, last - first), whole, whole, c]
        return pltpu.make_async_copy(src, own[index], local_sem.at[index])

    def core(index):
        buffer, first, last, kind = items[index]
        src = d_refs[buffer].at[pl.ds(first, last - first), whole, whole, 1 - c]
        return remote(
            src, got_core[index], send_sem.at[index, 0], recv_sem.at[index, 0], place(z, y, 1 - c, x)
        )

    def one(index):
        if items[index][3] == 0:
            src, where = own[index].at[whole, whole, 1 - y], place(z, 1 - y, c, x)
        else:
            src, where = own[index].at[whole, whole, whole, 1 - x], place(z, y, c, 1 - x)
        return remote(src, got_one[index], send_sem.at[index, 1], recv_sem.at[index, 1], where)

    def two(index):
        if items[index][3] == 0:
            src, where = own[index].at[whole, whole, y, 1 - x], place(z, y, c, 1 - x)
        else:
            src, where = own[index].at[whole, whole, 1 - y, x], place(z, 1 - y, c, x)
        return remote(src, got_two[index], send_sem.at[index, 2], recv_sem.at[index, 2], where)

    def send_z(index):
        def send(step):
            other = lax.rem(z + step + 1, depth)
            remote(
                own[index].at[whole, other, y, x], got_z[index].at[z],
                send_sem.at[index, 3], recv_sem.at[index, 3], place(other, y, c, x),
            ).start()

        loop(depth - 1, send)

    def add_into(target, source):
        target[...] = (target[...].astype(jnp.float32) + source[...].astype(jnp.float32)).astype(
            jnp.bfloat16
        )

    def sum_core(index):
        blocks = own[index].shape[0]

        def body(step):
            block, level = step // depth, lax.rem(step, depth)
            for row in range(2):
                for col in range(2):
                    add_into(own[index].at[block, level, row, col], got_core[index].at[block, level, row, col])

        lax.fori_loop(0, blocks * depth, lambda step, carry: (body(step), carry)[1], 0)

    def sum_one(index):
        blocks = own[index].shape[0]

        def body(step):
            block, level = step // depth, lax.rem(step, depth)
            for side in range(2):
                if items[index][3] == 0:
                    target = own[index].at[block, level, y, side]
                else:
                    target = own[index].at[block, level, side, x]
                add_into(target, got_one[index].at[block, level, side])

        lax.fori_loop(0, blocks * depth, lambda step, carry: (body(step), carry)[1], 0)

    def sum_two(index):
        blocks = own[index].shape[0]

        def body(step):
            block, level = step // depth, lax.rem(step, depth)
            add_into(own[index].at[block, level, y, x], got_two[index].at[block, level])

        lax.fori_loop(0, blocks * depth, lambda step, carry: (body(step), carry)[1], 0)

    def sum_z(index):
        buffer, first, last, kind = items[index]
        for block in range(last - first):
            running = own[index][block, z, y, x].astype(jnp.float32)

            def body(step, value):
                other = lax.rem(z + step, depth)
                return value + got_z[index][other, block].astype(jnp.float32)

            out_refs[buffer][first + block] = lax.fori_loop(1, depth, body, running)

    for index in range(count):
        local(index).start()
    pairs = (count + 1) // 2
    for step in range(pairs + 4):
        for phase in range(4, -1, -1):
            pair = step - phase
            if not 0 <= pair < pairs:
                continue
            for index in range(2 * pair, min(2 * pair + 2, count)):
                if phase == 0:
                    core(index).start()
                elif phase == 1:
                    local(index).wait()
                    core(index).wait_recv()
                    sum_core(index)
                    one(index).start()
                elif phase == 2:
                    one(index).wait_recv()
                    sum_one(index)
                    two(index).start()
                elif phase == 3:
                    two(index).wait_recv()
                    sum_two(index)
                    send_z(index)
                else:
                    landed = got_z[index].at[pl.ds(0, depth - 1)]
                    pltpu.make_async_copy(landed, landed, recv_sem.at[index, 3]).wait()
                    sum_z(index)
        if step == 0:
            lax.fori_loop(1, total, send_gain, 0)
    pltpu.make_async_copy(gains, gains, gain_sem.at[1]).wait()
    gain_out[...] = jnp.sum(gains[...], axis=0)
    for index in range(count):
        core(index).wait_send()
        one(index).wait_send()
        two(index).wait_send()
        gone = got_z[index].at[pl.ds(0, depth - 1)]
        pltpu.make_async_copy(gone, gone, send_sem.at[index, 3]).wait()
    rest = gains.at[pl.ds(0, total - 1)]
    pltpu.make_async_copy(rest, rest, gain_sem.at[0]).wait()


def scatter_all(depth, d_qkv, d_squares, d_kv, d_gains, collective):
    items = [
        (0, 0, 3, 0), (0, 3, 6, 1),
        (2, 0, 1, 0), (2, 1, 2, 1),
        (1, 0, 1, 0), (1, 1, 2, 1),
        (1, 2, 3, 0),
    ]
    count = len(items)
    parts = (d_qkv, d_squares, d_kv)
    own, core, one, two, along = [], [], [], [], []
    for buffer, first, last, kind in items:
        rows, width = parts[buffer].shape[-2:]
        blocks = last - first
        own.append(pltpu.VMEM((blocks, depth, 2, 2, rows, width), jnp.bfloat16))
        core.append(pltpu.VMEM((blocks, depth, 2, 2, rows, width), jnp.bfloat16))
        one.append(pltpu.VMEM((blocks, depth, 2, rows, width), jnp.bfloat16))
        two.append(pltpu.VMEM((blocks, depth, rows, width), jnp.bfloat16))
        along.append(pltpu.VMEM((depth, blocks, rows, width), jnp.bfloat16))
    outs = [jax.ShapeDtypeStruct((p.shape[0],) + p.shape[-2:], jnp.float32) for p in parts]
    outs.append(jax.ShapeDtypeStruct(d_gains.shape[1:], jnp.float32))
    vmem = pl.BlockSpec(memory_space=pltpu.VMEM)
    return pl.pallas_call(
        functools.partial(scatter_kernel, depth, items),
        out_shape=outs,
        in_specs=[ANY] * 4,
        out_specs=[vmem] * 4,
        scratch_shapes=own + core + one + two + along + [
            pltpu.VMEM(d_gains.shape, jnp.float32),
            pltpu.SemaphoreType.DMA((count,)),
            pltpu.SemaphoreType.DMA((count, 4)),
            pltpu.SemaphoreType.DMA((count, 4)),
            pltpu.SemaphoreType.DMA((2,)),
        ],
        compiler_params=pltpu.CompilerParams(
            collective_id=collective, has_side_effects=True, vmem_limit_bytes=60 * 2**20
        ),
    )(d_qkv, d_squares, d_kv, d_gains)


HEADS = 12
HEAD_DIM = 64
SPAN = 64
NEIGHBOURS = 2
NEIGH_LEN = 128
MICRO = 2
UNITS = MICRO * HEADS
AXES = ("blk", "head")
TILE = 256
LEAD = SPAN - 1
SCORE_SCALE = 1.0 / math.sqrt(HEAD_DIM)
LOG2E = math.log2(math.e)


def tile_at(ref, index, row):
    return ref[row, :, pl.ds(pl.multiple_of(index * TILE, TILE), TILE)]


def row_at(ref, index):
    return ref[:, pl.ds(pl.multiple_of(index * TILE, TILE), TILE)]


def tile_mask(key_tile, query_tile, first_row):
    key_place = key_tile * TILE + lax.broadcasted_iota(jnp.int32, (TILE, TILE), 0)
    query_place = query_tile * TILE + lax.broadcasted_iota(jnp.int32, (TILE, TILE), 1)
    return (key_place <= query_place) & (key_place >= first_row)


def attn_forward_kernel(low_ref, first_ref, qkv_ref, shifted_ref, mixed_ref, total_ref):
    tiles = qkv_ref.shape[-1] // TILE

    def one_query(query_tile, carry):
        query_t = tile_at(qkv_ref, query_tile, 0)
        first_row = row_at(first_ref, query_tile)

        def one_key(step, state):
            peak, weight, mixed = state
            key_tile = query_tile - step
            keys = tile_at(qkv_ref, key_tile, 1).T
            scores = jnp.dot(keys, query_t, preferred_element_type=jnp.float32) * (SCORE_SCALE * LOG2E)
            scores = jnp.where(tile_mask(key_tile, query_tile, first_row), scores, -1e30)
            new_peak = jnp.maximum(peak, jnp.max(scores, axis=0, keepdims=True))
            probs = jnp.exp2(scores - new_peak)
            fade = jnp.exp2(peak - new_peak)
            weight = weight * fade + jnp.sum(probs, axis=0, keepdims=True)
            mixed = mixed * fade + jnp.dot(
                tile_at(qkv_ref, key_tile, 2), probs.astype(jnp.bfloat16), preferred_element_type=jnp.float32
            )
            return new_peak, weight, mixed

        start = (
            jnp.full((1, TILE), -1e30, jnp.float32),
            jnp.zeros((1, TILE), jnp.float32),
            jnp.zeros((HEAD_DIM, TILE), jnp.float32),
        )
        steps = query_tile + 1 - low_ref[query_tile]
        peak, weight, mixed = lax.fori_loop(0, steps, one_key, start)
        columns = pl.ds(pl.multiple_of(query_tile * TILE, TILE), TILE)
        mixed_ref[:, columns] = mixed / weight
        total_ref[:, columns] = peak + jnp.log2(weight)
        return carry

    lax.fori_loop(0, tiles, one_query, 0)
    length = qkv_ref.shape[-1]

    def turn(step, carry):
        rows = pl.ds(pl.multiple_of(step * 16, 16), 16)
        shifted_ref[rows, :] = pltpu.roll(mixed_ref[rows, :], length - LEAD, 1).astype(jnp.bfloat16)
        return carry

    lax.fori_loop(0, HEAD_DIM // 16, turn, 0)


def attn_backward_kernel(
    low_ref, high_ref, first_ref, qkv_ref, shifted_ref, mixed_ref, total_ref, out_ref, grad_ref, dq_ref, delta_ref
):
    length = qkv_ref.shape[-1]
    tiles = length // TILE
    delta_ref[...] = jnp.zeros_like(delta_ref)

    def turn(step, carry):
        rows = pl.ds(pl.multiple_of(step * 16, 16), 16)
        grad = pltpu.roll(shifted_ref[rows, :].astype(jnp.float32), LEAD, 1)
        grad_ref[rows, :] = grad.astype(jnp.bfloat16)
        delta_ref[...] += jnp.sum(grad * mixed_ref[rows, :], axis=0, keepdims=True)
        dq_ref[rows, :] = jnp.zeros((16, length), jnp.float32)
        return carry

    lax.fori_loop(0, HEAD_DIM // 16, turn, 0)

    def one_key(key_tile, carry):
        key_t = tile_at(qkv_ref, key_tile, 1)
        keys = key_t.T
        values = tile_at(qkv_ref, key_tile, 2).T

        def one_query(query_tile, state):
            d_key, d_value = state
            query_t = tile_at(qkv_ref, query_tile, 0)
            grad_t = row_at(grad_ref, query_tile)
            scores = jnp.dot(keys, query_t, preferred_element_type=jnp.float32) * (SCORE_SCALE * LOG2E)
            allowed = tile_mask(key_tile, query_tile, row_at(first_ref, query_tile))
            probs = jnp.where(allowed, jnp.exp2(scores - row_at(total_ref, query_tile)), 0.0)
            d_probs = jnp.dot(values, grad_t, preferred_element_type=jnp.float32)
            d_scores = (probs * (d_probs - row_at(delta_ref, query_tile))).astype(jnp.bfloat16)
            d_value = d_value + jnp.dot(
                probs.astype(jnp.bfloat16), grad_t.T, preferred_element_type=jnp.float32
            )
            d_key = d_key + jnp.dot(d_scores, query_t.T, preferred_element_type=jnp.float32)
            columns = pl.ds(pl.multiple_of(query_tile * TILE, TILE), TILE)
            dq_ref[:, columns] += jnp.dot(key_t, d_scores, preferred_element_type=jnp.float32)
            return d_key, d_value

        zeros = jnp.zeros((TILE, HEAD_DIM), jnp.float32)
        d_key, d_value = lax.fori_loop(key_tile, high_ref[key_tile], one_query, (zeros, zeros))
        columns = pl.ds(pl.multiple_of(key_tile * TILE, TILE), TILE)
        out_ref[1, :, columns] = (d_key * SCORE_SCALE).T.astype(jnp.bfloat16)
        out_ref[2, :, columns] = d_value.T.astype(jnp.bfloat16)
        return carry

    lax.fori_loop(0, tiles, one_key, 0)

    def finish(step, carry):
        rows = pl.ds(pl.multiple_of(step * 16, 16), 16)
        out_ref[0, rows, :] = (dq_ref[rows, :] * SCORE_SCALE).astype(jnp.bfloat16)
        return carry

    lax.fori_loop(0, HEAD_DIM // 16, finish, 0)


SMEM = pl.BlockSpec(memory_space=pltpu.SMEM)
VMEM = pl.BlockSpec(memory_space=pltpu.VMEM)


def local_params():
    return pltpu.CompilerParams(vmem_limit_bytes=60 * 2**20)


def attn_forward(low, first, qkv):
    width, length = qkv.shape[1:]
    return pl.pallas_call(
        attn_forward_kernel,
        out_shape=[
            jax.ShapeDtypeStruct((width, length), jnp.bfloat16),
            jax.ShapeDtypeStruct((width, length), jnp.float32),
            jax.ShapeDtypeStruct((1, length), jnp.float32),
        ],
        in_specs=[SMEM, VMEM, VMEM],
        out_specs=[VMEM] * 3,
        compiler_params=local_params(),
        cost_estimate=pl.CostEstimate(flops=10**9, bytes_accessed=4 * 10**6, transcendentals=4 * 10**6),
    )(low, first, qkv)


def attn_backward(low, high, first, qkv, shifted, mixed, totals):
    width, length = qkv.shape[1:]
    return pl.pallas_call(
        attn_backward_kernel,
        out_shape=jax.ShapeDtypeStruct((3, width, length), jnp.bfloat16),
        in_specs=[SMEM, SMEM] + [VMEM] * 5,
        out_specs=VMEM,
        scratch_shapes=[
            pltpu.VMEM((width, length), jnp.bfloat16),
            pltpu.VMEM((width, length), jnp.float32),
            pltpu.VMEM((1, length), jnp.float32),
        ],
        compiler_params=local_params(),
        cost_estimate=pl.CostEstimate(flops=3 * 10**9, bytes_accessed=4 * 10**6, transcendentals=4 * 10**6),
    )(low, high, first, qkv, shifted, mixed, totals)


def dot_nn(left, right):
    return jnp.dot(left, right, preferred_element_type=jnp.float32)


def dot_nt(left, right):
    return lax.dot_general(left, right, (((1,), (1,)), ((), ())), preferred_element_type=jnp.float32)


def dot_tn(left, right):
    return lax.dot_general(left, right, (((0,), (0,)), ((), ())), preferred_element_type=jnp.float32)


def norm_parts(values):
    centred = values - jnp.mean(values, axis=-1, keepdims=True)
    scale = lax.rsqrt(jnp.mean(centred * centred, axis=-1, keepdims=True) + 1e-05)
    return centred * scale, scale


def norm_pull(values, gain, grad):
    unit, scale = norm_parts(values)
    scaled = grad * gain
    pulled = scale * (
        scaled
        - jnp.mean(scaled, axis=-1, keepdims=True)
        - unit * jnp.mean(scaled * unit, axis=-1, keepdims=True)
    )
    return pulled, jnp.sum(grad * unit, axis=0, keepdims=True)


def shift_rows(rows, lead):
    joined = jnp.concatenate([rows.astype(jnp.float32), lead.astype(jnp.float32)], axis=0)
    return pltpu.roll(joined, joined.shape[0] - LEAD, 0)[: rows.shape[0]]


def stack_pair(rows):
    lane = lax.broadcasted_iota(jnp.int32, rows.shape, 1)
    zero = jnp.zeros_like(rows)
    return jnp.concatenate(
        [jnp.where(lane < HEAD_DIM, rows, zero), jnp.where(lane < HEAD_DIM, zero, rows)], axis=0
    )


def unstack_pair(rows):
    lane = lax.broadcasted_iota(jnp.int32, (SPAN, 2 * HEAD_DIM), 1)
    return jnp.where(lane < HEAD_DIM, rows[:SPAN], rows[SPAN:])


def middle_kernel(
    att_ref, hid_ref, lead_hid_ref, grad_ref, lead_grad_ref, gain_ref, used_ref, sq_ref, kv_hbm, neigh_hbm,
    up_hbm, down_hbm,
    result_ref, first_ref, d_att_ref, n2_ref, d_cq_ref, cm_ref, gc_ref, ga_ref, gy_ref, act_ref, d_pair_ref,
    d_gain_ref, d_up_hbm,
    kv_ref, neigh_ref, up_ref, down_ref, att_rows, second_ref, cq_ref, pair_ref, prob_ref, acc_ref, d_n3_ref,
    n3_ref, n3t_ref, d_up_ref, sems,
):
    micro, tokens, width = hid_ref.shape
    rows = micro * tokens
    pulls = [
        pltpu.make_async_copy(src, dst, sems.at[index])
        for index, (src, dst) in enumerate(
            [(kv_hbm, kv_ref), (neigh_hbm, neigh_ref), (up_hbm, up_ref), (down_hbm, down_ref)]
        )
    ]
    for pull in pulls:
        pull.start()
    gain_cross, gain_mlp = gain_ref[1:2, :], gain_ref[2:3, :]
    for index in range(micro):
        part = pl.ds(index * tokens, tokens)
        hidden = shift_rows(hid_ref[index], lead_hid_ref[index])
        gy_ref[part, :] = shift_rows(grad_ref[index], lead_grad_ref[index]).astype(jnp.bfloat16)
        first_ref[part, :] = hidden + dot_tn(att_ref[index], sq_ref[0])
    n2_ref[...] = (norm_parts(first_ref[...])[0] * gain_cross).astype(jnp.bfloat16)
    cq_ref[...] = dot_nn(n2_ref[...], sq_ref[1]).astype(jnp.bfloat16)

    pulls[0].wait()
    pulls[1].wait()
    chunk = 256
    chunks = neigh_ref.shape[0] // chunk

    def make_pairs(step, carry):
        side, block = step // chunks, lax.rem(step, chunks)
        part = pl.ds(pl.multiple_of(block * chunk, chunk), chunk)
        pair_ref[side, part, :] = dot_nn(neigh_ref[part, :], kv_ref[side]).astype(jnp.bfloat16)
        return carry

    lax.fori_loop(0, 2 * chunks, make_pairs, 0)
    couples = HEADS // 2
    pair_rows = NEIGHBOURS * NEIGH_LEN
    groups = rows // SPAN

    def where(step):
        group, couple = step // couples, lax.rem(step, couples)
        tok = pl.ds(pl.multiple_of(group * SPAN, SPAN), SPAN)
        key = pl.ds(pl.multiple_of(group * pair_rows, pair_rows), pair_rows)
        lanes = pl.ds(pl.multiple_of(couple * 2 * HEAD_DIM, 2 * HEAD_DIM), 2 * HEAD_DIM)
        return tok, key, lanes

    def cross_step(step, carry):
        tok, key, lanes = where(step)
        query = stack_pair(cq_ref[tok, lanes])
        scores = dot_nt(query, pair_ref[0, key, lanes]) * SCORE_SCALE
        weights = jnp.exp(scores - jnp.max(scores, axis=-1, keepdims=True))
        probs = weights / jnp.sum(weights, axis=-1, keepdims=True)
        prob_ref[step] = probs
        mixed = unstack_pair(dot_nn(probs.astype(jnp.bfloat16), pair_ref[1, key, lanes]))
        cm_ref[tok, lanes] = (mixed * used_ref[tok, :]).astype(jnp.bfloat16)
        return carry

    lax.fori_loop(0, groups * couples, cross_step, 0)
    second_ref[...] = first_ref[...] + dot_nn(cm_ref[...], sq_ref[2])
    n3 = (norm_parts(second_ref[...])[0] * gain_mlp).astype(jnp.bfloat16)
    n3_ref[...] = n3
    n3t_ref[...] = n3.T
    acc_ref[...] = second_ref[...]
    d_n3_ref[...] = jnp.zeros_like(d_n3_ref)
    pulls[2].wait()
    pulls[3].wait()
    ff_blocks = up_ref.shape[1] // width

    def mlp_step(step, carry):
        cols = pl.ds(pl.multiple_of(step * width, width), width)
        upper = dot_nn(n3_ref[...], up_ref[:, cols])
        square = upper * upper
        flat = jnp.tanh(math.sqrt(2.0 / math.pi) * upper * (1.0 + 0.044715 * square))
        half = 0.5 * (1.0 + flat)
        active = (upper * half).astype(jnp.bfloat16)
        act_ref[:, cols] = active
        slope = half + 0.5 * upper * (1.0 - flat * flat) * math.sqrt(2.0 / math.pi) * (
            1.0 + 3.0 * 0.044715 * square
        )
        d_upper = (dot_nt(gy_ref[...], down_ref[cols, :]) * slope).astype(jnp.bfloat16)
        acc_ref[...] += dot_nn(active, down_ref[cols, :])
        d_n3_ref[...] += dot_nt(d_upper, up_ref[:, cols])
        d_up_ref[:, cols] = dot_nn(n3t_ref[...], d_upper).astype(jnp.bfloat16)
        pltpu.make_async_copy(d_up_ref.at[:, cols], d_up_hbm.at[:, cols], sems.at[4]).start()
        return carry

    lax.fori_loop(0, ff_blocks, mlp_step, 0)
    result_ref[...] = acc_ref[...].astype(jnp.bfloat16)
    pulled, d_gain_mlp = norm_pull(second_ref[...], gain_mlp, d_n3_ref[...])
    d_second = gy_ref[...].astype(jnp.float32) + pulled
    acc_ref[...] = d_second
    gc_ref[...] = d_second.astype(jnp.bfloat16)
    att_rows[...] = (
        dot_nt(gc_ref[...], sq_ref[2]).astype(jnp.bfloat16).astype(jnp.float32) * used_ref[...]
    ).astype(jnp.bfloat16)

    def cross_back(step, carry):
        tok, key, lanes = where(step)
        grad = stack_pair(att_rows[tok, lanes])
        query = stack_pair(cq_ref[tok, lanes])
        probs = prob_ref[step]
        d_probs = dot_nt(grad, pair_ref[1, key, lanes])
        d_scores = (
            probs * (d_probs - jnp.sum(probs * d_probs, axis=-1, keepdims=True))
        ).astype(jnp.bfloat16)
        d_query = unstack_pair(dot_nn(d_scores, pair_ref[0, key, lanes]))
        d_cq_ref[tok, lanes] = (d_query * SCORE_SCALE).astype(jnp.bfloat16)
        d_pair_ref[0, key, lanes] = (dot_tn(d_scores, query) * SCORE_SCALE).astype(jnp.bfloat16)
        d_pair_ref[1, key, lanes] = dot_tn(probs.astype(jnp.bfloat16), grad).astype(jnp.bfloat16)
        return carry

    lax.fori_loop(0, groups * couples, cross_back, 0)
    pulled, d_gain_cross = norm_pull(first_ref[...], gain_cross, dot_nt(d_cq_ref[...], sq_ref[1]))
    d_first = acc_ref[...] + pulled
    first_ref[...] = d_first
    ga_ref[...] = d_first.astype(jnp.bfloat16)
    for index in range(micro):
        d_att_ref[index] = dot_nt(sq_ref[0], ga_ref[pl.ds(index * tokens, tokens), :]).astype(jnp.bfloat16)
    d_gain_ref[...] = jnp.concatenate([d_gain_cross, d_gain_mlp, jnp.zeros((6, width), jnp.float32)], axis=0)
    pltpu.make_async_copy(d_up_ref, d_up_hbm, sems.at[4]).wait()


def middle(attended_t, hidden, lead_hid, grads, lead_grad, gains, used, squares, kv, neigh, up, down):
    micro, tokens, width = hidden.shape
    rows = micro * tokens
    ff = up.shape[1]
    low = jnp.bfloat16
    out_shape = [
        jax.ShapeDtypeStruct((rows, width), low),
        jax.ShapeDtypeStruct((rows, width), jnp.float32),
        jax.ShapeDtypeStruct((micro, width, tokens), low),
        jax.ShapeDtypeStruct((rows, width), low),
        jax.ShapeDtypeStruct((rows, width), low),
        jax.ShapeDtypeStruct((rows, width), low),
        jax.ShapeDtypeStruct((rows, width), low),
        jax.ShapeDtypeStruct((rows, width), low),
        jax.ShapeDtypeStruct((rows, width), low),
        jax.ShapeDtypeStruct((rows, ff), low),
        jax.ShapeDtypeStruct((2,) + neigh.shape, low),
        jax.ShapeDtypeStruct((8, width), jnp.float32),
        jax.ShapeDtypeStruct((width, ff), low),
    ]
    steps = rows // SPAN * HEADS // 2
    scratch = [
        pltpu.VMEM(kv.shape, low),
        pltpu.VMEM(neigh.shape, low),
        pltpu.VMEM(up.shape, low),
        pltpu.VMEM(down.shape, low),
        pltpu.VMEM((rows, width), low),
        pltpu.VMEM((rows, width), jnp.float32),
        pltpu.VMEM((rows, width), low),
        pltpu.VMEM((2,) + neigh.shape, low),
        pltpu.VMEM((steps, 2 * SPAN, NEIGHBOURS * NEIGH_LEN), jnp.float32),
        pltpu.VMEM((rows, width), jnp.float32),
        pltpu.VMEM((rows, width), jnp.float32),
        pltpu.VMEM((rows, width), low),
        pltpu.VMEM((width, rows), low),
        pltpu.VMEM((width, ff), low),
        pltpu.SemaphoreType.DMA((5,)),
    ]
    return pl.pallas_call(
        middle_kernel,
        out_shape=out_shape,
        in_specs=[VMEM] * 8 + [ANY] * 4,
        out_specs=[VMEM] * 12 + [ANY],
        scratch_shapes=scratch,
        compiler_params=local_params(),
        cost_estimate=pl.CostEstimate(flops=12 * 10**9, bytes_accessed=40 * 10**6, transcendentals=10**6),
    )(attended_t, hidden, lead_hid, grads, lead_grad, gains, used, squares, kv, neigh, up, down)


def last_kernel(depth, items, skew, *refs):
    count = len(items)
    (
        back_ref, result_ref, first_ref, n2_ref, d_cq_ref, cm_ref, gc_ref, ga_ref, gy_ref, act_ref, d_pair_ref,
        att_ref, neigh_ref, kv_ref, qkv_ref, hidden_ref, gain_ref, cos_ref, sin_ref, d_gain_rest_ref,
    ) = refs[:20]
    (
        output_ref, grad_in_ref, grad_neigh_ref, out_qkv, out_att, out_cq, out_co, out_kv, out_down, gain_out,
    ) = refs[20:30]
    full = refs[30 : 30 + count]
    got_core = refs[30 + count : 30 + 2 * count]
    got_one = refs[30 + 2 * count : 30 + 3 * count]
    got_two = refs[30 + 3 * count : 30 + 4 * count]
    got_z = refs[30 + 4 * count : 30 + 5 * count]
    (
        sent_ref, tail_first, tail_result, raw_ref, n1t_ref, d_n1_ref, temp_ref, gain_mine, gain_got, gain_z,
        send_sem, recv_sem, unit_send, unit_recv, tail_send, tail_recv, gain_send, gain_recv,
    ) = refs[30 + 5 * count :]
    micro, tokens, width = hidden_ref.shape
    total = depth * 8
    z, y, c, x = coords()
    me = lax.axis_index("blk") * 2 + lax.axis_index("head")
    mine, holder = unit_of(me, total)
    whole = slice(None)
    all_barrier(total, me)

    after = lax.rem(me + 1, total)
    after_at = (after // 2, lax.rem(after, 2))
    tails = []
    for index in range(micro):
        part = pl.ds(index * tokens + tokens - 64, 64)
        tails.append(
            remote(first_ref.at[part], tail_first.at[index], tail_send.at[index], tail_recv.at[index], after_at)
        )
        tails.append(
            remote(
                result_ref.at[part], tail_result.at[index],
                tail_send.at[micro + index], tail_recv.at[micro + index], after_at,
            )
        )

    def slot(device):
        return back_ref.at[:, :, pl.ds(pl.multiple_of(device * tokens, 128), tokens)]

    @pl.when(holder)
    def _():
        pltpu.make_async_copy(slot(me), sent_ref.at[mine], unit_recv).start()

        def send(step, carry):
            peer = lax.rem(me + step, total)
            remote(
                slot(peer), sent_ref.at[mine], unit_send, unit_recv, (peer // 2, lax.rem(peer, 2))
            ).start()
            return carry

        lax.fori_loop(1, total, send, 0)

    for tail in tails:
        tail.start()

    slab = full[0].shape[-2]

    def spread(index, block):
        buffer = full[index]
        cols = buffer.shape[-1]

        def body(level, carry):
            for place_in in range(8):
                at = pl.multiple_of((level * 8 + place_in) * slab, 8)
                buffer[block, level, place_in // 4, (place_in // 2) % 2, place_in % 2] = temp_ref[
                    pl.ds(at, slab), :cols
                ].astype(jnp.bfloat16)
            return carry

        lax.fori_loop(0, depth, body, 0)

    down_index = [index for index, item in enumerate(items) if item[0] == "down"]

    def make_down():
        def body(level, carry):
            cols = pl.ds(pl.multiple_of(level * width, width), width)
            temp_ref[...] = dot_tn(act_ref[:, cols], gy_ref[...])
            for place_in in range(8):
                for part, index in enumerate(down_index):
                    at = place_in * slab * len(down_index) + part * slab
                    full[index][0, level, place_in // 4, (place_in // 2) % 2, place_in % 2] = temp_ref[
                        pl.ds(at, slab), :
                    ].astype(jnp.bfloat16)
            return carry

        lax.fori_loop(0, depth, body, 0)

    def take_units():
        @pl.when(holder)
        def _():
            part = back_ref.at[:, :, pl.ds(0, tokens * (total - 1))]
            pltpu.make_async_copy(part, part, unit_send).wait()

        pltpu.make_async_copy(sent_ref, sent_ref, unit_recv).wait()
        half = HEAD_DIM // 2

        def body(head, carry):
            for index in range(micro):
                lanes = pl.ds(index * tokens, tokens)
                cosine, sine = cos_ref[index], sin_ref[index]
                for part in range(3):
                    value = sent_ref[index * HEADS + head, part].astype(jnp.float32)
                    at = pl.multiple_of(part * width + head * HEAD_DIM, HEAD_DIM)
                    if part < 2:
                        first_half, second_half = value[:half], value[half:]
                        value = jnp.concatenate(
                            [
                                first_half * cosine + second_half * sine,
                                second_half * cosine - first_half * sine,
                            ],
                            axis=0,
                        )
                    raw_ref[pl.ds(at, HEAD_DIM), lanes] = value.astype(jnp.bfloat16)
            return carry

        lax.fori_loop(0, HEADS, body, 0)
        for index in range(micro):
            normed = norm_parts(hidden_ref[index].astype(jnp.float32))[0] * gain_ref[0:1, :]
            n1t_ref[:, pl.ds(index * tokens, tokens)] = normed.astype(jnp.bfloat16).T

    def make(index):
        kind, which = items[index][:2]
        if kind == "down":
            if index == down_index[0]:
                make_down()
            return
        if kind == "kv":
            temp_ref[...] = dot_tn(neigh_ref[...], d_pair_ref[which])
        elif kind == "att":
            temp_ref[...] = dot_nn(att_ref[0], ga_ref[pl.ds(0, tokens), :])
            for step in range(1, micro):
                temp_ref[...] += dot_nn(att_ref[step], ga_ref[pl.ds(step * tokens, tokens), :])
        elif kind == "cq":
            temp_ref[...] = dot_tn(n2_ref[...], d_cq_ref[...])
        elif kind == "co":
            temp_ref[...] = dot_tn(cm_ref[...], gc_ref[...])
        else:
            if which == 0:
                take_units()
            for block in range(2):
                half = width // 2
                at = which * width + block * half
                temp_ref[:, :half] = dot_nt(n1t_ref[...], raw_ref[pl.ds(at, half), :])
                spread(index, block)
            return
        spread(index, 0)

    def core(index):
        return remote(
            full[index].at[whole, whole, whole, 1 - c], got_core[index],
            send_sem.at[index, 0], recv_sem.at[index, 0], place(z, y, 1 - c, x),
        )

    def one(index):
        if items[index][2] == 0:
            src, where = full[index].at[whole, whole, 1 - y, c], place(z, 1 - y, c, x)
        else:
            src, where = full[index].at[whole, whole, whole, c, 1 - x], place(z, y, c, 1 - x)
        return remote(src, got_one[index], send_sem.at[index, 1], recv_sem.at[index, 1], where)

    def two(index):
        if items[index][2] == 0:
            src, where = full[index].at[whole, whole, y, c, 1 - x], place(z, y, c, 1 - x)
        else:
            src, where = full[index].at[whole, whole, 1 - y, c, x], place(z, 1 - y, c, x)
        return remote(src, got_two[index], send_sem.at[index, 2], recv_sem.at[index, 2], where)

    def send_z(index):
        for step in range(1, depth):
            other = lax.rem(z + step, depth)
            remote(
                full[index].at[whole, other, y, c, x], got_z[index].at[z],
                send_sem.at[index, 3], recv_sem.at[index, 3], place(other, y, c, x),
            ).start()

    def add_into(target, source):
        target[...] = (target[...].astype(jnp.float32) + source[...].astype(jnp.float32)).astype(
            jnp.bfloat16
        )

    def each_level(index, body):
        blocks = full[index].shape[0]
        lax.fori_loop(
            0, blocks * depth, lambda step, carry: (body(step // depth, lax.rem(step, depth)), carry)[1], 0
        )

    def sum_core(index):
        def body(block, level):
            for row in range(2):
                for col in range(2):
                    add_into(
                        full[index].at[block, level, row, c, col], got_core[index].at[block, level, row, col]
                    )

        each_level(index, body)

    def sum_one(index):
        def body(block, level):
            for side in range(2):
                if items[index][2] == 0:
                    target = full[index].at[block, level, y, c, side]
                else:
                    target = full[index].at[block, level, side, c, x]
                add_into(target, got_one[index].at[block, level, side])

        each_level(index, body)

    def sum_two(index):
        each_level(
            index,
            lambda block, level: add_into(
                full[index].at[block, level, y, c, x], got_two[index].at[block, level]
            ),
        )

    def sum_z(index):
        kind, which = items[index][:2]
        for block in range(full[index].shape[0]):
            value = full[index][block, z, y, c, x].astype(jnp.float32)
            for step in range(1, depth):
                value = value + got_z[index][lax.rem(z + step, depth), block].astype(jnp.float32)
            if kind == "down":
                out_down[pl.ds(which * slab, slab), :] = value
            elif kind == "kv":
                out_kv[:, pl.ds(which * width, width)] = value
            elif kind == "qkv":
                out_qkv[:, pl.ds(which * width + block * (width // 2), width // 2)] = value
            else:
                {"att": out_att, "cq": out_cq, "co": out_co}[kind][...] = value

    def phase(index, number):
        if number == 0:
            make(index)
            core(index).start()
        elif number == 1:
            core(index).wait_recv()
            sum_core(index)
            one(index).start()
        elif number == 2:
            one(index).wait_recv()
            sum_one(index)
            two(index).start()
        elif number == 3:
            two(index).wait_recv()
            sum_two(index)
            send_z(index)
        else:
            landed = got_z[index].at[pl.ds(0, depth - 1)]
            pltpu.make_async_copy(landed, landed, recv_sem.at[index, 3]).wait()
            sum_z(index)

    def gain_copy(stage):
        where = (place(z, y, 1 - c, x), place(z, 1 - y, c, x), place(z, y, c, 1 - x))[stage]
        return remote(
            gain_mine.at[stage], gain_got.at[stage], gain_send.at[stage], gain_recv.at[stage], where
        )

    def gain_phase(number):
        if number == 0:
            gain_copy(0).start()
        elif number < 4:
            gain_copy(number - 1).wait_recv()
            gain_mine[number] = gain_mine[number - 1] + gain_got[number - 1]
            if number < 3:
                gain_copy(number).start()
            else:
                for step in range(1, depth):
                    other = lax.rem(z + step, depth)
                    remote(
                        gain_mine.at[3], gain_z.at[z], gain_send.at[3], gain_recv.at[3], place(other, y, c, x)
                    ).start()
        else:
            landed = gain_z.at[pl.ds(0, depth - 1)]
            pltpu.make_async_copy(landed, landed, gain_recv.at[3]).wait()
            value = gain_mine[3]
            for step in range(1, depth):
                value = value + gain_z[lax.rem(z + step, depth)]
            gain_out[...] = value

    def neighbours_part(block):
        chunk = 256
        part = pl.ds(block * chunk, chunk)
        grad_neigh_ref[part, :] = (
            dot_nt(d_pair_ref[0, part, :], kv_ref[0]) + dot_nt(d_pair_ref[1, part, :], kv_ref[1])
        ).astype(jnp.bfloat16)

    def input_part():
        half = width // 2
        blocks = qkv_ref.shape[0]
        d_n1_ref[...] = dot_nn(qkv_ref[0], raw_ref[pl.ds(0, half), :])
        for block in range(1, blocks):
            d_n1_ref[...] += dot_nn(qkv_ref[block], raw_ref[pl.ds(block * half, half), :])
        for tail in tails:
            tail.wait()
        d_gain = jnp.zeros((1, width), jnp.float32)
        for index in range(micro):
            part = pl.ds(index * tokens, tokens)
            d_normed = d_n1_ref[:, part].T
            pulled, part_gain = norm_pull(hidden_ref[index].astype(jnp.float32), gain_ref[0:1, :], d_normed)
            d_gain = d_gain + part_gain
            joined = jnp.concatenate([tail_first[index], first_ref[part, :]], axis=0)
            home = pltpu.roll(joined, joined.shape[0] - 1, 0)[:tokens]
            grad_in_ref[part, :] = (home + pulled).astype(jnp.bfloat16)
            joined = jnp.concatenate(
                [tail_result[index].astype(jnp.float32), result_ref[part, :].astype(jnp.float32)], axis=0
            )
            output_ref[part, :] = pltpu.roll(joined, joined.shape[0] - 1, 0)[:tokens].astype(jnp.bfloat16)
        gain_mine[0] = jnp.concatenate([d_gain, d_gain_rest_ref[0:7, :]], axis=0)

    pairs = (count + 1) // 2
    chunks = neigh_ref.shape[0] // 256
    for step in range(pairs + 1 + skew * 4):
        for number in range(4, -1, -1):
            pair = step - skew * number
            if 0 <= pair < pairs:
                for index in range(2 * pair, min(2 * pair + 2, count)):
                    phase(index, number)
            elif pair == pairs:
                if number == 0:
                    input_part()
                gain_phase(number)
        if 1 <= step <= chunks:
            neighbours_part(step - 1)
    for index in range(count):
        core(index).wait_send()
        one(index).wait_send()
        two(index).wait_send()
        gone = got_z[index].at[pl.ds(0, depth - 1)]
        pltpu.make_async_copy(gone, gone, send_sem.at[index, 3]).wait()
    for stage in range(3):
        gain_copy(stage).wait_send()
    gone = gain_z.at[pl.ds(0, depth - 1)]
    pltpu.make_async_copy(gone, gone, gain_send.at[3]).wait()


def last(depth, collective, ff, *args):
    hidden = args[15]
    micro, tokens, width = hidden.shape
    rows = micro * tokens
    total = depth * 8
    slab = width // total
    neigh_rows = args[12].shape[0]
    items = [
        ("down", 0, 0), ("down", 1, 1), ("down", 2, 0), ("down", 3, 1), ("kv", 0, 0), ("kv", 1, 1),
        ("att", 0, 0), ("cq", 0, 1), ("co", 0, 0), ("qkv", 0, 1), ("qkv", 1, 0), ("qkv", 2, 1),
    ]
    count = len(items)
    low, high = jnp.bfloat16, jnp.float32
    out_shape = [
        jax.ShapeDtypeStruct((rows, width), low),
        jax.ShapeDtypeStruct((rows, width), low),
        jax.ShapeDtypeStruct((neigh_rows, width), low),
        jax.ShapeDtypeStruct((slab, 3 * width), high),
        jax.ShapeDtypeStruct((slab, width), high),
        jax.ShapeDtypeStruct((slab, width), high),
        jax.ShapeDtypeStruct((slab, width), high),
        jax.ShapeDtypeStruct((slab, 2 * width), high),
        jax.ShapeDtypeStruct((ff // total, width), high),
        jax.ShapeDtypeStruct((8, width), high),
    ]
    full, core, one, two, along = [], [], [], [], []
    for kind, which, order in items:
        blocks, cols = (2, width // 2) if kind == "qkv" else (1, width)
        full.append(pltpu.VMEM((blocks, depth, 2, 2, 2, slab, cols), low))
        core.append(pltpu.VMEM((blocks, depth, 2, 2, slab, cols), low))
        one.append(pltpu.VMEM((blocks, depth, 2, slab, cols), low))
        two.append(pltpu.VMEM((blocks, depth, slab, cols), low))
        along.append(pltpu.VMEM((depth, blocks, slab, cols), low))
    dma = pltpu.SemaphoreType.DMA
    scratch = full + core + one + two + along + [
        pltpu.VMEM((UNITS, 3, HEAD_DIM, tokens), low),
        pltpu.VMEM((micro, 64, width), high),
        pltpu.VMEM((micro, 64, width), low),
        pltpu.VMEM((3 * width, rows), low),
        pltpu.VMEM((width, rows), low),
        pltpu.VMEM((width, rows), high),
        pltpu.VMEM((width, width), high),
        pltpu.VMEM((4, 8, width), high),
        pltpu.VMEM((3, 8, width), high),
        pltpu.VMEM((depth, 8, width), high),
        dma((count, 4)), dma((count, 4)), dma, dma, dma((2 * micro,)), dma((2 * micro,)), dma((4,)), dma((4,)),
    ]
    return pl.pallas_call(
        functools.partial(last_kernel, depth, items, 1),
        out_shape=out_shape,
        in_specs=[ANY] + [VMEM] * 19,
        out_specs=[VMEM] * 10,
        scratch_shapes=scratch,
        compiler_params=pltpu.CompilerParams(
            collective_id=collective, has_side_effects=True, vmem_limit_bytes=62 * 2**20
        ),
        cost_estimate=pl.CostEstimate(flops=10**10, bytes_accessed=40 * 10**6, transcendentals=0),
    )(*args)


def layer_norm(values, norm_gain):
    centred = values - jnp.mean(values, axis=-1, keepdims=True)
    spread = jnp.mean(centred * centred, axis=-1, keepdims=True)
    return centred * lax.rsqrt(spread + 1e-05) * norm_gain


def norm_backward(values, norm_gain, grad_out):
    result, pullback = jax.vjp(layer_norm, values, norm_gain)
    return pullback(grad_out)


def outer(left, right):
    return jnp.einsum("td,te->de", left, right, preferred_element_type=jnp.float32)


def turn_heads(values, cosine, sine):
    first_half, second_half = values[:, :32], values[:, 32:]
    return jnp.concatenate(
        [first_half * cosine - second_half * sine, second_half * cosine + first_half * sine], axis=1
    )


def on_device(
    hidden_in,
    segment_ids,
    neighbour_valid,
    neighbours,
    out_grad,
    norm_attn,
    w_qkv,
    w_attn_out,
    norm_cross,
    w_cross_q,
    w_cross_kv,
    w_cross_out,
    norm_mlp,
    w_up,
    w_down,
):
    micro, tok_count, model_width = hidden_in.shape
    blk_count = lax.axis_size("blk")
    depth = blk_count // 4
    total = blk_count * 2
    length = tok_count * total
    row_count = micro * tok_count
    gain_rows = norm_attn.shape[0]
    span_count = tok_count // SPAN
    pair_rows = NEIGHBOURS * NEIGH_LEN
    device = lax.axis_index(AXES)

    up_full = lax.all_gather(w_up, AXES, axis=0, tiled=True)
    down_full = lax.all_gather(w_down, AXES, axis=0, tiled=True)

    small = jnp.zeros((16, 128), jnp.bfloat16)
    for row, gain in enumerate((norm_attn, norm_cross, norm_mlp)):
        small = small.at[row, :gain_rows].set(gain)
    small = small.at[3 : 3 + micro, :tok_count].set(segment_ids.astype(jnp.bfloat16))
    got_qkv, got_sq, got_kv, got_small, lead_hid, lead_grad = gather_all(
        depth, w_qkv, w_attn_out, w_cross_q, w_cross_out, w_cross_kv, small, hidden_in, out_grad
    )
    gains = got_small[:, :3, :gain_rows].astype(jnp.float32).transpose(1, 0, 2).reshape(3, model_width)
    gain_attn = gains[0]
    seg_full = got_small[:, 3 : 3 + micro, :tok_count].transpose(1, 0, 2).reshape(micro, length)
    seg_full = seg_full.astype(jnp.int32)
    qkv_blocks = got_qkv.reshape(6, model_width, model_width // 2)
    squares = got_sq.reshape(3, model_width, model_width)
    kv_blocks = got_kv.reshape(2, model_width, model_width)

    token_index = device * tok_count + jnp.arange(tok_count, dtype=jnp.int32)
    first_of = jnp.sum(
        (seg_full[:, None, :] < segment_ids[:, :, None]).astype(jnp.int32), axis=-1
    )
    local_pos = token_index[None] - first_of
    frequency = jnp.exp(
        jnp.arange(HEAD_DIM // 2, dtype=jnp.float32) * (-2.0 * math.log(10000.0) / HEAD_DIM)
    )
    angles = frequency[:, None, None] * local_pos.astype(jnp.float32)[None]
    cosine, sine = jnp.cos(angles), jnp.sin(angles)

    unit, holder = unit_of(device, total)
    seg_unit = lax.dynamic_index_in_dim(seg_full, unit // HEADS, 0, keepdims=False)
    seg_tiles = seg_unit.reshape(length // TILE, TILE)
    tile_first = jnp.sum((seg_unit[None] < seg_tiles[:, :1]).astype(jnp.int32), axis=-1)
    inside = jnp.sum((seg_tiles[:, None, :] < seg_tiles[:, :, None]).astype(jnp.int32), axis=-1)
    tile_index = jnp.arange(length // TILE, dtype=jnp.int32)
    first_row = jnp.where(
        seg_tiles == seg_tiles[:, :1], tile_first[:, None], tile_index[:, None] * TILE + inside
    ).reshape(1, length)
    low = tile_first // TILE
    high = jnp.sum((low[None] <= tile_index[:, None]).astype(jnp.int32), axis=-1)
    low = jnp.where(holder, low, tile_index + 1)
    high = jnp.where(holder, high, 0)

    hidden = hidden_in.astype(jnp.float32)
    normed_attn = layer_norm(hidden, gain_attn).astype(jnp.bfloat16).reshape(row_count, model_width)
    raw = jnp.einsum("bde,td->bet", qkv_blocks, normed_attn, preferred_element_type=jnp.float32)
    raw = raw.reshape(3, HEADS, HEAD_DIM, micro, tok_count)
    rotated = jnp.stack(
        [turn_heads(raw[0], cosine, sine), turn_heads(raw[1], cosine, sine), raw[2]]
    ).astype(jnp.bfloat16)
    message = rotated.transpose(3, 1, 0, 2, 4).reshape(UNITS, 3, HEAD_DIM, tok_count)
    unit_qkv = to_units(total, message, 1)
    shifted, mixed, totals = attn_forward(low, first_row, unit_qkv)
    (attended_t,) = to_tokens(total, shifted[None], (), 2)
    attended_t = attended_t.reshape(micro, model_width, tok_count)

    shifted_index = token_index + LEAD
    used = jnp.where(
        shifted_index[None] < length, jnp.repeat(neighbour_valid, SPAN, axis=1).astype(jnp.float32), 0.0
    ).reshape(row_count, 1)
    neigh_rows = neighbours.reshape(micro * span_count * pair_rows, model_width)
    (
        result_rows, d_first, d_attended_t, normed_cross, d_cross_query, cross_mixed, d_second_low, d_first_low,
        grad_low, activated, d_pairs, d_gain_rest, d_up,
    ) = middle(
        attended_t, hidden_in, lead_hid, out_grad, lead_grad, gains, used, squares, kv_blocks, neigh_rows,
        up_full, down_full,
    )
    up_share = lax.psum_scatter(d_up, AXES, scatter_dimension=0, tiled=True).astype(jnp.float32)
    in_kernel = gain_rows % 8 == 0
    if not in_kernel:
        down_share = lax.psum_scatter(
            outer(activated, grad_low).astype(jnp.bfloat16), AXES, scatter_dimension=0, tiled=True
        ).astype(jnp.float32)
    unit_grad = to_units(total, d_attended_t.reshape(UNITS, 1, HEAD_DIM, tok_count), 3)
    unit_back = attn_backward(low, high, first_row, unit_qkv, unit_grad[0], mixed, totals)
    if in_kernel:
        (
            output, grad_in, grad_neighbours, s_qkv, s_att, s_cq, s_co, s_kv, s_down, s_gain,
        ) = last(
            depth, 5, w_up.shape[1],
            unit_back, result_rows, d_first, normed_cross, d_cross_query, cross_mixed, d_second_low, d_first_low,
            grad_low, activated, d_pairs, attended_t, neigh_rows, kv_blocks, qkv_blocks, hidden_in, gains,
            cosine.transpose(1, 0, 2), sine.transpose(1, 0, 2), d_gain_rest,
        )
        own_gain = lax.dynamic_slice_in_dim(s_gain, device * gain_rows, gain_rows, 1)
        return (
            output.reshape(hidden_in.shape), grad_in.reshape(hidden_in.shape),
            grad_neighbours.reshape(neighbours.shape),
            own_gain[0], s_qkv, s_att, own_gain[1], s_cq, s_kv, s_co, own_gain[2], up_share, s_down,
        )
    result_rows = result_rows.reshape(micro, tok_count, model_width)
    d_first = d_first.reshape(micro, tok_count, model_width)
    sent_t, tail_first, tail_result = to_tokens(
        total, unit_back, (d_first[:, tok_count - 64 :], result_rows[:, tok_count - 64 :]), 4
    )

    def unshift(rows, tail):
        return jnp.concatenate([tail[:, 1:], rows[:, : tok_count - LEAD]], axis=1)

    output = unshift(result_rows, tail_result)
    d_first_home = unshift(d_first, tail_first)
    sent_t = sent_t.reshape(micro, HEADS, 3, HEAD_DIM, tok_count).transpose(2, 1, 3, 0, 4)
    sent_t = sent_t.astype(jnp.float32)
    raw_t = jnp.stack(
        [turn_heads(sent_t[0], cosine, -sine), turn_heads(sent_t[1], cosine, -sine), sent_t[2]]
    ).astype(jnp.bfloat16).reshape(6, model_width // 2, row_count)
    d_normed_attn = jnp.einsum("bet,bde->td", raw_t, qkv_blocks, preferred_element_type=jnp.float32)
    d_hidden_in, d_gain_attn = norm_backward(
        hidden, gain_attn, d_normed_attn.reshape(micro, tok_count, model_width)
    )
    grad_in = (d_first_home + d_hidden_in).astype(jnp.bfloat16)

    d_keys, d_values = d_pairs[0], d_pairs[1]
    d_first_low = d_first_low.reshape(micro, tok_count, model_width)
    d_neigh = (
        jnp.einsum("te,de->td", d_keys, kv_blocks[0], preferred_element_type=jnp.float32)
        + jnp.einsum("te,de->td", d_values, kv_blocks[1], preferred_element_type=jnp.float32)
    ).astype(jnp.bfloat16)
    grad_neighbours = d_neigh.reshape(neighbours.shape)

    def blocks_of(array):
        return array.astype(jnp.bfloat16).reshape(
            array.shape[0], depth, 2, 2, 2, gain_rows, array.shape[-1]
        )

    d_qkv = jnp.einsum("td,bet->bde", normed_attn, raw_t, preferred_element_type=jnp.float32)
    d_sq = jnp.stack(
        [
            jnp.einsum("mdt,mte->de", attended_t, d_first_low, preferred_element_type=jnp.float32),
            outer(normed_cross, d_cross_query),
            outer(cross_mixed, d_second_low),
        ]
    )
    d_kv = jnp.stack([outer(neigh_rows, d_keys), outer(neigh_rows, d_values)])
    d_gains = jnp.stack([d_gain_attn, d_gain_rest[0], d_gain_rest[1]]).reshape(3, total, gain_rows)
    d_gains = jnp.zeros((total, 8, 128), jnp.float32).at[:, :3, :gain_rows].set(d_gains.transpose(1, 0, 2))
    s_qkv, s_sq, s_kv, s_gain = scatter_all(
        depth, blocks_of(d_qkv), blocks_of(d_sq), blocks_of(d_kv), d_gains, 6
    )
    return (
        output,
        grad_in,
        grad_neighbours,
        s_gain[0, :gain_rows],
        s_qkv.transpose(1, 0, 2).reshape(gain_rows, 3 * model_width),
        s_sq[0],
        s_gain[1, :gain_rows],
        s_sq[1],
        s_kv.transpose(1, 0, 2).reshape(gain_rows, 2 * model_width),
        s_sq[2],
        s_gain[2, :gain_rows],
        up_share,
        down_share,
    )


def solution(mesh):
    placed = (
        P(None, ("blk", "head"), None),
        P(None, ("blk", "head")),
        P(None, ("blk", "head")),
        P(None, ("blk", "head"), None, None, None),
        P(None, ("blk", "head"), None),
        P(("blk", "head")),
        P(("blk", "head"), None),
        P(("blk", "head"), None),
        P(("blk", "head")),
        P(("blk", "head"), None),
        P(("blk", "head"), None),
        P(("blk", "head"), None),
        P(("blk", "head")),
        P(("blk", "head"), None),
        P(("blk", "head"), None),
    )
    return jax.shard_map(
        on_device,
        mesh=mesh,
        in_specs=placed,
        out_specs=(
            P(None, ("blk", "head"), None),
            P(None, ("blk", "head"), None),
            P(None, ("blk", "head"), None, None, None),
            P(("blk", "head")),
            P(("blk", "head"), None),
            P(("blk", "head"), None),
            P(("blk", "head")),
            P(("blk", "head"), None),
            P(("blk", "head"), None),
            P(("blk", "head"), None),
            P(("blk", "head")),
            P(("blk", "head"), None),
            P(("blk", "head"), None),
        ),
        check_vma=False,
    )
```

```python
import functools
import math

import jax
import jax.numpy as jnp
from jax import lax
from jax.experimental import pallas as pl
from jax.experimental.pallas import tpu as pltpu
from jax.sharding import PartitionSpec as P

MESH = pl.DeviceIdType.MESH
ANY = pl.BlockSpec(memory_space=pl.ANY)


def coords():
    blk = lax.axis_index("blk")
    return blk // 4, (blk // 2) % 2, blk % 2, lax.axis_index("head")


def place(z, y, c, x):
    return (z * 4 + y * 2 + c, x)


def loop(count, body):
    if count <= 8:
        for step in range(count):
            body(step)
    else:
        lax.fori_loop(0, count, lambda step, carry: (body(step), carry)[1], 0)


def all_barrier(total, me):
    barrier = pltpu.get_barrier_semaphore()

    def greet(step, carry):
        peer = lax.rem(me + step, total)
        pl.semaphore_signal(
            barrier, inc=1, device_id=(peer // 2, lax.rem(peer, 2)), device_id_type=MESH
        )
        return carry

    lax.fori_loop(1, total, greet, 0)
    pl.semaphore_wait(barrier, total - 1)


def remote(src, dst, send, recv, where):
    return pltpu.make_async_remote_copy(
        src_ref=src, dst_ref=dst, send_sem=send, recv_sem=recv, device_id=where, device_id_type=MESH
    )


def gather_kernel(depth, items, *refs):
    count = len(items)
    w_refs = refs[:5]
    small_ref, hid_ref, grad_ref = refs[5:8]
    out_refs = refs[8:11]
    small_out, lead_hid, lead_grad = refs[11:14]
    own_sem, send_sem, recv_sem, misc_sem, lead_send, lead_recv = refs[14:]
    z, y, c, x = coords()
    total = depth * 8
    me = lax.axis_index("blk") * 2 + lax.axis_index("head")
    rows_per = w_refs[0].shape[0]

    def view(item, zs, ys, cs, xs):
        buffer, first, last, kind = item
        return out_refs[buffer].at[pl.ds(first, last - first), zs, ys, cs, xs]

    all_barrier(total, me)
    own_small = pltpu.make_async_copy(small_ref, small_out.at[me], misc_sem.at[1])
    own_small.start()

    def send_small(step, carry):
        peer = lax.rem(me + step, total)
        remote(
            small_ref, small_out.at[me], misc_sem.at[0], misc_sem.at[1], (peer // 2, lax.rem(peer, 2))
        ).start()
        return carry

    own = []
    for index, item in enumerate(items):
        buffer, first, last, kind = item
        width = out_refs[buffer].shape[-1]
        copies = []
        for block in range(first, last):
            if buffer == 1:
                src = w_refs[1 + block]
            else:
                src = w_refs[2 * buffer].at[:, pl.ds(block * width, width)]
            copies.append((src, out_refs[buffer].at[block, z, y, c, x]))
        for src, dst in copies:
            copy = pltpu.make_async_copy(src, dst, own_sem.at[index])
            copy.start()
        own.append(pltpu.make_async_copy(view(item, z, y, c, x), view(item, z, y, c, x), own_sem.at[index]))
    lax.fori_loop(1, total, send_small, 0)
    prev = lax.rem(me + total - 1, total)
    prev_at = (prev // 2, lax.rem(prev, 2))
    leads = [
        remote(hid_ref.at[:, pl.ds(0, 64)], lead_hid, lead_send.at[0], lead_recv.at[0], prev_at),
        remote(grad_ref.at[:, pl.ds(0, 64)], lead_grad, lead_send.at[1], lead_recv.at[1], prev_at),
    ]

    whole = slice(None)

    def phase_one(index):
        own[index].wait()
        item = items[index]

        def send(step):
            other = lax.rem(z + step + 1, depth)
            remote(
                view(item, z, y, c, x), view(item, z, y, c, x),
                send_sem.at[index, 0], recv_sem.at[index, 0], place(other, y, c, x),
            ).start()

        loop(depth - 1, send)

    def bulk(index, phase):
        item = items[index]
        first_x = item[3] == 0
        if phase == 1:
            ref = view(item, whole, y, c, x)
            where = place(z, y, c, 1 - x) if first_x else place(z, 1 - y, c, x)
        elif phase == 2:
            ref = view(item, whole, y, c, whole) if first_x else view(item, whole, whole, c, x)
            where = place(z, 1 - y, c, x) if first_x else place(z, y, c, 1 - x)
        else:
            ref = view(item, whole, whole, c, whole)
            where = place(z, y, 1 - c, x)
        return remote(ref, ref, send_sem.at[index, phase], recv_sem.at[index, phase], where)

    def arrived(index, phase):
        item = items[index]
        if phase == 0:
            ref = view(item, pl.ds(0, depth - 1), y, c, x)
            pltpu.make_async_copy(ref, ref, recv_sem.at[index, 0]).wait()
        else:
            bulk(index, phase).wait_recv()

    def sent(index, phase):
        item = items[index]
        if phase == 0:
            ref = view(item, pl.ds(0, depth - 1), y, c, x)
            pltpu.make_async_copy(ref, ref, send_sem.at[index, 0]).wait()
        else:
            bulk(index, phase).wait_send()

    pairs = (count + 1) // 2
    for step in range(pairs + 2 * 4):
        for phase in range(4, -1, -1):
            pair = step - 2 * phase
            if not 0 <= pair < pairs:
                continue
            for index in range(2 * pair, min(2 * pair + 2, count)):
                if phase == 0:
                    phase_one(index)
                else:
                    arrived(index, phase - 1)
                    if phase < 4:
                        bulk(index, phase).start()
        if step == 0:
            for lead in leads:
                lead.start()
    for index in range(count):
        for phase in range(4):
            sent(index, phase)
    for lead in leads:
        lead.wait()
    pltpu.make_async_copy(small_out, small_out, misc_sem.at[1]).wait()
    rest = small_out.at[pl.ds(0, total - 1)]
    pltpu.make_async_copy(rest, rest, misc_sem.at[0]).wait()


def gather_all(depth, w_qkv, w_attn_out, w_cross_q, w_cross_out, w_kv, small, hidden, grads):
    total = depth * 8
    rows = w_qkv.shape[0]
    items = [
        (0, 0, 3, 0), (0, 3, 6, 1),
        (2, 0, 1, 0), (2, 1, 2, 1),
        (1, 0, 1, 0), (1, 1, 2, 1),
        (1, 2, 3, 0),
    ]
    shapes = [
        (6, depth, 2, 2, 2, rows, w_qkv.shape[1] // 6),
        (3, depth, 2, 2, 2, rows, w_attn_out.shape[1]),
        (2, depth, 2, 2, 2, rows, w_kv.shape[1] // 2),
    ]
    lead_shape = (hidden.shape[0], 64, hidden.shape[2])
    outs = [jax.ShapeDtypeStruct(shape, jnp.bfloat16) for shape in shapes]
    outs += [jax.ShapeDtypeStruct((total,) + small.shape, small.dtype)]
    outs += [jax.ShapeDtypeStruct(lead_shape, jnp.bfloat16)] * 2
    count = len(items)
    return pl.pallas_call(
        functools.partial(gather_kernel, depth, items),
        out_shape=outs,
        in_specs=[ANY] * 8,
        out_specs=[ANY] * 6,
        scratch_shapes=[
            pltpu.SemaphoreType.DMA((count,)),
            pltpu.SemaphoreType.DMA((count, 4)),
            pltpu.SemaphoreType.DMA((count, 4)),
            pltpu.SemaphoreType.DMA((2,)),
            pltpu.SemaphoreType.DMA((2,)),
            pltpu.SemaphoreType.DMA((2,)),
        ],
        compiler_params=pltpu.CompilerParams(collective_id=0, has_side_effects=True),
    )(w_qkv, w_attn_out, w_cross_q, w_cross_out, w_kv, small, hidden, grads)


def unit_of(device, total):
    if total == 32:
        depth = device // 8
        middle = (depth == 1) | (depth == 2)
        end = 16 + (depth // 3) * 4 + (lax.rem(device, 8) // 4) * 2 + lax.rem(device, 2)
        unit = jnp.where(middle, device - 8, end)
        return unit, middle | (lax.rem(device // 2, 2) == 0)
    stride = total // UNITS
    return jnp.minimum(device // stride, UNITS - 1), (lax.rem(device, stride) == 0) & (device // stride < UNITS)


def to_units_kernel(total, src, dst, send_sem, recv_sem):
    me = lax.axis_index("blk") * 2 + lax.axis_index("head")
    mine, holder = unit_of(me, total)
    all_barrier(total, me)
    lanes = src.shape[-1]

    def slot(device):
        return dst.at[:, :, pl.ds(pl.multiple_of(device * lanes, 128), lanes)]

    @pl.when(holder)
    def _():
        pltpu.make_async_copy(src.at[mine], slot(me), recv_sem).start()

    def send(step, carry):
        peer = lax.rem(me + step, total)
        unit, held = unit_of(peer, total)

        @pl.when(held)
        def _():
            remote(src.at[unit], slot(me), send_sem, recv_sem, (peer // 2, lax.rem(peer, 2))).start()

        return carry

    lax.fori_loop(1, total, send, 0)

    @pl.when(holder)
    def _():
        part = src.at[pl.ds(0, UNITS - 1)]
        pltpu.make_async_copy(dst, dst, recv_sem).wait()
        pltpu.make_async_copy(part, part, send_sem).wait()

    @pl.when(jnp.logical_not(holder))
    def _():
        pltpu.make_async_copy(src, src, send_sem).wait()


def to_units(total, message, collective):
    units, parts, width, lanes = message.shape
    return pl.pallas_call(
        functools.partial(to_units_kernel, total),
        out_shape=jax.ShapeDtypeStruct((parts, width, lanes * total), message.dtype),
        in_specs=[ANY],
        out_specs=ANY,
        scratch_shapes=[pltpu.SemaphoreType.DMA, pltpu.SemaphoreType.DMA],
        compiler_params=pltpu.CompilerParams(collective_id=collective, has_side_effects=True),
    )(message)


def to_tokens_kernel(total, extras, *refs):
    src = refs[0]
    extra_in = refs[1 : 1 + extras]
    dst = refs[1 + extras]
    extra_out = refs[2 + extras : 2 + 2 * extras]
    send_sem, recv_sem, extra_send, extra_recv = refs[2 + 2 * extras :]
    me = lax.axis_index("blk") * 2 + lax.axis_index("head")
    mine, holder = unit_of(me, total)
    all_barrier(total, me)
    lanes = dst.shape[-1]
    after = lax.rem(me + 1, total)
    moves = [
        remote(
            extra_in[index], extra_out[index], extra_send.at[index], extra_recv.at[index],
            (after // 2, lax.rem(after, 2)),
        )
        for index in range(extras)
    ]
    for move in moves:
        move.start()

    def slot(device):
        return src.at[:, :, pl.ds(pl.multiple_of(device * lanes, 128), lanes)]

    @pl.when(holder)
    def _():
        pltpu.make_async_copy(slot(me), dst.at[mine], recv_sem).start()

        def send(step, carry):
            peer = lax.rem(me + step, total)
            remote(
                slot(peer), dst.at[mine], send_sem, recv_sem, (peer // 2, lax.rem(peer, 2))
            ).start()
            return carry

        lax.fori_loop(1, total, send, 0)

    pltpu.make_async_copy(dst, dst, recv_sem).wait()

    @pl.when(holder)
    def _():
        part = src.at[:, :, pl.ds(0, lanes * (total - 1))]
        pltpu.make_async_copy(part, part, send_sem).wait()

    for move in moves:
        move.wait()


def to_tokens(total, units, extra, collective):
    parts, width, length = units.shape
    count = len(extra)
    result = jax.ShapeDtypeStruct((UNITS, parts, width, length // total), units.dtype)
    return pl.pallas_call(
        functools.partial(to_tokens_kernel, total, count),
        out_shape=[result] + [jax.ShapeDtypeStruct(e.shape, e.dtype) for e in extra],
        in_specs=[ANY] * (1 + count),
        out_specs=[ANY] * (1 + count),
        scratch_shapes=[
            pltpu.SemaphoreType.DMA,
            pltpu.SemaphoreType.DMA,
            pltpu.SemaphoreType.DMA((max(count, 1),)),
            pltpu.SemaphoreType.DMA((max(count, 1),)),
        ],
        compiler_params=pltpu.CompilerParams(collective_id=collective, has_side_effects=True),
    )(units, *extra)


def scatter_kernel(depth, items, *refs):
    count = len(items)
    total = depth * 8
    d_refs = refs[:3]
    gain_ref = refs[3]
    out_refs = refs[4:7]
    gain_out = refs[7]
    own = refs[8 : 8 + count]
    got_core = refs[8 + count : 8 + 2 * count]
    got_one = refs[8 + 2 * count : 8 + 3 * count]
    got_two = refs[8 + 3 * count : 8 + 4 * count]
    got_z = refs[8 + 4 * count : 8 + 5 * count]
    gains, local_sem, send_sem, recv_sem, gain_sem = refs[8 + 5 * count :]
    z, y, c, x = coords()
    me = lax.axis_index("blk") * 2 + lax.axis_index("head")
    all_barrier(total, me)
    whole = slice(None)

    pltpu.make_async_copy(gain_ref.at[me], gains.at[me], gain_sem.at[1]).start()

    def send_gain(step, carry):
        peer = lax.rem(me + step, total)
        remote(
            gain_ref.at[peer], gains.at[me], gain_sem.at[0], gain_sem.at[1], (peer // 2, lax.rem(peer, 2))
        ).start()
        return carry

    def local(index):
        buffer, first, last, kind = items[index]
        src = d_refs[buffer].at[pl.ds(first, last - first), whole, whole, c]
        return pltpu.make_async_copy(src, own[index], local_sem.at[index])

    def core(index):
        buffer, first, last, kind = items[index]
        src = d_refs[buffer].at[pl.ds(first, last - first), whole, whole, 1 - c]
        return remote(
            src, got_core[index], send_sem.at[index, 0], recv_sem.at[index, 0], place(z, y, 1 - c, x)
        )

    def one(index):
        if items[index][3] == 0:
            src, where = own[index].at[whole, whole, 1 - y], place(z, 1 - y, c, x)
        else:
            src, where = own[index].at[whole, whole, whole, 1 - x], place(z, y, c, 1 - x)
        return remote(src, got_one[index], send_sem.at[index, 1], recv_sem.at[index, 1], where)

    def two(index):
        if items[index][3] == 0:
            src, where = own[index].at[whole, whole, y, 1 - x], place(z, y, c, 1 - x)
        else:
            src, where = own[index].at[whole, whole, 1 - y, x], place(z, 1 - y, c, x)
        return remote(src, got_two[index], send_sem.at[index, 2], recv_sem.at[index, 2], where)

    def send_z(index):
        def send(step):
            other = lax.rem(z + step + 1, depth)
            remote(
                own[index].at[whole, other, y, x], got_z[index].at[z],
                send_sem.at[index, 3], recv_sem.at[index, 3], place(other, y, c, x),
            ).start()

        loop(depth - 1, send)

    def add_into(target, source):
        target[...] = (target[...].astype(jnp.float32) + source[...].astype(jnp.float32)).astype(
            jnp.bfloat16
        )

    def sum_core(index):
        blocks = own[index].shape[0]

        def body(step):
            block, level = step // depth, lax.rem(step, depth)
            for row in range(2):
                for col in range(2):
                    add_into(own[index].at[block, level, row, col], got_core[index].at[block, level, row, col])

        lax.fori_loop(0, blocks * depth, lambda step, carry: (body(step), carry)[1], 0)

    def sum_one(index):
        blocks = own[index].shape[0]

        def body(step):
            block, level = step // depth, lax.rem(step, depth)
            for side in range(2):
                if items[index][3] == 0:
                    target = own[index].at[block, level, y, side]
                else:
                    target = own[index].at[block, level, side, x]
                add_into(target, got_one[index].at[block, level, side])

        lax.fori_loop(0, blocks * depth, lambda step, carry: (body(step), carry)[1], 0)

    def sum_two(index):
        blocks = own[index].shape[0]

        def body(step):
            block, level = step // depth, lax.rem(step, depth)
            add_into(own[index].at[block, level, y, x], got_two[index].at[block, level])

        lax.fori_loop(0, blocks * depth, lambda step, carry: (body(step), carry)[1], 0)

    def sum_z(index):
        buffer, first, last, kind = items[index]
        for block in range(last - first):
            running = own[index][block, z, y, x].astype(jnp.float32)

            def body(step, value):
                other = lax.rem(z + step, depth)
                return value + got_z[index][other, block].astype(jnp.float32)

            out_refs[buffer][first + block] = lax.fori_loop(1, depth, body, running)

    for index in range(count):
        local(index).start()
    pairs = (count + 1) // 2
    for step in range(pairs + 4):
        for phase in range(4, -1, -1):
            pair = step - phase
            if not 0 <= pair < pairs:
                continue
            for index in range(2 * pair, min(2 * pair + 2, count)):
                if phase == 0:
                    core(index).start()
                elif phase == 1:
                    local(index).wait()
                    core(index).wait_recv()
                    sum_core(index)
                    one(index).start()
                elif phase == 2:
                    one(index).wait_recv()
                    sum_one(index)
                    two(index).start()
                elif phase == 3:
                    two(index).wait_recv()
                    sum_two(index)
                    send_z(index)
                else:
                    landed = got_z[index].at[pl.ds(0, depth - 1)]
                    pltpu.make_async_copy(landed, landed, recv_sem.at[index, 3]).wait()
                    sum_z(index)
        if step == 0:
            lax.fori_loop(1, total, send_gain, 0)
    pltpu.make_async_copy(gains, gains, gain_sem.at[1]).wait()
    gain_out[...] = jnp.sum(gains[...], axis=0)
    for index in range(count):
        core(index).wait_send()
        one(index).wait_send()
        two(index).wait_send()
        gone = got_z[index].at[pl.ds(0, depth - 1)]
        pltpu.make_async_copy(gone, gone, send_sem.at[index, 3]).wait()
    rest = gains.at[pl.ds(0, total - 1)]
    pltpu.make_async_copy(rest, rest, gain_sem.at[0]).wait()


def scatter_all(depth, d_qkv, d_squares, d_kv, d_gains, collective):
    items = [
        (0, 0, 3, 0), (0, 3, 6, 1),
        (2, 0, 1, 0), (2, 1, 2, 1),
        (1, 0, 1, 0), (1, 1, 2, 1),
        (1, 2, 3, 0),
    ]
    count = len(items)
    parts = (d_qkv, d_squares, d_kv)
    own, core, one, two, along = [], [], [], [], []
    for buffer, first, last, kind in items:
        rows, width = parts[buffer].shape[-2:]
        blocks = last - first
        own.append(pltpu.VMEM((blocks, depth, 2, 2, rows, width), jnp.bfloat16))
        core.append(pltpu.VMEM((blocks, depth, 2, 2, rows, width), jnp.bfloat16))
        one.append(pltpu.VMEM((blocks, depth, 2, rows, width), jnp.bfloat16))
        two.append(pltpu.VMEM((blocks, depth, rows, width), jnp.bfloat16))
        along.append(pltpu.VMEM((depth, blocks, rows, width), jnp.bfloat16))
    outs = [jax.ShapeDtypeStruct((p.shape[0],) + p.shape[-2:], jnp.float32) for p in parts]
    outs.append(jax.ShapeDtypeStruct(d_gains.shape[1:], jnp.float32))
    vmem = pl.BlockSpec(memory_space=pltpu.VMEM)
    return pl.pallas_call(
        functools.partial(scatter_kernel, depth, items),
        out_shape=outs,
        in_specs=[ANY] * 4,
        out_specs=[vmem] * 4,
        scratch_shapes=own + core + one + two + along + [
            pltpu.VMEM(d_gains.shape, jnp.float32),
            pltpu.SemaphoreType.DMA((count,)),
            pltpu.SemaphoreType.DMA((count, 4)),
            pltpu.SemaphoreType.DMA((count, 4)),
            pltpu.SemaphoreType.DMA((2,)),
        ],
        compiler_params=pltpu.CompilerParams(
            collective_id=collective, has_side_effects=True, vmem_limit_bytes=60 * 2**20
        ),
    )(d_qkv, d_squares, d_kv, d_gains)


HEADS = 12
HEAD_DIM = 64
SPAN = 64
NEIGHBOURS = 2
NEIGH_LEN = 128
MICRO = 2
UNITS = MICRO * HEADS
AXES = ("blk", "head")
TILE = 512
LEAD = SPAN - 1
DOC_MAX = 2000
SCORE_SCALE = 1.0 / math.sqrt(HEAD_DIM)
LOG2E = math.log2(math.e)


def tile_at(ref, index, row):
    return ref[row, :, pl.ds(pl.multiple_of(index * TILE, TILE), TILE)]


def row_at(ref, index):
    return ref[:, pl.ds(pl.multiple_of(index * TILE, TILE), TILE)]


def tile_mask(key_tile, query_tile, first_row):
    key_place = key_tile * TILE + lax.broadcasted_iota(jnp.int32, (TILE, 1), 0)
    query_place = query_tile * TILE + lax.broadcasted_iota(jnp.int32, (1, TILE), 1)
    return (key_place <= query_place) & (key_place >= first_row)


def attn_forward_kernel(low_ref, first_ref, qkv_ref, shifted_ref, mixed_ref, total_ref):
    tiles = qkv_ref.shape[-1] // TILE

    def one_query(query_tile, carry):
        query_t = tile_at(qkv_ref, query_tile, 0)
        first_row = row_at(first_ref, query_tile)

        def one_key(step, state):
            peak, weight, mixed = state
            key_tile = query_tile - step
            keys = tile_at(qkv_ref, key_tile, 1).T
            scores = jnp.dot(keys, query_t, preferred_element_type=jnp.float32) * (SCORE_SCALE * LOG2E)
            scores = jnp.where(tile_mask(key_tile, query_tile, first_row), scores, -1e30)
            new_peak = jnp.maximum(peak, jnp.max(scores, axis=0, keepdims=True))
            probs = jnp.exp2(scores - new_peak)
            fade = jnp.exp2(peak - new_peak)
            weight = weight * fade + jnp.sum(probs, axis=0, keepdims=True)
            mixed = mixed * fade + jnp.dot(
                tile_at(qkv_ref, key_tile, 2), probs.astype(jnp.bfloat16), preferred_element_type=jnp.float32
            )
            return new_peak, weight, mixed

        start = (
            jnp.full((1, TILE), -1e30, jnp.float32),
            jnp.zeros((1, TILE), jnp.float32),
            jnp.zeros((HEAD_DIM, TILE), jnp.float32),
        )
        steps = query_tile + 1 - low_ref[query_tile]
        peak, weight, mixed = lax.fori_loop(0, steps, one_key, start)
        columns = pl.ds(pl.multiple_of(query_tile * TILE, TILE), TILE)
        mixed_ref[:, columns] = mixed / weight
        total_ref[:, columns] = peak + jnp.log2(weight)
        return carry

    lax.fori_loop(0, tiles, one_query, 0)
    length = qkv_ref.shape[-1]

    def turn(step, carry):
        rows = pl.ds(pl.multiple_of(step * 16, 16), 16)
        shifted_ref[rows, :] = pltpu.roll(mixed_ref[rows, :], length - LEAD, 1).astype(jnp.bfloat16)
        return carry

    lax.fori_loop(0, HEAD_DIM // 16, turn, 0)


def attn_backward_kernel(
    low_ref, high_ref, first_ref, qkv_ref, shifted_ref, mixed_ref, total_ref, out_ref, grad_ref, dq_ref, delta_ref
):
    length = qkv_ref.shape[-1]
    tiles = length // TILE
    delta_ref[...] = jnp.zeros_like(delta_ref)

    def turn(step, carry):
        rows = pl.ds(pl.multiple_of(step * 16, 16), 16)
        grad = pltpu.roll(shifted_ref[rows, :].astype(jnp.float32), LEAD, 1)
        grad_ref[rows, :] = grad.astype(jnp.bfloat16)
        delta_ref[...] += jnp.sum(grad * mixed_ref[rows, :], axis=0, keepdims=True)
        dq_ref[rows, :] = jnp.zeros((16, length), jnp.float32)
        return carry

    lax.fori_loop(0, HEAD_DIM // 16, turn, 0)

    def one_key(key_tile, carry):
        key_t = tile_at(qkv_ref, key_tile, 1)
        keys = key_t.T
        values = tile_at(qkv_ref, key_tile, 2).T

        def one_query(query_tile, state):
            d_key, d_value = state
            query_t = tile_at(qkv_ref, query_tile, 0)
            grad_t = row_at(grad_ref, query_tile)
            scores = jnp.dot(keys, query_t, preferred_element_type=jnp.float32) * (SCORE_SCALE * LOG2E)
            allowed = tile_mask(key_tile, query_tile, row_at(first_ref, query_tile))
            probs = jnp.where(allowed, jnp.exp2(scores - row_at(total_ref, query_tile)), 0.0)
            d_probs = jnp.dot(values, grad_t, preferred_element_type=jnp.float32)
            d_scores = (probs * (d_probs - row_at(delta_ref, query_tile))).astype(jnp.bfloat16)
            d_value = d_value + jnp.dot(
                probs.astype(jnp.bfloat16), grad_t.T, preferred_element_type=jnp.float32
            )
            d_key = d_key + jnp.dot(d_scores, query_t.T, preferred_element_type=jnp.float32)
            columns = pl.ds(pl.multiple_of(query_tile * TILE, TILE), TILE)
            dq_ref[:, columns] += jnp.dot(key_t, d_scores, preferred_element_type=jnp.float32)
            return d_key, d_value

        zeros = jnp.zeros((TILE, HEAD_DIM), jnp.float32)
        d_key, d_value = lax.fori_loop(key_tile, high_ref[key_tile], one_query, (zeros, zeros))
        columns = pl.ds(pl.multiple_of(key_tile * TILE, TILE), TILE)
        out_ref[1, :, columns] = (d_key * SCORE_SCALE).T.astype(jnp.bfloat16)
        out_ref[2, :, columns] = d_value.T.astype(jnp.bfloat16)
        return carry

    lax.fori_loop(0, tiles, one_key, 0)

    def finish(step, carry):
        rows = pl.ds(pl.multiple_of(step * 16, 16), 16)
        out_ref[0, rows, :] = (dq_ref[rows, :] * SCORE_SCALE).astype(jnp.bfloat16)
        return carry

    lax.fori_loop(0, HEAD_DIM // 16, finish, 0)


SMEM = pl.BlockSpec(memory_space=pltpu.SMEM)
VMEM = pl.BlockSpec(memory_space=pltpu.VMEM)


def local_params():
    return pltpu.CompilerParams(vmem_limit_bytes=60 * 2**20)


def attn_forward(low, first, qkv):
    width, length = qkv.shape[1:]
    return pl.pallas_call(
        attn_forward_kernel,
        out_shape=[
            jax.ShapeDtypeStruct((width, length), jnp.bfloat16),
            jax.ShapeDtypeStruct((width, length), jnp.float32),
            jax.ShapeDtypeStruct((1, length), jnp.float32),
        ],
        in_specs=[SMEM, VMEM, VMEM],
        out_specs=[VMEM] * 3,
        compiler_params=local_params(),
        cost_estimate=pl.CostEstimate(flops=10**9, bytes_accessed=4 * 10**6, transcendentals=4 * 10**6),
    )(low, first, qkv)


def attn_backward(low, high, first, qkv, shifted, mixed, totals):
    width, length = qkv.shape[1:]
    return pl.pallas_call(
        attn_backward_kernel,
        out_shape=jax.ShapeDtypeStruct((3, width, length), jnp.bfloat16),
        in_specs=[SMEM, SMEM] + [VMEM] * 5,
        out_specs=VMEM,
        scratch_shapes=[
            pltpu.VMEM((width, length), jnp.bfloat16),
            pltpu.VMEM((width, length), jnp.float32),
            pltpu.VMEM((1, length), jnp.float32),
        ],
        compiler_params=local_params(),
        cost_estimate=pl.CostEstimate(flops=3 * 10**9, bytes_accessed=4 * 10**6, transcendentals=4 * 10**6),
    )(low, high, first, qkv, shifted, mixed, totals)


def first_kernel(depth, items, *refs):
    count = len(items)
    w_refs = refs[:7]
    small_ref, hid_ref, grad_ref = refs[7:10]
    (
        qkv_out, sq_out, kv_out, up_out, down_out, lead_hid, lead_grad, gain_out, cos_out, sin_out,
        unit_out, mixed_out, total_out, start_out, att_out,
    ) = refs[10:25]
    (
        qkv_ref, small_all, hid_vmem, n1_ref, temp_ref, note_ref, turned_ref, doc_ref,
        own_sem, send_sem, recv_sem, misc_sem, lead_send, lead_recv, load_sem, unit_send, unit_recv,
        att_send, att_recv,
    ) = refs[25:]
    z, y, c, x = coords()
    total = depth * 8
    me = lax.axis_index("blk") * 2 + lax.axis_index("head")
    mine, holder = unit_of(me, total)
    slab = w_refs[0].shape[0]
    micro, tokens, width = hid_ref.shape
    homes = (qkv_ref, sq_out, kv_out, up_out, down_out)
    whole = slice(None)

    def view(item, zs, ys, cs, xs):
        buffer, first, last, kind = item
        if buffer == 4:
            return down_out.at[zs, ys, cs, xs, pl.ds(first, last - first)]
        return homes[buffer].at[pl.ds(first, last - first), zs, ys, cs, xs]

    load = pltpu.make_async_copy(hid_ref, hid_vmem, load_sem.at[0])
    load.start()
    own = []
    for index, item in enumerate(items):
        buffer, first, last, kind = item
        cols = homes[buffer].shape[-1]
        if buffer == 4:
            moves = [(w_refs[6].at[pl.ds(first, last - first)], view(item, z, y, c, x))]
        elif buffer == 1:
            moves = [(w_refs[1 + block], sq_out.at[block, z, y, c, x]) for block in range(first, last)]
        else:
            source = w_refs[(0, None, 4, 5)[buffer]]
            moves = [
                (source.at[:, pl.ds(block * cols, cols)], homes[buffer].at[block, z, y, c, x])
                for block in range(first, last)
            ]
        for src, dst in moves:
            pltpu.make_async_copy(src, dst, own_sem.at[index]).start()
        mirror = view(item, z, y, c, x)
        own.append(pltpu.make_async_copy(mirror, mirror, own_sem.at[index]))
    pltpu.make_async_copy(small_ref, small_all.at[me], misc_sem.at[1]).start()
    all_barrier(total, me)

    def send_small(step, carry):
        peer = lax.rem(me + step, total)
        remote(
            small_ref, small_all.at[me], misc_sem.at[0], misc_sem.at[1], (peer // 2, lax.rem(peer, 2))
        ).start()
        return carry

    prev = lax.rem(me + total - 1, total)
    prev_at = (prev // 2, lax.rem(prev, 2))
    leads = [
        remote(hid_ref.at[:, pl.ds(0, 64)], lead_hid, lead_send.at[0], lead_recv.at[0], prev_at),
        remote(grad_ref.at[:, pl.ds(0, 64)], lead_grad, lead_send.at[1], lead_recv.at[1], prev_at),
    ]

    def start(index):
        own[index].wait()
        item = items[index]
        for step in range(1, depth):
            other = lax.rem(z + step, depth)
            remote(
                view(item, z, y, c, x), view(item, z, y, c, x),
                send_sem.at[index, 0], recv_sem.at[index, 0], place(other, y, c, x),
            ).start()

    def bulk(index, phase):
        item = items[index]
        first_x = item[3] == 0
        if phase == 1:
            ref = view(item, whole, y, c, x)
            where = place(z, y, c, 1 - x) if first_x else place(z, 1 - y, c, x)
        elif phase == 2:
            ref = view(item, whole, y, c, whole) if first_x else view(item, whole, whole, c, x)
            where = place(z, 1 - y, c, x) if first_x else place(z, y, c, 1 - x)
        else:
            ref = view(item, whole, whole, c, whole)
            where = place(z, y, 1 - c, x)
        return remote(ref, ref, send_sem.at[index, phase], recv_sem.at[index, phase], where)

    def arrived(index, phase):
        if phase == 0:
            ref = view(items[index], pl.ds(0, depth - 1), y, c, x)
            pltpu.make_async_copy(ref, ref, recv_sem.at[index, 0]).wait()
        else:
            bulk(index, phase).wait_recv()

    def sent(index, phase):
        if phase == 0:
            ref = view(items[index], pl.ds(0, depth - 1), y, c, x)
            pltpu.make_async_copy(ref, ref, send_sem.at[index, 0]).wait()
        else:
            bulk(index, phase).wait_send()

    pairs = (count + 1) // 2

    def gather_step(step):
        for phase in range(4, -1, -1):
            pair = step - phase
            if not 0 <= pair < pairs:
                continue
            for index in range(2 * pair, min(2 * pair + 2, count)):
                if phase == 0:
                    start(index)
                else:
                    arrived(index, phase - 1)
                    if phase < 4:
                        bulk(index, phase).start()

    half_dim = HEAD_DIM // 2

    def tables():
        lane = lax.broadcasted_iota(jnp.int32, (half_dim, tokens), 1)
        order = lax.broadcasted_iota(jnp.int32, (half_dim, tokens), 0)
        frequency = jnp.exp(order.astype(jnp.float32) * (-2.0 * math.log(10000.0) / HEAD_DIM))
        angles = (me * tokens + lane).astype(jnp.float32) * frequency
        cos_out[...] = jnp.cos(angles)
        sin_out[...] = jnp.sin(angles)

    def normalise():
        load.wait()
        pltpu.make_async_copy(small_all, small_all, misc_sem.at[1]).wait()
        for peer in range(total):
            temp_ref[pl.ds(peer * slab, slab), pl.ds(0, 128)] = small_all[peer, :slab, :].astype(jnp.float32)
            doc_ref[pl.ds(peer, 1), :] = jnp.where(
                mine < HEADS, small_all[peer, 32:33, :].astype(jnp.float32), small_all[peer, 33:34, :].astype(jnp.float32)
            )
        turned = temp_ref[:, pl.ds(0, 128)].T
        gain_out[...] = jnp.concatenate(
            [turned[0:1], turned[32:33], turned[64:65], jnp.zeros((5, width), jnp.float32)], axis=0
        )
        for index in range(micro):
            unit_rows = norm_parts(hid_vmem[index].astype(jnp.float32))[0]
            n1_ref[pl.ds(index * tokens, tokens), :] = (unit_rows * gain_out[0:1, :]).astype(jnp.bfloat16)

    def project(part):
        cols = qkv_ref.shape[-1]
        heads = cols // HEAD_DIM
        for half in range(2):
            block = part * 2 + half
            for level in range(depth):
                for inner in range(8):
                    at = (level * 8 + inner) * slab
                    temp_ref[pl.ds(at, slab), :] = qkv_ref[
                        block, level, inner // 4, (inner // 2) % 2, inner % 2
                    ].astype(jnp.float32)
            raw = dot_nn(n1_ref[...], temp_ref[...].astype(jnp.bfloat16))
            for index in range(micro):
                raw_t = raw[index * tokens : (index + 1) * tokens].T
                for head in range(heads):
                    value = raw_t[head * HEAD_DIM : (head + 1) * HEAD_DIM]
                    if part < 2:
                        first_half, second_half = value[:half_dim], value[half_dim:]
                        value = jnp.concatenate(
                            [
                                first_half * cos_out[...] - second_half * sin_out[...],
                                second_half * cos_out[...] + first_half * sin_out[...],
                            ],
                            axis=0,
                        )
                    note_ref[index * HEADS + half * heads + head, part] = value.astype(jnp.bfloat16)

    def slot(device, part):
        return unit_out.at[part, :, pl.ds(pl.multiple_of(device * tokens, 128), tokens)]

    def send_part(part):
        @pl.when(holder)
        def _():
            pltpu.make_async_copy(note_ref.at[mine, part], slot(me, part), unit_recv).start()

        def send(step, carry):
            peer = lax.rem(me + step, total)
            unit, held = unit_of(peer, total)

            @pl.when(held)
            def _():
                remote(
                    note_ref.at[unit, part], slot(me, part), unit_send, unit_recv, (peer // 2, lax.rem(peer, 2))
                ).start()

            return carry

        lax.fori_loop(1, total, send, 0)

    def doc_starts():
        docs = doc_ref[...]
        lane = lax.broadcasted_iota(jnp.int32, docs.shape, 1)
        row = lax.broadcasted_iota(jnp.int32, docs.shape, 0)
        place_at = row * tokens + lane
        before = jnp.where(
            lane == 0, pltpu.roll(pltpu.roll(docs, 1, 0), 1, 1), pltpu.roll(docs, 1, 1)
        )
        begins = (docs != before) | (place_at == 0)
        value = jnp.where(begins, place_at, 0).astype(jnp.float32)
        step = 1
        while step < tokens:
            value = jnp.maximum(value, jnp.where(lane >= step, pltpu.roll(value, step, 1), 0.0))
            step *= 2
        carried = jnp.broadcast_to(jnp.max(value, axis=1, keepdims=True), docs.shape)
        carried = jnp.where(row >= 1, pltpu.roll(carried, 1, 0), 0.0)
        step = 1
        while step < total:
            carried = jnp.maximum(carried, jnp.where(row >= step, pltpu.roll(carried, step, 0), 0.0))
            step *= 2
        starts = jnp.maximum(value, carried).astype(jnp.int32)
        for peer in range(total):
            start_out[:, pl.ds(peer * tokens, tokens)] = starts[peer : peer + 1, :]

    length = tokens * total
    tiles = length // TILE
    reach = (TILE + DOC_MAX - 2) // TILE

    def open_units():
        @pl.when(holder)
        def _():
            part = note_ref.at[pl.ds(0, UNITS - 1)]
            pltpu.make_async_copy(unit_out, unit_out, unit_recv).wait()
            pltpu.make_async_copy(part, part, unit_send).wait()

        @pl.when(jnp.logical_not(holder))
        def _():
            pltpu.make_async_copy(note_ref, note_ref, unit_send).wait()

    def attend(query_tile):
        @pl.when(holder)
        def _():
            columns = pl.ds(query_tile * TILE, TILE)
            query_t = unit_out[0, :, columns]
            first_row = start_out[:, columns]

            def one_key(step, state):
                peak, weight, mixed = state
                key_tile = query_tile - step
                scores = dot_nn(tile_at(unit_out, key_tile, 1).T, query_t) * (SCORE_SCALE * LOG2E)
                scores = jnp.where(tile_mask(key_tile, query_tile, first_row), scores, -1e30)
                new_peak = jnp.maximum(peak, jnp.max(scores, axis=0, keepdims=True))
                probs = jnp.exp2(scores - new_peak)
                fade = jnp.exp2(peak - new_peak)
                weight = weight * fade + jnp.sum(probs, axis=0, keepdims=True)
                mixed = mixed * fade + dot_nn(tile_at(unit_out, key_tile, 2), probs.astype(jnp.bfloat16))
                return new_peak, weight, mixed

            begin = (
                jnp.full((1, TILE), -1e30, jnp.float32),
                jnp.zeros((1, TILE), jnp.float32),
                jnp.zeros((HEAD_DIM, TILE), jnp.float32),
            )
            peak, weight, mixed = lax.fori_loop(0, min(query_tile, reach) + 1, one_key, begin)
            mixed_out[:, columns] = mixed / weight
            total_out[:, columns] = peak + jnp.log2(weight)

    def back_slot(device):
        return turned_ref.at[:, pl.ds(pl.multiple_of(device * tokens, 128), tokens)]

    def send_back():
        @pl.when(holder)
        def _():
            def turn(step, carry):
                part = pl.ds(pl.multiple_of(step * 16, 16), 16)
                turned_ref[part, :] = pltpu.roll(mixed_out[part, :], length - LEAD, 1).astype(jnp.bfloat16)
                return carry

            lax.fori_loop(0, HEAD_DIM // 16, turn, 0)
            pltpu.make_async_copy(back_slot(me), att_out.at[mine], att_recv).start()

            def send(step, carry):
                peer = lax.rem(me + step, total)
                remote(
                    back_slot(peer), att_out.at[mine], att_send, att_recv, (peer // 2, lax.rem(peer, 2))
                ).start()
                return carry

            lax.fori_loop(1, total, send, 0)

    gather_step(0)
    lax.fori_loop(1, total, send_small, 0)
    tables()
    gather_step(1)
    gather_step(2)
    for lead in leads:
        lead.start()
    normalise()
    gather_step(3)
    doc_starts()
    for part in range(3):
        gather_step(4 + part)
        if part == 2:
            keep = pltpu.make_async_copy(qkv_ref, qkv_out, load_sem.at[1])
            keep.start()
        project(part)
        send_part(part)
    wait_steps = 2
    for step in range(wait_steps):
        gather_step(7 + step)
    open_units()
    for tile in range(tiles):
        attend(tile)
        if tile % 2 == 1 and tile < tiles - 1:
            gather_step(7 + wait_steps + tile // 2)
    send_back()
    for step in range(7 + wait_steps + (tiles - 1) // 2, pairs + 4):
        gather_step(step)
    for index in range(count):
        for phase in range(4):
            sent(index, phase)
    for lead in leads:
        lead.wait()
    keep.wait()
    rest = small_all.at[pl.ds(0, total - 1)]
    pltpu.make_async_copy(rest, rest, misc_sem.at[0]).wait()
    pltpu.make_async_copy(att_out, att_out, att_recv).wait()

    @pl.when(holder)
    def _():
        part = turned_ref.at[:, pl.ds(0, tokens * (total - 1))]
        pltpu.make_async_copy(part, part, att_send).wait()


def first(depth, w_qkv, w_attn_out, w_cross_q, w_cross_out, w_kv, w_up, w_down, small, hidden, grads):
    total = depth * 8
    rows = w_qkv.shape[0]
    down_rows = w_down.shape[0]
    micro, tokens, width = hidden.shape
    length = tokens * total
    third = down_rows // 3
    items = [
        (0, 0, 1, 0), (0, 1, 2, 1), (0, 2, 3, 0), (0, 3, 4, 1), (0, 4, 5, 0), (0, 5, 6, 1),
        (1, 0, 1, 0), (1, 1, 2, 1),
        (2, 0, 1, 0), (2, 1, 2, 1),
        (1, 2, 3, 0), (3, 0, 1, 1),
        (3, 1, 2, 0), (3, 2, 3, 1),
        (3, 3, 4, 0), (4, 0, third, 1),
        (4, third, 2 * third, 0), (4, 2 * third, down_rows, 1),
    ]
    count = len(items)
    low, high = jnp.bfloat16, jnp.float32
    spots = (depth, 2, 2, 2)
    qkv_shape = (6, *spots, rows, width // 2)
    out_shape = [
        jax.ShapeDtypeStruct(qkv_shape, low),
        jax.ShapeDtypeStruct((3, *spots, rows, width), low),
        jax.ShapeDtypeStruct((2, *spots, rows, width), low),
        jax.ShapeDtypeStruct((w_up.shape[1] // width, *spots, rows, width), low),
        jax.ShapeDtypeStruct((*spots, down_rows, width), low),
        jax.ShapeDtypeStruct((micro, 64, width), low),
        jax.ShapeDtypeStruct((micro, 64, width), low),
        jax.ShapeDtypeStruct((8, width), high),
        jax.ShapeDtypeStruct((HEAD_DIM // 2, tokens), high),
        jax.ShapeDtypeStruct((HEAD_DIM // 2, tokens), high),
        jax.ShapeDtypeStruct((3, HEAD_DIM, length), low),
        jax.ShapeDtypeStruct((HEAD_DIM, length), high),
        jax.ShapeDtypeStruct((1, length), high),
        jax.ShapeDtypeStruct((1, length), jnp.int32),
        jax.ShapeDtypeStruct((UNITS, HEAD_DIM, tokens), low),
    ]
    dma = pltpu.SemaphoreType.DMA
    return pl.pallas_call(
        functools.partial(first_kernel, depth, items),
        out_shape=out_shape,
        in_specs=[VMEM] * 8 + [ANY] * 2,
        out_specs=[ANY] * 7 + [VMEM] * 8,
        scratch_shapes=[
            pltpu.VMEM(qkv_shape, low),
            pltpu.VMEM((total,) + small.shape, low),
            pltpu.VMEM(hidden.shape, low),
            pltpu.VMEM((micro * tokens, width), low),
            pltpu.VMEM((width, width // 2), high),
            pltpu.VMEM((UNITS, 3, HEAD_DIM, tokens), low),
            pltpu.VMEM((HEAD_DIM, length), low),
            pltpu.VMEM((total, tokens), high),
            dma((count,)), dma((count, 4)), dma((count, 4)), dma((2,)), dma((2,)), dma((2,)), dma((2,)), dma, dma,
            dma, dma,
        ],
        compiler_params=pltpu.CompilerParams(
            collective_id=0, has_side_effects=True, vmem_limit_bytes=62 * 2**20
        ),
        cost_estimate=pl.CostEstimate(flops=10**9, bytes_accessed=20 * 10**6, transcendentals=0),
    )(w_qkv, w_attn_out, w_cross_q, w_cross_out, w_kv, w_up, w_down, small, hidden, grads)


def dot_nn(left, right):
    return jnp.dot(left, right, preferred_element_type=jnp.float32)


def dot_nt(left, right):
    return lax.dot_general(left, right, (((1,), (1,)), ((), ())), preferred_element_type=jnp.float32)


def dot_tn(left, right):
    return lax.dot_general(left, right, (((0,), (0,)), ((), ())), preferred_element_type=jnp.float32)


def norm_parts(values):
    centred = values - jnp.mean(values, axis=-1, keepdims=True)
    scale = lax.rsqrt(jnp.mean(centred * centred, axis=-1, keepdims=True) + 1e-05)
    return centred * scale, scale


def norm_pull(values, gain, grad):
    unit, scale = norm_parts(values)
    scaled = grad * gain
    pulled = scale * (
        scaled
        - jnp.mean(scaled, axis=-1, keepdims=True)
        - unit * jnp.mean(scaled * unit, axis=-1, keepdims=True)
    )
    return pulled, jnp.sum(grad * unit, axis=0, keepdims=True)


def shift_rows(rows, lead):
    joined = jnp.concatenate([rows.astype(jnp.float32), lead.astype(jnp.float32)], axis=0)
    return pltpu.roll(joined, joined.shape[0] - LEAD, 0)[: rows.shape[0]]


def stack_pair(rows):
    lane = lax.broadcasted_iota(jnp.int32, rows.shape, 1)
    zero = jnp.zeros_like(rows)
    return jnp.concatenate(
        [jnp.where(lane < HEAD_DIM, rows, zero), jnp.where(lane < HEAD_DIM, zero, rows)], axis=0
    )


def unstack_pair(rows):
    lane = lax.broadcasted_iota(jnp.int32, (SPAN, 2 * HEAD_DIM), 1)
    return jnp.where(lane < HEAD_DIM, rows[:SPAN], rows[SPAN:])


def middle_kernel(
    att_ref, hid_ref, lead_hid_ref, grad_ref, lead_grad_ref, gain_ref, used_ref, sq_ref, kv_hbm, neigh_hbm,
    up_hbm, down_hbm,
    result_ref, first_ref, d_att_ref, n2_ref, d_cq_ref, cm_ref, gc_ref, ga_ref, gy_ref, act_ref, d_pair_ref,
    d_gain_ref, d_up_hbm,
    kv_ref, neigh_ref, up_ref, down_ref, att_rows, second_ref, cq_ref, pair_ref, prob_ref, acc_ref, d_n3_ref,
    n3_ref, n3t_ref, d_up_ref, sems,
):
    micro, tokens, width = hid_ref.shape
    rows = micro * tokens
    pulls = [
        pltpu.make_async_copy(src, dst, sems.at[index])
        for index, (src, dst) in enumerate(
            [(kv_hbm, kv_ref), (neigh_hbm, neigh_ref), (up_hbm, up_ref), (down_hbm, down_ref)]
        )
    ]
    for pull in pulls:
        pull.start()
    gain_cross, gain_mlp = gain_ref[1:2, :], gain_ref[2:3, :]
    for index in range(micro):
        part = pl.ds(index * tokens, tokens)
        hidden = shift_rows(hid_ref[index], lead_hid_ref[index])
        gy_ref[part, :] = shift_rows(grad_ref[index], lead_grad_ref[index]).astype(jnp.bfloat16)
        first_ref[part, :] = hidden + dot_tn(att_ref[index], sq_ref[0])
    n2_ref[...] = (norm_parts(first_ref[...])[0] * gain_cross).astype(jnp.bfloat16)
    cq_ref[...] = dot_nn(n2_ref[...], sq_ref[1]).astype(jnp.bfloat16)

    pulls[0].wait()
    pulls[1].wait()
    chunk = 256
    chunks = neigh_ref.shape[0] // chunk

    def make_pairs(step, carry):
        side, block = step // chunks, lax.rem(step, chunks)
        part = pl.ds(pl.multiple_of(block * chunk, chunk), chunk)
        pair_ref[side, part, :] = dot_nn(neigh_ref[part, :], kv_ref[side]).astype(jnp.bfloat16)
        return carry

    lax.fori_loop(0, 2 * chunks, make_pairs, 0)
    couples = HEADS // 2
    pair_rows = NEIGHBOURS * NEIGH_LEN
    groups = rows // SPAN

    def where(step):
        group, couple = step // couples, lax.rem(step, couples)
        tok = pl.ds(pl.multiple_of(group * SPAN, SPAN), SPAN)
        key = pl.ds(pl.multiple_of(group * pair_rows, pair_rows), pair_rows)
        lanes = pl.ds(pl.multiple_of(couple * 2 * HEAD_DIM, 2 * HEAD_DIM), 2 * HEAD_DIM)
        return tok, key, lanes

    def cross_step(step, carry):
        tok, key, lanes = where(step)
        query = stack_pair(cq_ref[tok, lanes])
        scores = dot_nt(query, pair_ref[0, key, lanes]) * SCORE_SCALE
        weights = jnp.exp(scores - jnp.max(scores, axis=-1, keepdims=True))
        probs = weights / jnp.sum(weights, axis=-1, keepdims=True)
        prob_ref[step] = probs
        mixed = unstack_pair(dot_nn(probs.astype(jnp.bfloat16), pair_ref[1, key, lanes]))
        cm_ref[tok, lanes] = (mixed * used_ref[tok, :]).astype(jnp.bfloat16)
        return carry

    lax.fori_loop(0, groups * couples, cross_step, 0)
    second_ref[...] = first_ref[...] + dot_nn(cm_ref[...], sq_ref[2])
    n3 = (norm_parts(second_ref[...])[0] * gain_mlp).astype(jnp.bfloat16)
    n3_ref[...] = n3
    n3t_ref[...] = n3.T
    acc_ref[...] = second_ref[...]
    d_n3_ref[...] = jnp.zeros_like(d_n3_ref)
    pulls[2].wait()
    pulls[3].wait()
    ff_blocks = up_ref.shape[0]

    def mlp_step(step, carry):
        cols = pl.ds(pl.multiple_of(step * width, width), width)
        upper = dot_nn(n3_ref[...], up_ref[step])
        square = upper * upper
        flat = jnp.tanh(math.sqrt(2.0 / math.pi) * upper * (1.0 + 0.044715 * square))
        half = 0.5 * (1.0 + flat)
        active = (upper * half).astype(jnp.bfloat16)
        act_ref[:, cols] = active
        slope = half + 0.5 * upper * (1.0 - flat * flat) * math.sqrt(2.0 / math.pi) * (
            1.0 + 3.0 * 0.044715 * square
        )
        d_upper = (dot_nt(gy_ref[...], down_ref[cols, :]) * slope).astype(jnp.bfloat16)
        acc_ref[...] += dot_nn(active, down_ref[cols, :])
        d_n3_ref[...] += dot_nt(d_upper, up_ref[step])
        d_up_ref[:, cols] = dot_nn(n3t_ref[...], d_upper).astype(jnp.bfloat16)
        pltpu.make_async_copy(d_up_ref.at[:, cols], d_up_hbm.at[:, cols], sems.at[4]).start()
        return carry

    lax.fori_loop(0, ff_blocks, mlp_step, 0)
    result_ref[...] = acc_ref[...].astype(jnp.bfloat16)
    pulled, d_gain_mlp = norm_pull(second_ref[...], gain_mlp, d_n3_ref[...])
    d_second = gy_ref[...].astype(jnp.float32) + pulled
    acc_ref[...] = d_second
    gc_ref[...] = d_second.astype(jnp.bfloat16)
    att_rows[...] = (
        dot_nt(gc_ref[...], sq_ref[2]).astype(jnp.bfloat16).astype(jnp.float32) * used_ref[...]
    ).astype(jnp.bfloat16)

    def cross_back(step, carry):
        tok, key, lanes = where(step)
        grad = stack_pair(att_rows[tok, lanes])
        query = stack_pair(cq_ref[tok, lanes])
        probs = prob_ref[step]
        d_probs = dot_nt(grad, pair_ref[1, key, lanes])
        d_scores = (
            probs * (d_probs - jnp.sum(probs * d_probs, axis=-1, keepdims=True))
        ).astype(jnp.bfloat16)
        d_query = unstack_pair(dot_nn(d_scores, pair_ref[0, key, lanes]))
        d_cq_ref[tok, lanes] = (d_query * SCORE_SCALE).astype(jnp.bfloat16)
        d_pair_ref[0, key, lanes] = (dot_tn(d_scores, query) * SCORE_SCALE).astype(jnp.bfloat16)
        d_pair_ref[1, key, lanes] = dot_tn(probs.astype(jnp.bfloat16), grad).astype(jnp.bfloat16)
        return carry

    lax.fori_loop(0, groups * couples, cross_back, 0)
    pulled, d_gain_cross = norm_pull(first_ref[...], gain_cross, dot_nt(d_cq_ref[...], sq_ref[1]))
    d_first = acc_ref[...] + pulled
    first_ref[...] = d_first
    ga_ref[...] = d_first.astype(jnp.bfloat16)
    for index in range(micro):
        d_att_ref[index] = dot_nt(sq_ref[0], ga_ref[pl.ds(index * tokens, tokens), :]).astype(jnp.bfloat16)
    d_gain_ref[...] = jnp.concatenate([d_gain_cross, d_gain_mlp, jnp.zeros((6, width), jnp.float32)], axis=0)
    pltpu.make_async_copy(d_up_ref, d_up_hbm, sems.at[4]).wait()


def middle(attended_t, hidden, lead_hid, grads, lead_grad, gains, used, squares, kv, neigh, up, down):
    micro, tokens, width = hidden.shape
    rows = micro * tokens
    ff = up.shape[0] * width
    low = jnp.bfloat16
    out_shape = [
        jax.ShapeDtypeStruct((rows, width), low),
        jax.ShapeDtypeStruct((rows, width), jnp.float32),
        jax.ShapeDtypeStruct((micro, width, tokens), low),
        jax.ShapeDtypeStruct((rows, width), low),
        jax.ShapeDtypeStruct((rows, width), low),
        jax.ShapeDtypeStruct((rows, width), low),
        jax.ShapeDtypeStruct((rows, width), low),
        jax.ShapeDtypeStruct((rows, width), low),
        jax.ShapeDtypeStruct((rows, width), low),
        jax.ShapeDtypeStruct((rows, ff), low),
        jax.ShapeDtypeStruct((2,) + neigh.shape, low),
        jax.ShapeDtypeStruct((8, width), jnp.float32),
        jax.ShapeDtypeStruct((width, ff), low),
    ]
    steps = rows // SPAN * HEADS // 2
    scratch = [
        pltpu.VMEM(kv.shape, low),
        pltpu.VMEM(neigh.shape, low),
        pltpu.VMEM(up.shape, low),
        pltpu.VMEM(down.shape, low),
        pltpu.VMEM((rows, width), low),
        pltpu.VMEM((rows, width), jnp.float32),
        pltpu.VMEM((rows, width), low),
        pltpu.VMEM((2,) + neigh.shape, low),
        pltpu.VMEM((steps, 2 * SPAN, NEIGHBOURS * NEIGH_LEN), jnp.float32),
        pltpu.VMEM((rows, width), jnp.float32),
        pltpu.VMEM((rows, width), jnp.float32),
        pltpu.VMEM((rows, width), low),
        pltpu.VMEM((width, rows), low),
        pltpu.VMEM((width, ff), low),
        pltpu.SemaphoreType.DMA((5,)),
    ]
    return pl.pallas_call(
        middle_kernel,
        out_shape=out_shape,
        in_specs=[VMEM] * 8 + [ANY] * 4,
        out_specs=[VMEM] * 12 + [ANY],
        scratch_shapes=scratch,
        compiler_params=local_params(),
        cost_estimate=pl.CostEstimate(flops=12 * 10**9, bytes_accessed=40 * 10**6, transcendentals=10**6),
    )(attended_t, hidden, lead_hid, grads, lead_grad, gains, used, squares, kv, neigh, up, down)


def last_kernel(depth, items, skew, *refs):
    count = len(items)
    (
        back_ref, result_ref, first_ref, n2_ref, d_cq_ref, cm_ref, gc_ref, ga_ref, gy_ref, act_ref, d_pair_ref,
        att_ref, neigh_ref, kv_ref, qkv_ref, hidden_ref, gain_ref, cos_ref, sin_ref, d_gain_rest_ref,
    ) = refs[:20]
    (
        output_ref, grad_in_ref, grad_neigh_ref, out_qkv, out_att, out_cq, out_co, out_kv, out_down, gain_out,
    ) = refs[20:30]
    full = refs[30 : 30 + count]
    got_core = refs[30 + count : 30 + 2 * count]
    got_one = refs[30 + 2 * count : 30 + 3 * count]
    got_two = refs[30 + 3 * count : 30 + 4 * count]
    got_z = refs[30 + 4 * count : 30 + 5 * count]
    (
        sent_ref, tail_first, tail_result, raw_ref, n1t_ref, d_n1_ref, temp_ref, gain_mine, gain_got, gain_z,
        send_sem, recv_sem, unit_send, unit_recv, tail_send, tail_recv, gain_send, gain_recv,
    ) = refs[30 + 5 * count :]
    micro, tokens, width = hidden_ref.shape
    total = depth * 8
    z, y, c, x = coords()
    me = lax.axis_index("blk") * 2 + lax.axis_index("head")
    mine, holder = unit_of(me, total)
    whole = slice(None)
    all_barrier(total, me)

    after = lax.rem(me + 1, total)
    after_at = (after // 2, lax.rem(after, 2))
    tails = []
    for index in range(micro):
        part = pl.ds(index * tokens + tokens - 64, 64)
        tails.append(
            remote(first_ref.at[part], tail_first.at[index], tail_send.at[index], tail_recv.at[index], after_at)
        )
        tails.append(
            remote(
                result_ref.at[part], tail_result.at[index],
                tail_send.at[micro + index], tail_recv.at[micro + index], after_at,
            )
        )

    def slot(device):
        return back_ref.at[:, :, pl.ds(pl.multiple_of(device * tokens, 128), tokens)]

    @pl.when(holder)
    def _():
        pltpu.make_async_copy(slot(me), sent_ref.at[mine], unit_recv).start()

        def send(step, carry):
            peer = lax.rem(me + step, total)
            remote(
                slot(peer), sent_ref.at[mine], unit_send, unit_recv, (peer // 2, lax.rem(peer, 2))
            ).start()
            return carry

        lax.fori_loop(1, total, send, 0)

    for tail in tails:
        tail.start()

    slab = full[0].shape[-2]

    def spread(index, block):
        buffer = full[index]
        cols = buffer.shape[-1]

        def body(level, carry):
            for place_in in range(8):
                at = pl.multiple_of((level * 8 + place_in) * slab, 8)
                buffer[block, level, place_in // 4, (place_in // 2) % 2, place_in % 2] = temp_ref[
                    pl.ds(at, slab), :cols
                ].astype(jnp.bfloat16)
            return carry

        lax.fori_loop(0, depth, body, 0)

    down_index = [index for index, item in enumerate(items) if item[0] == "down"]

    def make_down():
        def body(level, carry):
            cols = pl.ds(pl.multiple_of(level * width, width), width)
            temp_ref[...] = dot_tn(act_ref[:, cols], gy_ref[...])
            for place_in in range(8):
                for part, index in enumerate(down_index):
                    at = place_in * slab * len(down_index) + part * slab
                    full[index][0, level, place_in // 4, (place_in // 2) % 2, place_in % 2] = temp_ref[
                        pl.ds(at, slab), :
                    ].astype(jnp.bfloat16)
            return carry

        lax.fori_loop(0, depth, body, 0)

    def take_units():
        @pl.when(holder)
        def _():
            part = back_ref.at[:, :, pl.ds(0, tokens * (total - 1))]
            pltpu.make_async_copy(part, part, unit_send).wait()

        pltpu.make_async_copy(sent_ref, sent_ref, unit_recv).wait()
        half = HEAD_DIM // 2

        def body(head, carry):
            for index in range(micro):
                lanes = pl.ds(index * tokens, tokens)
                cosine, sine = cos_ref[...], sin_ref[...]
                for part in range(3):
                    value = sent_ref[index * HEADS + head, part].astype(jnp.float32)
                    at = pl.multiple_of(part * width + head * HEAD_DIM, HEAD_DIM)
                    if part < 2:
                        first_half, second_half = value[:half], value[half:]
                        value = jnp.concatenate(
                            [
                                first_half * cosine + second_half * sine,
                                second_half * cosine - first_half * sine,
                            ],
                            axis=0,
                        )
                    raw_ref[pl.ds(at, HEAD_DIM), lanes] = value.astype(jnp.bfloat16)
            return carry

        lax.fori_loop(0, HEADS, body, 0)
        for index in range(micro):
            normed = norm_parts(hidden_ref[index].astype(jnp.float32))[0] * gain_ref[0:1, :]
            n1t_ref[:, pl.ds(index * tokens, tokens)] = normed.astype(jnp.bfloat16).T

    def make(index):
        kind, which = items[index][:2]
        if kind == "down":
            if index == down_index[0]:
                make_down()
            return
        if kind == "kv":
            temp_ref[...] = dot_tn(neigh_ref[...], d_pair_ref[which])
        elif kind == "att":
            temp_ref[...] = dot_nn(att_ref[0], ga_ref[pl.ds(0, tokens), :])
            for step in range(1, micro):
                temp_ref[...] += dot_nn(att_ref[step], ga_ref[pl.ds(step * tokens, tokens), :])
        elif kind == "cq":
            temp_ref[...] = dot_tn(n2_ref[...], d_cq_ref[...])
        elif kind == "co":
            temp_ref[...] = dot_tn(cm_ref[...], gc_ref[...])
        else:
            if which == 0:
                take_units()
            for block in range(2):
                half = width // 2
                at = which * width + block * half
                temp_ref[:, :half] = dot_nt(n1t_ref[...], raw_ref[pl.ds(at, half), :])
                spread(index, block)
            return
        spread(index, 0)

    def core(index):
        return remote(
            full[index].at[whole, whole, whole, 1 - c], got_core[index],
            send_sem.at[index, 0], recv_sem.at[index, 0], place(z, y, 1 - c, x),
        )

    def one(index):
        if items[index][2] == 0:
            src, where = full[index].at[whole, whole, 1 - y, c], place(z, 1 - y, c, x)
        else:
            src, where = full[index].at[whole, whole, whole, c, 1 - x], place(z, y, c, 1 - x)
        return remote(src, got_one[index], send_sem.at[index, 1], recv_sem.at[index, 1], where)

    def two(index):
        if items[index][2] == 0:
            src, where = full[index].at[whole, whole, y, c, 1 - x], place(z, y, c, 1 - x)
        else:
            src, where = full[index].at[whole, whole, 1 - y, c, x], place(z, 1 - y, c, x)
        return remote(src, got_two[index], send_sem.at[index, 2], recv_sem.at[index, 2], where)

    def send_z(index):
        for step in range(1, depth):
            other = lax.rem(z + step, depth)
            remote(
                full[index].at[whole, other, y, c, x], got_z[index].at[z],
                send_sem.at[index, 3], recv_sem.at[index, 3], place(other, y, c, x),
            ).start()

    def add_into(target, source):
        target[...] = (target[...].astype(jnp.float32) + source[...].astype(jnp.float32)).astype(
            jnp.bfloat16
        )

    def each_level(index, body):
        blocks = full[index].shape[0]
        lax.fori_loop(
            0, blocks * depth, lambda step, carry: (body(step // depth, lax.rem(step, depth)), carry)[1], 0
        )

    def sum_core(index):
        def body(block, level):
            for row in range(2):
                for col in range(2):
                    add_into(
                        full[index].at[block, level, row, c, col], got_core[index].at[block, level, row, col]
                    )

        each_level(index, body)

    def sum_one(index):
        def body(block, level):
            for side in range(2):
                if items[index][2] == 0:
                    target = full[index].at[block, level, y, c, side]
                else:
                    target = full[index].at[block, level, side, c, x]
                add_into(target, got_one[index].at[block, level, side])

        each_level(index, body)

    def sum_two(index):
        each_level(
            index,
            lambda block, level: add_into(
                full[index].at[block, level, y, c, x], got_two[index].at[block, level]
            ),
        )

    def sum_z(index):
        kind, which = items[index][:2]
        for block in range(full[index].shape[0]):
            value = full[index][block, z, y, c, x].astype(jnp.float32)
            for step in range(1, depth):
                value = value + got_z[index][lax.rem(z + step, depth), block].astype(jnp.float32)
            if kind == "down":
                out_down[pl.ds(which * slab, slab), :] = value
            elif kind == "kv":
                out_kv[:, pl.ds(which * width, width)] = value
            elif kind == "qkv":
                out_qkv[:, pl.ds(which * width + block * (width // 2), width // 2)] = value
            else:
                {"att": out_att, "cq": out_cq, "co": out_co}[kind][...] = value

    def phase(index, number):
        if number == 0:
            make(index)
            core(index).start()
        elif number == 1:
            core(index).wait_recv()
            sum_core(index)
            one(index).start()
        elif number == 2:
            one(index).wait_recv()
            sum_one(index)
            two(index).start()
        elif number == 3:
            two(index).wait_recv()
            sum_two(index)
            send_z(index)
        else:
            landed = got_z[index].at[pl.ds(0, depth - 1)]
            pltpu.make_async_copy(landed, landed, recv_sem.at[index, 3]).wait()
            sum_z(index)

    def gain_copy(stage):
        where = (place(z, y, 1 - c, x), place(z, 1 - y, c, x), place(z, y, c, 1 - x))[stage]
        return remote(
            gain_mine.at[stage], gain_got.at[stage], gain_send.at[stage], gain_recv.at[stage], where
        )

    def gain_phase(number):
        if number == 0:
            gain_copy(0).start()
        elif number < 4:
            gain_copy(number - 1).wait_recv()
            gain_mine[number] = gain_mine[number - 1] + gain_got[number - 1]
            if number < 3:
                gain_copy(number).start()
            else:
                for step in range(1, depth):
                    other = lax.rem(z + step, depth)
                    remote(
                        gain_mine.at[3], gain_z.at[z], gain_send.at[3], gain_recv.at[3], place(other, y, c, x)
                    ).start()
        else:
            landed = gain_z.at[pl.ds(0, depth - 1)]
            pltpu.make_async_copy(landed, landed, gain_recv.at[3]).wait()
            value = gain_mine[3]
            for step in range(1, depth):
                value = value + gain_z[lax.rem(z + step, depth)]
            gain_out[...] = value

    def neighbours_part(block):
        chunk = 256
        part = pl.ds(block * chunk, chunk)
        grad_neigh_ref[part, :] = (
            dot_nt(d_pair_ref[0, part, :], kv_ref[0]) + dot_nt(d_pair_ref[1, part, :], kv_ref[1])
        ).astype(jnp.bfloat16)

    def input_part():
        half = width // 2
        blocks = qkv_ref.shape[0]
        d_n1_ref[...] = dot_nn(qkv_ref[0], raw_ref[pl.ds(0, half), :])
        for block in range(1, blocks):
            d_n1_ref[...] += dot_nn(qkv_ref[block], raw_ref[pl.ds(block * half, half), :])
        for tail in tails:
            tail.wait()
        d_gain = jnp.zeros((1, width), jnp.float32)
        for index in range(micro):
            part = pl.ds(index * tokens, tokens)
            d_normed = d_n1_ref[:, part].T
            pulled, part_gain = norm_pull(hidden_ref[index].astype(jnp.float32), gain_ref[0:1, :], d_normed)
            d_gain = d_gain + part_gain
            joined = jnp.concatenate([tail_first[index], first_ref[part, :]], axis=0)
            home = pltpu.roll(joined, joined.shape[0] - 1, 0)[:tokens]
            grad_in_ref[part, :] = (home + pulled).astype(jnp.bfloat16)
            joined = jnp.concatenate(
                [tail_result[index].astype(jnp.float32), result_ref[part, :].astype(jnp.float32)], axis=0
            )
            output_ref[part, :] = pltpu.roll(joined, joined.shape[0] - 1, 0)[:tokens].astype(jnp.bfloat16)
        gain_mine[0] = jnp.concatenate([d_gain, d_gain_rest_ref[0:7, :]], axis=0)

    pairs = (count + 1) // 2
    chunks = neigh_ref.shape[0] // 256
    for step in range(pairs + skew * 4):
        for number in range(4, -1, -1):
            pair = step - skew * number
            if not 0 <= pair < pairs:
                continue
            for index in range(2 * pair, min(2 * pair + 2, count)):
                phase(index, number)
            if pair == pairs - 1:
                if number == 0:
                    input_part()
                gain_phase(number)
        if 1 <= step <= chunks:
            neighbours_part(step - 1)
    for index in range(count):
        core(index).wait_send()
        one(index).wait_send()
        two(index).wait_send()
        gone = got_z[index].at[pl.ds(0, depth - 1)]
        pltpu.make_async_copy(gone, gone, send_sem.at[index, 3]).wait()
    for stage in range(3):
        gain_copy(stage).wait_send()
    gone = gain_z.at[pl.ds(0, depth - 1)]
    pltpu.make_async_copy(gone, gone, gain_send.at[3]).wait()


def last(depth, collective, ff, *args):
    hidden = args[15]
    micro, tokens, width = hidden.shape
    rows = micro * tokens
    total = depth * 8
    slab = width // total
    neigh_rows = args[12].shape[0]
    items = [
        ("down", 0, 0), ("down", 1, 1), ("down", 2, 0), ("down", 3, 1), ("kv", 0, 0), ("kv", 1, 1),
        ("att", 0, 0), ("cq", 0, 1), ("co", 0, 0), ("qkv", 0, 1), ("qkv", 1, 0), ("qkv", 2, 1),
    ]
    count = len(items)
    low, high = jnp.bfloat16, jnp.float32
    out_shape = [
        jax.ShapeDtypeStruct((rows, width), low),
        jax.ShapeDtypeStruct((rows, width), low),
        jax.ShapeDtypeStruct((neigh_rows, width), low),
        jax.ShapeDtypeStruct((slab, 3 * width), high),
        jax.ShapeDtypeStruct((slab, width), high),
        jax.ShapeDtypeStruct((slab, width), high),
        jax.ShapeDtypeStruct((slab, width), high),
        jax.ShapeDtypeStruct((slab, 2 * width), high),
        jax.ShapeDtypeStruct((ff // total, width), high),
        jax.ShapeDtypeStruct((8, width), high),
    ]
    full, core, one, two, along = [], [], [], [], []
    for kind, which, order in items:
        blocks, cols = (2, width // 2) if kind == "qkv" else (1, width)
        full.append(pltpu.VMEM((blocks, depth, 2, 2, 2, slab, cols), low))
        core.append(pltpu.VMEM((blocks, depth, 2, 2, slab, cols), low))
        one.append(pltpu.VMEM((blocks, depth, 2, slab, cols), low))
        two.append(pltpu.VMEM((blocks, depth, slab, cols), low))
        along.append(pltpu.VMEM((depth, blocks, slab, cols), low))
    dma = pltpu.SemaphoreType.DMA
    scratch = full + core + one + two + along + [
        pltpu.VMEM((UNITS, 3, HEAD_DIM, tokens), low),
        pltpu.VMEM((micro, 64, width), high),
        pltpu.VMEM((micro, 64, width), low),
        pltpu.VMEM((3 * width, rows), low),
        pltpu.VMEM((width, rows), low),
        pltpu.VMEM((width, rows), high),
        pltpu.VMEM((width, width), high),
        pltpu.VMEM((4, 8, width), high),
        pltpu.VMEM((3, 8, width), high),
        pltpu.VMEM((depth, 8, width), high),
        dma((count, 4)), dma((count, 4)), dma, dma, dma((2 * micro,)), dma((2 * micro,)), dma((4,)), dma((4,)),
    ]
    return pl.pallas_call(
        functools.partial(last_kernel, depth, items, 2),
        out_shape=out_shape,
        in_specs=[ANY] + [VMEM] * 19,
        out_specs=[VMEM] * 10,
        scratch_shapes=scratch,
        compiler_params=pltpu.CompilerParams(
            collective_id=collective, has_side_effects=True, vmem_limit_bytes=62 * 2**20
        ),
        cost_estimate=pl.CostEstimate(flops=10**10, bytes_accessed=40 * 10**6, transcendentals=0),
    )(*args)


def finish_kernel(copies, *refs):
    for source, result in zip(refs[:copies], refs[copies:]):
        result[...] = source[...].astype(result.dtype)


def finish(arrays, low):
    arrays = [*arrays, low]
    copies = len(arrays)
    vmem = pl.BlockSpec(memory_space=pltpu.VMEM)
    return pl.pallas_call(
        functools.partial(finish_kernel, copies),
        out_shape=[jax.ShapeDtypeStruct(a.shape, a.dtype) for a in arrays[:-1]]
        + [jax.ShapeDtypeStruct(low.shape, jnp.float32)],
        in_specs=[vmem] * copies,
        out_specs=[vmem] * copies,
        compiler_params=pltpu.CompilerParams(vmem_limit_bytes=62 * 2**20),
    )(*arrays)


def layer_norm(values, norm_gain):
    centred = values - jnp.mean(values, axis=-1, keepdims=True)
    spread = jnp.mean(centred * centred, axis=-1, keepdims=True)
    return centred * lax.rsqrt(spread + 1e-05) * norm_gain


def norm_backward(values, norm_gain, grad_out):
    result, pullback = jax.vjp(layer_norm, values, norm_gain)
    return pullback(grad_out)


def outer(left, right):
    return jnp.einsum("td,te->de", left, right, preferred_element_type=jnp.float32)


def turn_heads(values, cosine, sine):
    first_half, second_half = values[:, :32], values[:, 32:]
    return jnp.concatenate(
        [first_half * cosine - second_half * sine, second_half * cosine + first_half * sine], axis=1
    )


def on_device(
    hidden_in,
    segment_ids,
    neighbour_valid,
    neighbours,
    out_grad,
    norm_attn,
    w_qkv,
    w_attn_out,
    norm_cross,
    w_cross_q,
    w_cross_kv,
    w_cross_out,
    norm_mlp,
    w_up,
    w_down,
):
    micro, tok_count, model_width = hidden_in.shape
    blk_count = lax.axis_size("blk")
    depth = blk_count // 4
    total = blk_count * 2
    length = tok_count * total
    row_count = micro * tok_count
    gain_rows = norm_attn.shape[0]
    span_count = tok_count // SPAN
    pair_rows = NEIGHBOURS * NEIGH_LEN
    device = lax.axis_index(AXES)

    in_kernel = gain_rows % 8 == 0
    token_index = device * tok_count + jnp.arange(tok_count, dtype=jnp.int32)
    if in_kernel:
        gain_lanes = jnp.concatenate(
            [jnp.broadcast_to(gain[:, None], (gain_rows, 32)) for gain in (norm_attn, norm_cross, norm_mlp, norm_mlp)],
            axis=1,
        )
        small = jnp.concatenate(
            [
                jnp.pad(gain_lanes, ((0, 32 - gain_rows), (0, 0))),
                jnp.pad(segment_ids.astype(jnp.bfloat16), ((0, 16 - micro), (0, 0))),
            ],
            axis=0,
        )
        (
            got_qkv, got_sq, got_kv, up_full, down_full, lead_hid, lead_grad, gains, cosine, sine,
            unit_qkv, mixed, totals, first_row, attended_t,
        ) = first(
            depth, w_qkv, w_attn_out, w_cross_q, w_cross_out, w_cross_kv, w_up, w_down, small, hidden_in, out_grad
        )
        up_full = up_full.reshape(-1, model_width, model_width)
        down_full = down_full.reshape(-1, model_width)
        attended_t = attended_t.reshape(micro, model_width, tok_count)
    else:
        up_full = lax.all_gather(w_up, AXES, axis=0, tiled=True)
        down_full = lax.all_gather(w_down, AXES, axis=0, tiled=True)
        up_full = up_full.reshape(model_width, -1, model_width).transpose(1, 0, 2)
        small = jnp.zeros((16, 128), jnp.bfloat16)
        for row, gain in enumerate((norm_attn, norm_cross, norm_mlp)):
            small = small.at[row, :gain_rows].set(gain)
        small = small.at[3 : 3 + micro, :tok_count].set(segment_ids.astype(jnp.bfloat16))
        got_qkv, got_sq, got_kv, got_small, lead_hid, lead_grad = gather_all(
            depth, w_qkv, w_attn_out, w_cross_q, w_cross_out, w_cross_kv, small, hidden_in, out_grad
        )
        gains = got_small[:, :3, :gain_rows].astype(jnp.float32).transpose(1, 0, 2).reshape(3, model_width)
        gain_attn = gains[0]
        seg_full = got_small[:, 3 : 3 + micro, :tok_count].transpose(1, 0, 2).reshape(micro, length)
        seg_full = seg_full.astype(jnp.int32)
    qkv_blocks = got_qkv.reshape(6, model_width, model_width // 2)
    squares = got_sq.reshape(3, model_width, model_width)
    kv_blocks = got_kv.reshape(2, model_width, model_width)


    unit, holder = unit_of(device, total)
    tile_index = jnp.arange(length // TILE, dtype=jnp.int32)
    if in_kernel:
        tile_first = first_row[0, ::TILE]
    else:
        seg_unit = lax.dynamic_index_in_dim(seg_full, unit // HEADS, 0, keepdims=False)
        seg_tiles = seg_unit.reshape(length // TILE, TILE)
        tile_first = jnp.sum((seg_unit[None] < seg_tiles[:, :1]).astype(jnp.int32), axis=-1)
        inside = jnp.sum((seg_tiles[:, None, :] < seg_tiles[:, :, None]).astype(jnp.int32), axis=-1)
        first_row = jnp.where(
            seg_tiles == seg_tiles[:, :1], tile_first[:, None], tile_index[:, None] * TILE + inside
        ).reshape(1, length)
    low = tile_first // TILE
    high = jnp.sum((low[None] <= tile_index[:, None]).astype(jnp.int32), axis=-1)
    low = jnp.where(holder, low, tile_index + 1)
    high = jnp.where(holder, high, 0)

    if not in_kernel:
        first_of = jnp.sum(
            (seg_full[:, None, :] < segment_ids[:, :, None]).astype(jnp.int32), axis=-1
        )
        local_pos = token_index[None] - first_of
        frequency = jnp.exp(
            jnp.arange(HEAD_DIM // 2, dtype=jnp.float32) * (-2.0 * math.log(10000.0) / HEAD_DIM)
        )
        angles = frequency[:, None, None] * local_pos.astype(jnp.float32)[None]
        cosine, sine = jnp.cos(angles), jnp.sin(angles)

        hidden = hidden_in.astype(jnp.float32)
        normed_attn = layer_norm(hidden, gain_attn).astype(jnp.bfloat16).reshape(row_count, model_width)
        raw = jnp.einsum("bde,td->bet", qkv_blocks, normed_attn, preferred_element_type=jnp.float32)
        raw = raw.reshape(3, HEADS, HEAD_DIM, micro, tok_count)
        rotated = jnp.stack(
            [turn_heads(raw[0], cosine, sine), turn_heads(raw[1], cosine, sine), raw[2]]
        ).astype(jnp.bfloat16)
        message = rotated.transpose(3, 1, 0, 2, 4).reshape(UNITS, 3, HEAD_DIM, tok_count)
        unit_qkv = to_units(total, message, 1)
        shifted, mixed, totals = attn_forward(low, first_row, unit_qkv)
        (attended_t,) = to_tokens(total, shifted[None], (), 2)
    attended_t = attended_t.reshape(micro, model_width, tok_count)

    shifted_index = token_index + LEAD
    used = jnp.where(
        shifted_index[None] < length, jnp.repeat(neighbour_valid, SPAN, axis=1).astype(jnp.float32), 0.0
    ).reshape(row_count, 1)
    neigh_rows = neighbours.reshape(micro * span_count * pair_rows, model_width)
    (
        result_rows, d_first, d_attended_t, normed_cross, d_cross_query, cross_mixed, d_second_low, d_first_low,
        grad_low, activated, d_pairs, d_gain_rest, d_up,
    ) = middle(
        attended_t, hidden_in, lead_hid, out_grad, lead_grad, gains, used, squares, kv_blocks, neigh_rows,
        up_full, down_full,
    )
    up_low = lax.psum_scatter(d_up, AXES, scatter_dimension=0, tiled=True)
    if not in_kernel:
        down_share = lax.psum_scatter(
            outer(activated, grad_low).astype(jnp.bfloat16), AXES, scatter_dimension=0, tiled=True
        ).astype(jnp.float32)
    unit_grad = to_units(total, d_attended_t.reshape(UNITS, 1, HEAD_DIM, tok_count), 3)
    unit_back = attn_backward(low, high, first_row, unit_qkv, unit_grad[0], mixed, totals)
    if in_kernel:
        (
            output, grad_in, grad_neighbours, s_qkv, s_att, s_cq, s_co, s_kv, s_down, s_gain,
        ) = last(
            depth, 5, w_up.shape[1],
            unit_back, result_rows, d_first, normed_cross, d_cross_query, cross_mixed, d_second_low, d_first_low,
            grad_low, activated, d_pairs, attended_t, neigh_rows, kv_blocks, qkv_blocks, hidden_in, gains,
            cosine, sine, d_gain_rest,
        )
        own_gain = lax.dynamic_slice_in_dim(s_gain, device * gain_rows, gain_rows, 1)
        (
            output, grad_in, grad_neighbours, s_qkv, s_att, s_cq, s_co, s_kv, s_down, up_share,
        ) = finish(
            [
                output, grad_in, grad_neighbours, s_qkv, s_att, s_cq, s_co, s_kv, s_down,
            ],
            up_low,
        )
        return (
            output.reshape(hidden_in.shape), grad_in.reshape(hidden_in.shape),
            grad_neighbours.reshape(neighbours.shape),
            own_gain[0], s_qkv, s_att, own_gain[1], s_cq, s_kv, s_co, own_gain[2], up_share, s_down,
        )
    up_share = up_low.astype(jnp.float32)
    result_rows = result_rows.reshape(micro, tok_count, model_width)
    d_first = d_first.reshape(micro, tok_count, model_width)
    sent_t, tail_first, tail_result = to_tokens(
        total, unit_back, (d_first[:, tok_count - 64 :], result_rows[:, tok_count - 64 :]), 4
    )

    def unshift(rows, tail):
        return jnp.concatenate([tail[:, 1:], rows[:, : tok_count - LEAD]], axis=1)

    output = unshift(result_rows, tail_result)
    d_first_home = unshift(d_first, tail_first)
    sent_t = sent_t.reshape(micro, HEADS, 3, HEAD_DIM, tok_count).transpose(2, 1, 3, 0, 4)
    sent_t = sent_t.astype(jnp.float32)
    raw_t = jnp.stack(
        [turn_heads(sent_t[0], cosine, -sine), turn_heads(sent_t[1], cosine, -sine), sent_t[2]]
    ).astype(jnp.bfloat16).reshape(6, model_width // 2, row_count)
    d_normed_attn = jnp.einsum("bet,bde->td", raw_t, qkv_blocks, preferred_element_type=jnp.float32)
    d_hidden_in, d_gain_attn = norm_backward(
        hidden, gain_attn, d_normed_attn.reshape(micro, tok_count, model_width)
    )
    grad_in = (d_first_home + d_hidden_in).astype(jnp.bfloat16)

    d_keys, d_values = d_pairs[0], d_pairs[1]
    d_first_low = d_first_low.reshape(micro, tok_count, model_width)
    d_neigh = (
        jnp.einsum("te,de->td", d_keys, kv_blocks[0], preferred_element_type=jnp.float32)
        + jnp.einsum("te,de->td", d_values, kv_blocks[1], preferred_element_type=jnp.float32)
    ).astype(jnp.bfloat16)
    grad_neighbours = d_neigh.reshape(neighbours.shape)

    def blocks_of(array):
        return array.astype(jnp.bfloat16).reshape(
            array.shape[0], depth, 2, 2, 2, gain_rows, array.shape[-1]
        )

    d_qkv = jnp.einsum("td,bet->bde", normed_attn, raw_t, preferred_element_type=jnp.float32)
    d_sq = jnp.stack(
        [
            jnp.einsum("mdt,mte->de", attended_t, d_first_low, preferred_element_type=jnp.float32),
            outer(normed_cross, d_cross_query),
            outer(cross_mixed, d_second_low),
        ]
    )
    d_kv = jnp.stack([outer(neigh_rows, d_keys), outer(neigh_rows, d_values)])
    d_gains = jnp.stack([d_gain_attn, d_gain_rest[0], d_gain_rest[1]]).reshape(3, total, gain_rows)
    d_gains = jnp.zeros((total, 8, 128), jnp.float32).at[:, :3, :gain_rows].set(d_gains.transpose(1, 0, 2))
    s_qkv, s_sq, s_kv, s_gain = scatter_all(
        depth, blocks_of(d_qkv), blocks_of(d_sq), blocks_of(d_kv), d_gains, 6
    )
    return (
        output,
        grad_in,
        grad_neighbours,
        s_gain[0, :gain_rows],
        s_qkv.transpose(1, 0, 2).reshape(gain_rows, 3 * model_width),
        s_sq[0],
        s_gain[1, :gain_rows],
        s_sq[1],
        s_kv.transpose(1, 0, 2).reshape(gain_rows, 2 * model_width),
        s_sq[2],
        s_gain[2, :gain_rows],
        up_share,
        down_share,
    )


def solution(mesh):
    placed = (
        P(None, ("blk", "head"), None),
        P(None, ("blk", "head")),
        P(None, ("blk", "head")),
        P(None, ("blk", "head"), None, None, None),
        P(None, ("blk", "head"), None),
        P(("blk", "head")),
        P(("blk", "head"), None),
        P(("blk", "head"), None),
        P(("blk", "head")),
        P(("blk", "head"), None),
        P(("blk", "head"), None),
        P(("blk", "head"), None),
        P(("blk", "head")),
        P(("blk", "head"), None),
        P(("blk", "head"), None),
    )
    return jax.shard_map(
        on_device,
        mesh=mesh,
        in_specs=placed,
        out_specs=(
            P(None, ("blk", "head"), None),
            P(None, ("blk", "head"), None),
            P(None, ("blk", "head"), None, None, None),
            P(("blk", "head")),
            P(("blk", "head"), None),
            P(("blk", "head"), None),
            P(("blk", "head")),
            P(("blk", "head"), None),
            P(("blk", "head"), None),
            P(("blk", "head"), None),
            P(("blk", "head")),
            P(("blk", "head"), None),
            P(("blk", "head"), None),
        ),
        check_vma=False,
    )
```

```python
import functools
import math

import jax
import jax.numpy as jnp
from jax import lax
from jax.experimental import pallas as pl
from jax.experimental.pallas import tpu as pltpu
from jax.sharding import PartitionSpec as P

MESH = pl.DeviceIdType.MESH
ANY = pl.BlockSpec(memory_space=pl.ANY)


def coords():
    blk = lax.axis_index("blk")
    return blk // 4, (blk // 2) % 2, blk % 2, lax.axis_index("head")


def place(z, y, c, x):
    return (z * 4 + y * 2 + c, x)


def loop(count, body):
    if count <= 8:
        for step in range(count):
            body(step)
    else:
        lax.fori_loop(0, count, lambda step, carry: (body(step), carry)[1], 0)


def all_barrier(total, me):
    barrier = pltpu.get_barrier_semaphore()

    def greet(step, carry):
        peer = lax.rem(me + step, total)
        pl.semaphore_signal(
            barrier, inc=1, device_id=(peer // 2, lax.rem(peer, 2)), device_id_type=MESH
        )
        return carry

    lax.fori_loop(1, total, greet, 0)
    pl.semaphore_wait(barrier, total - 1)


def remote(src, dst, send, recv, where):
    return pltpu.make_async_remote_copy(
        src_ref=src, dst_ref=dst, send_sem=send, recv_sem=recv, device_id=where, device_id_type=MESH
    )


def gather_kernel(depth, items, *refs):
    count = len(items)
    w_refs = refs[:5]
    small_ref, hid_ref, grad_ref = refs[5:8]
    out_refs = refs[8:11]
    small_out, lead_hid, lead_grad = refs[11:14]
    own_sem, send_sem, recv_sem, misc_sem, lead_send, lead_recv = refs[14:]
    z, y, c, x = coords()
    total = depth * 8
    me = lax.axis_index("blk") * 2 + lax.axis_index("head")
    rows_per = w_refs[0].shape[0]

    def view(item, zs, ys, cs, xs):
        buffer, first, last, kind = item
        return out_refs[buffer].at[pl.ds(first, last - first), zs, ys, cs, xs]

    all_barrier(total, me)
    own_small = pltpu.make_async_copy(small_ref, small_out.at[me], misc_sem.at[1])
    own_small.start()

    def send_small(step, carry):
        peer = lax.rem(me + step, total)
        remote(
            small_ref, small_out.at[me], misc_sem.at[0], misc_sem.at[1], (peer // 2, lax.rem(peer, 2))
        ).start()
        return carry

    own = []
    for index, item in enumerate(items):
        buffer, first, last, kind = item
        width = out_refs[buffer].shape[-1]
        copies = []
        for block in range(first, last):
            if buffer == 1:
                src = w_refs[1 + block]
            else:
                src = w_refs[2 * buffer].at[:, pl.ds(block * width, width)]
            copies.append((src, out_refs[buffer].at[block, z, y, c, x]))
        for src, dst in copies:
            copy = pltpu.make_async_copy(src, dst, own_sem.at[index])
            copy.start()
        own.append(pltpu.make_async_copy(view(item, z, y, c, x), view(item, z, y, c, x), own_sem.at[index]))
    lax.fori_loop(1, total, send_small, 0)
    prev = lax.rem(me + total - 1, total)
    prev_at = (prev // 2, lax.rem(prev, 2))
    leads = [
        remote(hid_ref.at[:, pl.ds(0, 64)], lead_hid, lead_send.at[0], lead_recv.at[0], prev_at),
        remote(grad_ref.at[:, pl.ds(0, 64)], lead_grad, lead_send.at[1], lead_recv.at[1], prev_at),
    ]

    whole = slice(None)

    def phase_one(index):
        own[index].wait()
        item = items[index]

        def send(step):
            other = lax.rem(z + step + 1, depth)
            remote(
                view(item, z, y, c, x), view(item, z, y, c, x),
                send_sem.at[index, 0], recv_sem.at[index, 0], place(other, y, c, x),
            ).start()

        loop(depth - 1, send)

    def bulk(index, phase):
        item = items[index]
        first_x = item[3] == 0
        if phase == 1:
            ref = view(item, whole, y, c, x)
            where = place(z, y, c, 1 - x) if first_x else place(z, 1 - y, c, x)
        elif phase == 2:
            ref = view(item, whole, y, c, whole) if first_x else view(item, whole, whole, c, x)
            where = place(z, 1 - y, c, x) if first_x else place(z, y, c, 1 - x)
        else:
            ref = view(item, whole, whole, c, whole)
            where = place(z, y, 1 - c, x)
        return remote(ref, ref, send_sem.at[index, phase], recv_sem.at[index, phase], where)

    def arrived(index, phase):
        item = items[index]
        if phase == 0:
            ref = view(item, pl.ds(0, depth - 1), y, c, x)
            pltpu.make_async_copy(ref, ref, recv_sem.at[index, 0]).wait()
        else:
            bulk(index, phase).wait_recv()

    def sent(index, phase):
        item = items[index]
        if phase == 0:
            ref = view(item, pl.ds(0, depth - 1), y, c, x)
            pltpu.make_async_copy(ref, ref, send_sem.at[index, 0]).wait()
        else:
            bulk(index, phase).wait_send()

    pairs = (count + 1) // 2
    for step in range(pairs + 2 * 4):
        for phase in range(4, -1, -1):
            pair = step - 2 * phase
            if not 0 <= pair < pairs:
                continue
            for index in range(2 * pair, min(2 * pair + 2, count)):
                if phase == 0:
                    phase_one(index)
                else:
                    arrived(index, phase - 1)
                    if phase < 4:
                        bulk(index, phase).start()
        if step == 0:
            for lead in leads:
                lead.start()
    for index in range(count):
        for phase in range(4):
            sent(index, phase)
    for lead in leads:
        lead.wait()
    pltpu.make_async_copy(small_out, small_out, misc_sem.at[1]).wait()
    rest = small_out.at[pl.ds(0, total - 1)]
    pltpu.make_async_copy(rest, rest, misc_sem.at[0]).wait()


def gather_all(depth, w_qkv, w_attn_out, w_cross_q, w_cross_out, w_kv, small, hidden, grads):
    total = depth * 8
    rows = w_qkv.shape[0]
    items = [
        (0, 0, 3, 0), (0, 3, 6, 1),
        (2, 0, 1, 0), (2, 1, 2, 1),
        (1, 0, 1, 0), (1, 1, 2, 1),
        (1, 2, 3, 0),
    ]
    shapes = [
        (6, depth, 2, 2, 2, rows, w_qkv.shape[1] // 6),
        (3, depth, 2, 2, 2, rows, w_attn_out.shape[1]),
        (2, depth, 2, 2, 2, rows, w_kv.shape[1] // 2),
    ]
    lead_shape = (hidden.shape[0], 64, hidden.shape[2])
    outs = [jax.ShapeDtypeStruct(shape, jnp.bfloat16) for shape in shapes]
    outs += [jax.ShapeDtypeStruct((total,) + small.shape, small.dtype)]
    outs += [jax.ShapeDtypeStruct(lead_shape, jnp.bfloat16)] * 2
    count = len(items)
    return pl.pallas_call(
        functools.partial(gather_kernel, depth, items),
        out_shape=outs,
        in_specs=[ANY] * 8,
        out_specs=[ANY] * 6,
        scratch_shapes=[
            pltpu.SemaphoreType.DMA((count,)),
            pltpu.SemaphoreType.DMA((count, 4)),
            pltpu.SemaphoreType.DMA((count, 4)),
            pltpu.SemaphoreType.DMA((2,)),
            pltpu.SemaphoreType.DMA((2,)),
            pltpu.SemaphoreType.DMA((2,)),
        ],
        compiler_params=pltpu.CompilerParams(collective_id=0, has_side_effects=True),
    )(w_qkv, w_attn_out, w_cross_q, w_cross_out, w_kv, small, hidden, grads)


def unit_of(device, total):
    if total == 32:
        depth = device // 8
        middle = (depth == 1) | (depth == 2)
        end = 16 + (depth // 3) * 4 + (lax.rem(device, 8) // 4) * 2 + lax.rem(device, 2)
        unit = jnp.where(middle, device - 8, end)
        return unit, middle | (lax.rem(device // 2, 2) == 0)
    stride = total // UNITS
    return jnp.minimum(device // stride, UNITS - 1), (lax.rem(device, stride) == 0) & (device // stride < UNITS)


def to_units_kernel(total, src, dst, send_sem, recv_sem):
    me = lax.axis_index("blk") * 2 + lax.axis_index("head")
    mine, holder = unit_of(me, total)
    all_barrier(total, me)
    lanes = src.shape[-1]

    def slot(device):
        return dst.at[:, :, pl.ds(pl.multiple_of(device * lanes, 128), lanes)]

    @pl.when(holder)
    def _():
        pltpu.make_async_copy(src.at[mine], slot(me), recv_sem).start()

    def send(step, carry):
        peer = lax.rem(me + step, total)
        unit, held = unit_of(peer, total)

        @pl.when(held)
        def _():
            remote(src.at[unit], slot(me), send_sem, recv_sem, (peer // 2, lax.rem(peer, 2))).start()

        return carry

    lax.fori_loop(1, total, send, 0)

    @pl.when(holder)
    def _():
        part = src.at[pl.ds(0, UNITS - 1)]
        pltpu.make_async_copy(dst, dst, recv_sem).wait()
        pltpu.make_async_copy(part, part, send_sem).wait()

    @pl.when(jnp.logical_not(holder))
    def _():
        pltpu.make_async_copy(src, src, send_sem).wait()


def to_units(total, message, collective):
    units, parts, width, lanes = message.shape
    return pl.pallas_call(
        functools.partial(to_units_kernel, total),
        out_shape=jax.ShapeDtypeStruct((parts, width, lanes * total), message.dtype),
        in_specs=[ANY],
        out_specs=ANY,
        scratch_shapes=[pltpu.SemaphoreType.DMA, pltpu.SemaphoreType.DMA],
        compiler_params=pltpu.CompilerParams(collective_id=collective, has_side_effects=True),
    )(message)


def to_tokens_kernel(total, extras, *refs):
    src = refs[0]
    extra_in = refs[1 : 1 + extras]
    dst = refs[1 + extras]
    extra_out = refs[2 + extras : 2 + 2 * extras]
    send_sem, recv_sem, extra_send, extra_recv = refs[2 + 2 * extras :]
    me = lax.axis_index("blk") * 2 + lax.axis_index("head")
    mine, holder = unit_of(me, total)
    all_barrier(total, me)
    lanes = dst.shape[-1]
    after = lax.rem(me + 1, total)
    moves = [
        remote(
            extra_in[index], extra_out[index], extra_send.at[index], extra_recv.at[index],
            (after // 2, lax.rem(after, 2)),
        )
        for index in range(extras)
    ]
    for move in moves:
        move.start()

    def slot(device):
        return src.at[:, :, pl.ds(pl.multiple_of(device * lanes, 128), lanes)]

    @pl.when(holder)
    def _():
        pltpu.make_async_copy(slot(me), dst.at[mine], recv_sem).start()

        def send(step, carry):
            peer = lax.rem(me + step, total)
            remote(
                slot(peer), dst.at[mine], send_sem, recv_sem, (peer // 2, lax.rem(peer, 2))
            ).start()
            return carry

        lax.fori_loop(1, total, send, 0)

    pltpu.make_async_copy(dst, dst, recv_sem).wait()

    @pl.when(holder)
    def _():
        part = src.at[:, :, pl.ds(0, lanes * (total - 1))]
        pltpu.make_async_copy(part, part, send_sem).wait()

    for move in moves:
        move.wait()


def to_tokens(total, units, extra, collective):
    parts, width, length = units.shape
    count = len(extra)
    result = jax.ShapeDtypeStruct((UNITS, parts, width, length // total), units.dtype)
    return pl.pallas_call(
        functools.partial(to_tokens_kernel, total, count),
        out_shape=[result] + [jax.ShapeDtypeStruct(e.shape, e.dtype) for e in extra],
        in_specs=[ANY] * (1 + count),
        out_specs=[ANY] * (1 + count),
        scratch_shapes=[
            pltpu.SemaphoreType.DMA,
            pltpu.SemaphoreType.DMA,
            pltpu.SemaphoreType.DMA((max(count, 1),)),
            pltpu.SemaphoreType.DMA((max(count, 1),)),
        ],
        compiler_params=pltpu.CompilerParams(collective_id=collective, has_side_effects=True),
    )(units, *extra)


def scatter_kernel(depth, items, *refs):
    count = len(items)
    total = depth * 8
    d_refs = refs[:3]
    gain_ref = refs[3]
    out_refs = refs[4:7]
    gain_out = refs[7]
    own = refs[8 : 8 + count]
    got_core = refs[8 + count : 8 + 2 * count]
    got_one = refs[8 + 2 * count : 8 + 3 * count]
    got_two = refs[8 + 3 * count : 8 + 4 * count]
    got_z = refs[8 + 4 * count : 8 + 5 * count]
    gains, local_sem, send_sem, recv_sem, gain_sem = refs[8 + 5 * count :]
    z, y, c, x = coords()
    me = lax.axis_index("blk") * 2 + lax.axis_index("head")
    all_barrier(total, me)
    whole = slice(None)

    pltpu.make_async_copy(gain_ref.at[me], gains.at[me], gain_sem.at[1]).start()

    def send_gain(step, carry):
        peer = lax.rem(me + step, total)
        remote(
            gain_ref.at[peer], gains.at[me], gain_sem.at[0], gain_sem.at[1], (peer // 2, lax.rem(peer, 2))
        ).start()
        return carry

    def local(index):
        buffer, first, last, kind = items[index]
        src = d_refs[buffer].at[pl.ds(first, last - first), whole, whole, c]
        return pltpu.make_async_copy(src, own[index], local_sem.at[index])

    def core(index):
        buffer, first, last, kind = items[index]
        src = d_refs[buffer].at[pl.ds(first, last - first), whole, whole, 1 - c]
        return remote(
            src, got_core[index], send_sem.at[index, 0], recv_sem.at[index, 0], place(z, y, 1 - c, x)
        )

    def one(index):
        if items[index][3] == 0:
            src, where = own[index].at[whole, whole, 1 - y], place(z, 1 - y, c, x)
        else:
            src, where = own[index].at[whole, whole, whole, 1 - x], place(z, y, c, 1 - x)
        return remote(src, got_one[index], send_sem.at[index, 1], recv_sem.at[index, 1], where)

    def two(index):
        if items[index][3] == 0:
            src, where = own[index].at[whole, whole, y, 1 - x], place(z, y, c, 1 - x)
        else:
            src, where = own[index].at[whole, whole, 1 - y, x], place(z, 1 - y, c, x)
        return remote(src, got_two[index], send_sem.at[index, 2], recv_sem.at[index, 2], where)

    def send_z(index):
        def send(step):
            other = lax.rem(z + step + 1, depth)
            remote(
                own[index].at[whole, other, y, x], got_z[index].at[z],
                send_sem.at[index, 3], recv_sem.at[index, 3], place(other, y, c, x),
            ).start()

        loop(depth - 1, send)

    def add_into(target, source):
        target[...] = (target[...].astype(jnp.float32) + source[...].astype(jnp.float32)).astype(
            jnp.bfloat16
        )

    def sum_core(index):
        blocks = own[index].shape[0]

        def body(step):
            block, level = step // depth, lax.rem(step, depth)
            for row in range(2):
                for col in range(2):
                    add_into(own[index].at[block, level, row, col], got_core[index].at[block, level, row, col])

        lax.fori_loop(0, blocks * depth, lambda step, carry: (body(step), carry)[1], 0)

    def sum_one(index):
        blocks = own[index].shape[0]

        def body(step):
            block, level = step // depth, lax.rem(step, depth)
            for side in range(2):
                if items[index][3] == 0:
                    target = own[index].at[block, level, y, side]
                else:
                    target = own[index].at[block, level, side, x]
                add_into(target, got_one[index].at[block, level, side])

        lax.fori_loop(0, blocks * depth, lambda step, carry: (body(step), carry)[1], 0)

    def sum_two(index):
        blocks = own[index].shape[0]

        def body(step):
            block, level = step // depth, lax.rem(step, depth)
            add_into(own[index].at[block, level, y, x], got_two[index].at[block, level])

        lax.fori_loop(0, blocks * depth, lambda step, carry: (body(step), carry)[1], 0)

    def sum_z(index):
        buffer, first, last, kind = items[index]
        for block in range(last - first):
            running = own[index][block, z, y, x].astype(jnp.float32)

            def body(step, value):
                other = lax.rem(z + step, depth)
                return value + got_z[index][other, block].astype(jnp.float32)

            out_refs[buffer][first + block] = lax.fori_loop(1, depth, body, running)

    for index in range(count):
        local(index).start()
    pairs = (count + 1) // 2
    for step in range(pairs + 4):
        for phase in range(4, -1, -1):
            pair = step - phase
            if not 0 <= pair < pairs:
                continue
            for index in range(2 * pair, min(2 * pair + 2, count)):
                if phase == 0:
                    core(index).start()
                elif phase == 1:
                    local(index).wait()
                    core(index).wait_recv()
                    sum_core(index)
                    one(index).start()
                elif phase == 2:
                    one(index).wait_recv()
                    sum_one(index)
                    two(index).start()
                elif phase == 3:
                    two(index).wait_recv()
                    sum_two(index)
                    send_z(index)
                else:
                    landed = got_z[index].at[pl.ds(0, depth - 1)]
                    pltpu.make_async_copy(landed, landed, recv_sem.at[index, 3]).wait()
                    sum_z(index)
        if step == 0:
            lax.fori_loop(1, total, send_gain, 0)
    pltpu.make_async_copy(gains, gains, gain_sem.at[1]).wait()
    gain_out[...] = jnp.sum(gains[...], axis=0)
    for index in range(count):
        core(index).wait_send()
        one(index).wait_send()
        two(index).wait_send()
        gone = got_z[index].at[pl.ds(0, depth - 1)]
        pltpu.make_async_copy(gone, gone, send_sem.at[index, 3]).wait()
    rest = gains.at[pl.ds(0, total - 1)]
    pltpu.make_async_copy(rest, rest, gain_sem.at[0]).wait()


def scatter_all(depth, d_qkv, d_squares, d_kv, d_gains, collective):
    items = [
        (0, 0, 3, 0), (0, 3, 6, 1),
        (2, 0, 1, 0), (2, 1, 2, 1),
        (1, 0, 1, 0), (1, 1, 2, 1),
        (1, 2, 3, 0),
    ]
    count = len(items)
    parts = (d_qkv, d_squares, d_kv)
    own, core, one, two, along = [], [], [], [], []
    for buffer, first, last, kind in items:
        rows, width = parts[buffer].shape[-2:]
        blocks = last - first
        own.append(pltpu.VMEM((blocks, depth, 2, 2, rows, width), jnp.bfloat16))
        core.append(pltpu.VMEM((blocks, depth, 2, 2, rows, width), jnp.bfloat16))
        one.append(pltpu.VMEM((blocks, depth, 2, rows, width), jnp.bfloat16))
        two.append(pltpu.VMEM((blocks, depth, rows, width), jnp.bfloat16))
        along.append(pltpu.VMEM((depth, blocks, rows, width), jnp.bfloat16))
    outs = [jax.ShapeDtypeStruct((p.shape[0],) + p.shape[-2:], jnp.float32) for p in parts]
    outs.append(jax.ShapeDtypeStruct(d_gains.shape[1:], jnp.float32))
    vmem = pl.BlockSpec(memory_space=pltpu.VMEM)
    return pl.pallas_call(
        functools.partial(scatter_kernel, depth, items),
        out_shape=outs,
        in_specs=[ANY] * 4,
        out_specs=[vmem] * 4,
        scratch_shapes=own + core + one + two + along + [
            pltpu.VMEM(d_gains.shape, jnp.float32),
            pltpu.SemaphoreType.DMA((count,)),
            pltpu.SemaphoreType.DMA((count, 4)),
            pltpu.SemaphoreType.DMA((count, 4)),
            pltpu.SemaphoreType.DMA((2,)),
        ],
        compiler_params=pltpu.CompilerParams(
            collective_id=collective, has_side_effects=True, vmem_limit_bytes=60 * 2**20
        ),
    )(d_qkv, d_squares, d_kv, d_gains)


HEADS = 12
HEAD_DIM = 64
SPAN = 64
NEIGHBOURS = 2
NEIGH_LEN = 128
MICRO = 2
UNITS = MICRO * HEADS
AXES = ("blk", "head")
TILE = 512
LEAD = SPAN - 1
DOC_MAX = 2000
SCORE_SCALE = 1.0 / math.sqrt(HEAD_DIM)
LOG2E = math.log2(math.e)


def tile_at(ref, index, row):
    return ref[row, :, pl.ds(pl.multiple_of(index * TILE, TILE), TILE)]


def row_at(ref, index):
    return ref[:, pl.ds(pl.multiple_of(index * TILE, TILE), TILE)]


def tile_mask(key_tile, query_tile, first_row):
    key_place = key_tile * TILE + lax.broadcasted_iota(jnp.int32, (TILE, 1), 0)
    query_place = query_tile * TILE + lax.broadcasted_iota(jnp.int32, (1, TILE), 1)
    return (key_place <= query_place) & (key_place >= first_row)


def attn_forward_kernel(low_ref, first_ref, qkv_ref, shifted_ref, mixed_ref, total_ref):
    tiles = qkv_ref.shape[-1] // TILE

    def one_query(query_tile, carry):
        query_t = tile_at(qkv_ref, query_tile, 0)
        first_row = row_at(first_ref, query_tile)

        def one_key(step, state):
            peak, weight, mixed = state
            key_tile = query_tile - step
            keys = tile_at(qkv_ref, key_tile, 1).T
            scores = jnp.dot(keys, query_t, preferred_element_type=jnp.float32) * (SCORE_SCALE * LOG2E)
            scores = jnp.where(tile_mask(key_tile, query_tile, first_row), scores, -1e30)
            new_peak = jnp.maximum(peak, jnp.max(scores, axis=0, keepdims=True))
            probs = jnp.exp2(scores - new_peak)
            fade = jnp.exp2(peak - new_peak)
            weight = weight * fade + jnp.sum(probs, axis=0, keepdims=True)
            mixed = mixed * fade + jnp.dot(
                tile_at(qkv_ref, key_tile, 2), probs.astype(jnp.bfloat16), preferred_element_type=jnp.float32
            )
            return new_peak, weight, mixed

        start = (
            jnp.full((1, TILE), -1e30, jnp.float32),
            jnp.zeros((1, TILE), jnp.float32),
            jnp.zeros((HEAD_DIM, TILE), jnp.float32),
        )
        steps = query_tile + 1 - low_ref[query_tile]
        peak, weight, mixed = lax.fori_loop(0, steps, one_key, start)
        columns = pl.ds(pl.multiple_of(query_tile * TILE, TILE), TILE)
        mixed_ref[:, columns] = mixed / weight
        total_ref[:, columns] = peak + jnp.log2(weight)
        return carry

    lax.fori_loop(0, tiles, one_query, 0)
    length = qkv_ref.shape[-1]

    def turn(step, carry):
        rows = pl.ds(pl.multiple_of(step * 16, 16), 16)
        shifted_ref[rows, :] = pltpu.roll(mixed_ref[rows, :], length - LEAD, 1).astype(jnp.bfloat16)
        return carry

    lax.fori_loop(0, HEAD_DIM // 16, turn, 0)


def attn_backward_kernel(
    low_ref, high_ref, first_ref, qkv_ref, shifted_ref, mixed_ref, total_ref, out_ref, grad_ref, dq_ref, delta_ref
):
    length = qkv_ref.shape[-1]
    tiles = length // TILE
    delta_ref[...] = jnp.zeros_like(delta_ref)

    def turn(step, carry):
        rows = pl.ds(pl.multiple_of(step * 16, 16), 16)
        grad = pltpu.roll(shifted_ref[rows, :].astype(jnp.float32), LEAD, 1)
        grad_ref[rows, :] = grad.astype(jnp.bfloat16)
        delta_ref[...] += jnp.sum(grad * mixed_ref[rows, :], axis=0, keepdims=True)
        dq_ref[rows, :] = jnp.zeros((16, length), jnp.float32)
        return carry

    lax.fori_loop(0, HEAD_DIM // 16, turn, 0)

    def one_key(key_tile, carry):
        key_t = tile_at(qkv_ref, key_tile, 1)
        keys = key_t.T
        values = tile_at(qkv_ref, key_tile, 2).T

        def one_query(query_tile, state):
            d_key, d_value = state
            query_t = tile_at(qkv_ref, query_tile, 0)
            grad_t = row_at(grad_ref, query_tile)
            scores = jnp.dot(keys, query_t, preferred_element_type=jnp.float32) * (SCORE_SCALE * LOG2E)
            allowed = tile_mask(key_tile, query_tile, row_at(first_ref, query_tile))
            probs = jnp.where(allowed, jnp.exp2(scores - row_at(total_ref, query_tile)), 0.0)
            d_probs = jnp.dot(values, grad_t, preferred_element_type=jnp.float32)
            d_scores = (probs * (d_probs - row_at(delta_ref, query_tile))).astype(jnp.bfloat16)
            d_value = d_value + jnp.dot(
                probs.astype(jnp.bfloat16), grad_t.T, preferred_element_type=jnp.float32
            )
            d_key = d_key + jnp.dot(d_scores, query_t.T, preferred_element_type=jnp.float32)
            columns = pl.ds(pl.multiple_of(query_tile * TILE, TILE), TILE)
            dq_ref[:, columns] += jnp.dot(key_t, d_scores, preferred_element_type=jnp.float32)
            return d_key, d_value

        zeros = jnp.zeros((TILE, HEAD_DIM), jnp.float32)
        d_key, d_value = lax.fori_loop(key_tile, high_ref[key_tile], one_query, (zeros, zeros))
        columns = pl.ds(pl.multiple_of(key_tile * TILE, TILE), TILE)
        out_ref[1, :, columns] = (d_key * SCORE_SCALE).T.astype(jnp.bfloat16)
        out_ref[2, :, columns] = d_value.T.astype(jnp.bfloat16)
        return carry

    lax.fori_loop(0, tiles, one_key, 0)

    def finish(step, carry):
        rows = pl.ds(pl.multiple_of(step * 16, 16), 16)
        out_ref[0, rows, :] = (dq_ref[rows, :] * SCORE_SCALE).astype(jnp.bfloat16)
        return carry

    lax.fori_loop(0, HEAD_DIM // 16, finish, 0)


SMEM = pl.BlockSpec(memory_space=pltpu.SMEM)
VMEM = pl.BlockSpec(memory_space=pltpu.VMEM)


def local_params():
    return pltpu.CompilerParams(vmem_limit_bytes=60 * 2**20)


def attn_forward(low, first, qkv):
    width, length = qkv.shape[1:]
    return pl.pallas_call(
        attn_forward_kernel,
        out_shape=[
            jax.ShapeDtypeStruct((width, length), jnp.bfloat16),
            jax.ShapeDtypeStruct((width, length), jnp.float32),
            jax.ShapeDtypeStruct((1, length), jnp.float32),
        ],
        in_specs=[SMEM, VMEM, VMEM],
        out_specs=[VMEM] * 3,
        compiler_params=local_params(),
        cost_estimate=pl.CostEstimate(flops=10**9, bytes_accessed=4 * 10**6, transcendentals=4 * 10**6),
    )(low, first, qkv)


def attn_backward(low, high, first, qkv, shifted, mixed, totals):
    width, length = qkv.shape[1:]
    return pl.pallas_call(
        attn_backward_kernel,
        out_shape=jax.ShapeDtypeStruct((3, width, length), jnp.bfloat16),
        in_specs=[SMEM, SMEM] + [VMEM] * 5,
        out_specs=VMEM,
        scratch_shapes=[
            pltpu.VMEM((width, length), jnp.bfloat16),
            pltpu.VMEM((width, length), jnp.float32),
            pltpu.VMEM((1, length), jnp.float32),
        ],
        compiler_params=local_params(),
        cost_estimate=pl.CostEstimate(flops=3 * 10**9, bytes_accessed=4 * 10**6, transcendentals=4 * 10**6),
    )(low, high, first, qkv, shifted, mixed, totals)


def dot_nn(left, right):
    return jnp.dot(left, right, preferred_element_type=jnp.float32)


def dot_nt(left, right):
    return lax.dot_general(left, right, (((1,), (1,)), ((), ())), preferred_element_type=jnp.float32)


def dot_tn(left, right):
    return lax.dot_general(left, right, (((0,), (0,)), ((), ())), preferred_element_type=jnp.float32)


def norm_parts(values):
    centred = values - jnp.mean(values, axis=-1, keepdims=True)
    scale = lax.rsqrt(jnp.mean(centred * centred, axis=-1, keepdims=True) + 1e-05)
    return centred * scale, scale


def norm_pull(values, gain, grad):
    unit, scale = norm_parts(values)
    scaled = grad * gain
    pulled = scale * (
        scaled
        - jnp.mean(scaled, axis=-1, keepdims=True)
        - unit * jnp.mean(scaled * unit, axis=-1, keepdims=True)
    )
    return pulled, jnp.sum(grad * unit, axis=0, keepdims=True)


def shift_rows(rows, lead):
    joined = jnp.concatenate([rows.astype(jnp.float32), lead.astype(jnp.float32)], axis=0)
    return pltpu.roll(joined, joined.shape[0] - LEAD, 0)[: rows.shape[0]]


def stack_pair(rows):
    lane = lax.broadcasted_iota(jnp.int32, rows.shape, 1)
    zero = jnp.zeros_like(rows)
    return jnp.concatenate(
        [jnp.where(lane < HEAD_DIM, rows, zero), jnp.where(lane < HEAD_DIM, zero, rows)], axis=0
    )


def unstack_pair(rows):
    lane = lax.broadcasted_iota(jnp.int32, (SPAN, 2 * HEAD_DIM), 1)
    return jnp.where(lane < HEAD_DIM, rows[:SPAN], rows[SPAN:])


def middle_kernel(
    att_ref, hid_ref, lead_hid_ref, grad_ref, lead_grad_ref, gain_ref, used_ref, sq_ref, kv_hbm, neigh_hbm,
    up_hbm, down_hbm,
    result_ref, first_ref, d_att_ref, n2_ref, d_cq_ref, cm_ref, gc_ref, ga_ref, gy_ref, act_ref, d_pair_ref,
    d_gain_ref, d_up_hbm,
    kv_ref, neigh_ref, up_ref, down_ref, att_rows, second_ref, cq_ref, pair_ref, prob_ref, acc_ref, d_n3_ref,
    n3_ref, n3t_ref, d_up_ref, sems,
):
    micro, tokens, width = hid_ref.shape
    rows = micro * tokens
    pulls = [
        pltpu.make_async_copy(src, dst, sems.at[index])
        for index, (src, dst) in enumerate(
            [(kv_hbm, kv_ref), (neigh_hbm, neigh_ref), (up_hbm, up_ref), (down_hbm, down_ref)]
        )
    ]
    for pull in pulls:
        pull.start()
    gain_cross, gain_mlp = gain_ref[1:2, :], gain_ref[2:3, :]
    for index in range(micro):
        part = pl.ds(index * tokens, tokens)
        hidden = shift_rows(hid_ref[index], lead_hid_ref[index])
        gy_ref[part, :] = shift_rows(grad_ref[index], lead_grad_ref[index]).astype(jnp.bfloat16)
        first_ref[part, :] = hidden + dot_tn(att_ref[index], sq_ref[0])
    n2_ref[...] = (norm_parts(first_ref[...])[0] * gain_cross).astype(jnp.bfloat16)
    cq_ref[...] = dot_nn(n2_ref[...], sq_ref[1]).astype(jnp.bfloat16)

    pulls[0].wait()
    pulls[1].wait()
    chunk = 256
    chunks = neigh_ref.shape[0] // chunk

    def make_pairs(step, carry):
        side, block = step // chunks, lax.rem(step, chunks)
        part = pl.ds(pl.multiple_of(block * chunk, chunk), chunk)
        pair_ref[side, part, :] = dot_nn(neigh_ref[part, :], kv_ref[side]).astype(jnp.bfloat16)
        return carry

    lax.fori_loop(0, 2 * chunks, make_pairs, 0)
    couples = HEADS // 2
    pair_rows = NEIGHBOURS * NEIGH_LEN
    groups = rows // SPAN

    def where(step):
        group, couple = step // couples, lax.rem(step, couples)
        tok = pl.ds(pl.multiple_of(group * SPAN, SPAN), SPAN)
        key = pl.ds(pl.multiple_of(group * pair_rows, pair_rows), pair_rows)
        lanes = pl.ds(pl.multiple_of(couple * 2 * HEAD_DIM, 2 * HEAD_DIM), 2 * HEAD_DIM)
        return tok, key, lanes

    def cross_step(step, carry):
        tok, key, lanes = where(step)
        query = stack_pair(cq_ref[tok, lanes])
        scores = dot_nt(query, pair_ref[0, key, lanes]) * SCORE_SCALE
        weights = jnp.exp(scores - jnp.max(scores, axis=-1, keepdims=True))
        probs = weights / jnp.sum(weights, axis=-1, keepdims=True)
        prob_ref[step] = probs
        mixed = unstack_pair(dot_nn(probs.astype(jnp.bfloat16), pair_ref[1, key, lanes]))
        cm_ref[tok, lanes] = (mixed * used_ref[tok, :]).astype(jnp.bfloat16)
        return carry

    lax.fori_loop(0, groups * couples, cross_step, 0)
    second_ref[...] = first_ref[...] + dot_nn(cm_ref[...], sq_ref[2])
    n3 = (norm_parts(second_ref[...])[0] * gain_mlp).astype(jnp.bfloat16)
    n3_ref[...] = n3
    n3t_ref[...] = n3.T
    acc_ref[...] = second_ref[...]
    d_n3_ref[...] = jnp.zeros_like(d_n3_ref)
    pulls[2].wait()
    pulls[3].wait()
    ff_blocks = up_ref.shape[0]

    def mlp_step(step, carry):
        cols = pl.ds(pl.multiple_of(step * width, width), width)
        upper = dot_nn(n3_ref[...], up_ref[step])
        square = upper * upper
        flat = jnp.tanh(math.sqrt(2.0 / math.pi) * upper * (1.0 + 0.044715 * square))
        half = 0.5 * (1.0 + flat)
        active = (upper * half).astype(jnp.bfloat16)
        act_ref[:, cols] = active
        slope = half + 0.5 * upper * (1.0 - flat * flat) * math.sqrt(2.0 / math.pi) * (
            1.0 + 3.0 * 0.044715 * square
        )
        d_upper = (dot_nt(gy_ref[...], down_ref[cols, :]) * slope).astype(jnp.bfloat16)
        acc_ref[...] += dot_nn(active, down_ref[cols, :])
        d_n3_ref[...] += dot_nt(d_upper, up_ref[step])
        d_up_ref[:, cols] = dot_nn(n3t_ref[...], d_upper).astype(jnp.bfloat16)
        pltpu.make_async_copy(d_up_ref.at[:, cols], d_up_hbm.at[:, cols], sems.at[4]).start()
        return carry

    lax.fori_loop(0, ff_blocks, mlp_step, 0)
    result_ref[...] = acc_ref[...].astype(jnp.bfloat16)
    pulled, d_gain_mlp = norm_pull(second_ref[...], gain_mlp, d_n3_ref[...])
    d_second = gy_ref[...].astype(jnp.float32) + pulled
    acc_ref[...] = d_second
    gc_ref[...] = d_second.astype(jnp.bfloat16)
    att_rows[...] = (
        dot_nt(gc_ref[...], sq_ref[2]).astype(jnp.bfloat16).astype(jnp.float32) * used_ref[...]
    ).astype(jnp.bfloat16)

    def cross_back(step, carry):
        tok, key, lanes = where(step)
        grad = stack_pair(att_rows[tok, lanes])
        query = stack_pair(cq_ref[tok, lanes])
        probs = prob_ref[step]
        d_probs = dot_nt(grad, pair_ref[1, key, lanes])
        d_scores = (
            probs * (d_probs - jnp.sum(probs * d_probs, axis=-1, keepdims=True))
        ).astype(jnp.bfloat16)
        d_query = unstack_pair(dot_nn(d_scores, pair_ref[0, key, lanes]))
        d_cq_ref[tok, lanes] = (d_query * SCORE_SCALE).astype(jnp.bfloat16)
        d_pair_ref[0, key, lanes] = (dot_tn(d_scores, query) * SCORE_SCALE).astype(jnp.bfloat16)
        d_pair_ref[1, key, lanes] = dot_tn(probs.astype(jnp.bfloat16), grad).astype(jnp.bfloat16)
        return carry

    lax.fori_loop(0, groups * couples, cross_back, 0)
    pulled, d_gain_cross = norm_pull(first_ref[...], gain_cross, dot_nt(d_cq_ref[...], sq_ref[1]))
    d_first = acc_ref[...] + pulled
    first_ref[...] = d_first
    ga_ref[...] = d_first.astype(jnp.bfloat16)
    for index in range(micro):
        d_att_ref[index] = dot_nt(sq_ref[0], ga_ref[pl.ds(index * tokens, tokens), :]).astype(jnp.bfloat16)
    d_gain_ref[...] = jnp.concatenate([d_gain_cross, d_gain_mlp, jnp.zeros((6, width), jnp.float32)], axis=0)
    pltpu.make_async_copy(d_up_ref, d_up_hbm, sems.at[4]).wait()


def middle(attended_t, hidden, lead_hid, grads, lead_grad, gains, used, squares, kv, neigh, up, down):
    micro, tokens, width = hidden.shape
    rows = micro * tokens
    ff = up.shape[0] * width
    low = jnp.bfloat16
    out_shape = [
        jax.ShapeDtypeStruct((rows, width), low),
        jax.ShapeDtypeStruct((rows, width), jnp.float32),
        jax.ShapeDtypeStruct((micro, width, tokens), low),
        jax.ShapeDtypeStruct((rows, width), low),
        jax.ShapeDtypeStruct((rows, width), low),
        jax.ShapeDtypeStruct((rows, width), low),
        jax.ShapeDtypeStruct((rows, width), low),
        jax.ShapeDtypeStruct((rows, width), low),
        jax.ShapeDtypeStruct((rows, width), low),
        jax.ShapeDtypeStruct((rows, ff), low),
        jax.ShapeDtypeStruct((2,) + neigh.shape, low),
        jax.ShapeDtypeStruct((8, width), jnp.float32),
        jax.ShapeDtypeStruct((width, ff), low),
    ]
    steps = rows // SPAN * HEADS // 2
    scratch = [
        pltpu.VMEM(kv.shape, low),
        pltpu.VMEM(neigh.shape, low),
        pltpu.VMEM(up.shape, low),
        pltpu.VMEM(down.shape, low),
        pltpu.VMEM((rows, width), low),
        pltpu.VMEM((rows, width), jnp.float32),
        pltpu.VMEM((rows, width), low),
        pltpu.VMEM((2,) + neigh.shape, low),
        pltpu.VMEM((steps, 2 * SPAN, NEIGHBOURS * NEIGH_LEN), jnp.float32),
        pltpu.VMEM((rows, width), jnp.float32),
        pltpu.VMEM((rows, width), jnp.float32),
        pltpu.VMEM((rows, width), low),
        pltpu.VMEM((width, rows), low),
        pltpu.VMEM((width, ff), low),
        pltpu.SemaphoreType.DMA((5,)),
    ]
    return pl.pallas_call(
        middle_kernel,
        out_shape=out_shape,
        in_specs=[VMEM] * 8 + [ANY] * 4,
        out_specs=[VMEM] * 12 + [ANY],
        scratch_shapes=scratch,
        compiler_params=local_params(),
        cost_estimate=pl.CostEstimate(flops=12 * 10**9, bytes_accessed=40 * 10**6, transcendentals=10**6),
    )(attended_t, hidden, lead_hid, grads, lead_grad, gains, used, squares, kv, neigh, up, down)


PLAN = (0, 0, 1, 0, 0, 1, 0, 0, 1, 1, 1, 0)


def front_kernel(depth, items, *refs):
    count = len(items)
    w_refs = refs[:7]
    small_ref, used_ref, neigh_ref, hid_ref, grad_hbm = refs[7:12]
    (
        qkv_out, sq_out, kv_out, up_out, down_out, d_up_hbm, gain_out, cos_out, sin_out,
        unit_out, mixed_out, total_out, start_out, att_out,
        result_ref, first_ref, d_att_ref, n2_ref, d_cq_ref, cm_ref, gc_ref, ga_ref, gy_ref, act_ref, d_pair_ref,
        d_gain_ref,
    ) = refs[12:38]
    (
        qkv_ref, small_all, hid_vmem, grad_ref, lead_hid, lead_grad, n1_ref, temp_ref, note_ref, turned_ref, doc_ref,
        stage_ref, sq_ref, kv_ref, up_ref, down_ref,
        att_rows, second_ref, cq_ref, pair_ref, prob_ref, acc_ref, d_n3_ref, n3_ref, n3t_ref, d_up_ref,
        own_sem, send_sem, recv_sem, misc_sem, lead_send, lead_recv, load_sem, unit_send, unit_recv,
        att_send, att_recv, stage_sem, up_sem,
    ) = refs[38:]
    z, y, c, x = coords()
    total = depth * 8
    me = lax.axis_index("blk") * 2 + lax.axis_index("head")
    mine, holder = unit_of(me, total)
    slab = w_refs[0].shape[0]
    micro, tokens, width = hid_ref.shape
    homes = (qkv_ref, sq_out, kv_out, up_out, down_out)
    whole = slice(None)

    def view(item, zs, ys, cs, xs):
        buffer, first, last, kind = item
        if buffer == 4:
            return down_out.at[zs, ys, cs, xs, pl.ds(first, last - first)]
        return homes[buffer].at[pl.ds(first, last - first), zs, ys, cs, xs]

    load = pltpu.make_async_copy(hid_ref, hid_vmem, load_sem.at[0])
    load.start()
    load_grad = pltpu.make_async_copy(grad_hbm, grad_ref, load_sem.at[2])
    load_grad.start()
    own = []
    for index, item in enumerate(items):
        buffer, first, last, kind = item
        cols = homes[buffer].shape[-1]
        if buffer == 4:
            moves = [(w_refs[6].at[pl.ds(first, last - first)], view(item, z, y, c, x))]
        elif buffer == 1:
            moves = [(w_refs[1 + block], sq_out.at[block, z, y, c, x]) for block in range(first, last)]
        else:
            source = w_refs[(0, None, 4, 5)[buffer]]
            moves = [
                (source.at[:, pl.ds(block * cols, cols)], homes[buffer].at[block, z, y, c, x])
                for block in range(first, last)
            ]
        for src, dst in moves:
            pltpu.make_async_copy(src, dst, own_sem.at[index]).start()
        mirror = view(item, z, y, c, x)
        own.append(pltpu.make_async_copy(mirror, mirror, own_sem.at[index]))
    pltpu.make_async_copy(small_ref, small_all.at[me], misc_sem.at[1]).start()
    all_barrier(total, me)

    def send_small(step, carry):
        peer = lax.rem(me + step, total)
        remote(
            small_ref, small_all.at[me], misc_sem.at[0], misc_sem.at[1], (peer // 2, lax.rem(peer, 2))
        ).start()
        return carry

    prev = lax.rem(me + total - 1, total)
    prev_at = (prev // 2, lax.rem(prev, 2))
    leads = [
        remote(hid_ref.at[:, pl.ds(0, 64)], lead_hid, lead_send.at[0], lead_recv.at[0], prev_at),
        remote(grad_hbm.at[:, pl.ds(0, 64)], lead_grad, lead_send.at[1], lead_recv.at[1], prev_at),
    ]

    def start(index):
        own[index].wait()
        item = items[index]
        for step in range(1, depth):
            other = lax.rem(z + step, depth)
            remote(
                view(item, z, y, c, x), view(item, z, y, c, x),
                send_sem.at[index, 0], recv_sem.at[index, 0], place(other, y, c, x),
            ).start()

    def bulk(index, phase):
        item = items[index]
        first_x = item[3] == 0
        if phase == 1:
            ref = view(item, whole, y, c, x)
            where = place(z, y, c, 1 - x) if first_x else place(z, 1 - y, c, x)
        elif phase == 2:
            ref = view(item, whole, y, c, whole) if first_x else view(item, whole, whole, c, x)
            where = place(z, 1 - y, c, x) if first_x else place(z, y, c, 1 - x)
        else:
            ref = view(item, whole, whole, c, whole)
            where = place(z, y, 1 - c, x)
        return remote(ref, ref, send_sem.at[index, phase], recv_sem.at[index, phase], where)

    def arrived(index, phase):
        if phase == 0:
            ref = view(items[index], pl.ds(0, depth - 1), y, c, x)
            pltpu.make_async_copy(ref, ref, recv_sem.at[index, 0]).wait()
        else:
            bulk(index, phase).wait_recv()

    def sent(index, phase):
        if phase == 0:
            ref = view(items[index], pl.ds(0, depth - 1), y, c, x)
            pltpu.make_async_copy(ref, ref, send_sem.at[index, 0]).wait()
        else:
            bulk(index, phase).wait_send()

    pairs = (count + 1) // 2

    def gather_step(step):
        for phase in range(4, -1, -1):
            pair = step - phase
            if not 0 <= pair < pairs:
                continue
            for index in range(2 * pair, min(2 * pair + 2, count)):
                if phase == 0:
                    start(index)
                else:
                    arrived(index, phase - 1)
                    if phase < 4:
                        bulk(index, phase).start()

    half_dim = HEAD_DIM // 2

    def tables():
        lane = lax.broadcasted_iota(jnp.int32, (half_dim, tokens), 1)
        order = lax.broadcasted_iota(jnp.int32, (half_dim, tokens), 0)
        frequency = jnp.exp(order.astype(jnp.float32) * (-2.0 * math.log(10000.0) / HEAD_DIM))
        angles = (me * tokens + lane).astype(jnp.float32) * frequency
        cos_out[...] = jnp.cos(angles)
        sin_out[...] = jnp.sin(angles)

    def normalise():
        load.wait()
        pltpu.make_async_copy(small_all, small_all, misc_sem.at[1]).wait()
        for peer in range(total):
            temp_ref[pl.ds(peer * slab, slab), pl.ds(0, 128)] = small_all[peer, :slab, :].astype(jnp.float32)
            doc_ref[pl.ds(peer, 1), :] = jnp.where(
                mine < HEADS, small_all[peer, 32:33, :].astype(jnp.float32), small_all[peer, 33:34, :].astype(jnp.float32)
            )
        turned = temp_ref[:, pl.ds(0, 128)].T
        gain_out[...] = jnp.concatenate(
            [turned[0:1], turned[32:33], turned[64:65], jnp.zeros((5, width), jnp.float32)], axis=0
        )
        for index in range(micro):
            unit_rows = norm_parts(hid_vmem[index].astype(jnp.float32))[0]
            n1_ref[pl.ds(index * tokens, tokens), :] = (unit_rows * gain_out[0:1, :]).astype(jnp.bfloat16)

    def project(part):
        cols = qkv_ref.shape[-1]
        heads = cols // HEAD_DIM
        for half in range(2):
            block = part * 2 + half
            for level in range(depth):
                for inner in range(8):
                    at = (level * 8 + inner) * slab
                    temp_ref[pl.ds(at, slab), :] = qkv_ref[
                        block, level, inner // 4, (inner // 2) % 2, inner % 2
                    ].astype(jnp.float32)
            raw = dot_nn(n1_ref[...], temp_ref[...].astype(jnp.bfloat16))
            for index in range(micro):
                raw_t = raw[index * tokens : (index + 1) * tokens].T
                for head in range(heads):
                    value = raw_t[head * HEAD_DIM : (head + 1) * HEAD_DIM]
                    if part < 2:
                        first_half, second_half = value[:half_dim], value[half_dim:]
                        value = jnp.concatenate(
                            [
                                first_half * cos_out[...] - second_half * sin_out[...],
                                second_half * cos_out[...] + first_half * sin_out[...],
                            ],
                            axis=0,
                        )
                    note_ref[index * HEADS + half * heads + head, part] = value.astype(jnp.bfloat16)

    def slot(device, part):
        return unit_out.at[part, :, pl.ds(pl.multiple_of(device * tokens, 128), tokens)]

    def send_part(part):
        @pl.when(holder)
        def _():
            pltpu.make_async_copy(note_ref.at[mine, part], slot(me, part), unit_recv).start()

        def send(step, carry):
            peer = lax.rem(me + step, total)
            unit, held = unit_of(peer, total)

            @pl.when(held)
            def _():
                remote(
                    note_ref.at[unit, part], slot(me, part), unit_send, unit_recv, (peer // 2, lax.rem(peer, 2))
                ).start()

            return carry

        lax.fori_loop(1, total, send, 0)

    def doc_starts():
        docs = doc_ref[...]
        lane = lax.broadcasted_iota(jnp.int32, docs.shape, 1)
        row = lax.broadcasted_iota(jnp.int32, docs.shape, 0)
        place_at = row * tokens + lane
        before = jnp.where(
            lane == 0, pltpu.roll(pltpu.roll(docs, 1, 0), 1, 1), pltpu.roll(docs, 1, 1)
        )
        begins = (docs != before) | (place_at == 0)
        value = jnp.where(begins, place_at, 0).astype(jnp.float32)
        step = 1
        while step < tokens:
            value = jnp.maximum(value, jnp.where(lane >= step, pltpu.roll(value, step, 1), 0.0))
            step *= 2
        carried = jnp.broadcast_to(jnp.max(value, axis=1, keepdims=True), docs.shape)
        carried = jnp.where(row >= 1, pltpu.roll(carried, 1, 0), 0.0)
        step = 1
        while step < total:
            carried = jnp.maximum(carried, jnp.where(row >= step, pltpu.roll(carried, step, 0), 0.0))
            step *= 2
        starts = jnp.maximum(value, carried).astype(jnp.int32)
        for peer in range(total):
            start_out[:, pl.ds(peer * tokens, tokens)] = starts[peer : peer + 1, :]

    length = tokens * total
    tiles = length // TILE
    reach = (TILE + DOC_MAX - 2) // TILE

    def open_units():
        @pl.when(holder)
        def _():
            part = note_ref.at[pl.ds(0, UNITS - 1)]
            pltpu.make_async_copy(unit_out, unit_out, unit_recv).wait()
            pltpu.make_async_copy(part, part, unit_send).wait()

        @pl.when(jnp.logical_not(holder))
        def _():
            pltpu.make_async_copy(note_ref, note_ref, unit_send).wait()

    def attend(query_tile):
        @pl.when(holder)
        def _():
            columns = pl.ds(query_tile * TILE, TILE)
            query_t = unit_out[0, :, columns]
            first_row = start_out[:, columns]

            def one_key(step, state):
                peak, weight, mixed = state
                key_tile = query_tile - step
                scores = dot_nn(tile_at(unit_out, key_tile, 1).T, query_t) * (SCORE_SCALE * LOG2E)
                scores = jnp.where(tile_mask(key_tile, query_tile, first_row), scores, -1e30)
                new_peak = jnp.maximum(peak, jnp.max(scores, axis=0, keepdims=True))
                probs = jnp.exp2(scores - new_peak)
                fade = jnp.exp2(peak - new_peak)
                weight = weight * fade + jnp.sum(probs, axis=0, keepdims=True)
                mixed = mixed * fade + dot_nn(tile_at(unit_out, key_tile, 2), probs.astype(jnp.bfloat16))
                return new_peak, weight, mixed

            begin = (
                jnp.full((1, TILE), -1e30, jnp.float32),
                jnp.zeros((1, TILE), jnp.float32),
                jnp.zeros((HEAD_DIM, TILE), jnp.float32),
            )
            peak, weight, mixed = lax.fori_loop(0, min(query_tile, reach) + 1, one_key, begin)
            mixed_out[:, columns] = mixed / weight
            total_out[:, columns] = peak + jnp.log2(weight)

    def back_slot(device):
        return turned_ref.at[:, pl.ds(pl.multiple_of(device * tokens, 128), tokens)]

    def send_back():
        @pl.when(holder)
        def _():
            def turn(step, carry):
                part = pl.ds(pl.multiple_of(step * 16, 16), 16)
                turned_ref[part, :] = pltpu.roll(mixed_out[part, :], length - LEAD, 1).astype(jnp.bfloat16)
                return carry

            lax.fori_loop(0, HEAD_DIM // 16, turn, 0)
            pltpu.make_async_copy(back_slot(me), att_out.at[mine], att_recv).start()

            def send(step, carry):
                peer = lax.rem(me + step, total)
                remote(
                    back_slot(peer), att_out.at[mine], att_send, att_recv, (peer // 2, lax.rem(peer, 2))
                ).start()
                return carry

            lax.fori_loop(1, total, send, 0)

    def unpack(jobs):
        copies = [
            pltpu.make_async_copy(source.at[block], stage_ref.at[slot_], stage_sem.at[slot_])
            for slot_, (source, block, target) in enumerate(jobs)
        ]
        for copy in copies:
            copy.start()
        for slot_, (source, block, target) in enumerate(jobs):
            copies[slot_].wait()

            def body(level, carry):
                for inner in range(4):
                    both = jnp.concatenate(
                        [stage_ref[slot_, level, inner // 2, inner % 2, side].astype(jnp.float32) for side in range(2)],
                        axis=0,
                    )
                    at = pl.multiple_of((level * 4 + inner) * 2 * slab, 16)
                    target[block, pl.ds(at, 2 * slab), :] = both.astype(jnp.bfloat16)
                return carry

            lax.fori_loop(0, depth, body, 0)

    def fetch_down():
        down_rows = down_out.shape[-2]

        def body(step, carry):
            level, rest_ = step // 8, lax.rem(step, 8)
            pltpu.make_async_copy(
                down_out.at[level, rest_ // 4, lax.rem(rest_ // 2, 2), lax.rem(rest_, 2)],
                down_ref.at[pl.ds(pl.multiple_of(step * down_rows, 16), down_rows)],
                stage_sem.at[2],
            ).start()
            return carry

        lax.fori_loop(0, total, body, 0)

    gather_step(0)
    lax.fori_loop(1, total, send_small, 0)
    tables()
    gather_step(1)
    gather_step(2)
    for lead in leads:
        lead.start()
    normalise()
    gather_step(3)
    doc_starts()
    for part in range(3):
        gather_step(4 + part)
        if part == 2:
            keep = pltpu.make_async_copy(qkv_ref, qkv_out, load_sem.at[1])
            keep.start()
        project(part)
        send_part(part)
    rows = micro * tokens
    done = {"tick": 7}

    def tick(number=1):
        for _ in range(number):
            if done["tick"] < pairs + 4:
                gather_step(done["tick"])
                done["tick"] += 1

    def make_key_values():
        chunk = 256
        chunks = neigh_ref.shape[0] // chunk

        def make_pairs(step, carry):
            side, block = step // chunks, lax.rem(step, chunks)
            part = pl.ds(pl.multiple_of(block * chunk, chunk), chunk)
            pair_ref[side, part, :] = dot_nn(neigh_ref[part, :], kv_ref[side]).astype(jnp.bfloat16)
            return carry

        lax.fori_loop(0, 2 * chunks, make_pairs, 0)
    couples = HEADS // 2
    pair_rows = NEIGHBOURS * NEIGH_LEN
    groups = rows // SPAN

    def where(group, couple):
        tok = pl.ds(pl.multiple_of(group * SPAN, SPAN), SPAN)
        key = pl.ds(pl.multiple_of(group * pair_rows, pair_rows), pair_rows)
        lanes = pl.ds(couple * 2 * HEAD_DIM, 2 * HEAD_DIM)
        return tok, key, lanes

    def cross_step(group, carry):
        for couple in range(couples):
            tok, key, lanes = where(group, couple)
            query = stack_pair(cq_ref[tok, lanes])
            scores = dot_nt(query, pair_ref[0, key, lanes]) * SCORE_SCALE
            weights = jnp.exp(scores - jnp.max(scores, axis=-1, keepdims=True))
            probs = weights / jnp.sum(weights, axis=-1, keepdims=True)
            prob_ref[group * couples + couple] = probs
            mixed = unstack_pair(dot_nn(probs.astype(jnp.bfloat16), pair_ref[1, key, lanes]))
            cm_ref[tok, lanes] = (mixed * used_ref[tok, :]).astype(jnp.bfloat16)
        return carry


    tick()
    unpack([(kv_out, 0, kv_ref), (kv_out, 1, kv_ref)])
    make_key_values()
    tick(PLAN[0])
    open_units()
    for tile in range(tiles):
        attend(tile)
        tick(PLAN[1 + tile])
    send_back()
    tick(PLAN[1 + tiles])
    unpack([(sq_out, 0, sq_ref), (sq_out, 1, sq_ref)])
    load_grad.wait()
    for lead in leads:
        lead.wait_recv()
    pltpu.make_async_copy(att_out, att_out, att_recv).wait()
    gain_cross, gain_mlp = gain_out[1:2, :], gain_out[2:3, :]
    for index in range(micro):
        part = pl.ds(index * tokens, tokens)
        hidden = shift_rows(hid_vmem[index], lead_hid[index])
        gy_ref[part, :] = shift_rows(grad_ref[index], lead_grad[index]).astype(jnp.bfloat16)
        first_ref[part, :] = hidden + dot_tn(att_out[index * HEADS : (index + 1) * HEADS].reshape(width, tokens), sq_ref[0])
    n2_ref[...] = (norm_parts(first_ref[...])[0] * gain_cross).astype(jnp.bfloat16)
    cq_ref[...] = dot_nn(n2_ref[...], sq_ref[1]).astype(jnp.bfloat16)

    tick(PLAN[2 + tiles])
    lax.fori_loop(0, groups // 2, cross_step, 0)
    tick(PLAN[3 + tiles])
    unpack([(sq_out, 2, sq_ref), (up_out, 0, up_ref)])
    lax.fori_loop(groups // 2, groups, cross_step, 0)
    second_ref[...] = first_ref[...] + dot_nn(cm_ref[...], sq_ref[2])
    n3 = (norm_parts(second_ref[...])[0] * gain_mlp).astype(jnp.bfloat16)
    n3_ref[...] = n3
    n3t_ref[...] = n3.T
    acc_ref[...] = second_ref[...]
    d_n3_ref[...] = jnp.zeros_like(d_n3_ref)
    tick(pairs + 4 - done["tick"])
    fetch_down()
    unpack([(up_out, 1, up_ref), (up_out, 2, up_ref)])
    unpack([(up_out, 3, up_ref)])
    pltpu.make_async_copy(down_ref, down_ref, stage_sem.at[2]).wait()
    ff_blocks = up_ref.shape[0]
    d_up_moves = []
    for step in range(ff_blocks):
        cols = pl.ds(step * width, width)
        upper = dot_nn(n3_ref[...], up_ref[step])
        square = upper * upper
        flat = jnp.tanh(math.sqrt(2.0 / math.pi) * upper * (1.0 + 0.044715 * square))
        half = 0.5 * (1.0 + flat)
        active = (upper * half).astype(jnp.bfloat16)
        act_ref[:, cols] = active
        slope = half + 0.5 * upper * (1.0 - flat * flat) * math.sqrt(2.0 / math.pi) * (
            1.0 + 3.0 * 0.044715 * square
        )
        d_upper = (dot_nt(gy_ref[...], down_ref[cols, :]) * slope).astype(jnp.bfloat16)
        acc_ref[...] += dot_nn(active, down_ref[cols, :])
        d_n3_ref[...] += dot_nt(d_upper, up_ref[step])
        if step >= 2:
            d_up_moves[step - 2].wait()
        d_up_ref[step % 2] = dot_nn(n3t_ref[...], d_upper).astype(jnp.bfloat16)
        move = pltpu.make_async_copy(d_up_ref.at[step % 2], d_up_hbm.at[:, cols], up_sem.at[step % 2])
        move.start()
        d_up_moves.append(move)
    result_ref[...] = acc_ref[...].astype(jnp.bfloat16)
    pulled, d_gain_mlp = norm_pull(second_ref[...], gain_mlp, d_n3_ref[...])
    d_second = gy_ref[...].astype(jnp.float32) + pulled
    acc_ref[...] = d_second
    gc_ref[...] = d_second.astype(jnp.bfloat16)
    att_rows[...] = (
        dot_nt(gc_ref[...], sq_ref[2]).astype(jnp.bfloat16).astype(jnp.float32) * used_ref[...]
    ).astype(jnp.bfloat16)

    def cross_back(group, carry):
        for couple in range(couples):
            tok, key, lanes = where(group, couple)
            grad = stack_pair(att_rows[tok, lanes])
            query = stack_pair(cq_ref[tok, lanes])
            probs = prob_ref[group * couples + couple]
            d_probs = dot_nt(grad, pair_ref[1, key, lanes])
            d_scores = (
                probs * (d_probs - jnp.sum(probs * d_probs, axis=-1, keepdims=True))
            ).astype(jnp.bfloat16)
            d_query = unstack_pair(dot_nn(d_scores, pair_ref[0, key, lanes]))
            d_cq_ref[tok, lanes] = (d_query * SCORE_SCALE).astype(jnp.bfloat16)
            d_pair_ref[0, key, lanes] = (dot_tn(d_scores, query) * SCORE_SCALE).astype(jnp.bfloat16)
            d_pair_ref[1, key, lanes] = dot_tn(probs.astype(jnp.bfloat16), grad).astype(jnp.bfloat16)
        return carry

    lax.fori_loop(0, groups, cross_back, 0)
    pulled, d_gain_cross = norm_pull(first_ref[...], gain_cross, dot_nt(d_cq_ref[...], sq_ref[1]))
    d_first = acc_ref[...] + pulled
    first_ref[...] = d_first
    ga_ref[...] = d_first.astype(jnp.bfloat16)
    for index in range(micro):
        d_att_ref[index] = dot_nt(sq_ref[0], ga_ref[pl.ds(index * tokens, tokens), :]).astype(jnp.bfloat16)
    d_gain_ref[...] = jnp.concatenate([d_gain_cross, d_gain_mlp, jnp.zeros((6, width), jnp.float32)], axis=0)
    for move in d_up_moves[-2:]:
        move.wait()


    for index in range(count):
        for phase in range(4):
            sent(index, phase)
    for lead in leads:
        lead.wait_send()
    keep.wait()
    rest = small_all.at[pl.ds(0, total - 1)]
    pltpu.make_async_copy(rest, rest, misc_sem.at[0]).wait()

    @pl.when(holder)
    def _():
        part = turned_ref.at[:, pl.ds(0, tokens * (total - 1))]
        pltpu.make_async_copy(part, part, att_send).wait()


def front(depth, w_qkv, w_attn_out, w_cross_q, w_cross_out, w_kv, w_up, w_down, small, used, neigh, hidden, grads):
    total = depth * 8
    rows = w_qkv.shape[0]
    down_rows = w_down.shape[0]
    micro, tokens, width = hidden.shape
    length = tokens * total
    third = down_rows // 3
    row_total = micro * tokens
    ff = w_up.shape[1]
    items = [
        (0, 0, 1, 0), (0, 1, 2, 1), (0, 2, 3, 0), (0, 3, 4, 1), (0, 4, 5, 0), (0, 5, 6, 1),
        (2, 0, 1, 0), (2, 1, 2, 1),
        (1, 0, 1, 0), (1, 1, 2, 1),
        (1, 2, 3, 0), (3, 0, 1, 1),
        (4, 0, third, 0), (4, third, 2 * third, 1),
        (4, 2 * third, down_rows, 0), (3, 1, 2, 1),
        (3, 2, 3, 0), (3, 3, 4, 1),
    ]
    count = len(items)
    low, high = jnp.bfloat16, jnp.float32
    spots = (depth, 2, 2, 2)
    qkv_shape = (6, *spots, rows, width // 2)
    out_shape = [
        jax.ShapeDtypeStruct(qkv_shape, low),
        jax.ShapeDtypeStruct((3, *spots, rows, width), low),
        jax.ShapeDtypeStruct((2, *spots, rows, width), low),
        jax.ShapeDtypeStruct((w_up.shape[1] // width, *spots, rows, width), low),
        jax.ShapeDtypeStruct((*spots, down_rows, width), low),
        jax.ShapeDtypeStruct((width, w_up.shape[1]), low),
        jax.ShapeDtypeStruct((8, width), high),
        jax.ShapeDtypeStruct((HEAD_DIM // 2, tokens), high),
        jax.ShapeDtypeStruct((HEAD_DIM // 2, tokens), high),
        jax.ShapeDtypeStruct((3, HEAD_DIM, length), low),
        jax.ShapeDtypeStruct((HEAD_DIM, length), high),
        jax.ShapeDtypeStruct((1, length), high),
        jax.ShapeDtypeStruct((1, length), jnp.int32),
        jax.ShapeDtypeStruct((UNITS, HEAD_DIM, tokens), low),
        jax.ShapeDtypeStruct((row_total, width), low),
        jax.ShapeDtypeStruct((row_total, width), high),
        jax.ShapeDtypeStruct((micro, width, tokens), low),
        jax.ShapeDtypeStruct((row_total, width), low),
        jax.ShapeDtypeStruct((row_total, width), low),
        jax.ShapeDtypeStruct((row_total, width), low),
        jax.ShapeDtypeStruct((row_total, width), low),
        jax.ShapeDtypeStruct((row_total, width), low),
        jax.ShapeDtypeStruct((row_total, width), low),
        jax.ShapeDtypeStruct((row_total, ff), low),
        jax.ShapeDtypeStruct((2,) + neigh.shape, low),
        jax.ShapeDtypeStruct((8, width), high),
    ]
    steps = row_total // SPAN * HEADS // 2
    dma = pltpu.SemaphoreType.DMA
    return pl.pallas_call(
        functools.partial(front_kernel, depth, items),
        out_shape=out_shape,
        in_specs=[VMEM] * 10 + [ANY] * 2,
        out_specs=[ANY] * 6 + [VMEM] * 20,
        scratch_shapes=[
            pltpu.VMEM(qkv_shape, low),
            pltpu.VMEM((total,) + small.shape, low),
            pltpu.VMEM(hidden.shape, low),
            pltpu.VMEM(hidden.shape, low),
            pltpu.VMEM((micro, 64, width), low),
            pltpu.VMEM((micro, 64, width), low),
            pltpu.VMEM((micro * tokens, width), low),
            pltpu.VMEM((width, width // 2), high),
            pltpu.VMEM((UNITS, 3, HEAD_DIM, tokens), low),
            pltpu.VMEM((HEAD_DIM, length), low),
            pltpu.VMEM((total, tokens), high),
            pltpu.VMEM((2, *spots, rows, width), low),
            pltpu.VMEM((3, width, width), low),
            pltpu.VMEM((2, width, width), low),
            pltpu.VMEM((ff // width, width, width), low),
            pltpu.VMEM((ff, width), low),
            pltpu.VMEM((row_total, width), low),
            pltpu.VMEM((row_total, width), high),
            pltpu.VMEM((row_total, width), low),
            pltpu.VMEM((2,) + neigh.shape, low),
            pltpu.VMEM((steps, 2 * SPAN, NEIGHBOURS * NEIGH_LEN), high),
            pltpu.VMEM((row_total, width), high),
            pltpu.VMEM((row_total, width), high),
            pltpu.VMEM((row_total, width), low),
            pltpu.VMEM((width, row_total), low),
            pltpu.VMEM((2, width, width), low),
            dma((count,)), dma((count, 4)), dma((count, 4)), dma((2,)), dma((2,)), dma((2,)), dma((3,)), dma, dma,
            dma, dma, dma((3,)), dma((2,)),
        ],
        compiler_params=pltpu.CompilerParams(
            collective_id=0, has_side_effects=True, vmem_limit_bytes=62 * 2**20
        ),
        cost_estimate=pl.CostEstimate(flops=10**9, bytes_accessed=20 * 10**6, transcendentals=0),
    )(w_qkv, w_attn_out, w_cross_q, w_cross_out, w_kv, w_up, w_down, small, used, neigh, hidden, grads)


def last_kernel(depth, items, skew, *refs):
    count = len(items)
    (
        back_ref, result_ref, first_ref, n2_ref, d_cq_ref, cm_ref, gc_ref, ga_ref, gy_ref, act_ref, d_pair_ref,
        att_ref, neigh_ref, kv_ref, qkv_ref, hidden_ref, gain_ref, cos_ref, sin_ref, d_gain_rest_ref,
    ) = refs[:20]
    (
        output_ref, grad_in_ref, grad_neigh_ref, out_qkv, out_att, out_cq, out_co, out_kv, out_down, gain_out,
    ) = refs[20:30]
    full = refs[30 : 30 + count]
    got_core = refs[30 + count : 30 + 2 * count]
    got_one = refs[30 + 2 * count : 30 + 3 * count]
    got_two = refs[30 + 3 * count : 30 + 4 * count]
    got_z = refs[30 + 4 * count : 30 + 5 * count]
    (
        sent_ref, tail_first, tail_result, raw_ref, n1t_ref, d_n1_ref, temp_ref, gain_mine, gain_got, gain_z,
        send_sem, recv_sem, unit_send, unit_recv, tail_send, tail_recv, gain_send, gain_recv,
    ) = refs[30 + 5 * count :]
    micro, tokens, width = hidden_ref.shape
    total = depth * 8
    z, y, c, x = coords()
    me = lax.axis_index("blk") * 2 + lax.axis_index("head")
    mine, holder = unit_of(me, total)
    whole = slice(None)
    all_barrier(total, me)

    after = lax.rem(me + 1, total)
    after_at = (after // 2, lax.rem(after, 2))
    tails = []
    for index in range(micro):
        part = pl.ds(index * tokens + tokens - 64, 64)
        tails.append(
            remote(first_ref.at[part], tail_first.at[index], tail_send.at[index], tail_recv.at[index], after_at)
        )
        tails.append(
            remote(
                result_ref.at[part], tail_result.at[index],
                tail_send.at[micro + index], tail_recv.at[micro + index], after_at,
            )
        )

    def slot(device):
        return back_ref.at[:, :, pl.ds(pl.multiple_of(device * tokens, 128), tokens)]

    @pl.when(holder)
    def _():
        pltpu.make_async_copy(slot(me), sent_ref.at[mine], unit_recv).start()

        def send(step, carry):
            peer = lax.rem(me + step, total)
            remote(
                slot(peer), sent_ref.at[mine], unit_send, unit_recv, (peer // 2, lax.rem(peer, 2))
            ).start()
            return carry

        lax.fori_loop(1, total, send, 0)

    for tail in tails:
        tail.start()

    slab = full[0].shape[-2]

    def spread(index, block):
        buffer = full[index]
        cols = buffer.shape[-1]

        def body(level, carry):
            for place_in in range(8):
                at = pl.multiple_of((level * 8 + place_in) * slab, 8)
                buffer[block, level, place_in // 4, (place_in // 2) % 2, place_in % 2] = temp_ref[
                    pl.ds(at, slab), :cols
                ].astype(jnp.bfloat16)
            return carry

        lax.fori_loop(0, depth, body, 0)

    down_index = [index for index, item in enumerate(items) if item[0] == "down"]

    def make_down():
        def body(level, carry):
            cols = pl.ds(pl.multiple_of(level * width, width), width)
            temp_ref[...] = dot_tn(act_ref[:, cols], gy_ref[...])
            for place_in in range(8):
                for part, index in enumerate(down_index):
                    at = place_in * slab * len(down_index) + part * slab
                    full[index][0, level, place_in // 4, (place_in // 2) % 2, place_in % 2] = temp_ref[
                        pl.ds(at, slab), :
                    ].astype(jnp.bfloat16)
            return carry

        lax.fori_loop(0, depth, body, 0)

    def take_units():
        @pl.when(holder)
        def _():
            part = back_ref.at[:, :, pl.ds(0, tokens * (total - 1))]
            pltpu.make_async_copy(part, part, unit_send).wait()

        pltpu.make_async_copy(sent_ref, sent_ref, unit_recv).wait()
        half = HEAD_DIM // 2

        def body(head, carry):
            for index in range(micro):
                lanes = pl.ds(index * tokens, tokens)
                cosine, sine = cos_ref[...], sin_ref[...]
                for part in range(3):
                    value = sent_ref[index * HEADS + head, part].astype(jnp.float32)
                    at = pl.multiple_of(part * width + head * HEAD_DIM, HEAD_DIM)
                    if part < 2:
                        first_half, second_half = value[:half], value[half:]
                        value = jnp.concatenate(
                            [
                                first_half * cosine + second_half * sine,
                                second_half * cosine - first_half * sine,
                            ],
                            axis=0,
                        )
                    raw_ref[pl.ds(at, HEAD_DIM), lanes] = value.astype(jnp.bfloat16)
            return carry

        lax.fori_loop(0, HEADS, body, 0)
        for index in range(micro):
            normed = norm_parts(hidden_ref[index].astype(jnp.float32))[0] * gain_ref[0:1, :]
            n1t_ref[:, pl.ds(index * tokens, tokens)] = normed.astype(jnp.bfloat16).T

    def make(index):
        kind, which = items[index][:2]
        if kind == "down":
            if index == down_index[0]:
                make_down()
            return
        if kind == "kv":
            temp_ref[...] = dot_tn(neigh_ref[...], d_pair_ref[which])
        elif kind == "att":
            temp_ref[...] = dot_nn(att_ref[0], ga_ref[pl.ds(0, tokens), :])
            for step in range(1, micro):
                temp_ref[...] += dot_nn(att_ref[step], ga_ref[pl.ds(step * tokens, tokens), :])
        elif kind == "cq":
            temp_ref[...] = dot_tn(n2_ref[...], d_cq_ref[...])
        elif kind == "co":
            temp_ref[...] = dot_tn(cm_ref[...], gc_ref[...])
        else:
            if which == 0:
                take_units()
            for block in range(2):
                half = width // 2
                at = which * width + block * half
                temp_ref[:, :half] = dot_nt(n1t_ref[...], raw_ref[pl.ds(at, half), :])
                spread(index, block)
            return
        spread(index, 0)

    def core(index):
        return remote(
            full[index].at[whole, whole, whole, 1 - c], got_core[index],
            send_sem.at[index, 0], recv_sem.at[index, 0], place(z, y, 1 - c, x),
        )

    def one(index):
        if items[index][2] == 0:
            src, where = full[index].at[whole, whole, 1 - y, c], place(z, 1 - y, c, x)
        else:
            src, where = full[index].at[whole, whole, whole, c, 1 - x], place(z, y, c, 1 - x)
        return remote(src, got_one[index], send_sem.at[index, 1], recv_sem.at[index, 1], where)

    def two(index):
        if items[index][2] == 0:
            src, where = full[index].at[whole, whole, y, c, 1 - x], place(z, y, c, 1 - x)
        else:
            src, where = full[index].at[whole, whole, 1 - y, c, x], place(z, 1 - y, c, x)
        return remote(src, got_two[index], send_sem.at[index, 2], recv_sem.at[index, 2], where)

    def send_z(index):
        for step in range(1, depth):
            other = lax.rem(z + step, depth)
            remote(
                full[index].at[whole, other, y, c, x], got_z[index].at[z],
                send_sem.at[index, 3], recv_sem.at[index, 3], place(other, y, c, x),
            ).start()

    def add_into(target, source):
        target[...] = (target[...].astype(jnp.float32) + source[...].astype(jnp.float32)).astype(
            jnp.bfloat16
        )

    def each_level(index, body):
        blocks = full[index].shape[0]
        lax.fori_loop(
            0, blocks * depth, lambda step, carry: (body(step // depth, lax.rem(step, depth)), carry)[1], 0
        )

    def sum_core(index):
        def body(block, level):
            for row in range(2):
                for col in range(2):
                    add_into(
                        full[index].at[block, level, row, c, col], got_core[index].at[block, level, row, col]
                    )

        each_level(index, body)

    def sum_one(index):
        def body(block, level):
            for side in range(2):
                if items[index][2] == 0:
                    target = full[index].at[block, level, y, c, side]
                else:
                    target = full[index].at[block, level, side, c, x]
                add_into(target, got_one[index].at[block, level, side])

        each_level(index, body)

    def sum_two(index):
        each_level(
            index,
            lambda block, level: add_into(
                full[index].at[block, level, y, c, x], got_two[index].at[block, level]
            ),
        )

    def sum_z(index):
        kind, which = items[index][:2]
        for block in range(full[index].shape[0]):
            value = full[index][block, z, y, c, x].astype(jnp.float32)
            for step in range(1, depth):
                value = value + got_z[index][lax.rem(z + step, depth), block].astype(jnp.float32)
            if kind == "down":
                out_down[pl.ds(which * slab, slab), :] = value
            elif kind == "kv":
                out_kv[:, pl.ds(which * width, width)] = value
            elif kind == "qkv":
                out_qkv[:, pl.ds(which * width + block * (width // 2), width // 2)] = value
            else:
                {"att": out_att, "cq": out_cq, "co": out_co}[kind][...] = value

    def phase(index, number):
        if number == 0:
            make(index)
            core(index).start()
        elif number == 1:
            core(index).wait_recv()
            sum_core(index)
            one(index).start()
        elif number == 2:
            one(index).wait_recv()
            sum_one(index)
            two(index).start()
        elif number == 3:
            two(index).wait_recv()
            sum_two(index)
            send_z(index)
        else:
            landed = got_z[index].at[pl.ds(0, depth - 1)]
            pltpu.make_async_copy(landed, landed, recv_sem.at[index, 3]).wait()
            sum_z(index)

    def gain_copy(stage):
        where = (place(z, y, 1 - c, x), place(z, 1 - y, c, x), place(z, y, c, 1 - x))[stage]
        return remote(
            gain_mine.at[stage], gain_got.at[stage], gain_send.at[stage], gain_recv.at[stage], where
        )

    def gain_phase(number):
        if number == 0:
            gain_copy(0).start()
        elif number < 4:
            gain_copy(number - 1).wait_recv()
            gain_mine[number] = gain_mine[number - 1] + gain_got[number - 1]
            if number < 3:
                gain_copy(number).start()
            else:
                for step in range(1, depth):
                    other = lax.rem(z + step, depth)
                    remote(
                        gain_mine.at[3], gain_z.at[z], gain_send.at[3], gain_recv.at[3], place(other, y, c, x)
                    ).start()
        else:
            landed = gain_z.at[pl.ds(0, depth - 1)]
            pltpu.make_async_copy(landed, landed, gain_recv.at[3]).wait()
            value = gain_mine[3]
            for step in range(1, depth):
                value = value + gain_z[lax.rem(z + step, depth)]
            gain_out[...] = value

    def neighbours_part(block):
        chunk = 256
        part = pl.ds(block * chunk, chunk)
        grad_neigh_ref[part, :] = (
            dot_nt(d_pair_ref[0, part, :], kv_ref[0]) + dot_nt(d_pair_ref[1, part, :], kv_ref[1])
        ).astype(jnp.bfloat16)

    def input_part():
        half = width // 2
        blocks = qkv_ref.shape[0]
        d_n1_ref[...] = dot_nn(qkv_ref[0], raw_ref[pl.ds(0, half), :])
        for block in range(1, blocks):
            d_n1_ref[...] += dot_nn(qkv_ref[block], raw_ref[pl.ds(block * half, half), :])
        for tail in tails:
            tail.wait()
        d_gain = jnp.zeros((1, width), jnp.float32)
        for index in range(micro):
            part = pl.ds(index * tokens, tokens)
            d_normed = d_n1_ref[:, part].T
            pulled, part_gain = norm_pull(hidden_ref[index].astype(jnp.float32), gain_ref[0:1, :], d_normed)
            d_gain = d_gain + part_gain
            joined = jnp.concatenate([tail_first[index], first_ref[part, :]], axis=0)
            home = pltpu.roll(joined, joined.shape[0] - 1, 0)[:tokens]
            grad_in_ref[part, :] = (home + pulled).astype(jnp.bfloat16)
            joined = jnp.concatenate(
                [tail_result[index].astype(jnp.float32), result_ref[part, :].astype(jnp.float32)], axis=0
            )
            output_ref[part, :] = pltpu.roll(joined, joined.shape[0] - 1, 0)[:tokens].astype(jnp.bfloat16)
        gain_mine[0] = jnp.concatenate([d_gain, d_gain_rest_ref[0:7, :]], axis=0)

    pairs = (count + 1) // 2
    chunks = neigh_ref.shape[0] // 256
    for step in range(pairs + skew * 4):
        for number in range(4, -1, -1):
            pair = step - skew * number
            if not 0 <= pair < pairs:
                continue
            for index in range(2 * pair, min(2 * pair + 2, count)):
                phase(index, number)
            if pair == pairs - 1:
                if number == 0:
                    input_part()
                gain_phase(number)
        if 1 <= step <= chunks:
            neighbours_part(step - 1)
    for index in range(count):
        core(index).wait_send()
        one(index).wait_send()
        two(index).wait_send()
        gone = got_z[index].at[pl.ds(0, depth - 1)]
        pltpu.make_async_copy(gone, gone, send_sem.at[index, 3]).wait()
    for stage in range(3):
        gain_copy(stage).wait_send()
    gone = gain_z.at[pl.ds(0, depth - 1)]
    pltpu.make_async_copy(gone, gone, gain_send.at[3]).wait()


def last(depth, collective, ff, *args):
    hidden = args[15]
    micro, tokens, width = hidden.shape
    rows = micro * tokens
    total = depth * 8
    slab = width // total
    neigh_rows = args[12].shape[0]
    items = [
        ("down", 0, 0), ("down", 1, 1), ("down", 2, 0), ("down", 3, 1), ("kv", 0, 0), ("kv", 1, 1),
        ("att", 0, 0), ("cq", 0, 1), ("co", 0, 0), ("qkv", 0, 1), ("qkv", 1, 0), ("qkv", 2, 1),
    ]
    count = len(items)
    low, high = jnp.bfloat16, jnp.float32
    out_shape = [
        jax.ShapeDtypeStruct((rows, width), low),
        jax.ShapeDtypeStruct((rows, width), low),
        jax.ShapeDtypeStruct((neigh_rows, width), low),
        jax.ShapeDtypeStruct((slab, 3 * width), high),
        jax.ShapeDtypeStruct((slab, width), high),
        jax.ShapeDtypeStruct((slab, width), high),
        jax.ShapeDtypeStruct((slab, width), high),
        jax.ShapeDtypeStruct((slab, 2 * width), high),
        jax.ShapeDtypeStruct((ff // total, width), high),
        jax.ShapeDtypeStruct((8, width), high),
    ]
    full, core, one, two, along = [], [], [], [], []
    for kind, which, order in items:
        blocks, cols = (2, width // 2) if kind == "qkv" else (1, width)
        full.append(pltpu.VMEM((blocks, depth, 2, 2, 2, slab, cols), low))
        core.append(pltpu.VMEM((blocks, depth, 2, 2, slab, cols), low))
        one.append(pltpu.VMEM((blocks, depth, 2, slab, cols), low))
        two.append(pltpu.VMEM((blocks, depth, slab, cols), low))
        along.append(pltpu.VMEM((depth, blocks, slab, cols), low))
    dma = pltpu.SemaphoreType.DMA
    scratch = full + core + one + two + along + [
        pltpu.VMEM((UNITS, 3, HEAD_DIM, tokens), low),
        pltpu.VMEM((micro, 64, width), high),
        pltpu.VMEM((micro, 64, width), low),
        pltpu.VMEM((3 * width, rows), low),
        pltpu.VMEM((width, rows), low),
        pltpu.VMEM((width, rows), high),
        pltpu.VMEM((width, width), high),
        pltpu.VMEM((4, 8, width), high),
        pltpu.VMEM((3, 8, width), high),
        pltpu.VMEM((depth, 8, width), high),
        dma((count, 4)), dma((count, 4)), dma, dma, dma((2 * micro,)), dma((2 * micro,)), dma((4,)), dma((4,)),
    ]
    return pl.pallas_call(
        functools.partial(last_kernel, depth, items, 2),
        out_shape=out_shape,
        in_specs=[ANY] + [VMEM] * 19,
        out_specs=[VMEM] * 10,
        scratch_shapes=scratch,
        compiler_params=pltpu.CompilerParams(
            collective_id=collective, has_side_effects=True, vmem_limit_bytes=62 * 2**20
        ),
        cost_estimate=pl.CostEstimate(flops=10**10, bytes_accessed=40 * 10**6, transcendentals=0),
    )(*args)


def finish_kernel(copies, *refs):
    for source, result in zip(refs[:copies], refs[copies:]):
        result[...] = source[...].astype(result.dtype)


def finish(arrays, low):
    arrays = [*arrays, low]
    copies = len(arrays)
    vmem = pl.BlockSpec(memory_space=pltpu.VMEM)
    return pl.pallas_call(
        functools.partial(finish_kernel, copies),
        out_shape=[jax.ShapeDtypeStruct(a.shape, a.dtype) for a in arrays[:-1]]
        + [jax.ShapeDtypeStruct(low.shape, jnp.float32)],
        in_specs=[vmem] * copies,
        out_specs=[vmem] * copies,
        compiler_params=pltpu.CompilerParams(vmem_limit_bytes=62 * 2**20),
    )(*arrays)


def layer_norm(values, norm_gain):
    centred = values - jnp.mean(values, axis=-1, keepdims=True)
    spread = jnp.mean(centred * centred, axis=-1, keepdims=True)
    return centred * lax.rsqrt(spread + 1e-05) * norm_gain


def norm_backward(values, norm_gain, grad_out):
    result, pullback = jax.vjp(layer_norm, values, norm_gain)
    return pullback(grad_out)


def outer(left, right):
    return jnp.einsum("td,te->de", left, right, preferred_element_type=jnp.float32)


def turn_heads(values, cosine, sine):
    first_half, second_half = values[:, :32], values[:, 32:]
    return jnp.concatenate(
        [first_half * cosine - second_half * sine, second_half * cosine + first_half * sine], axis=1
    )


def on_device(
    hidden_in,
    segment_ids,
    neighbour_valid,
    neighbours,
    out_grad,
    norm_attn,
    w_qkv,
    w_attn_out,
    norm_cross,
    w_cross_q,
    w_cross_kv,
    w_cross_out,
    norm_mlp,
    w_up,
    w_down,
):
    micro, tok_count, model_width = hidden_in.shape
    blk_count = lax.axis_size("blk")
    depth = blk_count // 4
    total = blk_count * 2
    length = tok_count * total
    row_count = micro * tok_count
    gain_rows = norm_attn.shape[0]
    span_count = tok_count // SPAN
    pair_rows = NEIGHBOURS * NEIGH_LEN
    device = lax.axis_index(AXES)

    in_kernel = gain_rows % 8 == 0
    token_index = device * tok_count + jnp.arange(tok_count, dtype=jnp.int32)
    shifted_index = token_index + LEAD
    used = jnp.where(
        shifted_index[None] < length, jnp.repeat(neighbour_valid, SPAN, axis=1).astype(jnp.float32), 0.0
    ).reshape(row_count, 1)
    neigh_rows = neighbours.reshape(micro * span_count * pair_rows, model_width)
    if in_kernel:
        gain_lanes = jnp.concatenate(
            [jnp.broadcast_to(gain[:, None], (gain_rows, 32)) for gain in (norm_attn, norm_cross, norm_mlp, norm_mlp)],
            axis=1,
        )
        small = jnp.concatenate(
            [
                jnp.pad(gain_lanes, ((0, 32 - gain_rows), (0, 0))),
                jnp.pad(segment_ids.astype(jnp.bfloat16), ((0, 16 - micro), (0, 0))),
            ],
            axis=0,
        )
        (
            got_qkv, got_sq, got_kv, up_full, down_full, d_up, gains, cosine, sine,
            unit_qkv, mixed, totals, first_row, attended_t,
            result_rows, d_first, d_attended_t, normed_cross, d_cross_query, cross_mixed, d_second_low, d_first_low,
            grad_low, activated, d_pairs, d_gain_rest,
        ) = front(
            depth, w_qkv, w_attn_out, w_cross_q, w_cross_out, w_cross_kv, w_up, w_down, small, used, neigh_rows,
            hidden_in, out_grad,
        )
        attended_t = attended_t.reshape(micro, model_width, tok_count)
    else:
        up_full = lax.all_gather(w_up, AXES, axis=0, tiled=True)
        down_full = lax.all_gather(w_down, AXES, axis=0, tiled=True)
        up_full = up_full.reshape(model_width, -1, model_width).transpose(1, 0, 2)
        small = jnp.zeros((16, 128), jnp.bfloat16)
        for row, gain in enumerate((norm_attn, norm_cross, norm_mlp)):
            small = small.at[row, :gain_rows].set(gain)
        small = small.at[3 : 3 + micro, :tok_count].set(segment_ids.astype(jnp.bfloat16))
        got_qkv, got_sq, got_kv, got_small, lead_hid, lead_grad = gather_all(
            depth, w_qkv, w_attn_out, w_cross_q, w_cross_out, w_cross_kv, small, hidden_in, out_grad
        )
        gains = got_small[:, :3, :gain_rows].astype(jnp.float32).transpose(1, 0, 2).reshape(3, model_width)
        gain_attn = gains[0]
        seg_full = got_small[:, 3 : 3 + micro, :tok_count].transpose(1, 0, 2).reshape(micro, length)
        seg_full = seg_full.astype(jnp.int32)
    qkv_blocks = got_qkv.reshape(6, model_width, model_width // 2)
    squares = got_sq.reshape(3, model_width, model_width)
    kv_blocks = got_kv.reshape(2, model_width, model_width)


    unit, holder = unit_of(device, total)
    tile_index = jnp.arange(length // TILE, dtype=jnp.int32)
    if in_kernel:
        tile_first = first_row[0, ::TILE]
    else:
        seg_unit = lax.dynamic_index_in_dim(seg_full, unit // HEADS, 0, keepdims=False)
        seg_tiles = seg_unit.reshape(length // TILE, TILE)
        tile_first = jnp.sum((seg_unit[None] < seg_tiles[:, :1]).astype(jnp.int32), axis=-1)
        inside = jnp.sum((seg_tiles[:, None, :] < seg_tiles[:, :, None]).astype(jnp.int32), axis=-1)
        first_row = jnp.where(
            seg_tiles == seg_tiles[:, :1], tile_first[:, None], tile_index[:, None] * TILE + inside
        ).reshape(1, length)
    low = tile_first // TILE
    high = jnp.sum((low[None] <= tile_index[:, None]).astype(jnp.int32), axis=-1)
    low = jnp.where(holder, low, tile_index + 1)
    high = jnp.where(holder, high, 0)

    if not in_kernel:
        first_of = jnp.sum(
            (seg_full[:, None, :] < segment_ids[:, :, None]).astype(jnp.int32), axis=-1
        )
        local_pos = token_index[None] - first_of
        frequency = jnp.exp(
            jnp.arange(HEAD_DIM // 2, dtype=jnp.float32) * (-2.0 * math.log(10000.0) / HEAD_DIM)
        )
        angles = frequency[:, None, None] * local_pos.astype(jnp.float32)[None]
        cosine, sine = jnp.cos(angles), jnp.sin(angles)

        hidden = hidden_in.astype(jnp.float32)
        normed_attn = layer_norm(hidden, gain_attn).astype(jnp.bfloat16).reshape(row_count, model_width)
        raw = jnp.einsum("bde,td->bet", qkv_blocks, normed_attn, preferred_element_type=jnp.float32)
        raw = raw.reshape(3, HEADS, HEAD_DIM, micro, tok_count)
        rotated = jnp.stack(
            [turn_heads(raw[0], cosine, sine), turn_heads(raw[1], cosine, sine), raw[2]]
        ).astype(jnp.bfloat16)
        message = rotated.transpose(3, 1, 0, 2, 4).reshape(UNITS, 3, HEAD_DIM, tok_count)
        unit_qkv = to_units(total, message, 1)
        shifted, mixed, totals = attn_forward(low, first_row, unit_qkv)
        (attended_t,) = to_tokens(total, shifted[None], (), 2)
    attended_t = attended_t.reshape(micro, model_width, tok_count)

    if not in_kernel:
        (
            result_rows, d_first, d_attended_t, normed_cross, d_cross_query, cross_mixed, d_second_low, d_first_low,
            grad_low, activated, d_pairs, d_gain_rest, d_up,
        ) = middle(
            attended_t, hidden_in, lead_hid, out_grad, lead_grad, gains, used, squares, kv_blocks, neigh_rows,
            up_full, down_full,
        )
    up_low = lax.psum_scatter(d_up, AXES, scatter_dimension=0, tiled=True)
    if not in_kernel:
        down_share = lax.psum_scatter(
            outer(activated, grad_low).astype(jnp.bfloat16), AXES, scatter_dimension=0, tiled=True
        ).astype(jnp.float32)
    unit_grad = to_units(total, d_attended_t.reshape(UNITS, 1, HEAD_DIM, tok_count), 3)
    unit_back = attn_backward(low, high, first_row, unit_qkv, unit_grad[0], mixed, totals)
    if in_kernel:
        (
            output, grad_in, grad_neighbours, s_qkv, s_att, s_cq, s_co, s_kv, s_down, s_gain,
        ) = last(
            depth, 5, w_up.shape[1],
            unit_back, result_rows, d_first, normed_cross, d_cross_query, cross_mixed, d_second_low, d_first_low,
            grad_low, activated, d_pairs, attended_t, neigh_rows, kv_blocks, qkv_blocks, hidden_in, gains,
            cosine, sine, d_gain_rest,
        )
        own_gain = lax.dynamic_slice_in_dim(s_gain, device * gain_rows, gain_rows, 1)
        (
            output, grad_in, grad_neighbours, s_qkv, s_att, s_cq, s_co, s_kv, s_down, up_share,
        ) = finish(
            [
                output, grad_in, grad_neighbours, s_qkv, s_att, s_cq, s_co, s_kv, s_down,
            ],
            up_low,
        )
        return (
            output.reshape(hidden_in.shape), grad_in.reshape(hidden_in.shape),
            grad_neighbours.reshape(neighbours.shape),
            own_gain[0], s_qkv, s_att, own_gain[1], s_cq, s_kv, s_co, own_gain[2], up_share, s_down,
        )
    up_share = up_low.astype(jnp.float32)
    result_rows = result_rows.reshape(micro, tok_count, model_width)
    d_first = d_first.reshape(micro, tok_count, model_width)
    sent_t, tail_first, tail_result = to_tokens(
        total, unit_back, (d_first[:, tok_count - 64 :], result_rows[:, tok_count - 64 :]), 4
    )

    def unshift(rows, tail):
        return jnp.concatenate([tail[:, 1:], rows[:, : tok_count - LEAD]], axis=1)

    output = unshift(result_rows, tail_result)
    d_first_home = unshift(d_first, tail_first)
    sent_t = sent_t.reshape(micro, HEADS, 3, HEAD_DIM, tok_count).transpose(2, 1, 3, 0, 4)
    sent_t = sent_t.astype(jnp.float32)
    raw_t = jnp.stack(
        [turn_heads(sent_t[0], cosine, -sine), turn_heads(sent_t[1], cosine, -sine), sent_t[2]]
    ).astype(jnp.bfloat16).reshape(6, model_width // 2, row_count)
    d_normed_attn = jnp.einsum("bet,bde->td", raw_t, qkv_blocks, preferred_element_type=jnp.float32)
    d_hidden_in, d_gain_attn = norm_backward(
        hidden, gain_attn, d_normed_attn.reshape(micro, tok_count, model_width)
    )
    grad_in = (d_first_home + d_hidden_in).astype(jnp.bfloat16)

    d_keys, d_values = d_pairs[0], d_pairs[1]
    d_first_low = d_first_low.reshape(micro, tok_count, model_width)
    d_neigh = (
        jnp.einsum("te,de->td", d_keys, kv_blocks[0], preferred_element_type=jnp.float32)
        + jnp.einsum("te,de->td", d_values, kv_blocks[1], preferred_element_type=jnp.float32)
    ).astype(jnp.bfloat16)
    grad_neighbours = d_neigh.reshape(neighbours.shape)

    def blocks_of(array):
        return array.astype(jnp.bfloat16).reshape(
            array.shape[0], depth, 2, 2, 2, gain_rows, array.shape[-1]
        )

    d_qkv = jnp.einsum("td,bet->bde", normed_attn, raw_t, preferred_element_type=jnp.float32)
    d_sq = jnp.stack(
        [
            jnp.einsum("mdt,mte->de", attended_t, d_first_low, preferred_element_type=jnp.float32),
            outer(normed_cross, d_cross_query),
            outer(cross_mixed, d_second_low),
        ]
    )
    d_kv = jnp.stack([outer(neigh_rows, d_keys), outer(neigh_rows, d_values)])
    d_gains = jnp.stack([d_gain_attn, d_gain_rest[0], d_gain_rest[1]]).reshape(3, total, gain_rows)
    d_gains = jnp.zeros((total, 8, 128), jnp.float32).at[:, :3, :gain_rows].set(d_gains.transpose(1, 0, 2))
    s_qkv, s_sq, s_kv, s_gain = scatter_all(
        depth, blocks_of(d_qkv), blocks_of(d_sq), blocks_of(d_kv), d_gains, 6
    )
    return (
        output,
        grad_in,
        grad_neighbours,
        s_gain[0, :gain_rows],
        s_qkv.transpose(1, 0, 2).reshape(gain_rows, 3 * model_width),
        s_sq[0],
        s_gain[1, :gain_rows],
        s_sq[1],
        s_kv.transpose(1, 0, 2).reshape(gain_rows, 2 * model_width),
        s_sq[2],
        s_gain[2, :gain_rows],
        up_share,
        down_share,
    )


def solution(mesh):
    placed = (
        P(None, ("blk", "head"), None),
        P(None, ("blk", "head")),
        P(None, ("blk", "head")),
        P(None, ("blk", "head"), None, None, None),
        P(None, ("blk", "head"), None),
        P(("blk", "head")),
        P(("blk", "head"), None),
        P(("blk", "head"), None),
        P(("blk", "head")),
        P(("blk", "head"), None),
        P(("blk", "head"), None),
        P(("blk", "head"), None),
        P(("blk", "head")),
        P(("blk", "head"), None),
        P(("blk", "head"), None),
    )
    return jax.shard_map(
        on_device,
        mesh=mesh,
        in_specs=placed,
        out_specs=(
            P(None, ("blk", "head"), None),
            P(None, ("blk", "head"), None),
            P(None, ("blk", "head"), None, None, None),
            P(("blk", "head")),
            P(("blk", "head"), None),
            P(("blk", "head"), None),
            P(("blk", "head")),
            P(("blk", "head"), None),
            P(("blk", "head"), None),
            P(("blk", "head"), None),
            P(("blk", "head")),
            P(("blk", "head"), None),
            P(("blk", "head"), None),
        ),
        check_vma=False,
    )
```

```python
import functools
import math

import jax
import jax.numpy as jnp
from jax import lax
from jax.experimental import pallas as pl
from jax.experimental.pallas import tpu as pltpu
from jax.sharding import PartitionSpec as P

MESH = pl.DeviceIdType.MESH
ANY = pl.BlockSpec(memory_space=pl.ANY)


def coords():
    blk = lax.axis_index("blk")
    return blk // 4, (blk // 2) % 2, blk % 2, lax.axis_index("head")


def place(z, y, c, x):
    return (z * 4 + y * 2 + c, x)


def loop(count, body):
    if count <= 8:
        for step in range(count):
            body(step)
    else:
        lax.fori_loop(0, count, lambda step, carry: (body(step), carry)[1], 0)


def all_barrier(total, me):
    barrier = pltpu.get_barrier_semaphore()

    def greet(step, carry):
        peer = lax.rem(me + step, total)
        pl.semaphore_signal(
            barrier, inc=1, device_id=(peer // 2, lax.rem(peer, 2)), device_id_type=MESH
        )
        return carry

    lax.fori_loop(1, total, greet, 0)
    pl.semaphore_wait(barrier, total - 1)


def remote(src, dst, send, recv, where):
    return pltpu.make_async_remote_copy(
        src_ref=src, dst_ref=dst, send_sem=send, recv_sem=recv, device_id=where, device_id_type=MESH
    )


def gather_kernel(depth, items, *refs):
    count = len(items)
    w_refs = refs[:5]
    small_ref, hid_ref, grad_ref = refs[5:8]
    out_refs = refs[8:11]
    small_out, lead_hid, lead_grad = refs[11:14]
    own_sem, send_sem, recv_sem, misc_sem, lead_send, lead_recv = refs[14:]
    z, y, c, x = coords()
    total = depth * 8
    me = lax.axis_index("blk") * 2 + lax.axis_index("head")
    rows_per = w_refs[0].shape[0]

    def view(item, zs, ys, cs, xs):
        buffer, first, last, kind = item
        return out_refs[buffer].at[pl.ds(first, last - first), zs, ys, cs, xs]

    all_barrier(total, me)
    own_small = pltpu.make_async_copy(small_ref, small_out.at[me], misc_sem.at[1])
    own_small.start()

    def send_small(step, carry):
        peer = lax.rem(me + step, total)
        remote(
            small_ref, small_out.at[me], misc_sem.at[0], misc_sem.at[1], (peer // 2, lax.rem(peer, 2))
        ).start()
        return carry

    own = []
    for index, item in enumerate(items):
        buffer, first, last, kind = item
        width = out_refs[buffer].shape[-1]
        copies = []
        for block in range(first, last):
            if buffer == 1:
                src = w_refs[1 + block]
            else:
                src = w_refs[2 * buffer].at[:, pl.ds(block * width, width)]
            copies.append((src, out_refs[buffer].at[block, z, y, c, x]))
        for src, dst in copies:
            copy = pltpu.make_async_copy(src, dst, own_sem.at[index])
            copy.start()
        own.append(pltpu.make_async_copy(view(item, z, y, c, x), view(item, z, y, c, x), own_sem.at[index]))
    lax.fori_loop(1, total, send_small, 0)
    prev = lax.rem(me + total - 1, total)
    prev_at = (prev // 2, lax.rem(prev, 2))
    leads = [
        remote(hid_ref.at[:, pl.ds(0, 64)], lead_hid, lead_send.at[0], lead_recv.at[0], prev_at),
        remote(grad_ref.at[:, pl.ds(0, 64)], lead_grad, lead_send.at[1], lead_recv.at[1], prev_at),
    ]

    whole = slice(None)

    def phase_one(index):
        own[index].wait()
        item = items[index]

        def send(step):
            other = lax.rem(z + step + 1, depth)
            remote(
                view(item, z, y, c, x), view(item, z, y, c, x),
                send_sem.at[index, 0], recv_sem.at[index, 0], place(other, y, c, x),
            ).start()

        loop(depth - 1, send)

    def bulk(index, phase):
        item = items[index]
        first_x = item[3] == 0
        if phase == 1:
            ref = view(item, whole, y, c, x)
            where = place(z, y, c, 1 - x) if first_x else place(z, 1 - y, c, x)
        elif phase == 2:
            ref = view(item, whole, y, c, whole) if first_x else view(item, whole, whole, c, x)
            where = place(z, 1 - y, c, x) if first_x else place(z, y, c, 1 - x)
        else:
            ref = view(item, whole, whole, c, whole)
            where = place(z, y, 1 - c, x)
        return remote(ref, ref, send_sem.at[index, phase], recv_sem.at[index, phase], where)

    def arrived(index, phase):
        item = items[index]
        if phase == 0:
            ref = view(item, pl.ds(0, depth - 1), y, c, x)
            pltpu.make_async_copy(ref, ref, recv_sem.at[index, 0]).wait()
        else:
            bulk(index, phase).wait_recv()

    def sent(index, phase):
        item = items[index]
        if phase == 0:
            ref = view(item, pl.ds(0, depth - 1), y, c, x)
            pltpu.make_async_copy(ref, ref, send_sem.at[index, 0]).wait()
        else:
            bulk(index, phase).wait_send()

    pairs = (count + 1) // 2
    for step in range(pairs + 2 * 4):
        for phase in range(4, -1, -1):
            pair = step - 2 * phase
            if not 0 <= pair < pairs:
                continue
            for index in range(2 * pair, min(2 * pair + 2, count)):
                if phase == 0:
                    phase_one(index)
                else:
                    arrived(index, phase - 1)
                    if phase < 4:
                        bulk(index, phase).start()
        if step == 0:
            for lead in leads:
                lead.start()
    for index in range(count):
        for phase in range(4):
            sent(index, phase)
    for lead in leads:
        lead.wait()
    pltpu.make_async_copy(small_out, small_out, misc_sem.at[1]).wait()
    rest = small_out.at[pl.ds(0, total - 1)]
    pltpu.make_async_copy(rest, rest, misc_sem.at[0]).wait()


def gather_all(depth, w_qkv, w_attn_out, w_cross_q, w_cross_out, w_kv, small, hidden, grads):
    total = depth * 8
    rows = w_qkv.shape[0]
    items = [
        (0, 0, 3, 0), (0, 3, 6, 1),
        (2, 0, 1, 0), (2, 1, 2, 1),
        (1, 0, 1, 0), (1, 1, 2, 1),
        (1, 2, 3, 0),
    ]
    shapes = [
        (6, depth, 2, 2, 2, rows, w_qkv.shape[1] // 6),
        (3, depth, 2, 2, 2, rows, w_attn_out.shape[1]),
        (2, depth, 2, 2, 2, rows, w_kv.shape[1] // 2),
    ]
    lead_shape = (hidden.shape[0], 64, hidden.shape[2])
    outs = [jax.ShapeDtypeStruct(shape, jnp.bfloat16) for shape in shapes]
    outs += [jax.ShapeDtypeStruct((total,) + small.shape, small.dtype)]
    outs += [jax.ShapeDtypeStruct(lead_shape, jnp.bfloat16)] * 2
    count = len(items)
    return pl.pallas_call(
        functools.partial(gather_kernel, depth, items),
        out_shape=outs,
        in_specs=[ANY] * 8,
        out_specs=[ANY] * 6,
        scratch_shapes=[
            pltpu.SemaphoreType.DMA((count,)),
            pltpu.SemaphoreType.DMA((count, 4)),
            pltpu.SemaphoreType.DMA((count, 4)),
            pltpu.SemaphoreType.DMA((2,)),
            pltpu.SemaphoreType.DMA((2,)),
            pltpu.SemaphoreType.DMA((2,)),
        ],
        compiler_params=pltpu.CompilerParams(collective_id=0, has_side_effects=True),
    )(w_qkv, w_attn_out, w_cross_q, w_cross_out, w_kv, small, hidden, grads)


def unit_of(device, total):
    if total == 32:
        depth = device // 8
        middle = (depth == 1) | (depth == 2)
        end = 16 + (depth // 3) * 4 + (lax.rem(device, 8) // 4) * 2 + lax.rem(device, 2)
        unit = jnp.where(middle, device - 8, end)
        return unit, middle | (lax.rem(device // 2, 2) == 0)
    stride = total // UNITS
    return jnp.minimum(device // stride, UNITS - 1), (lax.rem(device, stride) == 0) & (device // stride < UNITS)


def to_units_kernel(total, src, dst, send_sem, recv_sem):
    me = lax.axis_index("blk") * 2 + lax.axis_index("head")
    mine, holder = unit_of(me, total)
    all_barrier(total, me)
    lanes = src.shape[-1]

    def slot(device):
        return dst.at[:, :, pl.ds(pl.multiple_of(device * lanes, 128), lanes)]

    @pl.when(holder)
    def _():
        pltpu.make_async_copy(src.at[mine], slot(me), recv_sem).start()

    def send(step, carry):
        peer = lax.rem(me + step, total)
        unit, held = unit_of(peer, total)

        @pl.when(held)
        def _():
            remote(src.at[unit], slot(me), send_sem, recv_sem, (peer // 2, lax.rem(peer, 2))).start()

        return carry

    lax.fori_loop(1, total, send, 0)

    @pl.when(holder)
    def _():
        part = src.at[pl.ds(0, UNITS - 1)]
        pltpu.make_async_copy(dst, dst, recv_sem).wait()
        pltpu.make_async_copy(part, part, send_sem).wait()

    @pl.when(jnp.logical_not(holder))
    def _():
        pltpu.make_async_copy(src, src, send_sem).wait()


def to_units(total, message, collective):
    units, parts, width, lanes = message.shape
    return pl.pallas_call(
        functools.partial(to_units_kernel, total),
        out_shape=jax.ShapeDtypeStruct((parts, width, lanes * total), message.dtype),
        in_specs=[ANY],
        out_specs=ANY,
        scratch_shapes=[pltpu.SemaphoreType.DMA, pltpu.SemaphoreType.DMA],
        compiler_params=pltpu.CompilerParams(collective_id=collective, has_side_effects=True),
    )(message)


def to_tokens_kernel(total, extras, *refs):
    src = refs[0]
    extra_in = refs[1 : 1 + extras]
    dst = refs[1 + extras]
    extra_out = refs[2 + extras : 2 + 2 * extras]
    send_sem, recv_sem, extra_send, extra_recv = refs[2 + 2 * extras :]
    me = lax.axis_index("blk") * 2 + lax.axis_index("head")
    mine, holder = unit_of(me, total)
    all_barrier(total, me)
    lanes = dst.shape[-1]
    after = lax.rem(me + 1, total)
    moves = [
        remote(
            extra_in[index], extra_out[index], extra_send.at[index], extra_recv.at[index],
            (after // 2, lax.rem(after, 2)),
        )
        for index in range(extras)
    ]
    for move in moves:
        move.start()

    def slot(device):
        return src.at[:, :, pl.ds(pl.multiple_of(device * lanes, 128), lanes)]

    @pl.when(holder)
    def _():
        pltpu.make_async_copy(slot(me), dst.at[mine], recv_sem).start()

        def send(step, carry):
            peer = lax.rem(me + step, total)
            remote(
                slot(peer), dst.at[mine], send_sem, recv_sem, (peer // 2, lax.rem(peer, 2))
            ).start()
            return carry

        lax.fori_loop(1, total, send, 0)

    pltpu.make_async_copy(dst, dst, recv_sem).wait()

    @pl.when(holder)
    def _():
        part = src.at[:, :, pl.ds(0, lanes * (total - 1))]
        pltpu.make_async_copy(part, part, send_sem).wait()

    for move in moves:
        move.wait()


def to_tokens(total, units, extra, collective):
    parts, width, length = units.shape
    count = len(extra)
    result = jax.ShapeDtypeStruct((UNITS, parts, width, length // total), units.dtype)
    return pl.pallas_call(
        functools.partial(to_tokens_kernel, total, count),
        out_shape=[result] + [jax.ShapeDtypeStruct(e.shape, e.dtype) for e in extra],
        in_specs=[ANY] * (1 + count),
        out_specs=[ANY] * (1 + count),
        scratch_shapes=[
            pltpu.SemaphoreType.DMA,
            pltpu.SemaphoreType.DMA,
            pltpu.SemaphoreType.DMA((max(count, 1),)),
            pltpu.SemaphoreType.DMA((max(count, 1),)),
        ],
        compiler_params=pltpu.CompilerParams(collective_id=collective, has_side_effects=True),
    )(units, *extra)


def scatter_kernel(depth, items, *refs):
    count = len(items)
    total = depth * 8
    d_refs = refs[:3]
    gain_ref = refs[3]
    out_refs = refs[4:7]
    gain_out = refs[7]
    own = refs[8 : 8 + count]
    got_core = refs[8 + count : 8 + 2 * count]
    got_one = refs[8 + 2 * count : 8 + 3 * count]
    got_two = refs[8 + 3 * count : 8 + 4 * count]
    got_z = refs[8 + 4 * count : 8 + 5 * count]
    gains, local_sem, send_sem, recv_sem, gain_sem = refs[8 + 5 * count :]
    z, y, c, x = coords()
    me = lax.axis_index("blk") * 2 + lax.axis_index("head")
    all_barrier(total, me)
    whole = slice(None)

    pltpu.make_async_copy(gain_ref.at[me], gains.at[me], gain_sem.at[1]).start()

    def send_gain(step, carry):
        peer = lax.rem(me + step, total)
        remote(
            gain_ref.at[peer], gains.at[me], gain_sem.at[0], gain_sem.at[1], (peer // 2, lax.rem(peer, 2))
        ).start()
        return carry

    def local(index):
        buffer, first, last, kind = items[index]
        src = d_refs[buffer].at[pl.ds(first, last - first), whole, whole, c]
        return pltpu.make_async_copy(src, own[index], local_sem.at[index])

    def core(index):
        buffer, first, last, kind = items[index]
        src = d_refs[buffer].at[pl.ds(first, last - first), whole, whole, 1 - c]
        return remote(
            src, got_core[index], send_sem.at[index, 0], recv_sem.at[index, 0], place(z, y, 1 - c, x)
        )

    def one(index):
        if items[index][3] == 0:
            src, where = own[index].at[whole, whole, 1 - y], place(z, 1 - y, c, x)
        else:
            src, where = own[index].at[whole, whole, whole, 1 - x], place(z, y, c, 1 - x)
        return remote(src, got_one[index], send_sem.at[index, 1], recv_sem.at[index, 1], where)

    def two(index):
        if items[index][3] == 0:
            src, where = own[index].at[whole, whole, y, 1 - x], place(z, y, c, 1 - x)
        else:
            src, where = own[index].at[whole, whole, 1 - y, x], place(z, 1 - y, c, x)
        return remote(src, got_two[index], send_sem.at[index, 2], recv_sem.at[index, 2], where)

    def send_z(index):
        def send(step):
            other = lax.rem(z + step + 1, depth)
            remote(
                own[index].at[whole, other, y, x], got_z[index].at[z],
                send_sem.at[index, 3], recv_sem.at[index, 3], place(other, y, c, x),
            ).start()

        loop(depth - 1, send)

    def add_into(target, source):
        target[...] = (target[...].astype(jnp.float32) + source[...].astype(jnp.float32)).astype(
            jnp.bfloat16
        )

    def sum_core(index):
        blocks = own[index].shape[0]

        def body(step):
            block, level = step // depth, lax.rem(step, depth)
            for row in range(2):
                for col in range(2):
                    add_into(own[index].at[block, level, row, col], got_core[index].at[block, level, row, col])

        lax.fori_loop(0, blocks * depth, lambda step, carry: (body(step), carry)[1], 0)

    def sum_one(index):
        blocks = own[index].shape[0]

        def body(step):
            block, level = step // depth, lax.rem(step, depth)
            for side in range(2):
                if items[index][3] == 0:
                    target = own[index].at[block, level, y, side]
                else:
                    target = own[index].at[block, level, side, x]
                add_into(target, got_one[index].at[block, level, side])

        lax.fori_loop(0, blocks * depth, lambda step, carry: (body(step), carry)[1], 0)

    def sum_two(index):
        blocks = own[index].shape[0]

        def body(step):
            block, level = step // depth, lax.rem(step, depth)
            add_into(own[index].at[block, level, y, x], got_two[index].at[block, level])

        lax.fori_loop(0, blocks * depth, lambda step, carry: (body(step), carry)[1], 0)

    def sum_z(index):
        buffer, first, last, kind = items[index]
        for block in range(last - first):
            running = own[index][block, z, y, x].astype(jnp.float32)

            def body(step, value):
                other = lax.rem(z + step, depth)
                return value + got_z[index][other, block].astype(jnp.float32)

            out_refs[buffer][first + block] = lax.fori_loop(1, depth, body, running)

    for index in range(count):
        local(index).start()
    pairs = (count + 1) // 2
    for step in range(pairs + 4):
        for phase in range(4, -1, -1):
            pair = step - phase
            if not 0 <= pair < pairs:
                continue
            for index in range(2 * pair, min(2 * pair + 2, count)):
                if phase == 0:
                    core(index).start()
                elif phase == 1:
                    local(index).wait()
                    core(index).wait_recv()
                    sum_core(index)
                    one(index).start()
                elif phase == 2:
                    one(index).wait_recv()
                    sum_one(index)
                    two(index).start()
                elif phase == 3:
                    two(index).wait_recv()
                    sum_two(index)
                    send_z(index)
                else:
                    landed = got_z[index].at[pl.ds(0, depth - 1)]
                    pltpu.make_async_copy(landed, landed, recv_sem.at[index, 3]).wait()
                    sum_z(index)
        if step == 0:
            lax.fori_loop(1, total, send_gain, 0)
    pltpu.make_async_copy(gains, gains, gain_sem.at[1]).wait()
    gain_out[...] = jnp.sum(gains[...], axis=0)
    for index in range(count):
        core(index).wait_send()
        one(index).wait_send()
        two(index).wait_send()
        gone = got_z[index].at[pl.ds(0, depth - 1)]
        pltpu.make_async_copy(gone, gone, send_sem.at[index, 3]).wait()
    rest = gains.at[pl.ds(0, total - 1)]
    pltpu.make_async_copy(rest, rest, gain_sem.at[0]).wait()


def scatter_all(depth, d_qkv, d_squares, d_kv, d_gains, collective):
    items = [
        (0, 0, 3, 0), (0, 3, 6, 1),
        (2, 0, 1, 0), (2, 1, 2, 1),
        (1, 0, 1, 0), (1, 1, 2, 1),
        (1, 2, 3, 0),
    ]
    count = len(items)
    parts = (d_qkv, d_squares, d_kv)
    own, core, one, two, along = [], [], [], [], []
    for buffer, first, last, kind in items:
        rows, width = parts[buffer].shape[-2:]
        blocks = last - first
        own.append(pltpu.VMEM((blocks, depth, 2, 2, rows, width), jnp.bfloat16))
        core.append(pltpu.VMEM((blocks, depth, 2, 2, rows, width), jnp.bfloat16))
        one.append(pltpu.VMEM((blocks, depth, 2, rows, width), jnp.bfloat16))
        two.append(pltpu.VMEM((blocks, depth, rows, width), jnp.bfloat16))
        along.append(pltpu.VMEM((depth, blocks, rows, width), jnp.bfloat16))
    outs = [jax.ShapeDtypeStruct((p.shape[0],) + p.shape[-2:], jnp.float32) for p in parts]
    outs.append(jax.ShapeDtypeStruct(d_gains.shape[1:], jnp.float32))
    vmem = pl.BlockSpec(memory_space=pltpu.VMEM)
    return pl.pallas_call(
        functools.partial(scatter_kernel, depth, items),
        out_shape=outs,
        in_specs=[ANY] * 4,
        out_specs=[vmem] * 4,
        scratch_shapes=own + core + one + two + along + [
            pltpu.VMEM(d_gains.shape, jnp.float32),
            pltpu.SemaphoreType.DMA((count,)),
            pltpu.SemaphoreType.DMA((count, 4)),
            pltpu.SemaphoreType.DMA((count, 4)),
            pltpu.SemaphoreType.DMA((2,)),
        ],
        compiler_params=pltpu.CompilerParams(
            collective_id=collective, has_side_effects=True, vmem_limit_bytes=60 * 2**20
        ),
    )(d_qkv, d_squares, d_kv, d_gains)


HEADS = 12
HEAD_DIM = 64
SPAN = 64
NEIGHBOURS = 2
NEIGH_LEN = 128
MICRO = 2
UNITS = MICRO * HEADS
AXES = ("blk", "head")
TILE = 512
LEAD = SPAN - 1
DOC_MAX = 2000
SCORE_SCALE = 1.0 / math.sqrt(HEAD_DIM)
LOG2E = math.log2(math.e)


def tile_at(ref, index, row):
    return ref[row, :, pl.ds(pl.multiple_of(index * TILE, TILE), TILE)]


def row_at(ref, index):
    return ref[:, pl.ds(pl.multiple_of(index * TILE, TILE), TILE)]


def tile_mask(key_tile, query_tile, first_row, diagonal=True):
    key_place = key_tile * TILE + lax.broadcasted_iota(jnp.int32, (TILE, 1), 0)
    allowed = key_place >= first_row
    if diagonal:
        query_place = query_tile * TILE + lax.broadcasted_iota(jnp.int32, (1, TILE), 1)
        allowed = allowed & (key_place <= query_place)
    return allowed


def attn_forward_kernel(low_ref, first_ref, qkv_ref, shifted_ref, mixed_ref, total_ref):
    tiles = qkv_ref.shape[-1] // TILE

    def one_query(query_tile, carry):
        query_t = tile_at(qkv_ref, query_tile, 0)
        first_row = row_at(first_ref, query_tile)

        def one_key(step, state):
            peak, weight, mixed = state
            key_tile = query_tile - step
            keys = tile_at(qkv_ref, key_tile, 1).T
            scores = jnp.dot(keys, query_t, preferred_element_type=jnp.float32) * (SCORE_SCALE * LOG2E)
            scores = jnp.where(tile_mask(key_tile, query_tile, first_row), scores, -1e30)
            new_peak = jnp.maximum(peak, jnp.max(scores, axis=0, keepdims=True))
            probs = jnp.exp2(scores - new_peak)
            fade = jnp.exp2(peak - new_peak)
            weight = weight * fade + jnp.sum(probs, axis=0, keepdims=True)
            mixed = mixed * fade + jnp.dot(
                tile_at(qkv_ref, key_tile, 2), probs.astype(jnp.bfloat16), preferred_element_type=jnp.float32
            )
            return new_peak, weight, mixed

        start = (
            jnp.full((1, TILE), -1e30, jnp.float32),
            jnp.zeros((1, TILE), jnp.float32),
            jnp.zeros((HEAD_DIM, TILE), jnp.float32),
        )
        steps = query_tile + 1 - low_ref[query_tile]
        peak, weight, mixed = lax.fori_loop(0, steps, one_key, start)
        columns = pl.ds(pl.multiple_of(query_tile * TILE, TILE), TILE)
        mixed_ref[:, columns] = mixed / weight
        total_ref[:, columns] = peak + jnp.log2(weight)
        return carry

    lax.fori_loop(0, tiles, one_query, 0)
    length = qkv_ref.shape[-1]

    def turn(step, carry):
        rows = pl.ds(pl.multiple_of(step * 16, 16), 16)
        shifted_ref[rows, :] = pltpu.roll(mixed_ref[rows, :], length - LEAD, 1).astype(jnp.bfloat16)
        return carry

    lax.fori_loop(0, HEAD_DIM // 16, turn, 0)


def attn_backward_kernel(
    low_ref, high_ref, first_ref, qkv_ref, shifted_ref, mixed_ref, total_ref, out_ref, grad_ref, dq_ref, delta_ref
):
    length = qkv_ref.shape[-1]
    tiles = length // TILE
    delta_ref[...] = jnp.zeros_like(delta_ref)

    def turn(step, carry):
        rows = pl.ds(pl.multiple_of(step * 16, 16), 16)
        grad = pltpu.roll(shifted_ref[rows, :].astype(jnp.float32), LEAD, 1)
        grad_ref[rows, :] = grad.astype(jnp.bfloat16)
        delta_ref[...] += jnp.sum(grad * mixed_ref[rows, :], axis=0, keepdims=True)
        dq_ref[rows, :] = jnp.zeros((16, length), jnp.float32)
        return carry

    lax.fori_loop(0, HEAD_DIM // 16, turn, 0)

    def one_key(key_tile, carry):
        key_t = tile_at(qkv_ref, key_tile, 1)
        keys = key_t.T
        values = tile_at(qkv_ref, key_tile, 2).T

        def one_query(query_tile, state, diagonal=False):
            d_key, d_value = state
            query_t = tile_at(qkv_ref, query_tile, 0)
            grad_t = row_at(grad_ref, query_tile)
            scores = jnp.dot(keys, query_t, preferred_element_type=jnp.float32) * (SCORE_SCALE * LOG2E)
            allowed = tile_mask(key_tile, query_tile, row_at(first_ref, query_tile), diagonal)
            probs = jnp.where(allowed, jnp.exp2(scores - row_at(total_ref, query_tile)), 0.0)
            d_probs = jnp.dot(values, grad_t, preferred_element_type=jnp.float32)
            d_scores = (probs * (d_probs - row_at(delta_ref, query_tile))).astype(jnp.bfloat16)
            d_value = d_value + jnp.dot(
                probs.astype(jnp.bfloat16), grad_t.T, preferred_element_type=jnp.float32
            )
            d_key = d_key + jnp.dot(d_scores, query_t.T, preferred_element_type=jnp.float32)
            columns = pl.ds(pl.multiple_of(query_tile * TILE, TILE), TILE)
            dq_ref[:, columns] += jnp.dot(key_t, d_scores, preferred_element_type=jnp.float32)
            return d_key, d_value

        zeros = jnp.zeros((TILE, HEAD_DIM), jnp.float32)
        @pl.when(high_ref[key_tile] > key_tile)
        def _():
            state = one_query(key_tile, (zeros, zeros), diagonal=True)
            d_key, d_value = lax.fori_loop(key_tile + 1, high_ref[key_tile], one_query, state)
            columns = pl.ds(pl.multiple_of(key_tile * TILE, TILE), TILE)
            out_ref[1, :, columns] = (d_key * SCORE_SCALE).T.astype(jnp.bfloat16)
            out_ref[2, :, columns] = d_value.T.astype(jnp.bfloat16)

        return carry

    lax.fori_loop(0, tiles, one_key, 0)

    def finish(step, carry):
        rows = pl.ds(pl.multiple_of(step * 16, 16), 16)
        out_ref[0, rows, :] = (dq_ref[rows, :] * SCORE_SCALE).astype(jnp.bfloat16)
        return carry

    lax.fori_loop(0, HEAD_DIM // 16, finish, 0)


SMEM = pl.BlockSpec(memory_space=pltpu.SMEM)
VMEM = pl.BlockSpec(memory_space=pltpu.VMEM)


def local_params():
    return pltpu.CompilerParams(vmem_limit_bytes=60 * 2**20)


def attn_forward(low, first, qkv):
    width, length = qkv.shape[1:]
    return pl.pallas_call(
        attn_forward_kernel,
        out_shape=[
            jax.ShapeDtypeStruct((width, length), jnp.bfloat16),
            jax.ShapeDtypeStruct((width, length), jnp.float32),
            jax.ShapeDtypeStruct((1, length), jnp.float32),
        ],
        in_specs=[SMEM, VMEM, VMEM],
        out_specs=[VMEM] * 3,
        compiler_params=local_params(),
        cost_estimate=pl.CostEstimate(flops=10**9, bytes_accessed=4 * 10**6, transcendentals=4 * 10**6),
    )(low, first, qkv)


def attn_backward(low, high, first, qkv, shifted, mixed, totals):
    width, length = qkv.shape[1:]
    return pl.pallas_call(
        attn_backward_kernel,
        out_shape=jax.ShapeDtypeStruct((3, width, length), jnp.bfloat16),
        in_specs=[SMEM, SMEM] + [VMEM] * 5,
        out_specs=VMEM,
        scratch_shapes=[
            pltpu.VMEM((width, length), jnp.bfloat16),
            pltpu.VMEM((width, length), jnp.float32),
            pltpu.VMEM((1, length), jnp.float32),
        ],
        compiler_params=local_params(),
        cost_estimate=pl.CostEstimate(flops=3 * 10**9, bytes_accessed=4 * 10**6, transcendentals=4 * 10**6),
    )(low, high, first, qkv, shifted, mixed, totals)


def dot_nn(left, right):
    return jnp.dot(left, right, preferred_element_type=jnp.float32)


def dot_nt(left, right):
    return lax.dot_general(left, right, (((1,), (1,)), ((), ())), preferred_element_type=jnp.float32)


def dot_tn(left, right):
    return lax.dot_general(left, right, (((0,), (0,)), ((), ())), preferred_element_type=jnp.float32)


def norm_parts(values):
    centred = values - jnp.mean(values, axis=-1, keepdims=True)
    scale = lax.rsqrt(jnp.mean(centred * centred, axis=-1, keepdims=True) + 1e-05)
    return centred * scale, scale


def norm_pull(values, gain, grad):
    unit, scale = norm_parts(values)
    scaled = grad * gain
    pulled = scale * (
        scaled
        - jnp.mean(scaled, axis=-1, keepdims=True)
        - unit * jnp.mean(scaled * unit, axis=-1, keepdims=True)
    )
    return pulled, jnp.sum(grad * unit, axis=0, keepdims=True)


def shift_rows(rows, lead):
    joined = jnp.concatenate([rows.astype(jnp.float32), lead.astype(jnp.float32)], axis=0)
    return pltpu.roll(joined, joined.shape[0] - LEAD, 0)[: rows.shape[0]]


def stack_pair(rows):
    lane = lax.broadcasted_iota(jnp.int32, rows.shape, 1)
    zero = jnp.zeros_like(rows)
    return jnp.concatenate(
        [jnp.where(lane < HEAD_DIM, rows, zero), jnp.where(lane < HEAD_DIM, zero, rows)], axis=0
    )


def unstack_pair(rows):
    lane = lax.broadcasted_iota(jnp.int32, (SPAN, 2 * HEAD_DIM), 1)
    return jnp.where(lane < HEAD_DIM, rows[:SPAN], rows[SPAN:])


def middle_kernel(
    att_ref, hid_ref, lead_hid_ref, grad_ref, lead_grad_ref, gain_ref, used_ref, sq_ref, kv_hbm, neigh_hbm,
    up_hbm, down_hbm,
    result_ref, first_ref, d_att_ref, n2_ref, d_cq_ref, cm_ref, gc_ref, ga_ref, gy_ref, act_ref, d_pair_ref,
    d_gain_ref, d_up_hbm,
    kv_ref, neigh_ref, up_ref, down_ref, att_rows, second_ref, cq_ref, pair_ref, prob_ref, acc_ref, d_n3_ref,
    n3_ref, n3t_ref, d_up_ref, sems,
):
    micro, tokens, width = hid_ref.shape
    rows = micro * tokens
    pulls = [
        pltpu.make_async_copy(src, dst, sems.at[index])
        for index, (src, dst) in enumerate(
            [(kv_hbm, kv_ref), (neigh_hbm, neigh_ref), (up_hbm, up_ref), (down_hbm, down_ref)]
        )
    ]
    for pull in pulls:
        pull.start()
    gain_cross, gain_mlp = gain_ref[1:2, :], gain_ref[2:3, :]
    for index in range(micro):
        part = pl.ds(index * tokens, tokens)
        hidden = shift_rows(hid_ref[index], lead_hid_ref[index])
        gy_ref[part, :] = shift_rows(grad_ref[index], lead_grad_ref[index]).astype(jnp.bfloat16)
        first_ref[part, :] = hidden + dot_tn(att_ref[index], sq_ref[0])
    n2_ref[...] = (norm_parts(first_ref[...])[0] * gain_cross).astype(jnp.bfloat16)
    cq_ref[...] = dot_nn(n2_ref[...], sq_ref[1]).astype(jnp.bfloat16)

    pulls[0].wait()
    pulls[1].wait()
    chunk = 256
    chunks = neigh_ref.shape[0] // chunk

    def make_pairs(step, carry):
        side, block = step // chunks, lax.rem(step, chunks)
        part = pl.ds(pl.multiple_of(block * chunk, chunk), chunk)
        pair_ref[side, part, :] = dot_nn(neigh_ref[part, :], kv_ref[side]).astype(jnp.bfloat16)
        return carry

    lax.fori_loop(0, 2 * chunks, make_pairs, 0)
    couples = HEADS // 2
    pair_rows = NEIGHBOURS * NEIGH_LEN
    groups = rows // SPAN

    def where(step):
        group, couple = step // couples, lax.rem(step, couples)
        tok = pl.ds(pl.multiple_of(group * SPAN, SPAN), SPAN)
        key = pl.ds(pl.multiple_of(group * pair_rows, pair_rows), pair_rows)
        lanes = pl.ds(pl.multiple_of(couple * 2 * HEAD_DIM, 2 * HEAD_DIM), 2 * HEAD_DIM)
        return tok, key, lanes

    def cross_step(step, carry):
        tok, key, lanes = where(step)
        query = stack_pair(cq_ref[tok, lanes])
        scores = dot_nt(query, pair_ref[0, key, lanes]) * SCORE_SCALE
        weights = jnp.exp(scores - jnp.max(scores, axis=-1, keepdims=True))
        probs = weights / jnp.sum(weights, axis=-1, keepdims=True)
        prob_ref[step] = probs
        mixed = unstack_pair(dot_nn(probs.astype(jnp.bfloat16), pair_ref[1, key, lanes]))
        cm_ref[tok, lanes] = (mixed * used_ref[tok, :]).astype(jnp.bfloat16)
        return carry

    lax.fori_loop(0, groups * couples, cross_step, 0)
    second_ref[...] = first_ref[...] + dot_nn(cm_ref[...], sq_ref[2])
    n3 = (norm_parts(second_ref[...])[0] * gain_mlp).astype(jnp.bfloat16)
    n3_ref[...] = n3
    n3t_ref[...] = n3.T
    acc_ref[...] = second_ref[...]
    d_n3_ref[...] = jnp.zeros_like(d_n3_ref)
    pulls[2].wait()
    pulls[3].wait()
    ff_blocks = up_ref.shape[0]

    def mlp_step(step, carry):
        cols = pl.ds(pl.multiple_of(step * width, width), width)
        upper = dot_nn(n3_ref[...], up_ref[step])
        square = upper * upper
        flat = jnp.tanh(math.sqrt(2.0 / math.pi) * upper * (1.0 + 0.044715 * square))
        half = 0.5 * (1.0 + flat)
        active = (upper * half).astype(jnp.bfloat16)
        act_ref[:, cols] = active
        slope = half + 0.5 * upper * (1.0 - flat * flat) * math.sqrt(2.0 / math.pi) * (
            1.0 + 3.0 * 0.044715 * square
        )
        d_upper = (dot_nt(gy_ref[...], down_ref[cols, :]) * slope).astype(jnp.bfloat16)
        acc_ref[...] += dot_nn(active, down_ref[cols, :])
        d_n3_ref[...] += dot_nt(d_upper, up_ref[step])
        d_up_ref[:, cols] = dot_nn(n3t_ref[...], d_upper).astype(jnp.bfloat16)
        pltpu.make_async_copy(d_up_ref.at[:, cols], d_up_hbm.at[:, cols], sems.at[4]).start()
        return carry

    lax.fori_loop(0, ff_blocks, mlp_step, 0)
    result_ref[...] = acc_ref[...].astype(jnp.bfloat16)
    pulled, d_gain_mlp = norm_pull(second_ref[...], gain_mlp, d_n3_ref[...])
    d_second = gy_ref[...].astype(jnp.float32) + pulled
    acc_ref[...] = d_second
    gc_ref[...] = d_second.astype(jnp.bfloat16)
    att_rows[...] = (
        dot_nt(gc_ref[...], sq_ref[2]).astype(jnp.bfloat16).astype(jnp.float32) * used_ref[...]
    ).astype(jnp.bfloat16)

    def cross_back(step, carry):
        tok, key, lanes = where(step)
        grad = stack_pair(att_rows[tok, lanes])
        query = stack_pair(cq_ref[tok, lanes])
        probs = prob_ref[step]
        d_probs = dot_nt(grad, pair_ref[1, key, lanes])
        d_scores = (
            probs * (d_probs - jnp.sum(probs * d_probs, axis=-1, keepdims=True))
        ).astype(jnp.bfloat16)
        d_query = unstack_pair(dot_nn(d_scores, pair_ref[0, key, lanes]))
        d_cq_ref[tok, lanes] = (d_query * SCORE_SCALE).astype(jnp.bfloat16)
        d_pair_ref[0, key, lanes] = (dot_tn(d_scores, query) * SCORE_SCALE).astype(jnp.bfloat16)
        d_pair_ref[1, key, lanes] = dot_tn(probs.astype(jnp.bfloat16), grad).astype(jnp.bfloat16)
        return carry

    lax.fori_loop(0, groups * couples, cross_back, 0)
    pulled, d_gain_cross = norm_pull(first_ref[...], gain_cross, dot_nt(d_cq_ref[...], sq_ref[1]))
    d_first = acc_ref[...] + pulled
    first_ref[...] = d_first
    ga_ref[...] = d_first.astype(jnp.bfloat16)
    for index in range(micro):
        d_att_ref[index] = dot_nt(sq_ref[0], ga_ref[pl.ds(index * tokens, tokens), :]).astype(jnp.bfloat16)
    d_gain_ref[...] = jnp.concatenate([d_gain_cross, d_gain_mlp, jnp.zeros((6, width), jnp.float32)], axis=0)
    pltpu.make_async_copy(d_up_ref, d_up_hbm, sems.at[4]).wait()


def middle(attended_t, hidden, lead_hid, grads, lead_grad, gains, used, squares, kv, neigh, up, down):
    micro, tokens, width = hidden.shape
    rows = micro * tokens
    ff = up.shape[0] * width
    low = jnp.bfloat16
    out_shape = [
        jax.ShapeDtypeStruct((rows, width), low),
        jax.ShapeDtypeStruct((rows, width), jnp.float32),
        jax.ShapeDtypeStruct((micro, width, tokens), low),
        jax.ShapeDtypeStruct((rows, width), low),
        jax.ShapeDtypeStruct((rows, width), low),
        jax.ShapeDtypeStruct((rows, width), low),
        jax.ShapeDtypeStruct((rows, width), low),
        jax.ShapeDtypeStruct((rows, width), low),
        jax.ShapeDtypeStruct((rows, width), low),
        jax.ShapeDtypeStruct((rows, ff), low),
        jax.ShapeDtypeStruct((2,) + neigh.shape, low),
        jax.ShapeDtypeStruct((8, width), jnp.float32),
        jax.ShapeDtypeStruct((width, ff), low),
    ]
    steps = rows // SPAN * HEADS // 2
    scratch = [
        pltpu.VMEM(kv.shape, low),
        pltpu.VMEM(neigh.shape, low),
        pltpu.VMEM(up.shape, low),
        pltpu.VMEM(down.shape, low),
        pltpu.VMEM((rows, width), low),
        pltpu.VMEM((rows, width), jnp.float32),
        pltpu.VMEM((rows, width), low),
        pltpu.VMEM((2,) + neigh.shape, low),
        pltpu.VMEM((steps, 2 * SPAN, NEIGHBOURS * NEIGH_LEN), jnp.float32),
        pltpu.VMEM((rows, width), jnp.float32),
        pltpu.VMEM((rows, width), jnp.float32),
        pltpu.VMEM((rows, width), low),
        pltpu.VMEM((width, rows), low),
        pltpu.VMEM((width, ff), low),
        pltpu.SemaphoreType.DMA((5,)),
    ]
    return pl.pallas_call(
        middle_kernel,
        out_shape=out_shape,
        in_specs=[VMEM] * 8 + [ANY] * 4,
        out_specs=[VMEM] * 12 + [ANY],
        scratch_shapes=scratch,
        compiler_params=local_params(),
        cost_estimate=pl.CostEstimate(flops=12 * 10**9, bytes_accessed=40 * 10**6, transcendentals=10**6),
    )(attended_t, hidden, lead_hid, grads, lead_grad, gains, used, squares, kv, neigh, up, down)


PLAN = (0, 0, 1, 0, 0, 1, 0, 0, 1, 1, 1, 0)


def front_kernel(depth, items, *refs):
    count = len(items)
    w_refs = refs[:7]
    small_ref, used_ref, neigh_ref, hid_ref, grad_hbm = refs[7:12]
    (
        qkv_out, sq_out, kv_out, up_out, down_out, d_up_hbm, unit_hbm, mixed_hbm, act_hbm, d_pair_hbm,
        gain_out, cos_out, sin_out, total_out, start_out, att_out,
        result_ref, first_ref, back_out, n2_ref, d_cq_ref, cm_ref, gc_ref, ga_ref, gy_ref, d_gain_ref,
    ) = refs[12:38]
    (
        qkv_ref, small_all, hid_vmem, grad_ref, lead_hid, lead_grad, n1_ref, temp_ref, note_ref, turned_ref, doc_ref,
        stage_ref, sq_ref, kv_ref, up_ref, down_ref,
        att_rows, second_ref, cq_ref, pair_ref, prob_ref, acc_ref, d_n3_ref, n3_ref, n3t_ref, d_up_ref,
        own_sem, send_sem, recv_sem, misc_sem, lead_send, lead_recv, load_sem, unit_send, unit_recv,
        att_send, att_recv, stage_sem, up_sem, grad_send, grad_recv, store_sem,
        unit_out, mixed_out, act_ref, d_pair_ref, d_att_ref, d_upper_ref,
    ) = refs[38:]
    z, y, c, x = coords()
    total = depth * 8
    me = lax.axis_index("blk") * 2 + lax.axis_index("head")
    mine, holder = unit_of(me, total)
    slab = w_refs[0].shape[0]
    micro, tokens, width = hid_ref.shape
    homes = (qkv_ref, sq_out, kv_out, up_out, down_out)
    whole = slice(None)

    def view(item, zs, ys, cs, xs):
        buffer, first, last, kind = item
        if buffer == 4:
            return down_out.at[zs, ys, cs, xs, pl.ds(first, last - first)]
        return homes[buffer].at[pl.ds(first, last - first), zs, ys, cs, xs]

    load = pltpu.make_async_copy(hid_ref, hid_vmem, load_sem.at[0])
    load.start()
    load_grad = pltpu.make_async_copy(grad_hbm, grad_ref, load_sem.at[2])
    load_grad.start()
    own = []
    for index, item in enumerate(items):
        buffer, first, last, kind = item
        cols = homes[buffer].shape[-1]
        if buffer == 4:
            moves = [(w_refs[6].at[pl.ds(first, last - first)], view(item, z, y, c, x))]
        elif buffer == 1:
            moves = [(w_refs[1 + block], sq_out.at[block, z, y, c, x]) for block in range(first, last)]
        else:
            source = w_refs[(0, None, 4, 5)[buffer]]
            moves = [
                (source.at[:, pl.ds(block * cols, cols)], homes[buffer].at[block, z, y, c, x])
                for block in range(first, last)
            ]
        for src, dst in moves:
            pltpu.make_async_copy(src, dst, own_sem.at[index]).start()
        mirror = view(item, z, y, c, x)
        own.append(pltpu.make_async_copy(mirror, mirror, own_sem.at[index]))
    pltpu.make_async_copy(small_ref, small_all.at[me], misc_sem.at[1]).start()
    all_barrier(total, me)

    def send_small(step, carry):
        peer = lax.rem(me + step, total)
        remote(
            small_ref, small_all.at[me], misc_sem.at[0], misc_sem.at[1], (peer // 2, lax.rem(peer, 2))
        ).start()
        return carry

    prev = lax.rem(me + total - 1, total)
    prev_at = (prev // 2, lax.rem(prev, 2))
    leads = [
        remote(hid_ref.at[:, pl.ds(0, 64)], lead_hid, lead_send.at[0], lead_recv.at[0], prev_at),
        remote(grad_hbm.at[:, pl.ds(0, 64)], lead_grad, lead_send.at[1], lead_recv.at[1], prev_at),
    ]

    def start(index):
        own[index].wait()
        item = items[index]
        for step in range(1, depth):
            other = lax.rem(z + step, depth)
            remote(
                view(item, z, y, c, x), view(item, z, y, c, x),
                send_sem.at[index, 0], recv_sem.at[index, 0], place(other, y, c, x),
            ).start()

    def bulk(index, phase):
        item = items[index]
        first_x = item[3] == 0
        if phase == 1:
            ref = view(item, whole, y, c, x)
            where = place(z, y, c, 1 - x) if first_x else place(z, 1 - y, c, x)
        elif phase == 2:
            ref = view(item, whole, y, c, whole) if first_x else view(item, whole, whole, c, x)
            where = place(z, 1 - y, c, x) if first_x else place(z, y, c, 1 - x)
        else:
            ref = view(item, whole, whole, c, whole)
            where = place(z, y, 1 - c, x)
        return remote(ref, ref, send_sem.at[index, phase], recv_sem.at[index, phase], where)

    def arrived(index, phase):
        if phase == 0:
            ref = view(items[index], pl.ds(0, depth - 1), y, c, x)
            pltpu.make_async_copy(ref, ref, recv_sem.at[index, 0]).wait()
        else:
            bulk(index, phase).wait_recv()

    def sent(index, phase):
        if phase == 0:
            ref = view(items[index], pl.ds(0, depth - 1), y, c, x)
            pltpu.make_async_copy(ref, ref, send_sem.at[index, 0]).wait()
        else:
            bulk(index, phase).wait_send()

    pairs = (count + 1) // 2

    def gather_step(step):
        for phase in range(4, -1, -1):
            pair = step - phase
            if not 0 <= pair < pairs:
                continue
            for index in range(2 * pair, min(2 * pair + 2, count)):
                if phase == 0:
                    start(index)
                else:
                    arrived(index, phase - 1)
                    if phase < 4:
                        bulk(index, phase).start()

    half_dim = HEAD_DIM // 2

    def tables():
        lane = lax.broadcasted_iota(jnp.int32, (half_dim, tokens), 1)
        order = lax.broadcasted_iota(jnp.int32, (half_dim, tokens), 0)
        frequency = jnp.exp(order.astype(jnp.float32) * (-2.0 * math.log(10000.0) / HEAD_DIM))
        angles = (me * tokens + lane).astype(jnp.float32) * frequency
        cos_out[...] = jnp.cos(angles)
        sin_out[...] = jnp.sin(angles)

    def normalise():
        load.wait()
        pltpu.make_async_copy(small_all, small_all, misc_sem.at[1]).wait()
        for peer in range(total):
            temp_ref[pl.ds(peer * slab, slab), pl.ds(0, 128)] = small_all[peer, :slab, :].astype(jnp.float32)
            doc_ref[pl.ds(peer, 1), :] = jnp.where(
                mine < HEADS, small_all[peer, 32:33, :].astype(jnp.float32), small_all[peer, 33:34, :].astype(jnp.float32)
            )
        turned = temp_ref[:, pl.ds(0, 128)].T
        gain_out[...] = jnp.concatenate(
            [turned[0:1], turned[32:33], turned[64:65], jnp.zeros((5, width), jnp.float32)], axis=0
        )
        for index in range(micro):
            unit_rows = norm_parts(hid_vmem[index].astype(jnp.float32))[0]
            n1_ref[pl.ds(index * tokens, tokens), :] = (unit_rows * gain_out[0:1, :]).astype(jnp.bfloat16)

    def project(part):
        cols = qkv_ref.shape[-1]
        heads = cols // HEAD_DIM
        for half in range(2):
            block = part * 2 + half
            for level in range(depth):
                for inner in range(8):
                    at = (level * 8 + inner) * slab
                    temp_ref[pl.ds(at, slab), :] = qkv_ref[
                        block, level, inner // 4, (inner // 2) % 2, inner % 2
                    ].astype(jnp.float32)
            raw = dot_nn(n1_ref[...], temp_ref[...].astype(jnp.bfloat16))
            for index in range(micro):
                raw_t = raw[index * tokens : (index + 1) * tokens].T
                for head in range(heads):
                    value = raw_t[head * HEAD_DIM : (head + 1) * HEAD_DIM]
                    if part < 2:
                        first_half, second_half = value[:half_dim], value[half_dim:]
                        value = jnp.concatenate(
                            [
                                first_half * cos_out[...] - second_half * sin_out[...],
                                second_half * cos_out[...] + first_half * sin_out[...],
                            ],
                            axis=0,
                        )
                    note_ref[index * HEADS + half * heads + head, part] = value.astype(jnp.bfloat16)

    def slot(device, part):
        return unit_out.at[part, :, pl.ds(pl.multiple_of(device * tokens, 128), tokens)]

    def send_part(part):
        @pl.when(holder)
        def _():
            pltpu.make_async_copy(note_ref.at[mine, part], slot(me, part), unit_recv).start()

        def send(step, carry):
            peer = lax.rem(me + step, total)
            unit, held = unit_of(peer, total)

            @pl.when(held)
            def _():
                remote(
                    note_ref.at[unit, part], slot(me, part), unit_send, unit_recv, (peer // 2, lax.rem(peer, 2))
                ).start()

            return carry

        lax.fori_loop(1, total, send, 0)

    def doc_starts():
        docs = doc_ref[...]
        lane = lax.broadcasted_iota(jnp.int32, docs.shape, 1)
        row = lax.broadcasted_iota(jnp.int32, docs.shape, 0)
        place_at = row * tokens + lane
        before = jnp.where(
            lane == 0, pltpu.roll(pltpu.roll(docs, 1, 0), 1, 1), pltpu.roll(docs, 1, 1)
        )
        begins = (docs != before) | (place_at == 0)
        value = jnp.where(begins, place_at, 0).astype(jnp.float32)
        step = 1
        while step < tokens:
            value = jnp.maximum(value, jnp.where(lane >= step, pltpu.roll(value, step, 1), 0.0))
            step *= 2
        carried = jnp.broadcast_to(jnp.max(value, axis=1, keepdims=True), docs.shape)
        carried = jnp.where(row >= 1, pltpu.roll(carried, 1, 0), 0.0)
        step = 1
        while step < total:
            carried = jnp.maximum(carried, jnp.where(row >= step, pltpu.roll(carried, step, 0), 0.0))
            step *= 2
        starts = jnp.maximum(value, carried).astype(jnp.int32)
        for peer in range(total):
            start_out[:, pl.ds(peer * tokens, tokens)] = starts[peer : peer + 1, :]

    length = tokens * total
    tiles = length // TILE
    reach = (TILE + DOC_MAX - 2) // TILE

    def open_units():
        @pl.when(holder)
        def _():
            part = note_ref.at[pl.ds(0, UNITS - 1)]
            pltpu.make_async_copy(unit_out, unit_out, unit_recv).wait()
            pltpu.make_async_copy(part, part, unit_send).wait()

        @pl.when(jnp.logical_not(holder))
        def _():
            pltpu.make_async_copy(note_ref, note_ref, unit_send).wait()

    def attend(query_tile):
        @pl.when(holder)
        def _():
            columns = pl.ds(query_tile * TILE, TILE)
            query_t = unit_out[0, :, columns]
            first_row = start_out[:, columns]

            def one_key(step, state, diagonal=False):
                peak, weight, mixed = state
                key_tile = query_tile - step
                scores = dot_nn(tile_at(unit_out, key_tile, 1).T, query_t) * (SCORE_SCALE * LOG2E)
                allowed = tile_mask(key_tile, query_tile, first_row, diagonal)
                scores = jnp.where(allowed, scores, -1e30)
                new_peak = jnp.maximum(peak, jnp.max(scores, axis=0, keepdims=True))
                probs = jnp.exp2(scores - new_peak)
                fade = jnp.exp2(peak - new_peak)
                weight = weight * fade + jnp.sum(probs, axis=0, keepdims=True)
                mixed = mixed * fade + dot_nn(tile_at(unit_out, key_tile, 2), probs.astype(jnp.bfloat16))
                return new_peak, weight, mixed

            begin = (
                jnp.full((1, TILE), -1e30, jnp.float32),
                jnp.zeros((1, TILE), jnp.float32),
                jnp.zeros((HEAD_DIM, TILE), jnp.float32),
            )
            begin = one_key(0, begin, diagonal=True)
            peak, weight, mixed = lax.fori_loop(1, min(query_tile, reach) + 1, one_key, begin)
            mixed_out[:, columns] = mixed / weight
            total_out[:, columns] = peak + jnp.log2(weight)

    def back_slot(device):
        return turned_ref.at[:, pl.ds(pl.multiple_of(device * tokens, 128), tokens)]

    def send_back():
        @pl.when(holder)
        def _():
            def turn(step, carry):
                part = pl.ds(pl.multiple_of(step * 16, 16), 16)
                turned_ref[part, :] = pltpu.roll(mixed_out[part, :], length - LEAD, 1).astype(jnp.bfloat16)
                return carry

            lax.fori_loop(0, HEAD_DIM // 16, turn, 0)
            pltpu.make_async_copy(back_slot(me), att_out.at[mine], att_recv).start()

            def send(step, carry):
                peer = lax.rem(me + step, total)
                remote(
                    back_slot(peer), att_out.at[mine], att_send, att_recv, (peer // 2, lax.rem(peer, 2))
                ).start()
                return carry

            lax.fori_loop(1, total, send, 0)

    def unpack(jobs):
        copies = [
            pltpu.make_async_copy(source.at[block], stage_ref.at[slot_], stage_sem.at[slot_])
            for slot_, (source, block, target) in enumerate(jobs)
        ]
        for copy in copies:
            copy.start()
        for slot_, (source, block, target) in enumerate(jobs):
            copies[slot_].wait()

            def body(level, carry):
                for inner in range(4):
                    both = jnp.concatenate(
                        [stage_ref[slot_, level, inner // 2, inner % 2, side].astype(jnp.float32) for side in range(2)],
                        axis=0,
                    )
                    at = pl.multiple_of((level * 4 + inner) * 2 * slab, 16)
                    target[block, pl.ds(at, 2 * slab), :] = both.astype(jnp.bfloat16)
                return carry

            lax.fori_loop(0, depth, body, 0)

    def fetch_down():
        down_rows = down_out.shape[-2]

        def body(step, carry):
            level, rest_ = step // 8, lax.rem(step, 8)
            pltpu.make_async_copy(
                down_out.at[level, rest_ // 4, lax.rem(rest_ // 2, 2), lax.rem(rest_, 2)],
                down_ref.at[pl.ds(pl.multiple_of(step * down_rows, 16), down_rows)],
                stage_sem.at[2],
            ).start()
            return carry

        lax.fori_loop(0, total, body, 0)

    gather_step(0)
    lax.fori_loop(1, total, send_small, 0)
    tables()
    gather_step(1)
    gather_step(2)
    for lead in leads:
        lead.start()
    normalise()
    gather_step(3)
    doc_starts()
    for part in range(3):
        gather_step(4 + part)
        if part == 2:
            keep = pltpu.make_async_copy(qkv_ref, qkv_out, load_sem.at[1])
            keep.start()
        project(part)
        send_part(part)
    def grad_slot(device):
        return back_out.at[:, pl.ds(pl.multiple_of(device * tokens, 128), tokens)]

    def send_grads(index):
        @pl.when(holder & (mine // HEADS == index))
        def _():
            pltpu.make_async_copy(d_att_ref.at[mine], grad_slot(me), grad_recv).start()

        def send(step, carry):
            peer = lax.rem(me + step, total)
            unit, held = unit_of(peer, total)

            @pl.when(held & (unit // HEADS == index))
            def _():
                remote(
                    d_att_ref.at[unit], grad_slot(me), grad_send, grad_recv, (peer // 2, lax.rem(peer, 2))
                ).start()

            return carry

        lax.fori_loop(1, total, send, 0)

    stores = [
        pltpu.make_async_copy(source, target, store_sem.at[index])
        for index, (source, target) in enumerate(
            [(unit_out, unit_hbm), (mixed_out, mixed_hbm), (act_ref, act_hbm), (d_pair_ref, d_pair_hbm)]
        )
    ]
    rows = micro * tokens
    done = {"tick": 7}

    def tick(number=1):
        for _ in range(number):
            if done["tick"] < pairs + 4:
                gather_step(done["tick"])
                done["tick"] += 1

    def make_key_values():
        chunk = 256
        chunks = neigh_ref.shape[0] // chunk

        def make_pairs(step, carry):
            side, block = step // chunks, lax.rem(step, chunks)
            part = pl.ds(pl.multiple_of(block * chunk, chunk), chunk)
            pair_ref[side, part, :] = dot_nn(neigh_ref[part, :], kv_ref[side]).astype(jnp.bfloat16)
            return carry

        lax.fori_loop(0, 2 * chunks, make_pairs, 0)
    couples = HEADS // 2
    pair_rows = NEIGHBOURS * NEIGH_LEN
    groups = rows // SPAN

    def where(group, couple):
        tok = pl.ds(pl.multiple_of(group * SPAN, SPAN), SPAN)
        key = pl.ds(pl.multiple_of(group * pair_rows, pair_rows), pair_rows)
        lanes = pl.ds(couple * 2 * HEAD_DIM, 2 * HEAD_DIM)
        return tok, key, lanes

    def cross_step(group, carry):
        for couple in range(couples):
            tok, key, lanes = where(group, couple)
            query = stack_pair(cq_ref[tok, lanes])
            scores = dot_nt(query, pair_ref[0, key, lanes]) * SCORE_SCALE
            weights = jnp.exp(scores - jnp.max(scores, axis=-1, keepdims=True))
            probs = weights / jnp.sum(weights, axis=-1, keepdims=True)
            prob_ref[group * couples + couple] = probs
            mixed = unstack_pair(dot_nn(probs.astype(jnp.bfloat16), pair_ref[1, key, lanes]))
            cm_ref[tok, lanes] = (mixed * used_ref[tok, :]).astype(jnp.bfloat16)
        return carry


    tick()
    unpack([(kv_out, 0, kv_ref), (kv_out, 1, kv_ref)])
    make_key_values()
    tick(PLAN[0])
    open_units()
    for tile in range(tiles):
        attend(tile)
        tick(PLAN[1 + tile])
    send_back()
    stores[0].start()
    stores[1].start()
    tick(PLAN[1 + tiles])
    unpack([(sq_out, 0, sq_ref), (sq_out, 1, sq_ref)])
    load_grad.wait()
    for lead in leads:
        lead.wait_recv()
    pltpu.make_async_copy(att_out, att_out, att_recv).wait()
    gain_cross, gain_mlp = gain_out[1:2, :], gain_out[2:3, :]
    for index in range(micro):
        part = pl.ds(index * tokens, tokens)
        hidden = shift_rows(hid_vmem[index], lead_hid[index])
        gy_ref[part, :] = shift_rows(grad_ref[index], lead_grad[index]).astype(jnp.bfloat16)
        first_ref[part, :] = hidden + dot_tn(att_out[index * HEADS : (index + 1) * HEADS].reshape(width, tokens), sq_ref[0])
    n2_ref[...] = (norm_parts(first_ref[...])[0] * gain_cross).astype(jnp.bfloat16)
    cq_ref[...] = dot_nn(n2_ref[...], sq_ref[1]).astype(jnp.bfloat16)

    tick(PLAN[2 + tiles])
    lax.fori_loop(0, groups // 2, cross_step, 0)
    tick(PLAN[3 + tiles])
    unpack([(sq_out, 2, sq_ref), (up_out, 0, up_ref)])
    lax.fori_loop(groups // 2, groups, cross_step, 0)
    second_ref[...] = first_ref[...] + dot_nn(cm_ref[...], sq_ref[2])
    n3 = (norm_parts(second_ref[...])[0] * gain_mlp).astype(jnp.bfloat16)
    n3_ref[...] = n3
    n3t_ref[...] = n3.T
    acc_ref[...] = second_ref[...]
    d_n3_ref[...] = jnp.zeros_like(d_n3_ref)
    tick(pairs + 4 - done["tick"])
    fetch_down()
    unpack([(up_out, 1, up_ref), (up_out, 2, up_ref)])
    unpack([(up_out, 3, up_ref)])
    pltpu.make_async_copy(down_ref, down_ref, stage_sem.at[2]).wait()
    ff_blocks = up_ref.shape[0]
    for step in range(ff_blocks):
        cols = pl.ds(step * width, width)
        upper = dot_nn(n3_ref[...], up_ref[step])
        square = upper * upper
        flat = jnp.tanh(math.sqrt(2.0 / math.pi) * upper * (1.0 + 0.044715 * square))
        half = 0.5 * (1.0 + flat)
        active = (upper * half).astype(jnp.bfloat16)
        act_ref[:, cols] = active
        slope = half + 0.5 * upper * (1.0 - flat * flat) * math.sqrt(2.0 / math.pi) * (
            1.0 + 3.0 * 0.044715 * square
        )
        d_upper = (dot_nt(gy_ref[...], down_ref[cols, :]) * slope).astype(jnp.bfloat16)
        acc_ref[...] += dot_nn(active, down_ref[cols, :])
        d_n3_ref[...] += dot_nt(d_upper, up_ref[step])
        d_upper_ref[:, cols] = d_upper
    result_ref[...] = acc_ref[...].astype(jnp.bfloat16)
    stores[2].start()
    pulled, d_gain_mlp = norm_pull(second_ref[...], gain_mlp, d_n3_ref[...])
    d_second = gy_ref[...].astype(jnp.float32) + pulled
    acc_ref[...] = d_second
    gc_ref[...] = d_second.astype(jnp.bfloat16)
    att_rows[...] = (
        dot_nt(gc_ref[...], sq_ref[2]).astype(jnp.bfloat16).astype(jnp.float32) * used_ref[...]
    ).astype(jnp.bfloat16)

    def cross_back(group, carry):
        for couple in range(couples):
            tok, key, lanes = where(group, couple)
            grad = stack_pair(att_rows[tok, lanes])
            query = stack_pair(cq_ref[tok, lanes])
            probs = prob_ref[group * couples + couple]
            d_probs = dot_nt(grad, pair_ref[1, key, lanes])
            d_scores = (
                probs * (d_probs - jnp.sum(probs * d_probs, axis=-1, keepdims=True))
            ).astype(jnp.bfloat16)
            d_query = unstack_pair(dot_nn(d_scores, pair_ref[0, key, lanes]))
            d_cq_ref[tok, lanes] = (d_query * SCORE_SCALE).astype(jnp.bfloat16)
            d_pair_ref[0, key, lanes] = (dot_tn(d_scores, query) * SCORE_SCALE).astype(jnp.bfloat16)
            d_pair_ref[1, key, lanes] = dot_tn(probs.astype(jnp.bfloat16), grad).astype(jnp.bfloat16)
        return carry

    lax.fori_loop(0, groups, cross_back, 0)
    stores[3].start()
    pulled, d_gain_cross = norm_pull(first_ref[...], gain_cross, dot_nt(d_cq_ref[...], sq_ref[1]))
    d_first = acc_ref[...] + pulled
    first_ref[...] = d_first
    ga_ref[...] = d_first.astype(jnp.bfloat16)
    for index in range(micro):
        part = ga_ref[pl.ds(index * tokens, tokens), :]
        d_att_ref[index * HEADS : (index + 1) * HEADS] = (
            dot_nt(sq_ref[0], part).astype(jnp.bfloat16).reshape(HEADS, HEAD_DIM, tokens)
        )
        send_grads(index)
    d_gain_ref[...] = jnp.concatenate([d_gain_cross, d_gain_mlp, jnp.zeros((6, width), jnp.float32)], axis=0)
    d_up_moves = []
    for step in range(ff_blocks):
        cols = pl.ds(step * width, width)
        if step >= 2:
            d_up_moves[step - 2].wait()
        d_up_ref[step % 2] = dot_nn(n3t_ref[...], d_upper_ref[:, cols]).astype(jnp.bfloat16)
        move = pltpu.make_async_copy(d_up_ref.at[step % 2], d_up_hbm.at[:, cols], up_sem.at[step % 2])
        move.start()
        d_up_moves.append(move)
    for move in d_up_moves[-2:]:
        move.wait()


    for index in range(count):
        for phase in range(4):
            sent(index, phase)
    for lead in leads:
        lead.wait_send()
    keep.wait()
    rest = small_all.at[pl.ds(0, total - 1)]
    pltpu.make_async_copy(rest, rest, misc_sem.at[0]).wait()

    @pl.when(holder)
    def _():
        part = turned_ref.at[:, pl.ds(0, tokens * (total - 1))]
        pltpu.make_async_copy(part, part, att_send).wait()
    for store in stores:
        store.wait()

    @pl.when(holder)
    def _():
        part = d_att_ref.at[pl.ds(0, UNITS - 1)]
        pltpu.make_async_copy(back_out, back_out, grad_recv).wait()
        pltpu.make_async_copy(part, part, grad_send).wait()

    @pl.when(jnp.logical_not(holder))
    def _():
        pltpu.make_async_copy(d_att_ref, d_att_ref, grad_send).wait()


def front(depth, w_qkv, w_attn_out, w_cross_q, w_cross_out, w_kv, w_up, w_down, small, used, neigh, hidden, grads):
    total = depth * 8
    rows = w_qkv.shape[0]
    down_rows = w_down.shape[0]
    micro, tokens, width = hidden.shape
    length = tokens * total
    third = down_rows // 3
    row_total = micro * tokens
    ff = w_up.shape[1]
    items = [
        (0, 0, 1, 0), (0, 1, 2, 1), (0, 2, 3, 0), (0, 3, 4, 1), (0, 4, 5, 0), (0, 5, 6, 1),
        (2, 0, 1, 0), (2, 1, 2, 1),
        (1, 0, 1, 0), (1, 1, 2, 1),
        (1, 2, 3, 0), (3, 0, 1, 1),
        (4, 0, third, 0), (4, third, 2 * third, 1),
        (4, 2 * third, down_rows, 0), (3, 1, 2, 1),
        (3, 2, 3, 0), (3, 3, 4, 1),
    ]
    count = len(items)
    low, high = jnp.bfloat16, jnp.float32
    spots = (depth, 2, 2, 2)
    qkv_shape = (6, *spots, rows, width // 2)
    out_shape = [
        jax.ShapeDtypeStruct(qkv_shape, low),
        jax.ShapeDtypeStruct((3, *spots, rows, width), low),
        jax.ShapeDtypeStruct((2, *spots, rows, width), low),
        jax.ShapeDtypeStruct((w_up.shape[1] // width, *spots, rows, width), low),
        jax.ShapeDtypeStruct((*spots, down_rows, width), low),
        jax.ShapeDtypeStruct((width, w_up.shape[1]), low),
        jax.ShapeDtypeStruct((3, HEAD_DIM, length), low),
        jax.ShapeDtypeStruct((HEAD_DIM, length), high),
        jax.ShapeDtypeStruct((row_total, ff), low),
        jax.ShapeDtypeStruct((2,) + neigh.shape, low),
        jax.ShapeDtypeStruct((8, width), high),
        jax.ShapeDtypeStruct((HEAD_DIM // 2, tokens), high),
        jax.ShapeDtypeStruct((HEAD_DIM // 2, tokens), high),
        jax.ShapeDtypeStruct((1, length), high),
        jax.ShapeDtypeStruct((1, length), jnp.int32),
        jax.ShapeDtypeStruct((UNITS, HEAD_DIM, tokens), low),
        jax.ShapeDtypeStruct((row_total, width), low),
        jax.ShapeDtypeStruct((row_total, width), high),
        jax.ShapeDtypeStruct((HEAD_DIM, length), low),
        jax.ShapeDtypeStruct((row_total, width), low),
        jax.ShapeDtypeStruct((row_total, width), low),
        jax.ShapeDtypeStruct((row_total, width), low),
        jax.ShapeDtypeStruct((row_total, width), low),
        jax.ShapeDtypeStruct((row_total, width), low),
        jax.ShapeDtypeStruct((row_total, width), low),
        jax.ShapeDtypeStruct((8, width), high),
    ]
    steps = row_total // SPAN * HEADS // 2
    dma = pltpu.SemaphoreType.DMA
    return pl.pallas_call(
        functools.partial(front_kernel, depth, items),
        out_shape=out_shape,
        in_specs=[VMEM] * 10 + [ANY] * 2,
        out_specs=[ANY] * 10 + [VMEM] * 16,
        scratch_shapes=[
            pltpu.VMEM(qkv_shape, low),
            pltpu.VMEM((total,) + small.shape, low),
            pltpu.VMEM(hidden.shape, low),
            pltpu.VMEM(hidden.shape, low),
            pltpu.VMEM((micro, 64, width), low),
            pltpu.VMEM((micro, 64, width), low),
            pltpu.VMEM((micro * tokens, width), low),
            pltpu.VMEM((width, width // 2), high),
            pltpu.VMEM((UNITS, 3, HEAD_DIM, tokens), low),
            pltpu.VMEM((HEAD_DIM, length), low),
            pltpu.VMEM((total, tokens), high),
            pltpu.VMEM((2, *spots, rows, width), low),
            pltpu.VMEM((3, width, width), low),
            pltpu.VMEM((2, width, width), low),
            pltpu.VMEM((ff // width, width, width), low),
            pltpu.VMEM((ff, width), low),
            pltpu.VMEM((row_total, width), low),
            pltpu.VMEM((row_total, width), high),
            pltpu.VMEM((row_total, width), low),
            pltpu.VMEM((2,) + neigh.shape, low),
            pltpu.VMEM((steps, 2 * SPAN, NEIGHBOURS * NEIGH_LEN), high),
            pltpu.VMEM((row_total, width), high),
            pltpu.VMEM((row_total, width), high),
            pltpu.VMEM((row_total, width), low),
            pltpu.VMEM((width, row_total), low),
            pltpu.VMEM((2, width, width), low),
            dma((count,)), dma((count, 4)), dma((count, 4)), dma((2,)), dma((2,)), dma((2,)), dma((3,)), dma, dma,
            dma, dma, dma((3,)), dma((2,)), dma, dma, dma((4,)),
            pltpu.VMEM((3, HEAD_DIM, length), low),
            pltpu.VMEM((HEAD_DIM, length), high),
            pltpu.VMEM((row_total, ff), low),
            pltpu.VMEM((2,) + neigh.shape, low),
            pltpu.VMEM((UNITS, HEAD_DIM, tokens), low),
            pltpu.VMEM((row_total, ff), low),
        ],
        compiler_params=pltpu.CompilerParams(
            collective_id=0, has_side_effects=True, vmem_limit_bytes=62 * 2**20
        ),
        cost_estimate=pl.CostEstimate(flops=10**9, bytes_accessed=20 * 10**6, transcendentals=0),
    )(w_qkv, w_attn_out, w_cross_q, w_cross_out, w_kv, w_up, w_down, small, used, neigh, hidden, grads)


def last_kernel(depth, items, skew, *refs):
    count = len(items)
    back_ref, result_hbm, first_hbm = refs[:3]
    sources = refs[1:16]
    gain_ref, cos_ref, sin_ref, d_gain_rest_ref = refs[16:20]
    (
        output_ref, grad_in_ref, grad_neigh_ref, out_qkv, out_att, out_cq, out_co, out_kv, out_down, gain_out,
    ) = refs[20:30]
    full = refs[30 : 30 + count]
    got_core = refs[30 + count : 30 + 2 * count]
    got_one = refs[30 + 2 * count : 30 + 3 * count]
    got_two = refs[30 + 3 * count : 30 + 4 * count]
    got_z = refs[30 + 4 * count : 30 + 5 * count]
    (
        sent_ref, tail_first, tail_result, raw_ref, n1t_ref, d_n1_ref, temp_ref, gain_mine, gain_got, gain_z,
        send_sem, recv_sem, unit_send, unit_recv, tail_send, tail_recv, gain_send, gain_recv, load_sem,
    ) = refs[30 + 5 * count : -15]
    held_refs = refs[-15:]
    (
        result_ref, first_ref, n2_ref, d_cq_ref, cm_ref, gc_ref, ga_ref, gy_ref, act_ref, d_pair_ref,
        att_ref, neigh_ref, kv_ref, qkv_ref, hidden_ref,
    ) = held_refs
    loads = [
        pltpu.make_async_copy(source, target, load_sem.at[index])
        for index, (source, target) in enumerate(zip(sources, held_refs))
    ]
    for index in (8, 7, 11, 9, 10, 6, 2, 3, 4, 5, 12, 13, 14, 1, 0):
        loads[index].start()
    arrived = set()

    def need(*indices):
        for index in indices:
            if index not in arrived:
                arrived.add(index)
                loads[index].wait()

    micro, tokens, width = hidden_ref.shape
    total = depth * 8
    z, y, c, x = coords()
    me = lax.axis_index("blk") * 2 + lax.axis_index("head")
    mine, holder = unit_of(me, total)
    whole = slice(None)
    all_barrier(total, me)

    after = lax.rem(me + 1, total)
    after_at = (after // 2, lax.rem(after, 2))
    tails = []
    for index in range(micro):
        part = pl.ds(index * tokens + tokens - 64, 64)
        tails.append(
            remote(first_hbm.at[part], tail_first.at[index], tail_send.at[index], tail_recv.at[index], after_at)
        )
        tails.append(
            remote(
                result_hbm.at[part], tail_result.at[index],
                tail_send.at[micro + index], tail_recv.at[micro + index], after_at,
            )
        )

    def slot(device):
        return back_ref.at[:, :, pl.ds(pl.multiple_of(device * tokens, 128), tokens)]

    @pl.when(holder)
    def _():
        pltpu.make_async_copy(slot(me), sent_ref.at[mine], unit_recv).start()

        def send(step, carry):
            peer = lax.rem(me + step, total)
            remote(
                slot(peer), sent_ref.at[mine], unit_send, unit_recv, (peer // 2, lax.rem(peer, 2))
            ).start()
            return carry

        lax.fori_loop(1, total, send, 0)

    for tail in tails:
        tail.start()

    slab = full[0].shape[-2]

    def spread(index, block):
        buffer = full[index]
        cols = buffer.shape[-1]

        def body(level, carry):
            for place_in in range(8):
                at = pl.multiple_of((level * 8 + place_in) * slab, 8)
                buffer[block, level, place_in // 4, (place_in // 2) % 2, place_in % 2] = temp_ref[
                    pl.ds(at, slab), :cols
                ].astype(jnp.bfloat16)
            return carry

        lax.fori_loop(0, depth, body, 0)

    down_index = [index for index, item in enumerate(items) if item[0] == "down"]

    def make_down():
        need(7, 8)

        def body(level, carry):
            cols = pl.ds(pl.multiple_of(level * width, width), width)
            temp_ref[...] = dot_tn(act_ref[:, cols], gy_ref[...])
            for place_in in range(8):
                for part, index in enumerate(down_index):
                    at = place_in * slab * len(down_index) + part * slab
                    full[index][0, level, place_in // 4, (place_in // 2) % 2, place_in % 2] = temp_ref[
                        pl.ds(at, slab), :
                    ].astype(jnp.bfloat16)
            return carry

        lax.fori_loop(0, depth, body, 0)

    def take_units():
        @pl.when(holder)
        def _():
            part = back_ref.at[:, :, pl.ds(0, tokens * (total - 1))]
            pltpu.make_async_copy(part, part, unit_send).wait()

        pltpu.make_async_copy(sent_ref, sent_ref, unit_recv).wait()
        need(14)
        half = HEAD_DIM // 2

        def body(head, carry):
            for index in range(micro):
                lanes = pl.ds(index * tokens, tokens)
                cosine, sine = cos_ref[...], sin_ref[...]
                for part in range(3):
                    value = sent_ref[index * HEADS + head, part].astype(jnp.float32)
                    at = pl.multiple_of(part * width + head * HEAD_DIM, HEAD_DIM)
                    if part < 2:
                        first_half, second_half = value[:half], value[half:]
                        value = jnp.concatenate(
                            [
                                first_half * cosine + second_half * sine,
                                second_half * cosine - first_half * sine,
                            ],
                            axis=0,
                        )
                    raw_ref[pl.ds(at, HEAD_DIM), lanes] = value.astype(jnp.bfloat16)
            return carry

        lax.fori_loop(0, HEADS, body, 0)
        for index in range(micro):
            normed = norm_parts(hidden_ref[index].astype(jnp.float32))[0] * gain_ref[0:1, :]
            n1t_ref[:, pl.ds(index * tokens, tokens)] = normed.astype(jnp.bfloat16).T

    def make(index):
        kind, which = items[index][:2]
        if kind == "down":
            if index == down_index[0]:
                make_down()
            return
        if kind == "kv":
            need(9, 11)
            temp_ref[...] = dot_tn(neigh_ref[...], d_pair_ref[which])
        elif kind == "att":
            need(6, 10)
            temp_ref[...] = dot_nn(att_ref[0], ga_ref[pl.ds(0, tokens), :])
            for step in range(1, micro):
                temp_ref[...] += dot_nn(att_ref[step], ga_ref[pl.ds(step * tokens, tokens), :])
        elif kind == "cq":
            need(2, 3)
            temp_ref[...] = dot_tn(n2_ref[...], d_cq_ref[...])
        elif kind == "co":
            need(4, 5)
            temp_ref[...] = dot_tn(cm_ref[...], gc_ref[...])
        else:
            if which == 0:
                take_units()
            for block in range(2):
                half = width // 2
                at = which * width + block * half
                temp_ref[:, :half] = dot_nt(n1t_ref[...], raw_ref[pl.ds(at, half), :])
                spread(index, block)
            return
        spread(index, 0)

    def core(index):
        return remote(
            full[index].at[whole, whole, whole, 1 - c], got_core[index],
            send_sem.at[index, 0], recv_sem.at[index, 0], place(z, y, 1 - c, x),
        )

    def one(index):
        if items[index][2] == 0:
            src, where = full[index].at[whole, whole, 1 - y, c], place(z, 1 - y, c, x)
        else:
            src, where = full[index].at[whole, whole, whole, c, 1 - x], place(z, y, c, 1 - x)
        return remote(src, got_one[index], send_sem.at[index, 1], recv_sem.at[index, 1], where)

    def two(index):
        if items[index][2] == 0:
            src, where = full[index].at[whole, whole, y, c, 1 - x], place(z, y, c, 1 - x)
        else:
            src, where = full[index].at[whole, whole, 1 - y, c, x], place(z, 1 - y, c, x)
        return remote(src, got_two[index], send_sem.at[index, 2], recv_sem.at[index, 2], where)

    def send_z(index):
        for step in range(1, depth):
            other = lax.rem(z + step, depth)
            remote(
                full[index].at[whole, other, y, c, x], got_z[index].at[z],
                send_sem.at[index, 3], recv_sem.at[index, 3], place(other, y, c, x),
            ).start()

    def add_into(target, source):
        target[...] = (target[...].astype(jnp.float32) + source[...].astype(jnp.float32)).astype(
            jnp.bfloat16
        )

    def each_level(index, body):
        blocks = full[index].shape[0]
        lax.fori_loop(
            0, blocks * depth, lambda step, carry: (body(step // depth, lax.rem(step, depth)), carry)[1], 0
        )

    def sum_core(index):
        def body(block, level):
            for row in range(2):
                for col in range(2):
                    add_into(
                        full[index].at[block, level, row, c, col], got_core[index].at[block, level, row, col]
                    )

        each_level(index, body)

    def sum_one(index):
        def body(block, level):
            for side in range(2):
                if items[index][2] == 0:
                    target = full[index].at[block, level, y, c, side]
                else:
                    target = full[index].at[block, level, side, c, x]
                add_into(target, got_one[index].at[block, level, side])

        each_level(index, body)

    def sum_two(index):
        each_level(
            index,
            lambda block, level: add_into(
                full[index].at[block, level, y, c, x], got_two[index].at[block, level]
            ),
        )

    def sum_z(index):
        kind, which = items[index][:2]
        for block in range(full[index].shape[0]):
            value = full[index][block, z, y, c, x].astype(jnp.float32)
            for step in range(1, depth):
                value = value + got_z[index][lax.rem(z + step, depth), block].astype(jnp.float32)
            if kind == "down":
                out_down[pl.ds(which * slab, slab), :] = value
            elif kind == "kv":
                out_kv[:, pl.ds(which * width, width)] = value
            elif kind == "qkv":
                out_qkv[:, pl.ds(which * width + block * (width // 2), width // 2)] = value
            else:
                {"att": out_att, "cq": out_cq, "co": out_co}[kind][...] = value

    def phase(index, number):
        if number == 0:
            make(index)
            core(index).start()
        elif number == 1:
            core(index).wait_recv()
            sum_core(index)
            one(index).start()
        elif number == 2:
            one(index).wait_recv()
            sum_one(index)
            two(index).start()
        elif number == 3:
            two(index).wait_recv()
            sum_two(index)
            send_z(index)
        else:
            landed = got_z[index].at[pl.ds(0, depth - 1)]
            pltpu.make_async_copy(landed, landed, recv_sem.at[index, 3]).wait()
            sum_z(index)

    def gain_copy(stage):
        where = (place(z, y, 1 - c, x), place(z, 1 - y, c, x), place(z, y, c, 1 - x))[stage]
        return remote(
            gain_mine.at[stage], gain_got.at[stage], gain_send.at[stage], gain_recv.at[stage], where
        )

    def gain_phase(number):
        if number == 0:
            gain_copy(0).start()
        elif number < 4:
            gain_copy(number - 1).wait_recv()
            gain_mine[number] = gain_mine[number - 1] + gain_got[number - 1]
            if number < 3:
                gain_copy(number).start()
            else:
                for step in range(1, depth):
                    other = lax.rem(z + step, depth)
                    remote(
                        gain_mine.at[3], gain_z.at[z], gain_send.at[3], gain_recv.at[3], place(other, y, c, x)
                    ).start()
        else:
            landed = gain_z.at[pl.ds(0, depth - 1)]
            pltpu.make_async_copy(landed, landed, gain_recv.at[3]).wait()
            value = gain_mine[3]
            for step in range(1, depth):
                value = value + gain_z[lax.rem(z + step, depth)]
            gain_out[...] = value

    def neighbours_part(block):
        need(9, 12)
        chunk = 256
        part = pl.ds(block * chunk, chunk)
        grad_neigh_ref[part, :] = (
            dot_nt(d_pair_ref[0, part, :], kv_ref[0]) + dot_nt(d_pair_ref[1, part, :], kv_ref[1])
        ).astype(jnp.bfloat16)

    def input_part():
        half = width // 2
        need(0, 1, 13, 14)
        blocks = qkv_ref.shape[0]
        d_n1_ref[...] = dot_nn(qkv_ref[0], raw_ref[pl.ds(0, half), :])
        for block in range(1, blocks):
            d_n1_ref[...] += dot_nn(qkv_ref[block], raw_ref[pl.ds(block * half, half), :])
        for tail in tails:
            tail.wait()
        d_gain = jnp.zeros((1, width), jnp.float32)
        for index in range(micro):
            part = pl.ds(index * tokens, tokens)
            d_normed = d_n1_ref[:, part].T
            pulled, part_gain = norm_pull(hidden_ref[index].astype(jnp.float32), gain_ref[0:1, :], d_normed)
            d_gain = d_gain + part_gain
            joined = jnp.concatenate([tail_first[index], first_ref[part, :]], axis=0)
            home = pltpu.roll(joined, joined.shape[0] - 1, 0)[:tokens]
            grad_in_ref[part, :] = (home + pulled).astype(jnp.bfloat16)
            joined = jnp.concatenate(
                [tail_result[index].astype(jnp.float32), result_ref[part, :].astype(jnp.float32)], axis=0
            )
            output_ref[part, :] = pltpu.roll(joined, joined.shape[0] - 1, 0)[:tokens].astype(jnp.bfloat16)
        gain_mine[0] = jnp.concatenate([d_gain, d_gain_rest_ref[0:7, :]], axis=0)

    pairs = (count + 1) // 2
    chunks = neigh_ref.shape[0] // 256
    for step in range(pairs + skew * 4):
        for number in range(4, -1, -1):
            pair = step - skew * number
            if not 0 <= pair < pairs:
                continue
            for index in range(2 * pair, min(2 * pair + 2, count)):
                phase(index, number)
            if pair == pairs - 1:
                if number == 0:
                    input_part()
                gain_phase(number)
        if 1 <= step <= chunks:
            neighbours_part(step - 1)
    for index in range(count):
        core(index).wait_send()
        one(index).wait_send()
        two(index).wait_send()
        gone = got_z[index].at[pl.ds(0, depth - 1)]
        pltpu.make_async_copy(gone, gone, send_sem.at[index, 3]).wait()
    for stage in range(3):
        gain_copy(stage).wait_send()
    gone = gain_z.at[pl.ds(0, depth - 1)]
    pltpu.make_async_copy(gone, gone, gain_send.at[3]).wait()


def last(depth, collective, ff, *args):
    hidden = args[15]
    micro, tokens, width = hidden.shape
    rows = micro * tokens
    total = depth * 8
    slab = width // total
    neigh_rows = args[12].shape[0]
    items = [
        ("down", 0, 0), ("down", 1, 1), ("down", 2, 0), ("down", 3, 1), ("kv", 0, 0), ("kv", 1, 1),
        ("att", 0, 0), ("cq", 0, 1), ("co", 0, 0), ("qkv", 0, 1), ("qkv", 1, 0), ("qkv", 2, 1),
    ]
    count = len(items)
    low, high = jnp.bfloat16, jnp.float32
    out_shape = [
        jax.ShapeDtypeStruct((rows, width), low),
        jax.ShapeDtypeStruct((rows, width), low),
        jax.ShapeDtypeStruct((neigh_rows, width), low),
        jax.ShapeDtypeStruct((slab, 3 * width), high),
        jax.ShapeDtypeStruct((slab, width), high),
        jax.ShapeDtypeStruct((slab, width), high),
        jax.ShapeDtypeStruct((slab, width), high),
        jax.ShapeDtypeStruct((slab, 2 * width), high),
        jax.ShapeDtypeStruct((ff // total, width), high),
        jax.ShapeDtypeStruct((8, width), high),
    ]
    full, core, one, two, along = [], [], [], [], []
    for kind, which, order in items:
        blocks, cols = (2, width // 2) if kind == "qkv" else (1, width)
        full.append(pltpu.VMEM((blocks, depth, 2, 2, 2, slab, cols), low))
        core.append(pltpu.VMEM((blocks, depth, 2, 2, slab, cols), low))
        one.append(pltpu.VMEM((blocks, depth, 2, slab, cols), low))
        two.append(pltpu.VMEM((blocks, depth, slab, cols), low))
        along.append(pltpu.VMEM((depth, blocks, slab, cols), low))
    dma = pltpu.SemaphoreType.DMA
    scratch = full + core + one + two + along + [
        pltpu.VMEM((UNITS, 3, HEAD_DIM, tokens), low),
        pltpu.VMEM((micro, 64, width), high),
        pltpu.VMEM((micro, 64, width), low),
        pltpu.VMEM((3 * width, rows), low),
        pltpu.VMEM((width, rows), low),
        pltpu.VMEM((width, rows), high),
        pltpu.VMEM((width, width), high),
        pltpu.VMEM((4, 8, width), high),
        pltpu.VMEM((3, 8, width), high),
        pltpu.VMEM((depth, 8, width), high),
        dma((count, 4)), dma((count, 4)), dma, dma, dma((2 * micro,)), dma((2 * micro,)), dma((4,)), dma((4,)),
        dma((15,)),
    ] + [pltpu.VMEM(a.shape, a.dtype) for a in args[1:16]]
    return pl.pallas_call(
        functools.partial(last_kernel, depth, items, 2),
        out_shape=out_shape,
        in_specs=[ANY] * 16 + [VMEM] * 4,
        out_specs=[VMEM] * 10,
        scratch_shapes=scratch,
        compiler_params=pltpu.CompilerParams(
            collective_id=collective, has_side_effects=True, vmem_limit_bytes=62 * 2**20
        ),
        cost_estimate=pl.CostEstimate(flops=10**10, bytes_accessed=40 * 10**6, transcendentals=0),
    )(*args)


def finish_kernel(copies, *refs):
    for source, result in zip(refs[:copies], refs[copies:]):
        result[...] = source[...].astype(result.dtype)


def finish(arrays, low):
    arrays = [*arrays, low]
    copies = len(arrays)
    vmem = pl.BlockSpec(memory_space=pltpu.VMEM)
    return pl.pallas_call(
        functools.partial(finish_kernel, copies),
        out_shape=[jax.ShapeDtypeStruct(a.shape, a.dtype) for a in arrays[:-1]]
        + [jax.ShapeDtypeStruct(low.shape, jnp.float32)],
        in_specs=[vmem] * copies,
        out_specs=[vmem] * copies,
        compiler_params=pltpu.CompilerParams(vmem_limit_bytes=62 * 2**20),
    )(*arrays)


def layer_norm(values, norm_gain):
    centred = values - jnp.mean(values, axis=-1, keepdims=True)
    spread = jnp.mean(centred * centred, axis=-1, keepdims=True)
    return centred * lax.rsqrt(spread + 1e-05) * norm_gain


def norm_backward(values, norm_gain, grad_out):
    result, pullback = jax.vjp(layer_norm, values, norm_gain)
    return pullback(grad_out)


def outer(left, right):
    return jnp.einsum("td,te->de", left, right, preferred_element_type=jnp.float32)


def turn_heads(values, cosine, sine):
    first_half, second_half = values[:, :32], values[:, 32:]
    return jnp.concatenate(
        [first_half * cosine - second_half * sine, second_half * cosine + first_half * sine], axis=1
    )


def on_device(
    hidden_in,
    segment_ids,
    neighbour_valid,
    neighbours,
    out_grad,
    norm_attn,
    w_qkv,
    w_attn_out,
    norm_cross,
    w_cross_q,
    w_cross_kv,
    w_cross_out,
    norm_mlp,
    w_up,
    w_down,
):
    micro, tok_count, model_width = hidden_in.shape
    blk_count = lax.axis_size("blk")
    depth = blk_count // 4
    total = blk_count * 2
    length = tok_count * total
    row_count = micro * tok_count
    gain_rows = norm_attn.shape[0]
    span_count = tok_count // SPAN
    pair_rows = NEIGHBOURS * NEIGH_LEN
    device = lax.axis_index(AXES)

    in_kernel = gain_rows % 8 == 0
    token_index = device * tok_count + jnp.arange(tok_count, dtype=jnp.int32)
    shifted_index = token_index + LEAD
    used = jnp.where(
        shifted_index[None] < length, jnp.repeat(neighbour_valid, SPAN, axis=1).astype(jnp.float32), 0.0
    ).reshape(row_count, 1)
    neigh_rows = neighbours.reshape(micro * span_count * pair_rows, model_width)
    if in_kernel:
        gain_lanes = jnp.concatenate(
            [jnp.broadcast_to(gain[:, None], (gain_rows, 32)) for gain in (norm_attn, norm_cross, norm_mlp, norm_mlp)],
            axis=1,
        )
        small = jnp.concatenate(
            [
                jnp.pad(gain_lanes, ((0, 32 - gain_rows), (0, 0))),
                jnp.pad(segment_ids.astype(jnp.bfloat16), ((0, 16 - micro), (0, 0))),
            ],
            axis=0,
        )
        (
            got_qkv, got_sq, got_kv, up_full, down_full, d_up, unit_qkv, mixed, activated, d_pairs,
            gains, cosine, sine, totals, first_row, attended_t,
            result_rows, d_first, unit_grad, normed_cross, d_cross_query, cross_mixed, d_second_low, d_first_low,
            grad_low, d_gain_rest,
        ) = front(
            depth, w_qkv, w_attn_out, w_cross_q, w_cross_out, w_cross_kv, w_up, w_down, small, used, neigh_rows,
            hidden_in, out_grad,
        )
        attended_t = attended_t.reshape(micro, model_width, tok_count)
    else:
        up_full = lax.all_gather(w_up, AXES, axis=0, tiled=True)
        down_full = lax.all_gather(w_down, AXES, axis=0, tiled=True)
        up_full = up_full.reshape(model_width, -1, model_width).transpose(1, 0, 2)
        small = jnp.zeros((16, 128), jnp.bfloat16)
        for row, gain in enumerate((norm_attn, norm_cross, norm_mlp)):
            small = small.at[row, :gain_rows].set(gain)
        small = small.at[3 : 3 + micro, :tok_count].set(segment_ids.astype(jnp.bfloat16))
        got_qkv, got_sq, got_kv, got_small, lead_hid, lead_grad = gather_all(
            depth, w_qkv, w_attn_out, w_cross_q, w_cross_out, w_cross_kv, small, hidden_in, out_grad
        )
        gains = got_small[:, :3, :gain_rows].astype(jnp.float32).transpose(1, 0, 2).reshape(3, model_width)
        gain_attn = gains[0]
        seg_full = got_small[:, 3 : 3 + micro, :tok_count].transpose(1, 0, 2).reshape(micro, length)
        seg_full = seg_full.astype(jnp.int32)
    qkv_blocks = got_qkv.reshape(6, model_width, model_width // 2)
    squares = got_sq.reshape(3, model_width, model_width)
    kv_blocks = got_kv.reshape(2, model_width, model_width)


    unit, holder = unit_of(device, total)
    tile_index = jnp.arange(length // TILE, dtype=jnp.int32)
    if in_kernel:
        tile_first = first_row[0, ::TILE]
    else:
        seg_unit = lax.dynamic_index_in_dim(seg_full, unit // HEADS, 0, keepdims=False)
        seg_tiles = seg_unit.reshape(length // TILE, TILE)
        tile_first = jnp.sum((seg_unit[None] < seg_tiles[:, :1]).astype(jnp.int32), axis=-1)
        inside = jnp.sum((seg_tiles[:, None, :] < seg_tiles[:, :, None]).astype(jnp.int32), axis=-1)
        first_row = jnp.where(
            seg_tiles == seg_tiles[:, :1], tile_first[:, None], tile_index[:, None] * TILE + inside
        ).reshape(1, length)
    low = tile_first // TILE
    high = jnp.sum((low[None] <= tile_index[:, None]).astype(jnp.int32), axis=-1)
    low = jnp.where(holder, low, tile_index + 1)
    high = jnp.where(holder, high, 0)

    if not in_kernel:
        first_of = jnp.sum(
            (seg_full[:, None, :] < segment_ids[:, :, None]).astype(jnp.int32), axis=-1
        )
        local_pos = token_index[None] - first_of
        frequency = jnp.exp(
            jnp.arange(HEAD_DIM // 2, dtype=jnp.float32) * (-2.0 * math.log(10000.0) / HEAD_DIM)
        )
        angles = frequency[:, None, None] * local_pos.astype(jnp.float32)[None]
        cosine, sine = jnp.cos(angles), jnp.sin(angles)

        hidden = hidden_in.astype(jnp.float32)
        normed_attn = layer_norm(hidden, gain_attn).astype(jnp.bfloat16).reshape(row_count, model_width)
        raw = jnp.einsum("bde,td->bet", qkv_blocks, normed_attn, preferred_element_type=jnp.float32)
        raw = raw.reshape(3, HEADS, HEAD_DIM, micro, tok_count)
        rotated = jnp.stack(
            [turn_heads(raw[0], cosine, sine), turn_heads(raw[1], cosine, sine), raw[2]]
        ).astype(jnp.bfloat16)
        message = rotated.transpose(3, 1, 0, 2, 4).reshape(UNITS, 3, HEAD_DIM, tok_count)
        unit_qkv = to_units(total, message, 1)
        shifted, mixed, totals = attn_forward(low, first_row, unit_qkv)
        (attended_t,) = to_tokens(total, shifted[None], (), 2)
    attended_t = attended_t.reshape(micro, model_width, tok_count)

    if not in_kernel:
        (
            result_rows, d_first, d_attended_t, normed_cross, d_cross_query, cross_mixed, d_second_low, d_first_low,
            grad_low, activated, d_pairs, d_gain_rest, d_up,
        ) = middle(
            attended_t, hidden_in, lead_hid, out_grad, lead_grad, gains, used, squares, kv_blocks, neigh_rows,
            up_full, down_full,
        )
    up_low = lax.psum_scatter(d_up, AXES, scatter_dimension=0, tiled=True)
    if not in_kernel:
        down_share = lax.psum_scatter(
            outer(activated, grad_low).astype(jnp.bfloat16), AXES, scatter_dimension=0, tiled=True
        ).astype(jnp.float32)
    if not in_kernel:
        unit_grad = to_units(total, d_attended_t.reshape(UNITS, 1, HEAD_DIM, tok_count), 3)[0]
    unit_back = attn_backward(low, high, first_row, unit_qkv, unit_grad, mixed, totals)
    if in_kernel:
        (
            output, grad_in, grad_neighbours, s_qkv, s_att, s_cq, s_co, s_kv, s_down, s_gain,
        ) = last(
            depth, 5, w_up.shape[1],
            unit_back, result_rows, d_first, normed_cross, d_cross_query, cross_mixed, d_second_low, d_first_low,
            grad_low, activated, d_pairs, attended_t, neigh_rows, kv_blocks, qkv_blocks, hidden_in, gains,
            cosine, sine, d_gain_rest,
        )
        own_gain = lax.dynamic_slice_in_dim(s_gain, device * gain_rows, gain_rows, 1)
        (
            output, grad_in, grad_neighbours, s_qkv, s_att, s_cq, s_co, s_kv, s_down, up_share,
        ) = finish(
            [
                output, grad_in, grad_neighbours, s_qkv, s_att, s_cq, s_co, s_kv, s_down,
            ],
            up_low,
        )
        return (
            output.reshape(hidden_in.shape), grad_in.reshape(hidden_in.shape),
            grad_neighbours.reshape(neighbours.shape),
            own_gain[0], s_qkv, s_att, own_gain[1], s_cq, s_kv, s_co, own_gain[2], up_share, s_down,
        )
    up_share = up_low.astype(jnp.float32)
    result_rows = result_rows.reshape(micro, tok_count, model_width)
    d_first = d_first.reshape(micro, tok_count, model_width)
    sent_t, tail_first, tail_result = to_tokens(
        total, unit_back, (d_first[:, tok_count - 64 :], result_rows[:, tok_count - 64 :]), 4
    )

    def unshift(rows, tail):
        return jnp.concatenate([tail[:, 1:], rows[:, : tok_count - LEAD]], axis=1)

    output = unshift(result_rows, tail_result)
    d_first_home = unshift(d_first, tail_first)
    sent_t = sent_t.reshape(micro, HEADS, 3, HEAD_DIM, tok_count).transpose(2, 1, 3, 0, 4)
    sent_t = sent_t.astype(jnp.float32)
    raw_t = jnp.stack(
        [turn_heads(sent_t[0], cosine, -sine), turn_heads(sent_t[1], cosine, -sine), sent_t[2]]
    ).astype(jnp.bfloat16).reshape(6, model_width // 2, row_count)
    d_normed_attn = jnp.einsum("bet,bde->td", raw_t, qkv_blocks, preferred_element_type=jnp.float32)
    d_hidden_in, d_gain_attn = norm_backward(
        hidden, gain_attn, d_normed_attn.reshape(micro, tok_count, model_width)
    )
    grad_in = (d_first_home + d_hidden_in).astype(jnp.bfloat16)

    d_keys, d_values = d_pairs[0], d_pairs[1]
    d_first_low = d_first_low.reshape(micro, tok_count, model_width)
    d_neigh = (
        jnp.einsum("te,de->td", d_keys, kv_blocks[0], preferred_element_type=jnp.float32)
        + jnp.einsum("te,de->td", d_values, kv_blocks[1], preferred_element_type=jnp.float32)
    ).astype(jnp.bfloat16)
    grad_neighbours = d_neigh.reshape(neighbours.shape)

    def blocks_of(array):
        return array.astype(jnp.bfloat16).reshape(
            array.shape[0], depth, 2, 2, 2, gain_rows, array.shape[-1]
        )

    d_qkv = jnp.einsum("td,bet->bde", normed_attn, raw_t, preferred_element_type=jnp.float32)
    d_sq = jnp.stack(
        [
            jnp.einsum("mdt,mte->de", attended_t, d_first_low, preferred_element_type=jnp.float32),
            outer(normed_cross, d_cross_query),
            outer(cross_mixed, d_second_low),
        ]
    )
    d_kv = jnp.stack([outer(neigh_rows, d_keys), outer(neigh_rows, d_values)])
    d_gains = jnp.stack([d_gain_attn, d_gain_rest[0], d_gain_rest[1]]).reshape(3, total, gain_rows)
    d_gains = jnp.zeros((total, 8, 128), jnp.float32).at[:, :3, :gain_rows].set(d_gains.transpose(1, 0, 2))
    s_qkv, s_sq, s_kv, s_gain = scatter_all(
        depth, blocks_of(d_qkv), blocks_of(d_sq), blocks_of(d_kv), d_gains, 6
    )
    return (
        output,
        grad_in,
        grad_neighbours,
        s_gain[0, :gain_rows],
        s_qkv.transpose(1, 0, 2).reshape(gain_rows, 3 * model_width),
        s_sq[0],
        s_gain[1, :gain_rows],
        s_sq[1],
        s_kv.transpose(1, 0, 2).reshape(gain_rows, 2 * model_width),
        s_sq[2],
        s_gain[2, :gain_rows],
        up_share,
        down_share,
    )


def solution(mesh):
    placed = (
        P(None, ("blk", "head"), None),
        P(None, ("blk", "head")),
        P(None, ("blk", "head")),
        P(None, ("blk", "head"), None, None, None),
        P(None, ("blk", "head"), None),
        P(("blk", "head")),
        P(("blk", "head"), None),
        P(("blk", "head"), None),
        P(("blk", "head")),
        P(("blk", "head"), None),
        P(("blk", "head"), None),
        P(("blk", "head"), None),
        P(("blk", "head")),
        P(("blk", "head"), None),
        P(("blk", "head"), None),
    )
    return jax.shard_map(
        on_device,
        mesh=mesh,
        in_specs=placed,
        out_specs=(
            P(None, ("blk", "head"), None),
            P(None, ("blk", "head"), None),
            P(None, ("blk", "head"), None, None, None),
            P(("blk", "head")),
            P(("blk", "head"), None),
            P(("blk", "head"), None),
            P(("blk", "head")),
            P(("blk", "head"), None),
            P(("blk", "head"), None),
            P(("blk", "head"), None),
            P(("blk", "head")),
            P(("blk", "head"), None),
            P(("blk", "head"), None),
        ),
        check_vma=False,
    )
```

```python
import functools
import math

import jax
import jax.numpy as jnp
from jax import lax
from jax.experimental import pallas as pl
from jax.experimental.pallas import tpu as pltpu
from jax.sharding import PartitionSpec as P

MESH = pl.DeviceIdType.MESH
ANY = pl.BlockSpec(memory_space=pl.ANY)


def coords():
    blk = lax.axis_index("blk")
    return blk // 4, (blk // 2) % 2, blk % 2, lax.axis_index("head")


def place(z, y, c, x):
    return (z * 4 + y * 2 + c, x)


def loop(count, body):
    if count <= 8:
        for step in range(count):
            body(step)
    else:
        lax.fori_loop(0, count, lambda step, carry: (body(step), carry)[1], 0)


def all_barrier(total, me):
    barrier = pltpu.get_barrier_semaphore()

    def greet(step, carry):
        peer = lax.rem(me + step, total)
        pl.semaphore_signal(
            barrier, inc=1, device_id=(peer // 2, lax.rem(peer, 2)), device_id_type=MESH
        )
        return carry

    lax.fori_loop(1, total, greet, 0)
    pl.semaphore_wait(barrier, total - 1)


def remote(src, dst, send, recv, where):
    return pltpu.make_async_remote_copy(
        src_ref=src, dst_ref=dst, send_sem=send, recv_sem=recv, device_id=where, device_id_type=MESH
    )


def gather_kernel(depth, items, *refs):
    count = len(items)
    w_refs = refs[:5]
    small_ref, hid_ref, grad_ref = refs[5:8]
    out_refs = refs[8:11]
    small_out, lead_hid, lead_grad = refs[11:14]
    own_sem, send_sem, recv_sem, misc_sem, lead_send, lead_recv = refs[14:]
    z, y, c, x = coords()
    total = depth * 8
    me = lax.axis_index("blk") * 2 + lax.axis_index("head")
    rows_per = w_refs[0].shape[0]

    def view(item, zs, ys, cs, xs):
        buffer, first, last, kind = item
        return out_refs[buffer].at[pl.ds(first, last - first), zs, ys, cs, xs]

    all_barrier(total, me)
    own_small = pltpu.make_async_copy(small_ref, small_out.at[me], misc_sem.at[1])
    own_small.start()

    def send_small(step, carry):
        peer = lax.rem(me + step, total)
        remote(
            small_ref, small_out.at[me], misc_sem.at[0], misc_sem.at[1], (peer // 2, lax.rem(peer, 2))
        ).start()
        return carry

    own = []
    for index, item in enumerate(items):
        buffer, first, last, kind = item
        width = out_refs[buffer].shape[-1]
        copies = []
        for block in range(first, last):
            if buffer == 1:
                src = w_refs[1 + block]
            else:
                src = w_refs[2 * buffer].at[:, pl.ds(block * width, width)]
            copies.append((src, out_refs[buffer].at[block, z, y, c, x]))
        for src, dst in copies:
            copy = pltpu.make_async_copy(src, dst, own_sem.at[index])
            copy.start()
        own.append(pltpu.make_async_copy(view(item, z, y, c, x), view(item, z, y, c, x), own_sem.at[index]))
    lax.fori_loop(1, total, send_small, 0)
    prev = lax.rem(me + total - 1, total)
    prev_at = (prev // 2, lax.rem(prev, 2))
    leads = [
        remote(hid_ref.at[:, pl.ds(0, 64)], lead_hid, lead_send.at[0], lead_recv.at[0], prev_at),
        remote(grad_ref.at[:, pl.ds(0, 64)], lead_grad, lead_send.at[1], lead_recv.at[1], prev_at),
    ]

    whole = slice(None)

    def phase_one(index):
        own[index].wait()
        item = items[index]

        def send(step):
            other = lax.rem(z + step + 1, depth)
            remote(
                view(item, z, y, c, x), view(item, z, y, c, x),
                send_sem.at[index, 0], recv_sem.at[index, 0], place(other, y, c, x),
            ).start()

        loop(depth - 1, send)

    def bulk(index, phase):
        item = items[index]
        first_x = item[3] == 0
        if phase == 1:
            ref = view(item, whole, y, c, x)
            where = place(z, y, c, 1 - x) if first_x else place(z, 1 - y, c, x)
        elif phase == 2:
            ref = view(item, whole, y, c, whole) if first_x else view(item, whole, whole, c, x)
            where = place(z, 1 - y, c, x) if first_x else place(z, y, c, 1 - x)
        else:
            ref = view(item, whole, whole, c, whole)
            where = place(z, y, 1 - c, x)
        return remote(ref, ref, send_sem.at[index, phase], recv_sem.at[index, phase], where)

    def arrived(index, phase):
        item = items[index]
        if phase == 0:
            ref = view(item, pl.ds(0, depth - 1), y, c, x)
            pltpu.make_async_copy(ref, ref, recv_sem.at[index, 0]).wait()
        else:
            bulk(index, phase).wait_recv()

    def sent(index, phase):
        item = items[index]
        if phase == 0:
            ref = view(item, pl.ds(0, depth - 1), y, c, x)
            pltpu.make_async_copy(ref, ref, send_sem.at[index, 0]).wait()
        else:
            bulk(index, phase).wait_send()

    pairs = (count + 1) // 2
    for step in range(pairs + 2 * 4):
        for phase in range(4, -1, -1):
            pair = step - 2 * phase
            if not 0 <= pair < pairs:
                continue
            for index in range(2 * pair, min(2 * pair + 2, count)):
                if phase == 0:
                    phase_one(index)
                else:
                    arrived(index, phase - 1)
                    if phase < 4:
                        bulk(index, phase).start()
        if step == 0:
            for lead in leads:
                lead.start()
    for index in range(count):
        for phase in range(4):
            sent(index, phase)
    for lead in leads:
        lead.wait()
    pltpu.make_async_copy(small_out, small_out, misc_sem.at[1]).wait()
    rest = small_out.at[pl.ds(0, total - 1)]
    pltpu.make_async_copy(rest, rest, misc_sem.at[0]).wait()


def gather_all(depth, w_qkv, w_attn_out, w_cross_q, w_cross_out, w_kv, small, hidden, grads):
    total = depth * 8
    rows = w_qkv.shape[0]
    items = [
        (0, 0, 3, 0), (0, 3, 6, 1),
        (2, 0, 1, 0), (2, 1, 2, 1),
        (1, 0, 1, 0), (1, 1, 2, 1),
        (1, 2, 3, 0),
    ]
    shapes = [
        (6, depth, 2, 2, 2, rows, w_qkv.shape[1] // 6),
        (3, depth, 2, 2, 2, rows, w_attn_out.shape[1]),
        (2, depth, 2, 2, 2, rows, w_kv.shape[1] // 2),
    ]
    lead_shape = (hidden.shape[0], 64, hidden.shape[2])
    outs = [jax.ShapeDtypeStruct(shape, jnp.bfloat16) for shape in shapes]
    outs += [jax.ShapeDtypeStruct((total,) + small.shape, small.dtype)]
    outs += [jax.ShapeDtypeStruct(lead_shape, jnp.bfloat16)] * 2
    count = len(items)
    return pl.pallas_call(
        functools.partial(gather_kernel, depth, items),
        out_shape=outs,
        in_specs=[ANY] * 8,
        out_specs=[ANY] * 6,
        scratch_shapes=[
            pltpu.SemaphoreType.DMA((count,)),
            pltpu.SemaphoreType.DMA((count, 4)),
            pltpu.SemaphoreType.DMA((count, 4)),
            pltpu.SemaphoreType.DMA((2,)),
            pltpu.SemaphoreType.DMA((2,)),
            pltpu.SemaphoreType.DMA((2,)),
        ],
        compiler_params=pltpu.CompilerParams(collective_id=0, has_side_effects=True),
    )(w_qkv, w_attn_out, w_cross_q, w_cross_out, w_kv, small, hidden, grads)


def unit_of(device, total):
    if total == 32:
        depth = device // 8
        middle = (depth == 1) | (depth == 2)
        end = 16 + (depth // 3) * 4 + (lax.rem(device, 8) // 4) * 2 + lax.rem(device, 2)
        unit = jnp.where(middle, device - 8, end)
        return unit, middle | (lax.rem(device // 2, 2) == 0)
    stride = total // UNITS
    return jnp.minimum(device // stride, UNITS - 1), (lax.rem(device, stride) == 0) & (device // stride < UNITS)


def to_units_kernel(total, src, dst, send_sem, recv_sem):
    me = lax.axis_index("blk") * 2 + lax.axis_index("head")
    mine, holder = unit_of(me, total)
    all_barrier(total, me)
    lanes = src.shape[-1]

    def slot(device):
        return dst.at[:, :, pl.ds(pl.multiple_of(device * lanes, 128), lanes)]

    @pl.when(holder)
    def _():
        pltpu.make_async_copy(src.at[mine], slot(me), recv_sem).start()

    def send(step, carry):
        peer = lax.rem(me + step, total)
        unit, held = unit_of(peer, total)

        @pl.when(held)
        def _():
            remote(src.at[unit], slot(me), send_sem, recv_sem, (peer // 2, lax.rem(peer, 2))).start()

        return carry

    lax.fori_loop(1, total, send, 0)

    @pl.when(holder)
    def _():
        part = src.at[pl.ds(0, UNITS - 1)]
        pltpu.make_async_copy(dst, dst, recv_sem).wait()
        pltpu.make_async_copy(part, part, send_sem).wait()

    @pl.when(jnp.logical_not(holder))
    def _():
        pltpu.make_async_copy(src, src, send_sem).wait()


def to_units(total, message, collective):
    units, parts, width, lanes = message.shape
    return pl.pallas_call(
        functools.partial(to_units_kernel, total),
        out_shape=jax.ShapeDtypeStruct((parts, width, lanes * total), message.dtype),
        in_specs=[ANY],
        out_specs=ANY,
        scratch_shapes=[pltpu.SemaphoreType.DMA, pltpu.SemaphoreType.DMA],
        compiler_params=pltpu.CompilerParams(collective_id=collective, has_side_effects=True),
    )(message)


def to_tokens_kernel(total, extras, *refs):
    src = refs[0]
    extra_in = refs[1 : 1 + extras]
    dst = refs[1 + extras]
    extra_out = refs[2 + extras : 2 + 2 * extras]
    send_sem, recv_sem, extra_send, extra_recv = refs[2 + 2 * extras :]
    me = lax.axis_index("blk") * 2 + lax.axis_index("head")
    mine, holder = unit_of(me, total)
    all_barrier(total, me)
    lanes = dst.shape[-1]
    after = lax.rem(me + 1, total)
    moves = [
        remote(
            extra_in[index], extra_out[index], extra_send.at[index], extra_recv.at[index],
            (after // 2, lax.rem(after, 2)),
        )
        for index in range(extras)
    ]
    for move in moves:
        move.start()

    def slot(device):
        return src.at[:, :, pl.ds(pl.multiple_of(device * lanes, 128), lanes)]

    @pl.when(holder)
    def _():
        pltpu.make_async_copy(slot(me), dst.at[mine], recv_sem).start()

        def send(step, carry):
            peer = lax.rem(me + step, total)
            remote(
                slot(peer), dst.at[mine], send_sem, recv_sem, (peer // 2, lax.rem(peer, 2))
            ).start()
            return carry

        lax.fori_loop(1, total, send, 0)

    pltpu.make_async_copy(dst, dst, recv_sem).wait()

    @pl.when(holder)
    def _():
        part = src.at[:, :, pl.ds(0, lanes * (total - 1))]
        pltpu.make_async_copy(part, part, send_sem).wait()

    for move in moves:
        move.wait()


def to_tokens(total, units, extra, collective):
    parts, width, length = units.shape
    count = len(extra)
    result = jax.ShapeDtypeStruct((UNITS, parts, width, length // total), units.dtype)
    return pl.pallas_call(
        functools.partial(to_tokens_kernel, total, count),
        out_shape=[result] + [jax.ShapeDtypeStruct(e.shape, e.dtype) for e in extra],
        in_specs=[ANY] * (1 + count),
        out_specs=[ANY] * (1 + count),
        scratch_shapes=[
            pltpu.SemaphoreType.DMA,
            pltpu.SemaphoreType.DMA,
            pltpu.SemaphoreType.DMA((max(count, 1),)),
            pltpu.SemaphoreType.DMA((max(count, 1),)),
        ],
        compiler_params=pltpu.CompilerParams(collective_id=collective, has_side_effects=True),
    )(units, *extra)


def scatter_kernel(depth, items, *refs):
    count = len(items)
    total = depth * 8
    d_refs = refs[:3]
    gain_ref = refs[3]
    out_refs = refs[4:7]
    gain_out = refs[7]
    own = refs[8 : 8 + count]
    got_core = refs[8 + count : 8 + 2 * count]
    got_one = refs[8 + 2 * count : 8 + 3 * count]
    got_two = refs[8 + 3 * count : 8 + 4 * count]
    got_z = refs[8 + 4 * count : 8 + 5 * count]
    gains, local_sem, send_sem, recv_sem, gain_sem = refs[8 + 5 * count :]
    z, y, c, x = coords()
    me = lax.axis_index("blk") * 2 + lax.axis_index("head")
    all_barrier(total, me)
    whole = slice(None)

    pltpu.make_async_copy(gain_ref.at[me], gains.at[me], gain_sem.at[1]).start()

    def send_gain(step, carry):
        peer = lax.rem(me + step, total)
        remote(
            gain_ref.at[peer], gains.at[me], gain_sem.at[0], gain_sem.at[1], (peer // 2, lax.rem(peer, 2))
        ).start()
        return carry

    def local(index):
        buffer, first, last, kind = items[index]
        src = d_refs[buffer].at[pl.ds(first, last - first), whole, whole, c]
        return pltpu.make_async_copy(src, own[index], local_sem.at[index])

    def core(index):
        buffer, first, last, kind = items[index]
        src = d_refs[buffer].at[pl.ds(first, last - first), whole, whole, 1 - c]
        return remote(
            src, got_core[index], send_sem.at[index, 0], recv_sem.at[index, 0], place(z, y, 1 - c, x)
        )

    def one(index):
        if items[index][3] == 0:
            src, where = own[index].at[whole, whole, 1 - y], place(z, 1 - y, c, x)
        else:
            src, where = own[index].at[whole, whole, whole, 1 - x], place(z, y, c, 1 - x)
        return remote(src, got_one[index], send_sem.at[index, 1], recv_sem.at[index, 1], where)

    def two(index):
        if items[index][3] == 0:
            src, where = own[index].at[whole, whole, y, 1 - x], place(z, y, c, 1 - x)
        else:
            src, where = own[index].at[whole, whole, 1 - y, x], place(z, 1 - y, c, x)
        return remote(src, got_two[index], send_sem.at[index, 2], recv_sem.at[index, 2], where)

    def send_z(index):
        def send(step):
            other = lax.rem(z + step + 1, depth)
            remote(
                own[index].at[whole, other, y, x], got_z[index].at[z],
                send_sem.at[index, 3], recv_sem.at[index, 3], place(other, y, c, x),
            ).start()

        loop(depth - 1, send)

    def add_into(target, source):
        target[...] = (target[...].astype(jnp.float32) + source[...].astype(jnp.float32)).astype(
            jnp.bfloat16
        )

    def sum_core(index):
        blocks = own[index].shape[0]

        def body(step):
            block, level = step // depth, lax.rem(step, depth)
            for row in range(2):
                for col in range(2):
                    add_into(own[index].at[block, level, row, col], got_core[index].at[block, level, row, col])

        lax.fori_loop(0, blocks * depth, lambda step, carry: (body(step), carry)[1], 0)

    def sum_one(index):
        blocks = own[index].shape[0]

        def body(step):
            block, level = step // depth, lax.rem(step, depth)
            for side in range(2):
                if items[index][3] == 0:
                    target = own[index].at[block, level, y, side]
                else:
                    target = own[index].at[block, level, side, x]
                add_into(target, got_one[index].at[block, level, side])

        lax.fori_loop(0, blocks * depth, lambda step, carry: (body(step), carry)[1], 0)

    def sum_two(index):
        blocks = own[index].shape[0]

        def body(step):
            block, level = step // depth, lax.rem(step, depth)
            add_into(own[index].at[block, level, y, x], got_two[index].at[block, level])

        lax.fori_loop(0, blocks * depth, lambda step, carry: (body(step), carry)[1], 0)

    def sum_z(index):
        buffer, first, last, kind = items[index]
        for block in range(last - first):
            running = own[index][block, z, y, x].astype(jnp.float32)

            def body(step, value):
                other = lax.rem(z + step, depth)
                return value + got_z[index][other, block].astype(jnp.float32)

            out_refs[buffer][first + block] = lax.fori_loop(1, depth, body, running)

    for index in range(count):
        local(index).start()
    pairs = (count + 1) // 2
    for step in range(pairs + 4):
        for phase in range(4, -1, -1):
            pair = step - phase
            if not 0 <= pair < pairs:
                continue
            for index in range(2 * pair, min(2 * pair + 2, count)):
                if phase == 0:
                    core(index).start()
                elif phase == 1:
                    local(index).wait()
                    core(index).wait_recv()
                    sum_core(index)
                    one(index).start()
                elif phase == 2:
                    one(index).wait_recv()
                    sum_one(index)
                    two(index).start()
                elif phase == 3:
                    two(index).wait_recv()
                    sum_two(index)
                    send_z(index)
                else:
                    landed = got_z[index].at[pl.ds(0, depth - 1)]
                    pltpu.make_async_copy(landed, landed, recv_sem.at[index, 3]).wait()
                    sum_z(index)
        if step == 0:
            lax.fori_loop(1, total, send_gain, 0)
    pltpu.make_async_copy(gains, gains, gain_sem.at[1]).wait()
    gain_out[...] = jnp.sum(gains[...], axis=0)
    for index in range(count):
        core(index).wait_send()
        one(index).wait_send()
        two(index).wait_send()
        gone = got_z[index].at[pl.ds(0, depth - 1)]
        pltpu.make_async_copy(gone, gone, send_sem.at[index, 3]).wait()
    rest = gains.at[pl.ds(0, total - 1)]
    pltpu.make_async_copy(rest, rest, gain_sem.at[0]).wait()


def scatter_all(depth, d_qkv, d_squares, d_kv, d_gains, collective):
    items = [
        (0, 0, 3, 0), (0, 3, 6, 1),
        (2, 0, 1, 0), (2, 1, 2, 1),
        (1, 0, 1, 0), (1, 1, 2, 1),
        (1, 2, 3, 0),
    ]
    count = len(items)
    parts = (d_qkv, d_squares, d_kv)
    own, core, one, two, along = [], [], [], [], []
    for buffer, first, last, kind in items:
        rows, width = parts[buffer].shape[-2:]
        blocks = last - first
        own.append(pltpu.VMEM((blocks, depth, 2, 2, rows, width), jnp.bfloat16))
        core.append(pltpu.VMEM((blocks, depth, 2, 2, rows, width), jnp.bfloat16))
        one.append(pltpu.VMEM((blocks, depth, 2, rows, width), jnp.bfloat16))
        two.append(pltpu.VMEM((blocks, depth, rows, width), jnp.bfloat16))
        along.append(pltpu.VMEM((depth, blocks, rows, width), jnp.bfloat16))
    outs = [jax.ShapeDtypeStruct((p.shape[0],) + p.shape[-2:], jnp.float32) for p in parts]
    outs.append(jax.ShapeDtypeStruct(d_gains.shape[1:], jnp.float32))
    vmem = pl.BlockSpec(memory_space=pltpu.VMEM)
    return pl.pallas_call(
        functools.partial(scatter_kernel, depth, items),
        out_shape=outs,
        in_specs=[ANY] * 4,
        out_specs=[vmem] * 4,
        scratch_shapes=own + core + one + two + along + [
            pltpu.VMEM(d_gains.shape, jnp.float32),
            pltpu.SemaphoreType.DMA((count,)),
            pltpu.SemaphoreType.DMA((count, 4)),
            pltpu.SemaphoreType.DMA((count, 4)),
            pltpu.SemaphoreType.DMA((2,)),
        ],
        compiler_params=pltpu.CompilerParams(
            collective_id=collective, has_side_effects=True, vmem_limit_bytes=60 * 2**20
        ),
    )(d_qkv, d_squares, d_kv, d_gains)


HEADS = 12
HEAD_DIM = 64
SPAN = 64
NEIGHBOURS = 2
NEIGH_LEN = 128
MICRO = 2
UNITS = MICRO * HEADS
AXES = ("blk", "head")
TILE = 512
LEAD = SPAN - 1
DOC_MAX = 2000
SCORE_SCALE = 1.0 / math.sqrt(HEAD_DIM)
LOG2E = math.log2(math.e)


def tile_at(ref, index, row):
    return ref[row, :, pl.ds(pl.multiple_of(index * TILE, TILE), TILE)]


def row_at(ref, index):
    return ref[:, pl.ds(pl.multiple_of(index * TILE, TILE), TILE)]


def tile_mask(key_tile, query_tile, first_row, diagonal=True):
    key_place = key_tile * TILE + lax.broadcasted_iota(jnp.int32, (TILE, 1), 0)
    allowed = key_place >= first_row
    if diagonal:
        query_place = query_tile * TILE + lax.broadcasted_iota(jnp.int32, (1, TILE), 1)
        allowed = allowed & (key_place <= query_place)
    return allowed


def attn_forward_kernel(low_ref, first_ref, qkv_ref, shifted_ref, mixed_ref, total_ref):
    tiles = qkv_ref.shape[-1] // TILE

    def one_query(query_tile, carry):
        query_t = tile_at(qkv_ref, query_tile, 0)
        first_row = row_at(first_ref, query_tile)

        def one_key(step, state):
            peak, weight, mixed = state
            key_tile = query_tile - step
            keys = tile_at(qkv_ref, key_tile, 1).T
            scores = jnp.dot(keys, query_t, preferred_element_type=jnp.float32) * (SCORE_SCALE * LOG2E)
            scores = jnp.where(tile_mask(key_tile, query_tile, first_row), scores, -1e30)
            new_peak = jnp.maximum(peak, jnp.max(scores, axis=0, keepdims=True))
            probs = jnp.exp2(scores - new_peak)
            fade = jnp.exp2(peak - new_peak)
            weight = weight * fade + jnp.sum(probs, axis=0, keepdims=True)
            mixed = mixed * fade + jnp.dot(
                tile_at(qkv_ref, key_tile, 2), probs.astype(jnp.bfloat16), preferred_element_type=jnp.float32
            )
            return new_peak, weight, mixed

        start = (
            jnp.full((1, TILE), -1e30, jnp.float32),
            jnp.zeros((1, TILE), jnp.float32),
            jnp.zeros((HEAD_DIM, TILE), jnp.float32),
        )
        steps = query_tile + 1 - low_ref[query_tile]
        peak, weight, mixed = lax.fori_loop(0, steps, one_key, start)
        columns = pl.ds(pl.multiple_of(query_tile * TILE, TILE), TILE)
        mixed_ref[:, columns] = mixed / weight
        total_ref[:, columns] = peak + jnp.log2(weight)
        return carry

    lax.fori_loop(0, tiles, one_query, 0)
    length = qkv_ref.shape[-1]

    def turn(step, carry):
        rows = pl.ds(pl.multiple_of(step * 16, 16), 16)
        shifted_ref[rows, :] = pltpu.roll(mixed_ref[rows, :], length - LEAD, 1).astype(jnp.bfloat16)
        return carry

    lax.fori_loop(0, HEAD_DIM // 16, turn, 0)


def attn_backward_kernel(
    low_ref, high_ref, first_ref, qkv_ref, shifted_ref, mixed_ref, total_ref, out_ref, grad_ref, dq_ref, delta_ref
):
    length = qkv_ref.shape[-1]
    tiles = length // TILE
    delta_ref[...] = jnp.zeros_like(delta_ref)

    def turn(step, carry):
        rows = pl.ds(pl.multiple_of(step * 16, 16), 16)
        grad = pltpu.roll(shifted_ref[rows, :].astype(jnp.float32), LEAD, 1)
        grad_ref[rows, :] = grad.astype(jnp.bfloat16)
        delta_ref[...] += jnp.sum(grad * mixed_ref[rows, :], axis=0, keepdims=True)
        dq_ref[rows, :] = jnp.zeros((16, length), jnp.float32)
        return carry

    lax.fori_loop(0, HEAD_DIM // 16, turn, 0)

    def one_key(key_tile, carry):
        key_t = tile_at(qkv_ref, key_tile, 1)
        keys = key_t.T
        values = tile_at(qkv_ref, key_tile, 2).T

        def one_query(query_tile, state, diagonal=False):
            d_key, d_value = state
            query_t = tile_at(qkv_ref, query_tile, 0)
            grad_t = row_at(grad_ref, query_tile)
            scores = jnp.dot(keys, query_t, preferred_element_type=jnp.float32) * (SCORE_SCALE * LOG2E)
            allowed = tile_mask(key_tile, query_tile, row_at(first_ref, query_tile), diagonal)
            probs = jnp.where(allowed, jnp.exp2(scores - row_at(total_ref, query_tile)), 0.0)
            d_probs = jnp.dot(values, grad_t, preferred_element_type=jnp.float32)
            d_scores = (probs * (d_probs - row_at(delta_ref, query_tile))).astype(jnp.bfloat16)
            d_value = d_value + jnp.dot(
                probs.astype(jnp.bfloat16), grad_t.T, preferred_element_type=jnp.float32
            )
            d_key = d_key + jnp.dot(d_scores, query_t.T, preferred_element_type=jnp.float32)
            columns = pl.ds(pl.multiple_of(query_tile * TILE, TILE), TILE)
            dq_ref[:, columns] += jnp.dot(key_t, d_scores, preferred_element_type=jnp.float32)
            return d_key, d_value

        zeros = jnp.zeros((TILE, HEAD_DIM), jnp.float32)
        @pl.when(high_ref[key_tile] > key_tile)
        def _():
            state = one_query(key_tile, (zeros, zeros), diagonal=True)
            d_key, d_value = lax.fori_loop(key_tile + 1, high_ref[key_tile], one_query, state)
            columns = pl.ds(pl.multiple_of(key_tile * TILE, TILE), TILE)
            out_ref[1, :, columns] = (d_key * SCORE_SCALE).T.astype(jnp.bfloat16)
            out_ref[2, :, columns] = d_value.T.astype(jnp.bfloat16)

        return carry

    lax.fori_loop(0, tiles, one_key, 0)

    def finish(step, carry):
        rows = pl.ds(pl.multiple_of(step * 16, 16), 16)
        out_ref[0, rows, :] = (dq_ref[rows, :] * SCORE_SCALE).astype(jnp.bfloat16)
        return carry

    lax.fori_loop(0, HEAD_DIM // 16, finish, 0)


SMEM = pl.BlockSpec(memory_space=pltpu.SMEM)
VMEM = pl.BlockSpec(memory_space=pltpu.VMEM)


def local_params():
    return pltpu.CompilerParams(vmem_limit_bytes=60 * 2**20)


def attn_forward(low, first, qkv):
    width, length = qkv.shape[1:]
    return pl.pallas_call(
        attn_forward_kernel,
        out_shape=[
            jax.ShapeDtypeStruct((width, length), jnp.bfloat16),
            jax.ShapeDtypeStruct((width, length), jnp.float32),
            jax.ShapeDtypeStruct((1, length), jnp.float32),
        ],
        in_specs=[SMEM, VMEM, VMEM],
        out_specs=[VMEM] * 3,
        compiler_params=local_params(),
        cost_estimate=pl.CostEstimate(flops=10**9, bytes_accessed=4 * 10**6, transcendentals=4 * 10**6),
    )(low, first, qkv)


def attn_backward(low, high, first, qkv, shifted, mixed, totals):
    width, length = qkv.shape[1:]
    return pl.pallas_call(
        attn_backward_kernel,
        out_shape=jax.ShapeDtypeStruct((3, width, length), jnp.bfloat16),
        in_specs=[SMEM, SMEM] + [VMEM] * 5,
        out_specs=VMEM,
        scratch_shapes=[
            pltpu.VMEM((width, length), jnp.bfloat16),
            pltpu.VMEM((width, length), jnp.float32),
            pltpu.VMEM((1, length), jnp.float32),
        ],
        compiler_params=local_params(),
        cost_estimate=pl.CostEstimate(flops=3 * 10**9, bytes_accessed=4 * 10**6, transcendentals=4 * 10**6),
    )(low, high, first, qkv, shifted, mixed, totals)


def dot_nn(left, right):
    return jnp.dot(left, right, preferred_element_type=jnp.float32)


def dot_nt(left, right):
    return lax.dot_general(left, right, (((1,), (1,)), ((), ())), preferred_element_type=jnp.float32)


def dot_tn(left, right):
    return lax.dot_general(left, right, (((0,), (0,)), ((), ())), preferred_element_type=jnp.float32)


def norm_parts(values):
    centred = values - jnp.mean(values, axis=-1, keepdims=True)
    scale = lax.rsqrt(jnp.mean(centred * centred, axis=-1, keepdims=True) + 1e-05)
    return centred * scale, scale


def norm_pull(values, gain, grad):
    unit, scale = norm_parts(values)
    scaled = grad * gain
    pulled = scale * (
        scaled
        - jnp.mean(scaled, axis=-1, keepdims=True)
        - unit * jnp.mean(scaled * unit, axis=-1, keepdims=True)
    )
    return pulled, jnp.sum(grad * unit, axis=0, keepdims=True)


def shift_rows(rows, lead):
    joined = jnp.concatenate([rows.astype(jnp.float32), lead.astype(jnp.float32)], axis=0)
    return pltpu.roll(joined, joined.shape[0] - LEAD, 0)[: rows.shape[0]]


def stack_pair(rows):
    lane = lax.broadcasted_iota(jnp.int32, rows.shape, 1)
    zero = jnp.zeros_like(rows)
    return jnp.concatenate(
        [jnp.where(lane < HEAD_DIM, rows, zero), jnp.where(lane < HEAD_DIM, zero, rows)], axis=0
    )


def unstack_pair(rows):
    lane = lax.broadcasted_iota(jnp.int32, (SPAN, 2 * HEAD_DIM), 1)
    return jnp.where(lane < HEAD_DIM, rows[:SPAN], rows[SPAN:])


def middle_kernel(
    att_ref, hid_ref, lead_hid_ref, grad_ref, lead_grad_ref, gain_ref, used_ref, sq_ref, kv_hbm, neigh_hbm,
    up_hbm, down_hbm,
    result_ref, first_ref, d_att_ref, n2_ref, d_cq_ref, cm_ref, gc_ref, ga_ref, gy_ref, act_ref, d_pair_ref,
    d_gain_ref, d_up_hbm,
    kv_ref, neigh_ref, up_ref, down_ref, att_rows, second_ref, cq_ref, pair_ref, prob_ref, acc_ref, d_n3_ref,
    n3_ref, n3t_ref, d_up_ref, sems,
):
    micro, tokens, width = hid_ref.shape
    rows = micro * tokens
    pulls = [
        pltpu.make_async_copy(src, dst, sems.at[index])
        for index, (src, dst) in enumerate(
            [(kv_hbm, kv_ref), (neigh_hbm, neigh_ref), (up_hbm, up_ref), (down_hbm, down_ref)]
        )
    ]
    for pull in pulls:
        pull.start()
    gain_cross, gain_mlp = gain_ref[1:2, :], gain_ref[2:3, :]
    for index in range(micro):
        part = pl.ds(index * tokens, tokens)
        hidden = shift_rows(hid_ref[index], lead_hid_ref[index])
        gy_ref[part, :] = shift_rows(grad_ref[index], lead_grad_ref[index]).astype(jnp.bfloat16)
        first_ref[part, :] = hidden + dot_tn(att_ref[index], sq_ref[0])
    n2_ref[...] = (norm_parts(first_ref[...])[0] * gain_cross).astype(jnp.bfloat16)
    cq_ref[...] = dot_nn(n2_ref[...], sq_ref[1]).astype(jnp.bfloat16)

    pulls[0].wait()
    pulls[1].wait()
    chunk = 256
    chunks = neigh_ref.shape[0] // chunk

    def make_pairs(step, carry):
        side, block = step // chunks, lax.rem(step, chunks)
        part = pl.ds(pl.multiple_of(block * chunk, chunk), chunk)
        pair_ref[side, part, :] = dot_nn(neigh_ref[part, :], kv_ref[side]).astype(jnp.bfloat16)
        return carry

    lax.fori_loop(0, 2 * chunks, make_pairs, 0)
    couples = HEADS // 2
    pair_rows = NEIGHBOURS * NEIGH_LEN
    groups = rows // SPAN

    def where(step):
        group, couple = step // couples, lax.rem(step, couples)
        tok = pl.ds(pl.multiple_of(group * SPAN, SPAN), SPAN)
        key = pl.ds(pl.multiple_of(group * pair_rows, pair_rows), pair_rows)
        lanes = pl.ds(pl.multiple_of(couple * 2 * HEAD_DIM, 2 * HEAD_DIM), 2 * HEAD_DIM)
        return tok, key, lanes

    def cross_step(step, carry):
        tok, key, lanes = where(step)
        query = stack_pair(cq_ref[tok, lanes])
        scores = dot_nt(query, pair_ref[0, key, lanes]) * SCORE_SCALE
        weights = jnp.exp(scores - jnp.max(scores, axis=-1, keepdims=True))
        probs = weights / jnp.sum(weights, axis=-1, keepdims=True)
        prob_ref[step] = probs
        mixed = unstack_pair(dot_nn(probs.astype(jnp.bfloat16), pair_ref[1, key, lanes]))
        cm_ref[tok, lanes] = (mixed * used_ref[tok, :]).astype(jnp.bfloat16)
        return carry

    lax.fori_loop(0, groups * couples, cross_step, 0)
    second_ref[...] = first_ref[...] + dot_nn(cm_ref[...], sq_ref[2])
    n3 = (norm_parts(second_ref[...])[0] * gain_mlp).astype(jnp.bfloat16)
    n3_ref[...] = n3
    n3t_ref[...] = n3.T
    acc_ref[...] = second_ref[...]
    d_n3_ref[...] = jnp.zeros_like(d_n3_ref)
    pulls[2].wait()
    pulls[3].wait()
    ff_blocks = up_ref.shape[0]

    def mlp_step(step, carry):
        cols = pl.ds(pl.multiple_of(step * width, width), width)
        upper = dot_nn(n3_ref[...], up_ref[step])
        square = upper * upper
        flat = jnp.tanh(math.sqrt(2.0 / math.pi) * upper * (1.0 + 0.044715 * square))
        half = 0.5 * (1.0 + flat)
        active = (upper * half).astype(jnp.bfloat16)
        act_ref[:, cols] = active
        slope = half + 0.5 * upper * (1.0 - flat * flat) * math.sqrt(2.0 / math.pi) * (
            1.0 + 3.0 * 0.044715 * square
        )
        d_upper = (dot_nt(gy_ref[...], down_ref[cols, :]) * slope).astype(jnp.bfloat16)
        acc_ref[...] += dot_nn(active, down_ref[cols, :])
        d_n3_ref[...] += dot_nt(d_upper, up_ref[step])
        d_up_ref[:, cols] = dot_nn(n3t_ref[...], d_upper).astype(jnp.bfloat16)
        pltpu.make_async_copy(d_up_ref.at[:, cols], d_up_hbm.at[:, cols], sems.at[4]).start()
        return carry

    lax.fori_loop(0, ff_blocks, mlp_step, 0)
    result_ref[...] = acc_ref[...].astype(jnp.bfloat16)
    pulled, d_gain_mlp = norm_pull(second_ref[...], gain_mlp, d_n3_ref[...])
    d_second = gy_ref[...].astype(jnp.float32) + pulled
    acc_ref[...] = d_second
    gc_ref[...] = d_second.astype(jnp.bfloat16)
    att_rows[...] = (
        dot_nt(gc_ref[...], sq_ref[2]).astype(jnp.bfloat16).astype(jnp.float32) * used_ref[...]
    ).astype(jnp.bfloat16)

    def cross_back(step, carry):
        tok, key, lanes = where(step)
        grad = stack_pair(att_rows[tok, lanes])
        query = stack_pair(cq_ref[tok, lanes])
        probs = prob_ref[step]
        d_probs = dot_nt(grad, pair_ref[1, key, lanes])
        d_scores = (
            probs * (d_probs - jnp.sum(probs * d_probs, axis=-1, keepdims=True))
        ).astype(jnp.bfloat16)
        d_query = unstack_pair(dot_nn(d_scores, pair_ref[0, key, lanes]))
        d_cq_ref[tok, lanes] = (d_query * SCORE_SCALE).astype(jnp.bfloat16)
        d_pair_ref[0, key, lanes] = (dot_tn(d_scores, query) * SCORE_SCALE).astype(jnp.bfloat16)
        d_pair_ref[1, key, lanes] = dot_tn(probs.astype(jnp.bfloat16), grad).astype(jnp.bfloat16)
        return carry

    lax.fori_loop(0, groups * couples, cross_back, 0)
    pulled, d_gain_cross = norm_pull(first_ref[...], gain_cross, dot_nt(d_cq_ref[...], sq_ref[1]))
    d_first = acc_ref[...] + pulled
    first_ref[...] = d_first
    ga_ref[...] = d_first.astype(jnp.bfloat16)
    for index in range(micro):
        d_att_ref[index] = dot_nt(sq_ref[0], ga_ref[pl.ds(index * tokens, tokens), :]).astype(jnp.bfloat16)
    d_gain_ref[...] = jnp.concatenate([d_gain_cross, d_gain_mlp, jnp.zeros((6, width), jnp.float32)], axis=0)
    pltpu.make_async_copy(d_up_ref, d_up_hbm, sems.at[4]).wait()


def middle(attended_t, hidden, lead_hid, grads, lead_grad, gains, used, squares, kv, neigh, up, down):
    micro, tokens, width = hidden.shape
    rows = micro * tokens
    ff = up.shape[0] * width
    low = jnp.bfloat16
    out_shape = [
        jax.ShapeDtypeStruct((rows, width), low),
        jax.ShapeDtypeStruct((rows, width), jnp.float32),
        jax.ShapeDtypeStruct((micro, width, tokens), low),
        jax.ShapeDtypeStruct((rows, width), low),
        jax.ShapeDtypeStruct((rows, width), low),
        jax.ShapeDtypeStruct((rows, width), low),
        jax.ShapeDtypeStruct((rows, width), low),
        jax.ShapeDtypeStruct((rows, width), low),
        jax.ShapeDtypeStruct((rows, width), low),
        jax.ShapeDtypeStruct((rows, ff), low),
        jax.ShapeDtypeStruct((2,) + neigh.shape, low),
        jax.ShapeDtypeStruct((8, width), jnp.float32),
        jax.ShapeDtypeStruct((width, ff), low),
    ]
    steps = rows // SPAN * HEADS // 2
    scratch = [
        pltpu.VMEM(kv.shape, low),
        pltpu.VMEM(neigh.shape, low),
        pltpu.VMEM(up.shape, low),
        pltpu.VMEM(down.shape, low),
        pltpu.VMEM((rows, width), low),
        pltpu.VMEM((rows, width), jnp.float32),
        pltpu.VMEM((rows, width), low),
        pltpu.VMEM((2,) + neigh.shape, low),
        pltpu.VMEM((steps, 2 * SPAN, NEIGHBOURS * NEIGH_LEN), jnp.float32),
        pltpu.VMEM((rows, width), jnp.float32),
        pltpu.VMEM((rows, width), jnp.float32),
        pltpu.VMEM((rows, width), low),
        pltpu.VMEM((width, rows), low),
        pltpu.VMEM((width, ff), low),
        pltpu.SemaphoreType.DMA((5,)),
    ]
    return pl.pallas_call(
        middle_kernel,
        out_shape=out_shape,
        in_specs=[VMEM] * 8 + [ANY] * 4,
        out_specs=[VMEM] * 12 + [ANY],
        scratch_shapes=scratch,
        compiler_params=local_params(),
        cost_estimate=pl.CostEstimate(flops=12 * 10**9, bytes_accessed=40 * 10**6, transcendentals=10**6),
    )(attended_t, hidden, lead_hid, grads, lead_grad, gains, used, squares, kv, neigh, up, down)


PLAN = (0, 0, 1, 0, 0, 1, 0, 0, 1, 1, 1, 0)


def front_kernel(depth, items, *refs):
    count = len(items)
    w_refs = refs[:7]
    gain_in, seg_in, valid_in, neigh_ref, hid_ref, grad_hbm = refs[7:13]
    (
        qkv_out, sq_out, kv_out, up_out, down_out, d_up_hbm, unit_hbm, mixed_hbm, act_hbm, d_pair_hbm,
        gain_out, cos_out, sin_out, total_out, start_out, att_out,
        result_ref, first_ref, back_out, n2_ref, d_cq_ref, cm_ref, gc_ref, ga_ref, gy_ref, d_gain_ref,
    ) = refs[13:39]
    (
        qkv_ref, small_all, hid_vmem, grad_ref, lead_hid, lead_grad, n1_ref, temp_ref, note_ref, turned_ref, doc_ref,
        stage_ref, sq_ref, kv_ref, up_ref, down_ref,
        att_rows, second_ref, cq_ref, pair_ref, prob_ref, acc_ref, d_n3_ref, n3_ref, n3t_ref, d_up_ref,
        own_sem, send_sem, recv_sem, misc_sem, lead_send, lead_recv, load_sem, unit_send, unit_recv,
        att_send, att_recv, stage_sem, up_sem, grad_send, grad_recv, store_sem,
        unit_out, mixed_out, act_ref, d_pair_ref, d_att_ref, d_upper_ref, small_ref, used_ref,
    ) = refs[39:]
    z, y, c, x = coords()
    total = depth * 8
    me = lax.axis_index("blk") * 2 + lax.axis_index("head")
    mine, holder = unit_of(me, total)
    slab = w_refs[0].shape[0]
    micro, tokens, width = hid_ref.shape
    homes = (qkv_ref, sq_out, kv_out, up_out, down_out)
    whole = slice(None)

    def view(item, zs, ys, cs, xs):
        buffer, first, last, kind = item
        if buffer == 4:
            return down_out.at[zs, ys, cs, xs, pl.ds(first, last - first)]
        return homes[buffer].at[pl.ds(first, last - first), zs, ys, cs, xs]

    load = pltpu.make_async_copy(hid_ref, hid_vmem, load_sem.at[0])
    load.start()
    load_grad = pltpu.make_async_copy(grad_hbm, grad_ref, load_sem.at[2])
    load_grad.start()
    own = []
    for index, item in enumerate(items):
        buffer, first, last, kind = item
        cols = homes[buffer].shape[-1]
        if buffer == 4:
            moves = [(w_refs[6].at[pl.ds(first, last - first)], view(item, z, y, c, x))]
        elif buffer == 1:
            moves = [(w_refs[1 + block], sq_out.at[block, z, y, c, x]) for block in range(first, last)]
        else:
            source = w_refs[(0, None, 4, 5)[buffer]]
            moves = [
                (source.at[:, pl.ds(block * cols, cols)], homes[buffer].at[block, z, y, c, x])
                for block in range(first, last)
            ]
        for src, dst in moves:
            pltpu.make_async_copy(src, dst, own_sem.at[index]).start()
        mirror = view(item, z, y, c, x)
        own.append(pltpu.make_async_copy(mirror, mirror, own_sem.at[index]))
    turned_gain = gain_in[...].T[:32]
    lane_at = lax.broadcasted_iota(jnp.int32, (32, 128), 1)
    small_ref[0:32, :] = jnp.where(
        lane_at < 32, turned_gain[:, 0:1], jnp.where(lane_at < 64, turned_gain[:, 1:2], turned_gain[:, 2:3])
    ).astype(jnp.bfloat16)
    small_ref[32:48, :] = jnp.concatenate(
        [seg_in[...].astype(jnp.float32), jnp.zeros((16 - micro, 128), jnp.float32)], axis=0
    ).astype(jnp.bfloat16)
    row_at_ = lax.broadcasted_iota(jnp.int32, (micro * tokens, 1), 0)
    spans = tokens // SPAN
    flag = jnp.zeros((micro * tokens, 1), jnp.float32)
    for span in range(micro * spans):
        value = valid_in[span // spans, span % spans].astype(jnp.float32)
        flag = jnp.where(row_at_ // SPAN == span, value, flag)
    used_ref[...] = jnp.where(me * tokens + lax.rem(row_at_, tokens) + LEAD < tokens * total, flag, 0.0)
    pltpu.make_async_copy(small_ref, small_all.at[me], misc_sem.at[1]).start()
    all_barrier(total, me)

    def send_small(step, carry):
        peer = lax.rem(me + step, total)
        remote(
            small_ref, small_all.at[me], misc_sem.at[0], misc_sem.at[1], (peer // 2, lax.rem(peer, 2))
        ).start()
        return carry

    prev = lax.rem(me + total - 1, total)
    prev_at = (prev // 2, lax.rem(prev, 2))
    leads = [
        remote(hid_ref.at[:, pl.ds(0, 64)], lead_hid, lead_send.at[0], lead_recv.at[0], prev_at),
        remote(grad_hbm.at[:, pl.ds(0, 64)], lead_grad, lead_send.at[1], lead_recv.at[1], prev_at),
    ]

    def start(index):
        own[index].wait()
        item = items[index]
        for step in range(1, depth):
            other = lax.rem(z + step, depth)
            remote(
                view(item, z, y, c, x), view(item, z, y, c, x),
                send_sem.at[index, 0], recv_sem.at[index, 0], place(other, y, c, x),
            ).start()

    def bulk(index, phase):
        item = items[index]
        first_x = item[3] == 0
        if phase == 1:
            ref = view(item, whole, y, c, x)
            where = place(z, y, c, 1 - x) if first_x else place(z, 1 - y, c, x)
        elif phase == 2:
            ref = view(item, whole, y, c, whole) if first_x else view(item, whole, whole, c, x)
            where = place(z, 1 - y, c, x) if first_x else place(z, y, c, 1 - x)
        else:
            ref = view(item, whole, whole, c, whole)
            where = place(z, y, 1 - c, x)
        return remote(ref, ref, send_sem.at[index, phase], recv_sem.at[index, phase], where)

    def arrived(index, phase):
        if phase == 0:
            ref = view(items[index], pl.ds(0, depth - 1), y, c, x)
            pltpu.make_async_copy(ref, ref, recv_sem.at[index, 0]).wait()
        else:
            bulk(index, phase).wait_recv()

    def sent(index, phase):
        if phase == 0:
            ref = view(items[index], pl.ds(0, depth - 1), y, c, x)
            pltpu.make_async_copy(ref, ref, send_sem.at[index, 0]).wait()
        else:
            bulk(index, phase).wait_send()

    pairs = (count + 1) // 2

    def gather_step(step):
        for phase in range(4, -1, -1):
            pair = step - phase
            if not 0 <= pair < pairs:
                continue
            for index in range(2 * pair, min(2 * pair + 2, count)):
                if phase == 0:
                    start(index)
                else:
                    arrived(index, phase - 1)
                    if phase < 4:
                        bulk(index, phase).start()

    half_dim = HEAD_DIM // 2

    def tables():
        lane = lax.broadcasted_iota(jnp.int32, (half_dim, tokens), 1)
        order = lax.broadcasted_iota(jnp.int32, (half_dim, tokens), 0)
        frequency = jnp.exp(order.astype(jnp.float32) * (-2.0 * math.log(10000.0) / HEAD_DIM))
        angles = (me * tokens + lane).astype(jnp.float32) * frequency
        cos_out[...] = jnp.cos(angles)
        sin_out[...] = jnp.sin(angles)

    def normalise():
        load.wait()
        pltpu.make_async_copy(small_all, small_all, misc_sem.at[1]).wait()
        for peer in range(total):
            temp_ref[pl.ds(peer * slab, slab), pl.ds(0, 128)] = small_all[peer, :slab, :].astype(jnp.float32)
            doc_ref[pl.ds(peer, 1), :] = jnp.where(
                mine < HEADS, small_all[peer, 32:33, :].astype(jnp.float32), small_all[peer, 33:34, :].astype(jnp.float32)
            )
        turned = temp_ref[:, pl.ds(0, 128)].T
        gain_out[...] = jnp.concatenate(
            [turned[0:1], turned[32:33], turned[64:65], jnp.zeros((5, width), jnp.float32)], axis=0
        )
        for index in range(micro):
            unit_rows = norm_parts(hid_vmem[index].astype(jnp.float32))[0]
            n1_ref[pl.ds(index * tokens, tokens), :] = (unit_rows * gain_out[0:1, :]).astype(jnp.bfloat16)

    def project(part):
        cols = qkv_ref.shape[-1]
        heads = cols // HEAD_DIM
        for half in range(2):
            block = part * 2 + half
            for level in range(depth):
                for inner in range(8):
                    at = (level * 8 + inner) * slab
                    temp_ref[pl.ds(at, slab), :] = qkv_ref[
                        block, level, inner // 4, (inner // 2) % 2, inner % 2
                    ].astype(jnp.float32)
            raw = dot_nn(n1_ref[...], temp_ref[...].astype(jnp.bfloat16))
            for index in range(micro):
                raw_t = raw[index * tokens : (index + 1) * tokens].T
                for head in range(heads):
                    value = raw_t[head * HEAD_DIM : (head + 1) * HEAD_DIM]
                    if part < 2:
                        first_half, second_half = value[:half_dim], value[half_dim:]
                        value = jnp.concatenate(
                            [
                                first_half * cos_out[...] - second_half * sin_out[...],
                                second_half * cos_out[...] + first_half * sin_out[...],
                            ],
                            axis=0,
                        )
                    note_ref[index * HEADS + half * heads + head, part] = value.astype(jnp.bfloat16)

    def slot(device, part):
        return unit_out.at[part, :, pl.ds(pl.multiple_of(device * tokens, 128), tokens)]

    def send_part(part):
        @pl.when(holder)
        def _():
            pltpu.make_async_copy(note_ref.at[mine, part], slot(me, part), unit_recv).start()

        def send(step, carry):
            peer = lax.rem(me + step, total)
            unit, held = unit_of(peer, total)

            @pl.when(held)
            def _():
                remote(
                    note_ref.at[unit, part], slot(me, part), unit_send, unit_recv, (peer // 2, lax.rem(peer, 2))
                ).start()

            return carry

        lax.fori_loop(1, total, send, 0)

    def doc_starts():
        docs = doc_ref[...]
        lane = lax.broadcasted_iota(jnp.int32, docs.shape, 1)
        row = lax.broadcasted_iota(jnp.int32, docs.shape, 0)
        place_at = row * tokens + lane
        before = jnp.where(
            lane == 0, pltpu.roll(pltpu.roll(docs, 1, 0), 1, 1), pltpu.roll(docs, 1, 1)
        )
        begins = (docs != before) | (place_at == 0)
        value = jnp.where(begins, place_at, 0).astype(jnp.float32)
        step = 1
        while step < tokens:
            value = jnp.maximum(value, jnp.where(lane >= step, pltpu.roll(value, step, 1), 0.0))
            step *= 2
        carried = jnp.broadcast_to(jnp.max(value, axis=1, keepdims=True), docs.shape)
        carried = jnp.where(row >= 1, pltpu.roll(carried, 1, 0), 0.0)
        step = 1
        while step < total:
            carried = jnp.maximum(carried, jnp.where(row >= step, pltpu.roll(carried, step, 0), 0.0))
            step *= 2
        starts = jnp.maximum(value, carried).astype(jnp.int32)
        for peer in range(total):
            start_out[:, pl.ds(peer * tokens, tokens)] = starts[peer : peer + 1, :]

    length = tokens * total
    tiles = length // TILE
    reach = (TILE + DOC_MAX - 2) // TILE

    def open_units():
        @pl.when(holder)
        def _():
            part = note_ref.at[pl.ds(0, UNITS - 1)]
            pltpu.make_async_copy(unit_out, unit_out, unit_recv).wait()
            pltpu.make_async_copy(part, part, unit_send).wait()

        @pl.when(jnp.logical_not(holder))
        def _():
            pltpu.make_async_copy(note_ref, note_ref, unit_send).wait()

    def attend(query_tile):
        @pl.when(holder)
        def _():
            columns = pl.ds(query_tile * TILE, TILE)
            query_t = unit_out[0, :, columns]
            first_row = start_out[:, columns]

            def one_key(step, state, diagonal=False):
                peak, weight, mixed = state
                key_tile = query_tile - step
                scores = dot_nn(tile_at(unit_out, key_tile, 1).T, query_t) * (SCORE_SCALE * LOG2E)
                allowed = tile_mask(key_tile, query_tile, first_row, diagonal)
                scores = jnp.where(allowed, scores, -1e30)
                new_peak = jnp.maximum(peak, jnp.max(scores, axis=0, keepdims=True))
                probs = jnp.exp2(scores - new_peak)
                fade = jnp.exp2(peak - new_peak)
                weight = weight * fade + jnp.sum(probs, axis=0, keepdims=True)
                mixed = mixed * fade + dot_nn(tile_at(unit_out, key_tile, 2), probs.astype(jnp.bfloat16))
                return new_peak, weight, mixed

            begin = (
                jnp.full((1, TILE), -1e30, jnp.float32),
                jnp.zeros((1, TILE), jnp.float32),
                jnp.zeros((HEAD_DIM, TILE), jnp.float32),
            )
            begin = one_key(0, begin, diagonal=True)
            peak, weight, mixed = lax.fori_loop(1, min(query_tile, reach) + 1, one_key, begin)
            mixed_out[:, columns] = mixed / weight
            total_out[:, columns] = peak + jnp.log2(weight)

    def back_slot(device):
        return turned_ref.at[:, pl.ds(pl.multiple_of(device * tokens, 128), tokens)]

    def send_back():
        @pl.when(holder)
        def _():
            def turn(step, carry):
                part = pl.ds(pl.multiple_of(step * 16, 16), 16)
                turned_ref[part, :] = pltpu.roll(mixed_out[part, :], length - LEAD, 1).astype(jnp.bfloat16)
                return carry

            lax.fori_loop(0, HEAD_DIM // 16, turn, 0)
            pltpu.make_async_copy(back_slot(me), att_out.at[mine], att_recv).start()

            def send(step, carry):
                peer = lax.rem(me + step, total)
                remote(
                    back_slot(peer), att_out.at[mine], att_send, att_recv, (peer // 2, lax.rem(peer, 2))
                ).start()
                return carry

            lax.fori_loop(1, total, send, 0)

    def unpack(jobs):
        copies = [
            pltpu.make_async_copy(source.at[block], stage_ref.at[slot_], stage_sem.at[slot_])
            for slot_, (source, block, target) in enumerate(jobs)
        ]
        for copy in copies:
            copy.start()
        for slot_, (source, block, target) in enumerate(jobs):
            copies[slot_].wait()

            def body(level, carry):
                for inner in range(4):
                    both = jnp.concatenate(
                        [stage_ref[slot_, level, inner // 2, inner % 2, side].astype(jnp.float32) for side in range(2)],
                        axis=0,
                    )
                    at = pl.multiple_of((level * 4 + inner) * 2 * slab, 16)
                    target[block, pl.ds(at, 2 * slab), :] = both.astype(jnp.bfloat16)
                return carry

            lax.fori_loop(0, depth, body, 0)

    def fetch_down():
        down_rows = down_out.shape[-2]

        def body(step, carry):
            level, rest_ = step // 8, lax.rem(step, 8)
            pltpu.make_async_copy(
                down_out.at[level, rest_ // 4, lax.rem(rest_ // 2, 2), lax.rem(rest_, 2)],
                down_ref.at[pl.ds(pl.multiple_of(step * down_rows, 16), down_rows)],
                stage_sem.at[2],
            ).start()
            return carry

        lax.fori_loop(0, total, body, 0)

    gather_step(0)
    lax.fori_loop(1, total, send_small, 0)
    tables()
    gather_step(1)
    gather_step(2)
    for lead in leads:
        lead.start()
    normalise()
    gather_step(3)
    doc_starts()
    for part in range(3):
        gather_step(4 + part)
        if part == 2:
            keep = pltpu.make_async_copy(qkv_ref, qkv_out, load_sem.at[1])
            keep.start()
        project(part)
        send_part(part)
    def grad_slot(device):
        return back_out.at[:, pl.ds(pl.multiple_of(device * tokens, 128), tokens)]

    def send_grads(index):
        @pl.when(holder & (mine // HEADS == index))
        def _():
            pltpu.make_async_copy(d_att_ref.at[mine], grad_slot(me), grad_recv).start()

        def send(step, carry):
            peer = lax.rem(me + step, total)
            unit, held = unit_of(peer, total)

            @pl.when(held & (unit // HEADS == index))
            def _():
                remote(
                    d_att_ref.at[unit], grad_slot(me), grad_send, grad_recv, (peer // 2, lax.rem(peer, 2))
                ).start()

            return carry

        lax.fori_loop(1, total, send, 0)

    stores = [
        pltpu.make_async_copy(source, target, store_sem.at[index])
        for index, (source, target) in enumerate(
            [(unit_out, unit_hbm), (mixed_out, mixed_hbm), (act_ref, act_hbm), (d_pair_ref, d_pair_hbm)]
        )
    ]
    rows = micro * tokens
    done = {"tick": 7}

    def tick(number=1):
        for _ in range(number):
            if done["tick"] < pairs + 4:
                gather_step(done["tick"])
                done["tick"] += 1

    def make_key_values():
        chunk = 256
        chunks = neigh_ref.shape[0] // chunk

        def make_pairs(step, carry):
            side, block = step // chunks, lax.rem(step, chunks)
            part = pl.ds(pl.multiple_of(block * chunk, chunk), chunk)
            pair_ref[side, part, :] = dot_nn(neigh_ref[part, :], kv_ref[side]).astype(jnp.bfloat16)
            return carry

        lax.fori_loop(0, 2 * chunks, make_pairs, 0)
    couples = HEADS // 2
    pair_rows = NEIGHBOURS * NEIGH_LEN
    groups = rows // SPAN

    def where(group, couple):
        tok = pl.ds(pl.multiple_of(group * SPAN, SPAN), SPAN)
        key = pl.ds(pl.multiple_of(group * pair_rows, pair_rows), pair_rows)
        lanes = pl.ds(couple * 2 * HEAD_DIM, 2 * HEAD_DIM)
        return tok, key, lanes

    def cross_step(group, carry):
        for couple in range(couples):
            tok, key, lanes = where(group, couple)
            query = stack_pair(cq_ref[tok, lanes])
            scores = dot_nt(query, pair_ref[0, key, lanes]) * SCORE_SCALE
            weights = jnp.exp(scores - jnp.max(scores, axis=-1, keepdims=True))
            probs = weights / jnp.sum(weights, axis=-1, keepdims=True)
            prob_ref[group * couples + couple] = probs
            mixed = unstack_pair(dot_nn(probs.astype(jnp.bfloat16), pair_ref[1, key, lanes]))
            cm_ref[tok, lanes] = (mixed * used_ref[tok, :]).astype(jnp.bfloat16)
        return carry


    tick()
    unpack([(kv_out, 0, kv_ref), (kv_out, 1, kv_ref)])
    make_key_values()
    tick(PLAN[0])
    open_units()
    for tile in range(tiles):
        attend(tile)
        tick(PLAN[1 + tile])
    send_back()
    stores[0].start()
    stores[1].start()
    tick(PLAN[1 + tiles])
    unpack([(sq_out, 0, sq_ref), (sq_out, 1, sq_ref)])
    load_grad.wait()
    for lead in leads:
        lead.wait_recv()
    pltpu.make_async_copy(att_out, att_out, att_recv).wait()
    gain_cross, gain_mlp = gain_out[1:2, :], gain_out[2:3, :]
    for index in range(micro):
        part = pl.ds(index * tokens, tokens)
        hidden = shift_rows(hid_vmem[index], lead_hid[index])
        gy_ref[part, :] = shift_rows(grad_ref[index], lead_grad[index]).astype(jnp.bfloat16)
        first_ref[part, :] = hidden + dot_tn(att_out[index * HEADS : (index + 1) * HEADS].reshape(width, tokens), sq_ref[0])
    n2_ref[...] = (norm_parts(first_ref[...])[0] * gain_cross).astype(jnp.bfloat16)
    cq_ref[...] = dot_nn(n2_ref[...], sq_ref[1]).astype(jnp.bfloat16)

    tick(PLAN[2 + tiles])
    lax.fori_loop(0, groups // 2, cross_step, 0)
    tick(PLAN[3 + tiles])
    unpack([(sq_out, 2, sq_ref), (up_out, 0, up_ref)])
    lax.fori_loop(groups // 2, groups, cross_step, 0)
    second_ref[...] = first_ref[...] + dot_nn(cm_ref[...], sq_ref[2])
    n3 = (norm_parts(second_ref[...])[0] * gain_mlp).astype(jnp.bfloat16)
    n3_ref[...] = n3
    n3t_ref[...] = n3.T
    acc_ref[...] = second_ref[...]
    d_n3_ref[...] = jnp.zeros_like(d_n3_ref)
    tick(pairs + 4 - done["tick"])
    fetch_down()
    unpack([(up_out, 1, up_ref), (up_out, 2, up_ref)])
    unpack([(up_out, 3, up_ref)])
    pltpu.make_async_copy(down_ref, down_ref, stage_sem.at[2]).wait()
    ff_blocks = up_ref.shape[0]
    for step in range(ff_blocks):
        cols = pl.ds(step * width, width)
        upper = dot_nn(n3_ref[...], up_ref[step])
        square = upper * upper
        flat = jnp.tanh(math.sqrt(2.0 / math.pi) * upper * (1.0 + 0.044715 * square))
        half = 0.5 * (1.0 + flat)
        active = (upper * half).astype(jnp.bfloat16)
        act_ref[:, cols] = active
        slope = half + 0.5 * upper * (1.0 - flat * flat) * math.sqrt(2.0 / math.pi) * (
            1.0 + 3.0 * 0.044715 * square
        )
        d_upper = (dot_nt(gy_ref[...], down_ref[cols, :]) * slope).astype(jnp.bfloat16)
        acc_ref[...] += dot_nn(active, down_ref[cols, :])
        d_n3_ref[...] += dot_nt(d_upper, up_ref[step])
        d_upper_ref[:, cols] = d_upper
    result_ref[...] = acc_ref[...].astype(jnp.bfloat16)
    stores[2].start()
    pulled, d_gain_mlp = norm_pull(second_ref[...], gain_mlp, d_n3_ref[...])
    d_second = gy_ref[...].astype(jnp.float32) + pulled
    acc_ref[...] = d_second
    gc_ref[...] = d_second.astype(jnp.bfloat16)
    att_rows[...] = (
        dot_nt(gc_ref[...], sq_ref[2]).astype(jnp.bfloat16).astype(jnp.float32) * used_ref[...]
    ).astype(jnp.bfloat16)

    def cross_back(group, carry):
        for couple in range(couples):
            tok, key, lanes = where(group, couple)
            grad = stack_pair(att_rows[tok, lanes])
            query = stack_pair(cq_ref[tok, lanes])
            probs = prob_ref[group * couples + couple]
            d_probs = dot_nt(grad, pair_ref[1, key, lanes])
            d_scores = (
                probs * (d_probs - jnp.sum(probs * d_probs, axis=-1, keepdims=True))
            ).astype(jnp.bfloat16)
            d_query = unstack_pair(dot_nn(d_scores, pair_ref[0, key, lanes]))
            d_cq_ref[tok, lanes] = (d_query * SCORE_SCALE).astype(jnp.bfloat16)
            d_pair_ref[0, key, lanes] = (dot_tn(d_scores, query) * SCORE_SCALE).astype(jnp.bfloat16)
            d_pair_ref[1, key, lanes] = dot_tn(probs.astype(jnp.bfloat16), grad).astype(jnp.bfloat16)
        return carry

    lax.fori_loop(0, groups, cross_back, 0)
    stores[3].start()
    pulled, d_gain_cross = norm_pull(first_ref[...], gain_cross, dot_nt(d_cq_ref[...], sq_ref[1]))
    d_first = acc_ref[...] + pulled
    first_ref[...] = d_first
    ga_ref[...] = d_first.astype(jnp.bfloat16)
    for index in range(micro):
        part = ga_ref[pl.ds(index * tokens, tokens), :]
        d_att_ref[index * HEADS : (index + 1) * HEADS] = (
            dot_nt(sq_ref[0], part).astype(jnp.bfloat16).reshape(HEADS, HEAD_DIM, tokens)
        )
        send_grads(index)
    d_gain_ref[...] = jnp.concatenate([d_gain_cross, d_gain_mlp, jnp.zeros((6, width), jnp.float32)], axis=0)
    d_up_moves = []
    for step in range(ff_blocks):
        cols = pl.ds(step * width, width)
        if step >= 2:
            d_up_moves[step - 2].wait()
        d_up_ref[step % 2] = dot_nn(n3t_ref[...], d_upper_ref[:, cols]).astype(jnp.bfloat16)
        move = pltpu.make_async_copy(d_up_ref.at[step % 2], d_up_hbm.at[:, cols], up_sem.at[step % 2])
        move.start()
        d_up_moves.append(move)
    for move in d_up_moves[-2:]:
        move.wait()


    for index in range(count):
        for phase in range(4):
            sent(index, phase)
    for lead in leads:
        lead.wait_send()
    keep.wait()
    rest = small_all.at[pl.ds(0, total - 1)]
    pltpu.make_async_copy(rest, rest, misc_sem.at[0]).wait()

    @pl.when(holder)
    def _():
        part = turned_ref.at[:, pl.ds(0, tokens * (total - 1))]
        pltpu.make_async_copy(part, part, att_send).wait()
    for store in stores:
        store.wait()

    @pl.when(holder)
    def _():
        part = d_att_ref.at[pl.ds(0, UNITS - 1)]
        pltpu.make_async_copy(back_out, back_out, grad_recv).wait()
        pltpu.make_async_copy(part, part, grad_send).wait()

    @pl.when(jnp.logical_not(holder))
    def _():
        pltpu.make_async_copy(d_att_ref, d_att_ref, grad_send).wait()


def front(
    depth, w_qkv, w_attn_out, w_cross_q, w_cross_out, w_kv, w_up, w_down, own_gains, segments, valid, neigh, hidden, grads
):
    total = depth * 8
    rows = w_qkv.shape[0]
    down_rows = w_down.shape[0]
    micro, tokens, width = hidden.shape
    length = tokens * total
    third = down_rows // 3
    row_total = micro * tokens
    ff = w_up.shape[1]
    items = [
        (0, 0, 1, 0), (0, 1, 2, 1), (0, 2, 3, 0), (0, 3, 4, 1), (0, 4, 5, 0), (0, 5, 6, 1),
        (2, 0, 1, 0), (2, 1, 2, 1),
        (1, 0, 1, 0), (1, 1, 2, 1),
        (1, 2, 3, 0), (3, 0, 1, 1),
        (4, 0, third, 0), (4, third, 2 * third, 1),
        (4, 2 * third, down_rows, 0), (3, 1, 2, 1),
        (3, 2, 3, 0), (3, 3, 4, 1),
    ]
    count = len(items)
    low, high = jnp.bfloat16, jnp.float32
    spots = (depth, 2, 2, 2)
    qkv_shape = (6, *spots, rows, width // 2)
    out_shape = [
        jax.ShapeDtypeStruct(qkv_shape, low),
        jax.ShapeDtypeStruct((3, *spots, rows, width), low),
        jax.ShapeDtypeStruct((2, *spots, rows, width), low),
        jax.ShapeDtypeStruct((w_up.shape[1] // width, *spots, rows, width), low),
        jax.ShapeDtypeStruct((*spots, down_rows, width), low),
        jax.ShapeDtypeStruct((width, w_up.shape[1]), low),
        jax.ShapeDtypeStruct((3, HEAD_DIM, length), low),
        jax.ShapeDtypeStruct((HEAD_DIM, length), high),
        jax.ShapeDtypeStruct((row_total, ff), low),
        jax.ShapeDtypeStruct((2,) + neigh.shape, low),
        jax.ShapeDtypeStruct((8, width), high),
        jax.ShapeDtypeStruct((HEAD_DIM // 2, tokens), high),
        jax.ShapeDtypeStruct((HEAD_DIM // 2, tokens), high),
        jax.ShapeDtypeStruct((1, length), high),
        jax.ShapeDtypeStruct((1, length), jnp.int32),
        jax.ShapeDtypeStruct((UNITS, HEAD_DIM, tokens), low),
        jax.ShapeDtypeStruct((row_total, width), low),
        jax.ShapeDtypeStruct((row_total, width), high),
        jax.ShapeDtypeStruct((HEAD_DIM, length), low),
        jax.ShapeDtypeStruct((row_total, width), low),
        jax.ShapeDtypeStruct((row_total, width), low),
        jax.ShapeDtypeStruct((row_total, width), low),
        jax.ShapeDtypeStruct((row_total, width), low),
        jax.ShapeDtypeStruct((row_total, width), low),
        jax.ShapeDtypeStruct((row_total, width), low),
        jax.ShapeDtypeStruct((8, width), high),
    ]
    steps = row_total // SPAN * HEADS // 2
    dma = pltpu.SemaphoreType.DMA
    return pl.pallas_call(
        functools.partial(front_kernel, depth, items),
        out_shape=out_shape,
        in_specs=[VMEM] * 9 + [SMEM] + [VMEM] + [ANY] * 2,
        out_specs=[ANY] * 10 + [VMEM] * 16,
        scratch_shapes=[
            pltpu.VMEM(qkv_shape, low),
            pltpu.VMEM((total, 48, 128), low),
            pltpu.VMEM(hidden.shape, low),
            pltpu.VMEM(hidden.shape, low),
            pltpu.VMEM((micro, 64, width), low),
            pltpu.VMEM((micro, 64, width), low),
            pltpu.VMEM((micro * tokens, width), low),
            pltpu.VMEM((width, width // 2), high),
            pltpu.VMEM((UNITS, 3, HEAD_DIM, tokens), low),
            pltpu.VMEM((HEAD_DIM, length), low),
            pltpu.VMEM((total, tokens), high),
            pltpu.VMEM((2, *spots, rows, width), low),
            pltpu.VMEM((3, width, width), low),
            pltpu.VMEM((2, width, width), low),
            pltpu.VMEM((ff // width, width, width), low),
            pltpu.VMEM((ff, width), low),
            pltpu.VMEM((row_total, width), low),
            pltpu.VMEM((row_total, width), high),
            pltpu.VMEM((row_total, width), low),
            pltpu.VMEM((2,) + neigh.shape, low),
            pltpu.VMEM((steps, 2 * SPAN, NEIGHBOURS * NEIGH_LEN), high),
            pltpu.VMEM((row_total, width), high),
            pltpu.VMEM((row_total, width), high),
            pltpu.VMEM((row_total, width), low),
            pltpu.VMEM((width, row_total), low),
            pltpu.VMEM((2, width, width), low),
            dma((count,)), dma((count, 4)), dma((count, 4)), dma((2,)), dma((2,)), dma((2,)), dma((3,)), dma, dma,
            dma, dma, dma((3,)), dma((2,)), dma, dma, dma((4,)),
            pltpu.VMEM((3, HEAD_DIM, length), low),
            pltpu.VMEM((HEAD_DIM, length), high),
            pltpu.VMEM((row_total, ff), low),
            pltpu.VMEM((2,) + neigh.shape, low),
            pltpu.VMEM((UNITS, HEAD_DIM, tokens), low),
            pltpu.VMEM((row_total, ff), low),
            pltpu.VMEM((48, 128), low),
            pltpu.VMEM((row_total, 1), high),
        ],
        compiler_params=pltpu.CompilerParams(
            collective_id=0, has_side_effects=True, vmem_limit_bytes=62 * 2**20
        ),
        cost_estimate=pl.CostEstimate(flops=10**9, bytes_accessed=20 * 10**6, transcendentals=0),
    )(w_qkv, w_attn_out, w_cross_q, w_cross_out, w_kv, w_up, w_down, own_gains, segments, valid, neigh, hidden, grads)


def last_kernel(depth, items, skew, *refs):
    count = len(items)
    back_ref, result_hbm, first_hbm = refs[:3]
    sources = refs[1:16]
    gain_ref, cos_ref, sin_ref, d_gain_rest_ref = refs[16:20]
    (
        output_ref, grad_in_ref, grad_neigh_ref, out_qkv, out_att, out_cq, out_co, out_kv, out_down, gain_out,
    ) = refs[20:30]
    full = refs[30 : 30 + count]
    got_core = refs[30 + count : 30 + 2 * count]
    got_one = refs[30 + 2 * count : 30 + 3 * count]
    got_two = refs[30 + 3 * count : 30 + 4 * count]
    got_z = refs[30 + 4 * count : 30 + 5 * count]
    (
        sent_ref, tail_first, tail_result, raw_ref, n1t_ref, d_n1_ref, temp_ref, gain_mine, gain_got, gain_z,
        send_sem, recv_sem, unit_send, unit_recv, tail_send, tail_recv, gain_send, gain_recv, load_sem,
    ) = refs[30 + 5 * count : -15]
    held_refs = refs[-15:]
    (
        result_ref, first_ref, n2_ref, d_cq_ref, cm_ref, gc_ref, ga_ref, gy_ref, act_ref, d_pair_ref,
        att_ref, neigh_ref, kv_ref, qkv_ref, hidden_ref,
    ) = held_refs
    loads = [
        pltpu.make_async_copy(source, target, load_sem.at[index])
        for index, (source, target) in enumerate(zip(sources, held_refs))
    ]
    for index in (8, 7, 11, 9, 10, 6, 2, 3, 4, 5, 12, 13, 14, 1, 0):
        loads[index].start()
    arrived = set()

    def need(*indices):
        for index in indices:
            if index not in arrived:
                arrived.add(index)
                loads[index].wait()

    micro, tokens, width = hidden_ref.shape
    total = depth * 8
    z, y, c, x = coords()
    me = lax.axis_index("blk") * 2 + lax.axis_index("head")
    mine, holder = unit_of(me, total)
    whole = slice(None)
    all_barrier(total, me)

    after = lax.rem(me + 1, total)
    after_at = (after // 2, lax.rem(after, 2))
    tails = []
    for index in range(micro):
        part = pl.ds(index * tokens + tokens - 64, 64)
        tails.append(
            remote(first_hbm.at[part], tail_first.at[index], tail_send.at[index], tail_recv.at[index], after_at)
        )
        tails.append(
            remote(
                result_hbm.at[part], tail_result.at[index],
                tail_send.at[micro + index], tail_recv.at[micro + index], after_at,
            )
        )

    def slot(device):
        return back_ref.at[:, :, pl.ds(pl.multiple_of(device * tokens, 128), tokens)]

    @pl.when(holder)
    def _():
        pltpu.make_async_copy(slot(me), sent_ref.at[mine], unit_recv).start()

        def send(step, carry):
            peer = lax.rem(me + step, total)
            remote(
                slot(peer), sent_ref.at[mine], unit_send, unit_recv, (peer // 2, lax.rem(peer, 2))
            ).start()
            return carry

        lax.fori_loop(1, total, send, 0)

    for tail in tails:
        tail.start()

    slab = full[0].shape[-2]

    def spread(index, block):
        buffer = full[index]
        cols = buffer.shape[-1]

        def body(level, carry):
            for place_in in range(8):
                at = pl.multiple_of((level * 8 + place_in) * slab, 8)
                buffer[block, level, place_in // 4, (place_in // 2) % 2, place_in % 2] = temp_ref[
                    pl.ds(at, slab), :cols
                ].astype(jnp.bfloat16)
            return carry

        lax.fori_loop(0, depth, body, 0)

    down_index = [index for index, item in enumerate(items) if item[0] == "down"]

    def make_down():
        need(7, 8)

        def body(level, carry):
            cols = pl.ds(pl.multiple_of(level * width, width), width)
            temp_ref[...] = dot_tn(act_ref[:, cols], gy_ref[...])
            for place_in in range(8):
                for part, index in enumerate(down_index):
                    at = place_in * slab * len(down_index) + part * slab
                    full[index][0, level, place_in // 4, (place_in // 2) % 2, place_in % 2] = temp_ref[
                        pl.ds(at, slab), :
                    ].astype(jnp.bfloat16)
            return carry

        lax.fori_loop(0, depth, body, 0)

    def take_units():
        @pl.when(holder)
        def _():
            part = back_ref.at[:, :, pl.ds(0, tokens * (total - 1))]
            pltpu.make_async_copy(part, part, unit_send).wait()

        pltpu.make_async_copy(sent_ref, sent_ref, unit_recv).wait()
        need(14)
        half = HEAD_DIM // 2

        def body(head, carry):
            for index in range(micro):
                lanes = pl.ds(index * tokens, tokens)
                cosine, sine = cos_ref[...], sin_ref[...]
                for part in range(3):
                    value = sent_ref[index * HEADS + head, part].astype(jnp.float32)
                    at = pl.multiple_of(part * width + head * HEAD_DIM, HEAD_DIM)
                    if part < 2:
                        first_half, second_half = value[:half], value[half:]
                        value = jnp.concatenate(
                            [
                                first_half * cosine + second_half * sine,
                                second_half * cosine - first_half * sine,
                            ],
                            axis=0,
                        )
                    raw_ref[pl.ds(at, HEAD_DIM), lanes] = value.astype(jnp.bfloat16)
            return carry

        lax.fori_loop(0, HEADS, body, 0)
        for index in range(micro):
            normed = norm_parts(hidden_ref[index].astype(jnp.float32))[0] * gain_ref[0:1, :]
            n1t_ref[:, pl.ds(index * tokens, tokens)] = normed.astype(jnp.bfloat16).T

    def make(index):
        kind, which = items[index][:2]
        if kind == "down":
            if index == down_index[0]:
                make_down()
            return
        if kind == "kv":
            need(9, 11)
            temp_ref[...] = dot_tn(neigh_ref[...], d_pair_ref[which])
        elif kind == "att":
            need(6, 10)
            temp_ref[...] = dot_nn(att_ref[0], ga_ref[pl.ds(0, tokens), :])
            for step in range(1, micro):
                temp_ref[...] += dot_nn(att_ref[step], ga_ref[pl.ds(step * tokens, tokens), :])
        elif kind == "cq":
            need(2, 3)
            temp_ref[...] = dot_tn(n2_ref[...], d_cq_ref[...])
        elif kind == "co":
            need(4, 5)
            temp_ref[...] = dot_tn(cm_ref[...], gc_ref[...])
        else:
            if which == 0:
                take_units()
            for block in range(2):
                half = width // 2
                at = which * width + block * half
                temp_ref[:, :half] = dot_nt(n1t_ref[...], raw_ref[pl.ds(at, half), :])
                spread(index, block)
            return
        spread(index, 0)

    def core(index):
        return remote(
            full[index].at[whole, whole, whole, 1 - c], got_core[index],
            send_sem.at[index, 0], recv_sem.at[index, 0], place(z, y, 1 - c, x),
        )

    def one(index):
        if items[index][2] == 0:
            src, where = full[index].at[whole, whole, 1 - y, c], place(z, 1 - y, c, x)
        else:
            src, where = full[index].at[whole, whole, whole, c, 1 - x], place(z, y, c, 1 - x)
        return remote(src, got_one[index], send_sem.at[index, 1], recv_sem.at[index, 1], where)

    def two(index):
        if items[index][2] == 0:
            src, where = full[index].at[whole, whole, y, c, 1 - x], place(z, y, c, 1 - x)
        else:
            src, where = full[index].at[whole, whole, 1 - y, c, x], place(z, 1 - y, c, x)
        return remote(src, got_two[index], send_sem.at[index, 2], recv_sem.at[index, 2], where)

    def send_z(index):
        for step in range(1, depth):
            other = lax.rem(z + step, depth)
            remote(
                full[index].at[whole, other, y, c, x], got_z[index].at[z],
                send_sem.at[index, 3], recv_sem.at[index, 3], place(other, y, c, x),
            ).start()

    def add_into(target, source):
        target[...] = (target[...].astype(jnp.float32) + source[...].astype(jnp.float32)).astype(
            jnp.bfloat16
        )

    def each_level(index, body):
        blocks = full[index].shape[0]
        lax.fori_loop(
            0, blocks * depth, lambda step, carry: (body(step // depth, lax.rem(step, depth)), carry)[1], 0
        )

    def sum_core(index):
        def body(block, level):
            for row in range(2):
                for col in range(2):
                    add_into(
                        full[index].at[block, level, row, c, col], got_core[index].at[block, level, row, col]
                    )

        each_level(index, body)

    def sum_one(index):
        def body(block, level):
            for side in range(2):
                if items[index][2] == 0:
                    target = full[index].at[block, level, y, c, side]
                else:
                    target = full[index].at[block, level, side, c, x]
                add_into(target, got_one[index].at[block, level, side])

        each_level(index, body)

    def sum_two(index):
        each_level(
            index,
            lambda block, level: add_into(
                full[index].at[block, level, y, c, x], got_two[index].at[block, level]
            ),
        )

    def sum_z(index):
        kind, which = items[index][:2]
        for block in range(full[index].shape[0]):
            value = full[index][block, z, y, c, x].astype(jnp.float32)
            for step in range(1, depth):
                value = value + got_z[index][lax.rem(z + step, depth), block].astype(jnp.float32)
            if kind == "down":
                out_down[pl.ds(which * slab, slab), :] = value
            elif kind == "kv":
                out_kv[:, pl.ds(which * width, width)] = value
            elif kind == "qkv":
                out_qkv[:, pl.ds(which * width + block * (width // 2), width // 2)] = value
            else:
                {"att": out_att, "cq": out_cq, "co": out_co}[kind][...] = value

    def phase(index, number):
        if number == 0:
            make(index)
            core(index).start()
        elif number == 1:
            core(index).wait_recv()
            sum_core(index)
            one(index).start()
        elif number == 2:
            one(index).wait_recv()
            sum_one(index)
            two(index).start()
        elif number == 3:
            two(index).wait_recv()
            sum_two(index)
            send_z(index)
        else:
            landed = got_z[index].at[pl.ds(0, depth - 1)]
            pltpu.make_async_copy(landed, landed, recv_sem.at[index, 3]).wait()
            sum_z(index)

    def gain_copy(stage):
        where = (place(z, y, 1 - c, x), place(z, 1 - y, c, x), place(z, y, c, 1 - x))[stage]
        return remote(
            gain_mine.at[stage], gain_got.at[stage], gain_send.at[stage], gain_recv.at[stage], where
        )

    def gain_phase(number):
        if number == 0:
            gain_copy(0).start()
        elif number < 4:
            gain_copy(number - 1).wait_recv()
            gain_mine[number] = gain_mine[number - 1] + gain_got[number - 1]
            if number < 3:
                gain_copy(number).start()
            else:
                for step in range(1, depth):
                    other = lax.rem(z + step, depth)
                    remote(
                        gain_mine.at[3], gain_z.at[z], gain_send.at[3], gain_recv.at[3], place(other, y, c, x)
                    ).start()
        else:
            landed = gain_z.at[pl.ds(0, depth - 1)]
            pltpu.make_async_copy(landed, landed, gain_recv.at[3]).wait()
            value = gain_mine[3]
            for step in range(1, depth):
                value = value + gain_z[lax.rem(z + step, depth)]
            gain_out[...] = value

    def neighbours_part(block):
        need(9, 12)
        chunk = 256
        part = pl.ds(block * chunk, chunk)
        grad_neigh_ref[part, :] = (
            dot_nt(d_pair_ref[0, part, :], kv_ref[0]) + dot_nt(d_pair_ref[1, part, :], kv_ref[1])
        ).astype(jnp.bfloat16)

    def input_part():
        half = width // 2
        need(0, 1, 13, 14)
        blocks = qkv_ref.shape[0]
        d_n1_ref[...] = dot_nn(qkv_ref[0], raw_ref[pl.ds(0, half), :])
        for block in range(1, blocks):
            d_n1_ref[...] += dot_nn(qkv_ref[block], raw_ref[pl.ds(block * half, half), :])
        for tail in tails:
            tail.wait()
        d_gain = jnp.zeros((1, width), jnp.float32)
        for index in range(micro):
            part = pl.ds(index * tokens, tokens)
            d_normed = d_n1_ref[:, part].T
            pulled, part_gain = norm_pull(hidden_ref[index].astype(jnp.float32), gain_ref[0:1, :], d_normed)
            d_gain = d_gain + part_gain
            joined = jnp.concatenate([tail_first[index], first_ref[part, :]], axis=0)
            home = pltpu.roll(joined, joined.shape[0] - 1, 0)[:tokens]
            grad_in_ref[part, :] = (home + pulled).astype(jnp.bfloat16)
            joined = jnp.concatenate(
                [tail_result[index].astype(jnp.float32), result_ref[part, :].astype(jnp.float32)], axis=0
            )
            output_ref[part, :] = pltpu.roll(joined, joined.shape[0] - 1, 0)[:tokens].astype(jnp.bfloat16)
        gain_mine[0] = jnp.concatenate([d_gain, d_gain_rest_ref[0:7, :]], axis=0)

    pairs = (count + 1) // 2
    chunks = neigh_ref.shape[0] // 256
    for step in range(pairs + skew * 4):
        for number in range(4, -1, -1):
            pair = step - skew * number
            if not 0 <= pair < pairs:
                continue
            for index in range(2 * pair, min(2 * pair + 2, count)):
                phase(index, number)
            if pair == pairs - 1:
                if number == 0:
                    input_part()
                gain_phase(number)
        if 1 <= step <= chunks:
            neighbours_part(step - 1)
    for index in range(count):
        core(index).wait_send()
        one(index).wait_send()
        two(index).wait_send()
        gone = got_z[index].at[pl.ds(0, depth - 1)]
        pltpu.make_async_copy(gone, gone, send_sem.at[index, 3]).wait()
    for stage in range(3):
        gain_copy(stage).wait_send()
    gone = gain_z.at[pl.ds(0, depth - 1)]
    pltpu.make_async_copy(gone, gone, gain_send.at[3]).wait()


def last(depth, collective, ff, *args):
    hidden = args[15]
    micro, tokens, width = hidden.shape
    rows = micro * tokens
    total = depth * 8
    slab = width // total
    neigh_rows = args[12].shape[0]
    items = [
        ("down", 0, 0), ("down", 1, 1), ("down", 2, 0), ("down", 3, 1), ("kv", 0, 0), ("kv", 1, 1),
        ("att", 0, 0), ("cq", 0, 1), ("co", 0, 0), ("qkv", 0, 1), ("qkv", 1, 0), ("qkv", 2, 1),
    ]
    count = len(items)
    low, high = jnp.bfloat16, jnp.float32
    out_shape = [
        jax.ShapeDtypeStruct((rows, width), low),
        jax.ShapeDtypeStruct((rows, width), low),
        jax.ShapeDtypeStruct((neigh_rows, width), low),
        jax.ShapeDtypeStruct((slab, 3 * width), high),
        jax.ShapeDtypeStruct((slab, width), high),
        jax.ShapeDtypeStruct((slab, width), high),
        jax.ShapeDtypeStruct((slab, width), high),
        jax.ShapeDtypeStruct((slab, 2 * width), high),
        jax.ShapeDtypeStruct((ff // total, width), high),
        jax.ShapeDtypeStruct((8, width), high),
    ]
    full, core, one, two, along = [], [], [], [], []
    for kind, which, order in items:
        blocks, cols = (2, width // 2) if kind == "qkv" else (1, width)
        full.append(pltpu.VMEM((blocks, depth, 2, 2, 2, slab, cols), low))
        core.append(pltpu.VMEM((blocks, depth, 2, 2, slab, cols), low))
        one.append(pltpu.VMEM((blocks, depth, 2, slab, cols), low))
        two.append(pltpu.VMEM((blocks, depth, slab, cols), low))
        along.append(pltpu.VMEM((depth, blocks, slab, cols), low))
    dma = pltpu.SemaphoreType.DMA
    scratch = full + core + one + two + along + [
        pltpu.VMEM((UNITS, 3, HEAD_DIM, tokens), low),
        pltpu.VMEM((micro, 64, width), high),
        pltpu.VMEM((micro, 64, width), low),
        pltpu.VMEM((3 * width, rows), low),
        pltpu.VMEM((width, rows), low),
        pltpu.VMEM((width, rows), high),
        pltpu.VMEM((width, width), high),
        pltpu.VMEM((4, 8, width), high),
        pltpu.VMEM((3, 8, width), high),
        pltpu.VMEM((depth, 8, width), high),
        dma((count, 4)), dma((count, 4)), dma, dma, dma((2 * micro,)), dma((2 * micro,)), dma((4,)), dma((4,)),
        dma((15,)),
    ] + [pltpu.VMEM(a.shape, a.dtype) for a in args[1:16]]
    return pl.pallas_call(
        functools.partial(last_kernel, depth, items, 2),
        out_shape=out_shape,
        in_specs=[ANY] * 16 + [VMEM] * 4,
        out_specs=[VMEM] * 10,
        scratch_shapes=scratch,
        compiler_params=pltpu.CompilerParams(
            collective_id=collective, has_side_effects=True, vmem_limit_bytes=62 * 2**20
        ),
        cost_estimate=pl.CostEstimate(flops=10**10, bytes_accessed=40 * 10**6, transcendentals=0),
    )(*args)


def finish_kernel(copies, *refs):
    for source, result in zip(refs[:copies], refs[copies:]):
        result[...] = source[...].astype(result.dtype)


def finish(arrays, low):
    arrays = [*arrays, low]
    copies = len(arrays)
    vmem = pl.BlockSpec(memory_space=pltpu.VMEM)
    return pl.pallas_call(
        functools.partial(finish_kernel, copies),
        out_shape=[jax.ShapeDtypeStruct(a.shape, a.dtype) for a in arrays[:-1]]
        + [jax.ShapeDtypeStruct(low.shape, jnp.float32)],
        in_specs=[vmem] * copies,
        out_specs=[vmem] * copies,
        compiler_params=pltpu.CompilerParams(vmem_limit_bytes=62 * 2**20),
    )(*arrays)


def layer_norm(values, norm_gain):
    centred = values - jnp.mean(values, axis=-1, keepdims=True)
    spread = jnp.mean(centred * centred, axis=-1, keepdims=True)
    return centred * lax.rsqrt(spread + 1e-05) * norm_gain


def norm_backward(values, norm_gain, grad_out):
    result, pullback = jax.vjp(layer_norm, values, norm_gain)
    return pullback(grad_out)


def outer(left, right):
    return jnp.einsum("td,te->de", left, right, preferred_element_type=jnp.float32)


def turn_heads(values, cosine, sine):
    first_half, second_half = values[:, :32], values[:, 32:]
    return jnp.concatenate(
        [first_half * cosine - second_half * sine, second_half * cosine + first_half * sine], axis=1
    )


def on_device(
    hidden_in,
    segment_ids,
    neighbour_valid,
    neighbours,
    out_grad,
    norm_attn,
    w_qkv,
    w_attn_out,
    norm_cross,
    w_cross_q,
    w_cross_kv,
    w_cross_out,
    norm_mlp,
    w_up,
    w_down,
):
    micro, tok_count, model_width = hidden_in.shape
    blk_count = lax.axis_size("blk")
    depth = blk_count // 4
    total = blk_count * 2
    length = tok_count * total
    row_count = micro * tok_count
    gain_rows = norm_attn.shape[0]
    span_count = tok_count // SPAN
    pair_rows = NEIGHBOURS * NEIGH_LEN
    device = lax.axis_index(AXES)

    in_kernel = gain_rows % 8 == 0
    token_index = device * tok_count + jnp.arange(tok_count, dtype=jnp.int32)
    shifted_index = token_index + LEAD
    used = jnp.where(
        shifted_index[None] < length, jnp.repeat(neighbour_valid, SPAN, axis=1).astype(jnp.float32), 0.0
    ).reshape(row_count, 1)
    neigh_rows = neighbours.reshape(micro * span_count * pair_rows, model_width)
    if in_kernel:
        own_gains = jnp.pad(
            jnp.stack([norm_attn, norm_cross, norm_mlp]).astype(jnp.float32), ((0, 125), (0, 128 - gain_rows))
        )
        (
            got_qkv, got_sq, got_kv, up_full, down_full, d_up, unit_qkv, mixed, activated, d_pairs,
            gains, cosine, sine, totals, first_row, attended_t,
            result_rows, d_first, unit_grad, normed_cross, d_cross_query, cross_mixed, d_second_low, d_first_low,
            grad_low, d_gain_rest,
        ) = front(
            depth, w_qkv, w_attn_out, w_cross_q, w_cross_out, w_cross_kv, w_up, w_down, own_gains, segment_ids,
            neighbour_valid, neigh_rows, hidden_in, out_grad,
        )
        attended_t = attended_t.reshape(micro, model_width, tok_count)
    else:
        up_full = lax.all_gather(w_up, AXES, axis=0, tiled=True)
        down_full = lax.all_gather(w_down, AXES, axis=0, tiled=True)
        up_full = up_full.reshape(model_width, -1, model_width).transpose(1, 0, 2)
        small = jnp.zeros((16, 128), jnp.bfloat16)
        for row, gain in enumerate((norm_attn, norm_cross, norm_mlp)):
            small = small.at[row, :gain_rows].set(gain)
        small = small.at[3 : 3 + micro, :tok_count].set(segment_ids.astype(jnp.bfloat16))
        got_qkv, got_sq, got_kv, got_small, lead_hid, lead_grad = gather_all(
            depth, w_qkv, w_attn_out, w_cross_q, w_cross_out, w_cross_kv, small, hidden_in, out_grad
        )
        gains = got_small[:, :3, :gain_rows].astype(jnp.float32).transpose(1, 0, 2).reshape(3, model_width)
        gain_attn = gains[0]
        seg_full = got_small[:, 3 : 3 + micro, :tok_count].transpose(1, 0, 2).reshape(micro, length)
        seg_full = seg_full.astype(jnp.int32)
    qkv_blocks = got_qkv.reshape(6, model_width, model_width // 2)
    squares = got_sq.reshape(3, model_width, model_width)
    kv_blocks = got_kv.reshape(2, model_width, model_width)


    unit, holder = unit_of(device, total)
    tile_index = jnp.arange(length // TILE, dtype=jnp.int32)
    if in_kernel:
        tile_first = first_row[0, ::TILE]
    else:
        seg_unit = lax.dynamic_index_in_dim(seg_full, unit // HEADS, 0, keepdims=False)
        seg_tiles = seg_unit.reshape(length // TILE, TILE)
        tile_first = jnp.sum((seg_unit[None] < seg_tiles[:, :1]).astype(jnp.int32), axis=-1)
        inside = jnp.sum((seg_tiles[:, None, :] < seg_tiles[:, :, None]).astype(jnp.int32), axis=-1)
        first_row = jnp.where(
            seg_tiles == seg_tiles[:, :1], tile_first[:, None], tile_index[:, None] * TILE + inside
        ).reshape(1, length)
    low = tile_first // TILE
    high = jnp.sum((low[None] <= tile_index[:, None]).astype(jnp.int32), axis=-1)
    low = jnp.where(holder, low, tile_index + 1)
    high = jnp.where(holder, high, 0)

    if not in_kernel:
        first_of = jnp.sum(
            (seg_full[:, None, :] < segment_ids[:, :, None]).astype(jnp.int32), axis=-1
        )
        local_pos = token_index[None] - first_of
        frequency = jnp.exp(
            jnp.arange(HEAD_DIM // 2, dtype=jnp.float32) * (-2.0 * math.log(10000.0) / HEAD_DIM)
        )
        angles = frequency[:, None, None] * local_pos.astype(jnp.float32)[None]
        cosine, sine = jnp.cos(angles), jnp.sin(angles)

        hidden = hidden_in.astype(jnp.float32)
        normed_attn = layer_norm(hidden, gain_attn).astype(jnp.bfloat16).reshape(row_count, model_width)
        raw = jnp.einsum("bde,td->bet", qkv_blocks, normed_attn, preferred_element_type=jnp.float32)
        raw = raw.reshape(3, HEADS, HEAD_DIM, micro, tok_count)
        rotated = jnp.stack(
            [turn_heads(raw[0], cosine, sine), turn_heads(raw[1], cosine, sine), raw[2]]
        ).astype(jnp.bfloat16)
        message = rotated.transpose(3, 1, 0, 2, 4).reshape(UNITS, 3, HEAD_DIM, tok_count)
        unit_qkv = to_units(total, message, 1)
        shifted, mixed, totals = attn_forward(low, first_row, unit_qkv)
        (attended_t,) = to_tokens(total, shifted[None], (), 2)
    attended_t = attended_t.reshape(micro, model_width, tok_count)

    if not in_kernel:
        (
            result_rows, d_first, d_attended_t, normed_cross, d_cross_query, cross_mixed, d_second_low, d_first_low,
            grad_low, activated, d_pairs, d_gain_rest, d_up,
        ) = middle(
            attended_t, hidden_in, lead_hid, out_grad, lead_grad, gains, used, squares, kv_blocks, neigh_rows,
            up_full, down_full,
        )
    up_low = lax.psum_scatter(d_up, AXES, scatter_dimension=0, tiled=True)
    if not in_kernel:
        down_share = lax.psum_scatter(
            outer(activated, grad_low).astype(jnp.bfloat16), AXES, scatter_dimension=0, tiled=True
        ).astype(jnp.float32)
    if not in_kernel:
        unit_grad = to_units(total, d_attended_t.reshape(UNITS, 1, HEAD_DIM, tok_count), 3)[0]
    unit_back = attn_backward(low, high, first_row, unit_qkv, unit_grad, mixed, totals)
    if in_kernel:
        (
            output, grad_in, grad_neighbours, s_qkv, s_att, s_cq, s_co, s_kv, s_down, s_gain,
        ) = last(
            depth, 5, w_up.shape[1],
            unit_back, result_rows, d_first, normed_cross, d_cross_query, cross_mixed, d_second_low, d_first_low,
            grad_low, activated, d_pairs, attended_t, neigh_rows, kv_blocks, qkv_blocks, hidden_in, gains,
            cosine, sine, d_gain_rest,
        )
        own_gain = lax.dynamic_slice_in_dim(s_gain, device * gain_rows, gain_rows, 1)
        (
            output, grad_in, grad_neighbours, s_qkv, s_att, s_cq, s_co, s_kv, s_down, up_share,
        ) = finish(
            [
                output, grad_in, grad_neighbours, s_qkv, s_att, s_cq, s_co, s_kv, s_down,
            ],
            up_low,
        )
        return (
            output.reshape(hidden_in.shape), grad_in.reshape(hidden_in.shape),
            grad_neighbours.reshape(neighbours.shape),
            own_gain[0], s_qkv, s_att, own_gain[1], s_cq, s_kv, s_co, own_gain[2], up_share, s_down,
        )
    up_share = up_low.astype(jnp.float32)
    result_rows = result_rows.reshape(micro, tok_count, model_width)
    d_first = d_first.reshape(micro, tok_count, model_width)
    sent_t, tail_first, tail_result = to_tokens(
        total, unit_back, (d_first[:, tok_count - 64 :], result_rows[:, tok_count - 64 :]), 4
    )

    def unshift(rows, tail):
        return jnp.concatenate([tail[:, 1:], rows[:, : tok_count - LEAD]], axis=1)

    output = unshift(result_rows, tail_result)
    d_first_home = unshift(d_first, tail_first)
    sent_t = sent_t.reshape(micro, HEADS, 3, HEAD_DIM, tok_count).transpose(2, 1, 3, 0, 4)
    sent_t = sent_t.astype(jnp.float32)
    raw_t = jnp.stack(
        [turn_heads(sent_t[0], cosine, -sine), turn_heads(sent_t[1], cosine, -sine), sent_t[2]]
    ).astype(jnp.bfloat16).reshape(6, model_width // 2, row_count)
    d_normed_attn = jnp.einsum("bet,bde->td", raw_t, qkv_blocks, preferred_element_type=jnp.float32)
    d_hidden_in, d_gain_attn = norm_backward(
        hidden, gain_attn, d_normed_attn.reshape(micro, tok_count, model_width)
    )
    grad_in = (d_first_home + d_hidden_in).astype(jnp.bfloat16)

    d_keys, d_values = d_pairs[0], d_pairs[1]
    d_first_low = d_first_low.reshape(micro, tok_count, model_width)
    d_neigh = (
        jnp.einsum("te,de->td", d_keys, kv_blocks[0], preferred_element_type=jnp.float32)
        + jnp.einsum("te,de->td", d_values, kv_blocks[1], preferred_element_type=jnp.float32)
    ).astype(jnp.bfloat16)
    grad_neighbours = d_neigh.reshape(neighbours.shape)

    def blocks_of(array):
        return array.astype(jnp.bfloat16).reshape(
            array.shape[0], depth, 2, 2, 2, gain_rows, array.shape[-1]
        )

    d_qkv = jnp.einsum("td,bet->bde", normed_attn, raw_t, preferred_element_type=jnp.float32)
    d_sq = jnp.stack(
        [
            jnp.einsum("mdt,mte->de", attended_t, d_first_low, preferred_element_type=jnp.float32),
            outer(normed_cross, d_cross_query),
            outer(cross_mixed, d_second_low),
        ]
    )
    d_kv = jnp.stack([outer(neigh_rows, d_keys), outer(neigh_rows, d_values)])
    d_gains = jnp.stack([d_gain_attn, d_gain_rest[0], d_gain_rest[1]]).reshape(3, total, gain_rows)
    d_gains = jnp.zeros((total, 8, 128), jnp.float32).at[:, :3, :gain_rows].set(d_gains.transpose(1, 0, 2))
    s_qkv, s_sq, s_kv, s_gain = scatter_all(
        depth, blocks_of(d_qkv), blocks_of(d_sq), blocks_of(d_kv), d_gains, 6
    )
    return (
        output,
        grad_in,
        grad_neighbours,
        s_gain[0, :gain_rows],
        s_qkv.transpose(1, 0, 2).reshape(gain_rows, 3 * model_width),
        s_sq[0],
        s_gain[1, :gain_rows],
        s_sq[1],
        s_kv.transpose(1, 0, 2).reshape(gain_rows, 2 * model_width),
        s_sq[2],
        s_gain[2, :gain_rows],
        up_share,
        down_share,
    )


def solution(mesh):
    placed = (
        P(None, ("blk", "head"), None),
        P(None, ("blk", "head")),
        P(None, ("blk", "head")),
        P(None, ("blk", "head"), None, None, None),
        P(None, ("blk", "head"), None),
        P(("blk", "head")),
        P(("blk", "head"), None),
        P(("blk", "head"), None),
        P(("blk", "head")),
        P(("blk", "head"), None),
        P(("blk", "head"), None),
        P(("blk", "head"), None),
        P(("blk", "head")),
        P(("blk", "head"), None),
        P(("blk", "head"), None),
    )
    return jax.shard_map(
        on_device,
        mesh=mesh,
        in_specs=placed,
        out_specs=(
            P(None, ("blk", "head"), None),
            P(None, ("blk", "head"), None),
            P(None, ("blk", "head"), None, None, None),
            P(("blk", "head")),
            P(("blk", "head"), None),
            P(("blk", "head"), None),
            P(("blk", "head")),
            P(("blk", "head"), None),
            P(("blk", "head"), None),
            P(("blk", "head"), None),
            P(("blk", "head")),
            P(("blk", "head"), None),
            P(("blk", "head"), None),
        ),
        check_vma=False,
    )
```

```python
import functools
import math

import jax
import jax.numpy as jnp
from jax import lax
from jax.experimental import pallas as pl
from jax.experimental.pallas import tpu as pltpu
from jax.sharding import PartitionSpec as P

MESH = pl.DeviceIdType.MESH
ANY = pl.BlockSpec(memory_space=pl.ANY)


def coords():
    blk = lax.axis_index("blk")
    return blk // 4, (blk // 2) % 2, blk % 2, lax.axis_index("head")


def place(z, y, c, x):
    return (z * 4 + y * 2 + c, x)


def loop(count, body):
    if count <= 8:
        for step in range(count):
            body(step)
    else:
        lax.fori_loop(0, count, lambda step, carry: (body(step), carry)[1], 0)


def all_barrier(total, me):
    barrier = pltpu.get_barrier_semaphore()

    def greet(step, carry):
        peer = lax.rem(me + step, total)
        pl.semaphore_signal(
            barrier, inc=1, device_id=(peer // 2, lax.rem(peer, 2)), device_id_type=MESH
        )
        return carry

    lax.fori_loop(1, total, greet, 0)
    pl.semaphore_wait(barrier, total - 1)


def remote(src, dst, send, recv, where):
    return pltpu.make_async_remote_copy(
        src_ref=src, dst_ref=dst, send_sem=send, recv_sem=recv, device_id=where, device_id_type=MESH
    )


def gather_kernel(depth, items, *refs):
    count = len(items)
    w_refs = refs[:5]
    small_ref, hid_ref, grad_ref = refs[5:8]
    out_refs = refs[8:11]
    small_out, lead_hid, lead_grad = refs[11:14]
    own_sem, send_sem, recv_sem, misc_sem, lead_send, lead_recv = refs[14:]
    z, y, c, x = coords()
    total = depth * 8
    me = lax.axis_index("blk") * 2 + lax.axis_index("head")
    rows_per = w_refs[0].shape[0]

    def view(item, zs, ys, cs, xs):
        buffer, first, last, kind = item
        return out_refs[buffer].at[pl.ds(first, last - first), zs, ys, cs, xs]

    all_barrier(total, me)
    own_small = pltpu.make_async_copy(small_ref, small_out.at[me], misc_sem.at[1])
    own_small.start()

    def send_small(step, carry):
        peer = lax.rem(me + step, total)
        remote(
            small_ref, small_out.at[me], misc_sem.at[0], misc_sem.at[1], (peer // 2, lax.rem(peer, 2))
        ).start()
        return carry

    own = []
    for index, item in enumerate(items):
        buffer, first, last, kind = item
        width = out_refs[buffer].shape[-1]
        copies = []
        for block in range(first, last):
            if buffer == 1:
                src = w_refs[1 + block]
            else:
                src = w_refs[2 * buffer].at[:, pl.ds(block * width, width)]
            copies.append((src, out_refs[buffer].at[block, z, y, c, x]))
        for src, dst in copies:
            copy = pltpu.make_async_copy(src, dst, own_sem.at[index])
            copy.start()
        own.append(pltpu.make_async_copy(view(item, z, y, c, x), view(item, z, y, c, x), own_sem.at[index]))
    lax.fori_loop(1, total, send_small, 0)
    prev = lax.rem(me + total - 1, total)
    prev_at = (prev // 2, lax.rem(prev, 2))
    leads = [
        remote(hid_ref.at[:, pl.ds(0, 64)], lead_hid, lead_send.at[0], lead_recv.at[0], prev_at),
        remote(grad_ref.at[:, pl.ds(0, 64)], lead_grad, lead_send.at[1], lead_recv.at[1], prev_at),
    ]

    whole = slice(None)

    def phase_one(index):
        own[index].wait()
        item = items[index]

        def send(step):
            other = lax.rem(z + step + 1, depth)
            remote(
                view(item, z, y, c, x), view(item, z, y, c, x),
                send_sem.at[index, 0], recv_sem.at[index, 0], place(other, y, c, x),
            ).start()

        loop(depth - 1, send)

    def bulk(index, phase):
        item = items[index]
        first_x = item[3] == 0
        if phase == 1:
            ref = view(item, whole, y, c, x)
            where = place(z, y, c, 1 - x) if first_x else place(z, 1 - y, c, x)
        elif phase == 2:
            ref = view(item, whole, y, c, whole) if first_x else view(item, whole, whole, c, x)
            where = place(z, 1 - y, c, x) if first_x else place(z, y, c, 1 - x)
        else:
            ref = view(item, whole, whole, c, whole)
            where = place(z, y, 1 - c, x)
        return remote(ref, ref, send_sem.at[index, phase], recv_sem.at[index, phase], where)

    def arrived(index, phase):
        item = items[index]
        if phase == 0:
            ref = view(item, pl.ds(0, depth - 1), y, c, x)
            pltpu.make_async_copy(ref, ref, recv_sem.at[index, 0]).wait()
        else:
            bulk(index, phase).wait_recv()

    def sent(index, phase):
        item = items[index]
        if phase == 0:
            ref = view(item, pl.ds(0, depth - 1), y, c, x)
            pltpu.make_async_copy(ref, ref, send_sem.at[index, 0]).wait()
        else:
            bulk(index, phase).wait_send()

    pairs = (count + 1) // 2
    for step in range(pairs + 2 * 4):
        for phase in range(4, -1, -1):
            pair = step - 2 * phase
            if not 0 <= pair < pairs:
                continue
            for index in range(2 * pair, min(2 * pair + 2, count)):
                if phase == 0:
                    phase_one(index)
                else:
                    arrived(index, phase - 1)
                    if phase < 4:
                        bulk(index, phase).start()
        if step == 0:
            for lead in leads:
                lead.start()
    for index in range(count):
        for phase in range(4):
            sent(index, phase)
    for lead in leads:
        lead.wait()
    pltpu.make_async_copy(small_out, small_out, misc_sem.at[1]).wait()
    rest = small_out.at[pl.ds(0, total - 1)]
    pltpu.make_async_copy(rest, rest, misc_sem.at[0]).wait()


def gather_all(depth, w_qkv, w_attn_out, w_cross_q, w_cross_out, w_kv, small, hidden, grads):
    total = depth * 8
    rows = w_qkv.shape[0]
    items = [
        (0, 0, 3, 0), (0, 3, 6, 1),
        (2, 0, 1, 0), (2, 1, 2, 1),
        (1, 0, 1, 0), (1, 1, 2, 1),
        (1, 2, 3, 0),
    ]
    shapes = [
        (6, depth, 2, 2, 2, rows, w_qkv.shape[1] // 6),
        (3, depth, 2, 2, 2, rows, w_attn_out.shape[1]),
        (2, depth, 2, 2, 2, rows, w_kv.shape[1] // 2),
    ]
    lead_shape = (hidden.shape[0], 64, hidden.shape[2])
    outs = [jax.ShapeDtypeStruct(shape, jnp.bfloat16) for shape in shapes]
    outs += [jax.ShapeDtypeStruct((total,) + small.shape, small.dtype)]
    outs += [jax.ShapeDtypeStruct(lead_shape, jnp.bfloat16)] * 2
    count = len(items)
    return pl.pallas_call(
        functools.partial(gather_kernel, depth, items),
        out_shape=outs,
        in_specs=[ANY] * 8,
        out_specs=[ANY] * 6,
        scratch_shapes=[
            pltpu.SemaphoreType.DMA((count,)),
            pltpu.SemaphoreType.DMA((count, 4)),
            pltpu.SemaphoreType.DMA((count, 4)),
            pltpu.SemaphoreType.DMA((2,)),
            pltpu.SemaphoreType.DMA((2,)),
            pltpu.SemaphoreType.DMA((2,)),
        ],
        compiler_params=pltpu.CompilerParams(collective_id=0, has_side_effects=True),
    )(w_qkv, w_attn_out, w_cross_q, w_cross_out, w_kv, small, hidden, grads)


def unit_of(device, total):
    if total == 32:
        depth = device // 8
        middle = (depth == 1) | (depth == 2)
        end = 16 + (depth // 3) * 4 + (lax.rem(device, 8) // 4) * 2 + lax.rem(device, 2)
        unit = jnp.where(middle, device - 8, end)
        return unit, middle | (lax.rem(device // 2, 2) == 0)
    stride = total // UNITS
    return jnp.minimum(device // stride, UNITS - 1), (lax.rem(device, stride) == 0) & (device // stride < UNITS)


def to_units_kernel(total, src, dst, send_sem, recv_sem):
    me = lax.axis_index("blk") * 2 + lax.axis_index("head")
    mine, holder = unit_of(me, total)
    all_barrier(total, me)
    lanes = src.shape[-1]

    def slot(device):
        return dst.at[:, :, pl.ds(pl.multiple_of(device * lanes, 128), lanes)]

    @pl.when(holder)
    def _():
        pltpu.make_async_copy(src.at[mine], slot(me), recv_sem).start()

    def send(step, carry):
        peer = lax.rem(me + step, total)
        unit, held = unit_of(peer, total)

        @pl.when(held)
        def _():
            remote(src.at[unit], slot(me), send_sem, recv_sem, (peer // 2, lax.rem(peer, 2))).start()

        return carry

    lax.fori_loop(1, total, send, 0)

    @pl.when(holder)
    def _():
        part = src.at[pl.ds(0, UNITS - 1)]
        pltpu.make_async_copy(dst, dst, recv_sem).wait()
        pltpu.make_async_copy(part, part, send_sem).wait()

    @pl.when(jnp.logical_not(holder))
    def _():
        pltpu.make_async_copy(src, src, send_sem).wait()


def to_units(total, message, collective):
    units, parts, width, lanes = message.shape
    return pl.pallas_call(
        functools.partial(to_units_kernel, total),
        out_shape=jax.ShapeDtypeStruct((parts, width, lanes * total), message.dtype),
        in_specs=[ANY],
        out_specs=ANY,
        scratch_shapes=[pltpu.SemaphoreType.DMA, pltpu.SemaphoreType.DMA],
        compiler_params=pltpu.CompilerParams(collective_id=collective, has_side_effects=True),
    )(message)


def to_tokens_kernel(total, extras, *refs):
    src = refs[0]
    extra_in = refs[1 : 1 + extras]
    dst = refs[1 + extras]
    extra_out = refs[2 + extras : 2 + 2 * extras]
    send_sem, recv_sem, extra_send, extra_recv = refs[2 + 2 * extras :]
    me = lax.axis_index("blk") * 2 + lax.axis_index("head")
    mine, holder = unit_of(me, total)
    all_barrier(total, me)
    lanes = dst.shape[-1]
    after = lax.rem(me + 1, total)
    moves = [
        remote(
            extra_in[index], extra_out[index], extra_send.at[index], extra_recv.at[index],
            (after // 2, lax.rem(after, 2)),
        )
        for index in range(extras)
    ]
    for move in moves:
        move.start()

    def slot(device):
        return src.at[:, :, pl.ds(pl.multiple_of(device * lanes, 128), lanes)]

    @pl.when(holder)
    def _():
        pltpu.make_async_copy(slot(me), dst.at[mine], recv_sem).start()

        def send(step, carry):
            peer = lax.rem(me + step, total)
            remote(
                slot(peer), dst.at[mine], send_sem, recv_sem, (peer // 2, lax.rem(peer, 2))
            ).start()
            return carry

        lax.fori_loop(1, total, send, 0)

    pltpu.make_async_copy(dst, dst, recv_sem).wait()

    @pl.when(holder)
    def _():
        part = src.at[:, :, pl.ds(0, lanes * (total - 1))]
        pltpu.make_async_copy(part, part, send_sem).wait()

    for move in moves:
        move.wait()


def to_tokens(total, units, extra, collective):
    parts, width, length = units.shape
    count = len(extra)
    result = jax.ShapeDtypeStruct((UNITS, parts, width, length // total), units.dtype)
    return pl.pallas_call(
        functools.partial(to_tokens_kernel, total, count),
        out_shape=[result] + [jax.ShapeDtypeStruct(e.shape, e.dtype) for e in extra],
        in_specs=[ANY] * (1 + count),
        out_specs=[ANY] * (1 + count),
        scratch_shapes=[
            pltpu.SemaphoreType.DMA,
            pltpu.SemaphoreType.DMA,
            pltpu.SemaphoreType.DMA((max(count, 1),)),
            pltpu.SemaphoreType.DMA((max(count, 1),)),
        ],
        compiler_params=pltpu.CompilerParams(collective_id=collective, has_side_effects=True),
    )(units, *extra)


def scatter_kernel(depth, items, *refs):
    count = len(items)
    total = depth * 8
    d_refs = refs[:3]
    gain_ref = refs[3]
    out_refs = refs[4:7]
    gain_out = refs[7]
    own = refs[8 : 8 + count]
    got_core = refs[8 + count : 8 + 2 * count]
    got_one = refs[8 + 2 * count : 8 + 3 * count]
    got_two = refs[8 + 3 * count : 8 + 4 * count]
    got_z = refs[8 + 4 * count : 8 + 5 * count]
    gains, local_sem, send_sem, recv_sem, gain_sem = refs[8 + 5 * count :]
    z, y, c, x = coords()
    me = lax.axis_index("blk") * 2 + lax.axis_index("head")
    all_barrier(total, me)
    whole = slice(None)

    pltpu.make_async_copy(gain_ref.at[me], gains.at[me], gain_sem.at[1]).start()

    def send_gain(step, carry):
        peer = lax.rem(me + step, total)
        remote(
            gain_ref.at[peer], gains.at[me], gain_sem.at[0], gain_sem.at[1], (peer // 2, lax.rem(peer, 2))
        ).start()
        return carry

    def local(index):
        buffer, first, last, kind = items[index]
        src = d_refs[buffer].at[pl.ds(first, last - first), whole, whole, c]
        return pltpu.make_async_copy(src, own[index], local_sem.at[index])

    def core(index):
        buffer, first, last, kind = items[index]
        src = d_refs[buffer].at[pl.ds(first, last - first), whole, whole, 1 - c]
        return remote(
            src, got_core[index], send_sem.at[index, 0], recv_sem.at[index, 0], place(z, y, 1 - c, x)
        )

    def one(index):
        if items[index][3] == 0:
            src, where = own[index].at[whole, whole, 1 - y], place(z, 1 - y, c, x)
        else:
            src, where = own[index].at[whole, whole, whole, 1 - x], place(z, y, c, 1 - x)
        return remote(src, got_one[index], send_sem.at[index, 1], recv_sem.at[index, 1], where)

    def two(index):
        if items[index][3] == 0:
            src, where = own[index].at[whole, whole, y, 1 - x], place(z, y, c, 1 - x)
        else:
            src, where = own[index].at[whole, whole, 1 - y, x], place(z, 1 - y, c, x)
        return remote(src, got_two[index], send_sem.at[index, 2], recv_sem.at[index, 2], where)

    def send_z(index):
        def send(step):
            other = lax.rem(z + step + 1, depth)
            remote(
                own[index].at[whole, other, y, x], got_z[index].at[z],
                send_sem.at[index, 3], recv_sem.at[index, 3], place(other, y, c, x),
            ).start()

        loop(depth - 1, send)

    def add_into(target, source):
        target[...] = (target[...].astype(jnp.float32) + source[...].astype(jnp.float32)).astype(
            jnp.bfloat16
        )

    def sum_core(index):
        blocks = own[index].shape[0]

        def body(step):
            block, level = step // depth, lax.rem(step, depth)
            for row in range(2):
                for col in range(2):
                    add_into(own[index].at[block, level, row, col], got_core[index].at[block, level, row, col])

        lax.fori_loop(0, blocks * depth, lambda step, carry: (body(step), carry)[1], 0)

    def sum_one(index):
        blocks = own[index].shape[0]

        def body(step):
            block, level = step // depth, lax.rem(step, depth)
            for side in range(2):
                if items[index][3] == 0:
                    target = own[index].at[block, level, y, side]
                else:
                    target = own[index].at[block, level, side, x]
                add_into(target, got_one[index].at[block, level, side])

        lax.fori_loop(0, blocks * depth, lambda step, carry: (body(step), carry)[1], 0)

    def sum_two(index):
        blocks = own[index].shape[0]

        def body(step):
            block, level = step // depth, lax.rem(step, depth)
            add_into(own[index].at[block, level, y, x], got_two[index].at[block, level])

        lax.fori_loop(0, blocks * depth, lambda step, carry: (body(step), carry)[1], 0)

    def sum_z(index):
        buffer, first, last, kind = items[index]
        for block in range(last - first):
            running = own[index][block, z, y, x].astype(jnp.float32)

            def body(step, value):
                other = lax.rem(z + step, depth)
                return value + got_z[index][other, block].astype(jnp.float32)

            out_refs[buffer][first + block] = lax.fori_loop(1, depth, body, running)

    for index in range(count):
        local(index).start()
    pairs = (count + 1) // 2
    for step in range(pairs + 4):
        for phase in range(4, -1, -1):
            pair = step - phase
            if not 0 <= pair < pairs:
                continue
            for index in range(2 * pair, min(2 * pair + 2, count)):
                if phase == 0:
                    core(index).start()
                elif phase == 1:
                    local(index).wait()
                    core(index).wait_recv()
                    sum_core(index)
                    one(index).start()
                elif phase == 2:
                    one(index).wait_recv()
                    sum_one(index)
                    two(index).start()
                elif phase == 3:
                    two(index).wait_recv()
                    sum_two(index)
                    send_z(index)
                else:
                    landed = got_z[index].at[pl.ds(0, depth - 1)]
                    pltpu.make_async_copy(landed, landed, recv_sem.at[index, 3]).wait()
                    sum_z(index)
        if step == 0:
            lax.fori_loop(1, total, send_gain, 0)
    pltpu.make_async_copy(gains, gains, gain_sem.at[1]).wait()
    gain_out[...] = jnp.sum(gains[...], axis=0)
    for index in range(count):
        core(index).wait_send()
        one(index).wait_send()
        two(index).wait_send()
        gone = got_z[index].at[pl.ds(0, depth - 1)]
        pltpu.make_async_copy(gone, gone, send_sem.at[index, 3]).wait()
    rest = gains.at[pl.ds(0, total - 1)]
    pltpu.make_async_copy(rest, rest, gain_sem.at[0]).wait()


def scatter_all(depth, d_qkv, d_squares, d_kv, d_gains, collective):
    items = [
        (0, 0, 3, 0), (0, 3, 6, 1),
        (2, 0, 1, 0), (2, 1, 2, 1),
        (1, 0, 1, 0), (1, 1, 2, 1),
        (1, 2, 3, 0),
    ]
    count = len(items)
    parts = (d_qkv, d_squares, d_kv)
    own, core, one, two, along = [], [], [], [], []
    for buffer, first, last, kind in items:
        rows, width = parts[buffer].shape[-2:]
        blocks = last - first
        own.append(pltpu.VMEM((blocks, depth, 2, 2, rows, width), jnp.bfloat16))
        core.append(pltpu.VMEM((blocks, depth, 2, 2, rows, width), jnp.bfloat16))
        one.append(pltpu.VMEM((blocks, depth, 2, rows, width), jnp.bfloat16))
        two.append(pltpu.VMEM((blocks, depth, rows, width), jnp.bfloat16))
        along.append(pltpu.VMEM((depth, blocks, rows, width), jnp.bfloat16))
    outs = [jax.ShapeDtypeStruct((p.shape[0],) + p.shape[-2:], jnp.float32) for p in parts]
    outs.append(jax.ShapeDtypeStruct(d_gains.shape[1:], jnp.float32))
    vmem = pl.BlockSpec(memory_space=pltpu.VMEM)
    return pl.pallas_call(
        functools.partial(scatter_kernel, depth, items),
        out_shape=outs,
        in_specs=[ANY] * 4,
        out_specs=[vmem] * 4,
        scratch_shapes=own + core + one + two + along + [
            pltpu.VMEM(d_gains.shape, jnp.float32),
            pltpu.SemaphoreType.DMA((count,)),
            pltpu.SemaphoreType.DMA((count, 4)),
            pltpu.SemaphoreType.DMA((count, 4)),
            pltpu.SemaphoreType.DMA((2,)),
        ],
        compiler_params=pltpu.CompilerParams(
            collective_id=collective, has_side_effects=True, vmem_limit_bytes=60 * 2**20
        ),
    )(d_qkv, d_squares, d_kv, d_gains)


HEADS = 12
HEAD_DIM = 64
SPAN = 64
NEIGHBOURS = 2
NEIGH_LEN = 128
MICRO = 2
UNITS = MICRO * HEADS
AXES = ("blk", "head")
TILE = 512
LEAD = SPAN - 1
DOC_MAX = 2000
SCORE_SCALE = 1.0 / math.sqrt(HEAD_DIM)
LOG2E = math.log2(math.e)


def tile_at(ref, index, row):
    return ref[row, :, pl.ds(pl.multiple_of(index * TILE, TILE), TILE)]


def row_at(ref, index):
    return ref[:, pl.ds(pl.multiple_of(index * TILE, TILE), TILE)]


def tile_mask(key_tile, query_tile, first_row, diagonal=True):
    key_place = key_tile * TILE + lax.broadcasted_iota(jnp.int32, (TILE, 1), 0)
    allowed = key_place >= first_row
    if diagonal:
        query_place = query_tile * TILE + lax.broadcasted_iota(jnp.int32, (1, TILE), 1)
        allowed = allowed & (key_place <= query_place)
    return allowed


def attn_forward_kernel(low_ref, first_ref, qkv_ref, shifted_ref, mixed_ref, total_ref):
    tiles = qkv_ref.shape[-1] // TILE

    def one_query(query_tile, carry):
        query_t = tile_at(qkv_ref, query_tile, 0)
        first_row = row_at(first_ref, query_tile)

        def one_key(step, state):
            peak, weight, mixed = state
            key_tile = query_tile - step
            keys = tile_at(qkv_ref, key_tile, 1).T
            scores = jnp.dot(keys, query_t, preferred_element_type=jnp.float32) * (SCORE_SCALE * LOG2E)
            scores = jnp.where(tile_mask(key_tile, query_tile, first_row), scores, -1e30)
            new_peak = jnp.maximum(peak, jnp.max(scores, axis=0, keepdims=True))
            probs = jnp.exp2(scores - new_peak)
            fade = jnp.exp2(peak - new_peak)
            weight = weight * fade + jnp.sum(probs, axis=0, keepdims=True)
            mixed = mixed * fade + jnp.dot(
                tile_at(qkv_ref, key_tile, 2), probs.astype(jnp.bfloat16), preferred_element_type=jnp.float32
            )
            return new_peak, weight, mixed

        start = (
            jnp.full((1, TILE), -1e30, jnp.float32),
            jnp.zeros((1, TILE), jnp.float32),
            jnp.zeros((HEAD_DIM, TILE), jnp.float32),
        )
        steps = query_tile + 1 - low_ref[query_tile]
        peak, weight, mixed = lax.fori_loop(0, steps, one_key, start)
        columns = pl.ds(pl.multiple_of(query_tile * TILE, TILE), TILE)
        mixed_ref[:, columns] = mixed / weight
        total_ref[:, columns] = peak + jnp.log2(weight)
        return carry

    lax.fori_loop(0, tiles, one_query, 0)
    length = qkv_ref.shape[-1]

    def turn(step, carry):
        rows = pl.ds(pl.multiple_of(step * 16, 16), 16)
        shifted_ref[rows, :] = pltpu.roll(mixed_ref[rows, :], length - LEAD, 1).astype(jnp.bfloat16)
        return carry

    lax.fori_loop(0, HEAD_DIM // 16, turn, 0)


def attn_backward_kernel(
    low_ref, high_ref, first_ref, qkv_ref, shifted_ref, mixed_ref, total_ref, out_ref, grad_ref, dq_ref, delta_ref
):
    length = qkv_ref.shape[-1]
    tiles = length // TILE
    delta_ref[...] = jnp.zeros_like(delta_ref)

    def turn(step, carry):
        rows = pl.ds(pl.multiple_of(step * 16, 16), 16)
        grad = pltpu.roll(shifted_ref[rows, :].astype(jnp.float32), LEAD, 1)
        grad_ref[rows, :] = grad.astype(jnp.bfloat16)
        delta_ref[...] += jnp.sum(grad * mixed_ref[rows, :], axis=0, keepdims=True)
        dq_ref[rows, :] = jnp.zeros((16, length), jnp.float32)
        return carry

    lax.fori_loop(0, HEAD_DIM // 16, turn, 0)

    def one_key(key_tile, carry):
        key_t = tile_at(qkv_ref, key_tile, 1)
        keys = key_t.T
        values = tile_at(qkv_ref, key_tile, 2).T

        def one_query(query_tile, state, diagonal=False):
            d_key, d_value = state
            query_t = tile_at(qkv_ref, query_tile, 0)
            grad_t = row_at(grad_ref, query_tile)
            scores = jnp.dot(keys, query_t, preferred_element_type=jnp.float32) * (SCORE_SCALE * LOG2E)
            allowed = tile_mask(key_tile, query_tile, row_at(first_ref, query_tile), diagonal)
            probs = jnp.where(allowed, jnp.exp2(scores - row_at(total_ref, query_tile)), 0.0)
            d_probs = jnp.dot(values, grad_t, preferred_element_type=jnp.float32)
            d_scores = (probs * (d_probs - row_at(delta_ref, query_tile))).astype(jnp.bfloat16)
            d_value = d_value + jnp.dot(
                probs.astype(jnp.bfloat16), grad_t.T, preferred_element_type=jnp.float32
            )
            d_key = d_key + jnp.dot(d_scores, query_t.T, preferred_element_type=jnp.float32)
            columns = pl.ds(pl.multiple_of(query_tile * TILE, TILE), TILE)
            dq_ref[:, columns] += jnp.dot(key_t, d_scores, preferred_element_type=jnp.float32)
            return d_key, d_value

        zeros = jnp.zeros((TILE, HEAD_DIM), jnp.float32)
        @pl.when(high_ref[key_tile] > key_tile)
        def _():
            state = one_query(key_tile, (zeros, zeros), diagonal=True)
            d_key, d_value = lax.fori_loop(key_tile + 1, high_ref[key_tile], one_query, state)
            columns = pl.ds(pl.multiple_of(key_tile * TILE, TILE), TILE)
            out_ref[1, :, columns] = (d_key * SCORE_SCALE).T.astype(jnp.bfloat16)
            out_ref[2, :, columns] = d_value.T.astype(jnp.bfloat16)

        return carry

    lax.fori_loop(0, tiles, one_key, 0)

    def finish(step, carry):
        rows = pl.ds(pl.multiple_of(step * 16, 16), 16)
        out_ref[0, rows, :] = (dq_ref[rows, :] * SCORE_SCALE).astype(jnp.bfloat16)
        return carry

    lax.fori_loop(0, HEAD_DIM // 16, finish, 0)


SMEM = pl.BlockSpec(memory_space=pltpu.SMEM)
VMEM = pl.BlockSpec(memory_space=pltpu.VMEM)


def local_params():
    return pltpu.CompilerParams(vmem_limit_bytes=60 * 2**20)


def attn_forward(low, first, qkv):
    width, length = qkv.shape[1:]
    return pl.pallas_call(
        attn_forward_kernel,
        out_shape=[
            jax.ShapeDtypeStruct((width, length), jnp.bfloat16),
            jax.ShapeDtypeStruct((width, length), jnp.float32),
            jax.ShapeDtypeStruct((1, length), jnp.float32),
        ],
        in_specs=[SMEM, VMEM, VMEM],
        out_specs=[VMEM] * 3,
        compiler_params=local_params(),
        cost_estimate=pl.CostEstimate(flops=10**9, bytes_accessed=4 * 10**6, transcendentals=4 * 10**6),
    )(low, first, qkv)


def attn_backward(low, high, first, qkv, shifted, mixed, totals):
    width, length = qkv.shape[1:]
    return pl.pallas_call(
        attn_backward_kernel,
        out_shape=jax.ShapeDtypeStruct((3, width, length), jnp.bfloat16),
        in_specs=[SMEM, SMEM] + [VMEM] * 5,
        out_specs=VMEM,
        scratch_shapes=[
            pltpu.VMEM((width, length), jnp.bfloat16),
            pltpu.VMEM((width, length), jnp.float32),
            pltpu.VMEM((1, length), jnp.float32),
        ],
        compiler_params=local_params(),
        cost_estimate=pl.CostEstimate(flops=3 * 10**9, bytes_accessed=4 * 10**6, transcendentals=4 * 10**6),
    )(low, high, first, qkv, shifted, mixed, totals)


def dot_nn(left, right):
    return jnp.dot(left, right, preferred_element_type=jnp.float32)


def dot_nt(left, right):
    return lax.dot_general(left, right, (((1,), (1,)), ((), ())), preferred_element_type=jnp.float32)


def dot_tn(left, right):
    return lax.dot_general(left, right, (((0,), (0,)), ((), ())), preferred_element_type=jnp.float32)


def norm_parts(values):
    centred = values - jnp.mean(values, axis=-1, keepdims=True)
    scale = lax.rsqrt(jnp.mean(centred * centred, axis=-1, keepdims=True) + 1e-05)
    return centred * scale, scale


def norm_pull(values, gain, grad):
    unit, scale = norm_parts(values)
    scaled = grad * gain
    pulled = scale * (
        scaled
        - jnp.mean(scaled, axis=-1, keepdims=True)
        - unit * jnp.mean(scaled * unit, axis=-1, keepdims=True)
    )
    return pulled, jnp.sum(grad * unit, axis=0, keepdims=True)


def shift_rows(rows, lead):
    joined = jnp.concatenate([rows.astype(jnp.float32), lead.astype(jnp.float32)], axis=0)
    return pltpu.roll(joined, joined.shape[0] - LEAD, 0)[: rows.shape[0]]


def stack_pair(rows):
    lane = lax.broadcasted_iota(jnp.int32, rows.shape, 1)
    zero = jnp.zeros_like(rows)
    return jnp.concatenate(
        [jnp.where(lane < HEAD_DIM, rows, zero), jnp.where(lane < HEAD_DIM, zero, rows)], axis=0
    )


def unstack_pair(rows):
    lane = lax.broadcasted_iota(jnp.int32, (SPAN, 2 * HEAD_DIM), 1)
    return jnp.where(lane < HEAD_DIM, rows[:SPAN], rows[SPAN:])


def middle_kernel(
    att_ref, hid_ref, lead_hid_ref, grad_ref, lead_grad_ref, gain_ref, used_ref, sq_ref, kv_hbm, neigh_hbm,
    up_hbm, down_hbm,
    result_ref, first_ref, d_att_ref, n2_ref, d_cq_ref, cm_ref, gc_ref, ga_ref, gy_ref, act_ref, d_pair_ref,
    d_gain_ref, d_up_hbm,
    kv_ref, neigh_ref, up_ref, down_ref, att_rows, second_ref, cq_ref, pair_ref, prob_ref, acc_ref, d_n3_ref,
    n3_ref, n3t_ref, d_up_ref, sems,
):
    micro, tokens, width = hid_ref.shape
    rows = micro * tokens
    pulls = [
        pltpu.make_async_copy(src, dst, sems.at[index])
        for index, (src, dst) in enumerate(
            [(kv_hbm, kv_ref), (neigh_hbm, neigh_ref), (up_hbm, up_ref), (down_hbm, down_ref)]
        )
    ]
    for pull in pulls:
        pull.start()
    gain_cross, gain_mlp = gain_ref[1:2, :], gain_ref[2:3, :]
    for index in range(micro):
        part = pl.ds(index * tokens, tokens)
        hidden = shift_rows(hid_ref[index], lead_hid_ref[index])
        gy_ref[part, :] = shift_rows(grad_ref[index], lead_grad_ref[index]).astype(jnp.bfloat16)
        first_ref[part, :] = hidden + dot_tn(att_ref[index], sq_ref[0])
    n2_ref[...] = (norm_parts(first_ref[...])[0] * gain_cross).astype(jnp.bfloat16)
    cq_ref[...] = dot_nn(n2_ref[...], sq_ref[1]).astype(jnp.bfloat16)

    pulls[0].wait()
    pulls[1].wait()
    chunk = 256
    chunks = neigh_ref.shape[0] // chunk

    def make_pairs(step, carry):
        side, block = step // chunks, lax.rem(step, chunks)
        part = pl.ds(pl.multiple_of(block * chunk, chunk), chunk)
        pair_ref[side, part, :] = dot_nn(neigh_ref[part, :], kv_ref[side]).astype(jnp.bfloat16)
        return carry

    lax.fori_loop(0, 2 * chunks, make_pairs, 0)
    couples = HEADS // 2
    pair_rows = NEIGHBOURS * NEIGH_LEN
    groups = rows // SPAN

    def where(step):
        group, couple = step // couples, lax.rem(step, couples)
        tok = pl.ds(pl.multiple_of(group * SPAN, SPAN), SPAN)
        key = pl.ds(pl.multiple_of(group * pair_rows, pair_rows), pair_rows)
        lanes = pl.ds(pl.multiple_of(couple * 2 * HEAD_DIM, 2 * HEAD_DIM), 2 * HEAD_DIM)
        return tok, key, lanes

    def cross_step(step, carry):
        tok, key, lanes = where(step)
        query = stack_pair(cq_ref[tok, lanes])
        scores = dot_nt(query, pair_ref[0, key, lanes]) * SCORE_SCALE
        weights = jnp.exp(scores - jnp.max(scores, axis=-1, keepdims=True))
        probs = weights / jnp.sum(weights, axis=-1, keepdims=True)
        prob_ref[step] = probs
        mixed = unstack_pair(dot_nn(probs.astype(jnp.bfloat16), pair_ref[1, key, lanes]))
        cm_ref[tok, lanes] = (mixed * used_ref[tok, :]).astype(jnp.bfloat16)
        return carry

    lax.fori_loop(0, groups * couples, cross_step, 0)
    second_ref[...] = first_ref[...] + dot_nn(cm_ref[...], sq_ref[2])
    n3 = (norm_parts(second_ref[...])[0] * gain_mlp).astype(jnp.bfloat16)
    n3_ref[...] = n3
    n3t_ref[...] = n3.T
    acc_ref[...] = second_ref[...]
    d_n3_ref[...] = jnp.zeros_like(d_n3_ref)
    pulls[2].wait()
    pulls[3].wait()
    ff_blocks = up_ref.shape[0]

    def mlp_step(step, carry):
        cols = pl.ds(pl.multiple_of(step * width, width), width)
        upper = dot_nn(n3_ref[...], up_ref[step])
        square = upper * upper
        flat = jnp.tanh(math.sqrt(2.0 / math.pi) * upper * (1.0 + 0.044715 * square))
        half = 0.5 * (1.0 + flat)
        active = (upper * half).astype(jnp.bfloat16)
        act_ref[:, cols] = active
        slope = half + 0.5 * upper * (1.0 - flat * flat) * math.sqrt(2.0 / math.pi) * (
            1.0 + 3.0 * 0.044715 * square
        )
        d_upper = (dot_nt(gy_ref[...], down_ref[cols, :]) * slope).astype(jnp.bfloat16)
        acc_ref[...] += dot_nn(active, down_ref[cols, :])
        d_n3_ref[...] += dot_nt(d_upper, up_ref[step])
        d_up_ref[:, cols] = dot_nn(n3t_ref[...], d_upper).astype(jnp.bfloat16)
        pltpu.make_async_copy(d_up_ref.at[:, cols], d_up_hbm.at[:, cols], sems.at[4]).start()
        return carry

    lax.fori_loop(0, ff_blocks, mlp_step, 0)
    result_ref[...] = acc_ref[...].astype(jnp.bfloat16)
    pulled, d_gain_mlp = norm_pull(second_ref[...], gain_mlp, d_n3_ref[...])
    d_second = gy_ref[...].astype(jnp.float32) + pulled
    acc_ref[...] = d_second
    gc_ref[...] = d_second.astype(jnp.bfloat16)
    att_rows[...] = (
        dot_nt(gc_ref[...], sq_ref[2]).astype(jnp.bfloat16).astype(jnp.float32) * used_ref[...]
    ).astype(jnp.bfloat16)

    def cross_back(step, carry):
        tok, key, lanes = where(step)
        grad = stack_pair(att_rows[tok, lanes])
        query = stack_pair(cq_ref[tok, lanes])
        probs = prob_ref[step]
        d_probs = dot_nt(grad, pair_ref[1, key, lanes])
        d_scores = (
            probs * (d_probs - jnp.sum(probs * d_probs, axis=-1, keepdims=True))
        ).astype(jnp.bfloat16)
        d_query = unstack_pair(dot_nn(d_scores, pair_ref[0, key, lanes]))
        d_cq_ref[tok, lanes] = (d_query * SCORE_SCALE).astype(jnp.bfloat16)
        d_pair_ref[0, key, lanes] = (dot_tn(d_scores, query) * SCORE_SCALE).astype(jnp.bfloat16)
        d_pair_ref[1, key, lanes] = dot_tn(probs.astype(jnp.bfloat16), grad).astype(jnp.bfloat16)
        return carry

    lax.fori_loop(0, groups * couples, cross_back, 0)
    pulled, d_gain_cross = norm_pull(first_ref[...], gain_cross, dot_nt(d_cq_ref[...], sq_ref[1]))
    d_first = acc_ref[...] + pulled
    first_ref[...] = d_first
    ga_ref[...] = d_first.astype(jnp.bfloat16)
    for index in range(micro):
        d_att_ref[index] = dot_nt(sq_ref[0], ga_ref[pl.ds(index * tokens, tokens), :]).astype(jnp.bfloat16)
    d_gain_ref[...] = jnp.concatenate([d_gain_cross, d_gain_mlp, jnp.zeros((6, width), jnp.float32)], axis=0)
    pltpu.make_async_copy(d_up_ref, d_up_hbm, sems.at[4]).wait()


def middle(attended_t, hidden, lead_hid, grads, lead_grad, gains, used, squares, kv, neigh, up, down):
    micro, tokens, width = hidden.shape
    rows = micro * tokens
    ff = up.shape[0] * width
    low = jnp.bfloat16
    out_shape = [
        jax.ShapeDtypeStruct((rows, width), low),
        jax.ShapeDtypeStruct((rows, width), jnp.float32),
        jax.ShapeDtypeStruct((micro, width, tokens), low),
        jax.ShapeDtypeStruct((rows, width), low),
        jax.ShapeDtypeStruct((rows, width), low),
        jax.ShapeDtypeStruct((rows, width), low),
        jax.ShapeDtypeStruct((rows, width), low),
        jax.ShapeDtypeStruct((rows, width), low),
        jax.ShapeDtypeStruct((rows, width), low),
        jax.ShapeDtypeStruct((rows, ff), low),
        jax.ShapeDtypeStruct((2,) + neigh.shape, low),
        jax.ShapeDtypeStruct((8, width), jnp.float32),
        jax.ShapeDtypeStruct((width, ff), low),
    ]
    steps = rows // SPAN * HEADS // 2
    scratch = [
        pltpu.VMEM(kv.shape, low),
        pltpu.VMEM(neigh.shape, low),
        pltpu.VMEM(up.shape, low),
        pltpu.VMEM(down.shape, low),
        pltpu.VMEM((rows, width), low),
        pltpu.VMEM((rows, width), jnp.float32),
        pltpu.VMEM((rows, width), low),
        pltpu.VMEM((2,) + neigh.shape, low),
        pltpu.VMEM((steps, 2 * SPAN, NEIGHBOURS * NEIGH_LEN), jnp.float32),
        pltpu.VMEM((rows, width), jnp.float32),
        pltpu.VMEM((rows, width), jnp.float32),
        pltpu.VMEM((rows, width), low),
        pltpu.VMEM((width, rows), low),
        pltpu.VMEM((width, ff), low),
        pltpu.SemaphoreType.DMA((5,)),
    ]
    return pl.pallas_call(
        middle_kernel,
        out_shape=out_shape,
        in_specs=[VMEM] * 8 + [ANY] * 4,
        out_specs=[VMEM] * 12 + [ANY],
        scratch_shapes=scratch,
        compiler_params=local_params(),
        cost_estimate=pl.CostEstimate(flops=12 * 10**9, bytes_accessed=40 * 10**6, transcendentals=10**6),
    )(attended_t, hidden, lead_hid, grads, lead_grad, gains, used, squares, kv, neigh, up, down)


PLAN = (0, 0, 1, 0, 0, 1, 0, 0, 1, 1, 1, 0)


def front_kernel(depth, items, *refs):
    count = len(items)
    w_refs = refs[:7]
    gain_in, seg_in, valid_in, neigh_ref, hid_ref, grad_hbm = refs[7:13]
    (
        qkv_out, sq_out, kv_out, up_out, down_out, d_up_hbm, unit_hbm, mixed_hbm, act_hbm, d_pair_hbm,
        gain_out, cos_out, sin_out, total_out, start_out, att_out,
        result_ref, first_ref, back_out, n2_ref, d_cq_ref, cm_ref, gc_ref, ga_ref, gy_ref, d_gain_ref,
    ) = refs[13:39]
    (
        qkv_ref, small_all, hid_vmem, grad_ref, lead_hid, lead_grad, n1_ref, temp_ref, note_ref, turned_ref, doc_ref,
        stage_ref, sq_ref, kv_ref, up_ref, down_ref,
        att_rows, second_ref, cq_ref, pair_ref, prob_ref, acc_ref, d_n3_ref, n3_ref, n3t_ref, d_up_ref,
        own_sem, send_sem, recv_sem, misc_sem, lead_send, lead_recv, load_sem, unit_send, unit_recv,
        att_send, att_recv, stage_sem, up_sem, grad_send, grad_recv, store_sem,
        unit_out, mixed_out, act_ref, d_pair_ref, d_att_ref, d_upper_ref, small_ref, used_ref,
    ) = refs[39:]
    z, y, c, x = coords()
    total = depth * 8
    me = lax.axis_index("blk") * 2 + lax.axis_index("head")
    mine, holder = unit_of(me, total)
    slab = w_refs[0].shape[0]
    micro, tokens, width = hid_ref.shape
    homes = (qkv_ref, sq_out, kv_out, up_out, down_out)
    whole = slice(None)

    def view(item, zs, ys, cs, xs):
        buffer, first, last, kind = item
        if buffer == 4:
            return down_out.at[zs, ys, cs, xs, pl.ds(first, last - first)]
        return homes[buffer].at[pl.ds(first, last - first), zs, ys, cs, xs]

    load = pltpu.make_async_copy(hid_ref, hid_vmem, load_sem.at[0])
    load.start()
    load_grad = pltpu.make_async_copy(grad_hbm, grad_ref, load_sem.at[2])
    load_grad.start()
    own = []
    for index, item in enumerate(items):
        buffer, first, last, kind = item
        cols = homes[buffer].shape[-1]
        if buffer == 4:
            moves = [(w_refs[6].at[pl.ds(first, last - first)], view(item, z, y, c, x))]
        elif buffer == 1:
            moves = [(w_refs[1 + block], sq_out.at[block, z, y, c, x]) for block in range(first, last)]
        else:
            source = w_refs[(0, None, 4, 5)[buffer]]
            moves = [
                (source.at[:, pl.ds(block * cols, cols)], homes[buffer].at[block, z, y, c, x])
                for block in range(first, last)
            ]
        for src, dst in moves:
            pltpu.make_async_copy(src, dst, own_sem.at[index]).start()
        mirror = view(item, z, y, c, x)
        own.append(pltpu.make_async_copy(mirror, mirror, own_sem.at[index]))
    turned_gain = gain_in[...].T[:32]
    lane_at = lax.broadcasted_iota(jnp.int32, (32, 128), 1)
    small_ref[0:32, :] = jnp.where(
        lane_at < 32, turned_gain[:, 0:1], jnp.where(lane_at < 64, turned_gain[:, 1:2], turned_gain[:, 2:3])
    ).astype(jnp.bfloat16)
    small_ref[32:48, :] = jnp.concatenate(
        [seg_in[...].astype(jnp.float32), jnp.zeros((16 - micro, 128), jnp.float32)], axis=0
    ).astype(jnp.bfloat16)
    row_at_ = lax.broadcasted_iota(jnp.int32, (micro * tokens, 1), 0)
    spans = tokens // SPAN
    flag = jnp.zeros((micro * tokens, 1), jnp.float32)
    for span in range(micro * spans):
        value = valid_in[span // spans, span % spans].astype(jnp.float32)
        flag = jnp.where(row_at_ // SPAN == span, value, flag)
    used_ref[...] = jnp.where(me * tokens + lax.rem(row_at_, tokens) + LEAD < tokens * total, flag, 0.0)
    pltpu.make_async_copy(small_ref, small_all.at[me], misc_sem.at[1]).start()
    all_barrier(total, me)

    def send_small(step, carry):
        peer = lax.rem(me + step, total)
        remote(
            small_ref, small_all.at[me], misc_sem.at[0], misc_sem.at[1], (peer // 2, lax.rem(peer, 2))
        ).start()
        return carry

    prev = lax.rem(me + total - 1, total)
    prev_at = (prev // 2, lax.rem(prev, 2))
    leads = [
        remote(hid_ref.at[:, pl.ds(0, 64)], lead_hid, lead_send.at[0], lead_recv.at[0], prev_at),
        remote(grad_hbm.at[:, pl.ds(0, 64)], lead_grad, lead_send.at[1], lead_recv.at[1], prev_at),
    ]

    def start(index):
        own[index].wait()
        item = items[index]
        for step in range(1, depth):
            other = lax.rem(z + step, depth)
            remote(
                view(item, z, y, c, x), view(item, z, y, c, x),
                send_sem.at[index, 0], recv_sem.at[index, 0], place(other, y, c, x),
            ).start()

    def bulk(index, phase):
        item = items[index]
        first_x = item[3] == 0
        if phase == 1:
            ref = view(item, whole, y, c, x)
            where = place(z, y, c, 1 - x) if first_x else place(z, 1 - y, c, x)
        elif phase == 2:
            ref = view(item, whole, y, c, whole) if first_x else view(item, whole, whole, c, x)
            where = place(z, 1 - y, c, x) if first_x else place(z, y, c, 1 - x)
        else:
            ref = view(item, whole, whole, c, whole)
            where = place(z, y, 1 - c, x)
        return remote(ref, ref, send_sem.at[index, phase], recv_sem.at[index, phase], where)

    def arrived(index, phase):
        if phase == 0:
            ref = view(items[index], pl.ds(0, depth - 1), y, c, x)
            pltpu.make_async_copy(ref, ref, recv_sem.at[index, 0]).wait()
        else:
            bulk(index, phase).wait_recv()

    def sent(index, phase):
        if phase == 0:
            ref = view(items[index], pl.ds(0, depth - 1), y, c, x)
            pltpu.make_async_copy(ref, ref, send_sem.at[index, 0]).wait()
        else:
            bulk(index, phase).wait_send()

    pairs = (count + 1) // 2

    def gather_step(step):
        for phase in range(4, -1, -1):
            pair = step - phase
            if not 0 <= pair < pairs:
                continue
            for index in range(2 * pair, min(2 * pair + 2, count)):
                if phase == 0:
                    start(index)
                else:
                    arrived(index, phase - 1)
                    if phase < 4:
                        bulk(index, phase).start()

    half_dim = HEAD_DIM // 2

    def tables():
        lane = lax.broadcasted_iota(jnp.int32, (half_dim, tokens), 1)
        order = lax.broadcasted_iota(jnp.int32, (half_dim, tokens), 0)
        frequency = jnp.exp(order.astype(jnp.float32) * (-2.0 * math.log(10000.0) / HEAD_DIM))
        angles = (me * tokens + lane).astype(jnp.float32) * frequency
        cos_out[...] = jnp.cos(angles)
        sin_out[...] = jnp.sin(angles)

    def normalise():
        load.wait()
        pltpu.make_async_copy(small_all, small_all, misc_sem.at[1]).wait()
        for peer in range(total):
            temp_ref[pl.ds(peer * slab, slab), pl.ds(0, 128)] = small_all[peer, :slab, :].astype(jnp.float32)
            doc_ref[pl.ds(peer, 1), :] = jnp.where(
                mine < HEADS, small_all[peer, 32:33, :].astype(jnp.float32), small_all[peer, 33:34, :].astype(jnp.float32)
            )
        turned = temp_ref[:, pl.ds(0, 128)].T
        gain_out[...] = jnp.concatenate(
            [turned[0:1], turned[32:33], turned[64:65], jnp.zeros((5, width), jnp.float32)], axis=0
        )
        for index in range(micro):
            unit_rows = norm_parts(hid_vmem[index].astype(jnp.float32))[0]
            n1_ref[pl.ds(index * tokens, tokens), :] = (unit_rows * gain_out[0:1, :]).astype(jnp.bfloat16)

    def project(part):
        cols = qkv_ref.shape[-1]
        heads = cols // HEAD_DIM
        for half in range(2):
            block = part * 2 + half
            for level in range(depth):
                for inner in range(8):
                    at = (level * 8 + inner) * slab
                    temp_ref[pl.ds(at, slab), :] = qkv_ref[
                        block, level, inner // 4, (inner // 2) % 2, inner % 2
                    ].astype(jnp.float32)
            raw = dot_nn(n1_ref[...], temp_ref[...].astype(jnp.bfloat16))
            for index in range(micro):
                raw_t = raw[index * tokens : (index + 1) * tokens].T
                for head in range(heads):
                    value = raw_t[head * HEAD_DIM : (head + 1) * HEAD_DIM]
                    if part < 2:
                        first_half, second_half = value[:half_dim], value[half_dim:]
                        value = jnp.concatenate(
                            [
                                first_half * cos_out[...] - second_half * sin_out[...],
                                second_half * cos_out[...] + first_half * sin_out[...],
                            ],
                            axis=0,
                        )
                    note_ref[index * HEADS + half * heads + head, part] = value.astype(jnp.bfloat16)

    def slot(device, part):
        return unit_out.at[part, :, pl.ds(pl.multiple_of(device * tokens, 128), tokens)]

    def send_part(part):
        @pl.when(holder)
        def _():
            pltpu.make_async_copy(note_ref.at[mine, part], slot(me, part), unit_recv).start()

        def send(step, carry):
            peer = lax.rem(me + step, total)
            unit, held = unit_of(peer, total)

            @pl.when(held)
            def _():
                remote(
                    note_ref.at[unit, part], slot(me, part), unit_send, unit_recv, (peer // 2, lax.rem(peer, 2))
                ).start()

            return carry

        lax.fori_loop(1, total, send, 0)

    def doc_starts():
        docs = doc_ref[...]
        lane = lax.broadcasted_iota(jnp.int32, docs.shape, 1)
        row = lax.broadcasted_iota(jnp.int32, docs.shape, 0)
        place_at = row * tokens + lane
        before = jnp.where(
            lane == 0, pltpu.roll(pltpu.roll(docs, 1, 0), 1, 1), pltpu.roll(docs, 1, 1)
        )
        begins = (docs != before) | (place_at == 0)
        value = jnp.where(begins, place_at, 0).astype(jnp.float32)
        step = 1
        while step < tokens:
            value = jnp.maximum(value, jnp.where(lane >= step, pltpu.roll(value, step, 1), 0.0))
            step *= 2
        carried = jnp.broadcast_to(jnp.max(value, axis=1, keepdims=True), docs.shape)
        carried = jnp.where(row >= 1, pltpu.roll(carried, 1, 0), 0.0)
        step = 1
        while step < total:
            carried = jnp.maximum(carried, jnp.where(row >= step, pltpu.roll(carried, step, 0), 0.0))
            step *= 2
        starts = jnp.maximum(value, carried).astype(jnp.int32)
        for peer in range(total):
            start_out[:, pl.ds(peer * tokens, tokens)] = starts[peer : peer + 1, :]

    length = tokens * total
    tiles = length // TILE
    reach = (TILE + DOC_MAX - 2) // TILE

    def open_units():
        @pl.when(holder)
        def _():
            part = note_ref.at[pl.ds(0, UNITS - 1)]
            pltpu.make_async_copy(unit_out, unit_out, unit_recv).wait()
            pltpu.make_async_copy(part, part, unit_send).wait()

        @pl.when(jnp.logical_not(holder))
        def _():
            pltpu.make_async_copy(note_ref, note_ref, unit_send).wait()

    def attend(query_tile):
        @pl.when(holder)
        def _():
            columns = pl.ds(query_tile * TILE, TILE)
            query_t = unit_out[0, :, columns]
            first_row = start_out[:, columns]

            def one_key(step, state, diagonal=False):
                peak, weight, mixed = state
                key_tile = query_tile - step
                scores = dot_nn(tile_at(unit_out, key_tile, 1).T, query_t) * (SCORE_SCALE * LOG2E)
                allowed = tile_mask(key_tile, query_tile, first_row, diagonal)
                scores = jnp.where(allowed, scores, -1e30)
                new_peak = jnp.maximum(peak, jnp.max(scores, axis=0, keepdims=True))
                probs = jnp.exp2(scores - new_peak)
                fade = jnp.exp2(peak - new_peak)
                weight = weight * fade + jnp.sum(probs, axis=0, keepdims=True)
                mixed = mixed * fade + dot_nn(tile_at(unit_out, key_tile, 2), probs.astype(jnp.bfloat16))
                return new_peak, weight, mixed

            begin = (
                jnp.full((1, TILE), -1e30, jnp.float32),
                jnp.zeros((1, TILE), jnp.float32),
                jnp.zeros((HEAD_DIM, TILE), jnp.float32),
            )
            begin = one_key(0, begin, diagonal=True)
            peak, weight, mixed = lax.fori_loop(1, min(query_tile, reach) + 1, one_key, begin)
            mixed_out[:, columns] = mixed / weight
            total_out[:, columns] = peak + jnp.log2(weight)

    def back_slot(device):
        return turned_ref.at[:, pl.ds(pl.multiple_of(device * tokens, 128), tokens)]

    def send_back():
        @pl.when(holder)
        def _():
            def turn(step, carry):
                part = pl.ds(pl.multiple_of(step * 16, 16), 16)
                turned_ref[part, :] = pltpu.roll(mixed_out[part, :], length - LEAD, 1).astype(jnp.bfloat16)
                return carry

            lax.fori_loop(0, HEAD_DIM // 16, turn, 0)
            pltpu.make_async_copy(back_slot(me), att_out.at[mine], att_recv).start()

            def send(step, carry):
                peer = lax.rem(me + step, total)
                remote(
                    back_slot(peer), att_out.at[mine], att_send, att_recv, (peer // 2, lax.rem(peer, 2))
                ).start()
                return carry

            lax.fori_loop(1, total, send, 0)

    def unpack(jobs):
        copies = [
            pltpu.make_async_copy(source.at[block], stage_ref.at[slot_], stage_sem.at[slot_])
            for slot_, (source, block, target) in enumerate(jobs)
        ]
        for copy in copies:
            copy.start()
        for slot_, (source, block, target) in enumerate(jobs):
            copies[slot_].wait()

            def body(level, carry):
                for inner in range(4):
                    both = jnp.concatenate(
                        [stage_ref[slot_, level, inner // 2, inner % 2, side].astype(jnp.float32) for side in range(2)],
                        axis=0,
                    )
                    at = pl.multiple_of((level * 4 + inner) * 2 * slab, 16)
                    target[block, pl.ds(at, 2 * slab), :] = both.astype(jnp.bfloat16)
                return carry

            lax.fori_loop(0, depth, body, 0)

    def fetch_down():
        down_rows = down_out.shape[-2]

        def body(step, carry):
            level, rest_ = step // 8, lax.rem(step, 8)
            pltpu.make_async_copy(
                down_out.at[level, rest_ // 4, lax.rem(rest_ // 2, 2), lax.rem(rest_, 2)],
                down_ref.at[pl.ds(pl.multiple_of(step * down_rows, 16), down_rows)],
                stage_sem.at[2],
            ).start()
            return carry

        lax.fori_loop(0, total, body, 0)

    gather_step(0)
    lax.fori_loop(1, total, send_small, 0)
    tables()
    gather_step(1)
    gather_step(2)
    for lead in leads:
        lead.start()
    normalise()
    gather_step(3)
    doc_starts()
    for part in range(3):
        gather_step(4 + part)
        if part == 2:
            keep = pltpu.make_async_copy(qkv_ref, qkv_out, load_sem.at[1])
            keep.start()
        project(part)
        send_part(part)
    def grad_slot(device):
        return back_out.at[:, pl.ds(pl.multiple_of(device * tokens, 128), tokens)]

    def send_grads(index):
        @pl.when(holder & (mine // HEADS == index))
        def _():
            pltpu.make_async_copy(d_att_ref.at[mine], grad_slot(me), grad_recv).start()

        def send(step, carry):
            peer = lax.rem(me + step, total)
            unit, held = unit_of(peer, total)

            @pl.when(held & (unit // HEADS == index))
            def _():
                remote(
                    d_att_ref.at[unit], grad_slot(me), grad_send, grad_recv, (peer // 2, lax.rem(peer, 2))
                ).start()

            return carry

        lax.fori_loop(1, total, send, 0)

    stores = [
        pltpu.make_async_copy(source, target, store_sem.at[index])
        for index, (source, target) in enumerate(
            [(unit_out, unit_hbm), (mixed_out, mixed_hbm), (act_ref, act_hbm), (d_pair_ref, d_pair_hbm)]
        )
    ]
    rows = micro * tokens
    done = {"tick": 7}

    def tick(number=1):
        for _ in range(number):
            if done["tick"] < pairs + 4:
                gather_step(done["tick"])
                done["tick"] += 1

    def make_key_values():
        chunk = 256
        chunks = neigh_ref.shape[0] // chunk

        def make_pairs(step, carry):
            side, block = step // chunks, lax.rem(step, chunks)
            part = pl.ds(pl.multiple_of(block * chunk, chunk), chunk)
            pair_ref[side, part, :] = dot_nn(neigh_ref[part, :], kv_ref[side]).astype(jnp.bfloat16)
            return carry

        lax.fori_loop(0, 2 * chunks, make_pairs, 0)
    couples = HEADS // 2
    pair_rows = NEIGHBOURS * NEIGH_LEN
    groups = rows // SPAN

    def where(group, couple):
        tok = pl.ds(pl.multiple_of(group * SPAN, SPAN), SPAN)
        key = pl.ds(pl.multiple_of(group * pair_rows, pair_rows), pair_rows)
        lanes = pl.ds(couple * 2 * HEAD_DIM, 2 * HEAD_DIM)
        return tok, key, lanes

    def cross_step(group, carry):
        for couple in range(couples):
            tok, key, lanes = where(group, couple)
            query = stack_pair(cq_ref[tok, lanes])
            scores = dot_nt(query, pair_ref[0, key, lanes]) * SCORE_SCALE
            weights = jnp.exp(scores - jnp.max(scores, axis=-1, keepdims=True))
            probs = weights / jnp.sum(weights, axis=-1, keepdims=True)
            prob_ref[group * couples + couple] = probs
            mixed = unstack_pair(dot_nn(probs.astype(jnp.bfloat16), pair_ref[1, key, lanes]))
            cm_ref[tok, lanes] = (mixed * used_ref[tok, :]).astype(jnp.bfloat16)
        return carry


    tick()
    unpack([(kv_out, 0, kv_ref), (kv_out, 1, kv_ref)])
    make_key_values()
    tick(PLAN[0])
    open_units()
    for tile in range(tiles):
        attend(tile)
        tick(PLAN[1 + tile])
    send_back()
    stores[0].start()
    stores[1].start()
    tick(PLAN[1 + tiles])
    unpack([(sq_out, 0, sq_ref), (sq_out, 1, sq_ref)])
    load_grad.wait()
    for lead in leads:
        lead.wait_recv()
    pltpu.make_async_copy(att_out, att_out, att_recv).wait()
    gain_cross, gain_mlp = gain_out[1:2, :], gain_out[2:3, :]
    for index in range(micro):
        part = pl.ds(index * tokens, tokens)
        hidden = shift_rows(hid_vmem[index], lead_hid[index])
        gy_ref[part, :] = shift_rows(grad_ref[index], lead_grad[index]).astype(jnp.bfloat16)
        first_ref[part, :] = hidden + dot_tn(att_out[index * HEADS : (index + 1) * HEADS].reshape(width, tokens), sq_ref[0])
    n2_ref[...] = (norm_parts(first_ref[...])[0] * gain_cross).astype(jnp.bfloat16)
    cq_ref[...] = dot_nn(n2_ref[...], sq_ref[1]).astype(jnp.bfloat16)

    tick(PLAN[2 + tiles])
    lax.fori_loop(0, groups // 2, cross_step, 0)
    tick(PLAN[3 + tiles])
    unpack([(sq_out, 2, sq_ref), (up_out, 0, up_ref)])
    lax.fori_loop(groups // 2, groups, cross_step, 0)
    second_ref[...] = first_ref[...] + dot_nn(cm_ref[...], sq_ref[2])
    n3 = (norm_parts(second_ref[...])[0] * gain_mlp).astype(jnp.bfloat16)
    n3_ref[...] = n3
    n3t_ref[...] = n3.T
    acc_ref[...] = second_ref[...]
    d_n3_ref[...] = jnp.zeros_like(d_n3_ref)
    tick(pairs + 4 - done["tick"])
    fetch_down()
    unpack([(up_out, 1, up_ref), (up_out, 2, up_ref)])
    unpack([(up_out, 3, up_ref)])
    pltpu.make_async_copy(down_ref, down_ref, stage_sem.at[2]).wait()
    ff_blocks = up_ref.shape[0]
    for step in range(ff_blocks):
        cols = pl.ds(step * width, width)
        upper = dot_nn(n3_ref[...], up_ref[step])
        square = upper * upper
        flat = jnp.tanh(math.sqrt(2.0 / math.pi) * upper * (1.0 + 0.044715 * square))
        half = 0.5 * (1.0 + flat)
        active = (upper * half).astype(jnp.bfloat16)
        act_ref[:, cols] = active
        slope = half + 0.5 * upper * (1.0 - flat * flat) * math.sqrt(2.0 / math.pi) * (
            1.0 + 3.0 * 0.044715 * square
        )
        d_upper = (dot_nt(gy_ref[...], down_ref[cols, :]) * slope).astype(jnp.bfloat16)
        acc_ref[...] += dot_nn(active, down_ref[cols, :])
        d_n3_ref[...] += dot_nt(d_upper, up_ref[step])
        d_upper_ref[:, cols] = d_upper
    result_ref[...] = acc_ref[...].astype(jnp.bfloat16)
    stores[2].start()
    pulled, d_gain_mlp = norm_pull(second_ref[...], gain_mlp, d_n3_ref[...])
    d_second = gy_ref[...].astype(jnp.float32) + pulled
    acc_ref[...] = d_second
    gc_ref[...] = d_second.astype(jnp.bfloat16)
    att_rows[...] = (
        dot_nt(gc_ref[...], sq_ref[2]).astype(jnp.bfloat16).astype(jnp.float32) * used_ref[...]
    ).astype(jnp.bfloat16)

    def cross_back(group, carry):
        for couple in range(couples):
            tok, key, lanes = where(group, couple)
            grad = stack_pair(att_rows[tok, lanes])
            query = stack_pair(cq_ref[tok, lanes])
            probs = prob_ref[group * couples + couple]
            d_probs = dot_nt(grad, pair_ref[1, key, lanes])
            d_scores = (
                probs * (d_probs - jnp.sum(probs * d_probs, axis=-1, keepdims=True))
            ).astype(jnp.bfloat16)
            d_query = unstack_pair(dot_nn(d_scores, pair_ref[0, key, lanes]))
            d_cq_ref[tok, lanes] = (d_query * SCORE_SCALE).astype(jnp.bfloat16)
            d_pair_ref[0, key, lanes] = (dot_tn(d_scores, query) * SCORE_SCALE).astype(jnp.bfloat16)
            d_pair_ref[1, key, lanes] = dot_tn(probs.astype(jnp.bfloat16), grad).astype(jnp.bfloat16)
        return carry

    lax.fori_loop(0, groups, cross_back, 0)
    stores[3].start()
    pulled, d_gain_cross = norm_pull(first_ref[...], gain_cross, dot_nt(d_cq_ref[...], sq_ref[1]))
    d_first = acc_ref[...] + pulled
    first_ref[...] = d_first
    ga_ref[...] = d_first.astype(jnp.bfloat16)
    for index in range(micro):
        part = ga_ref[pl.ds(index * tokens, tokens), :]
        d_att_ref[index * HEADS : (index + 1) * HEADS] = (
            dot_nt(sq_ref[0], part).astype(jnp.bfloat16).reshape(HEADS, HEAD_DIM, tokens)
        )
        send_grads(index)
    d_gain_ref[...] = jnp.concatenate([d_gain_cross, d_gain_mlp, jnp.zeros((6, width), jnp.float32)], axis=0)
    d_up_moves = []
    for step in range(ff_blocks):
        cols = pl.ds(step * width, width)
        if step >= 2:
            d_up_moves[step - 2].wait()
        d_up_ref[step % 2] = dot_nn(n3t_ref[...], d_upper_ref[:, cols]).astype(jnp.bfloat16)
        move = pltpu.make_async_copy(d_up_ref.at[step % 2], d_up_hbm.at[:, cols], up_sem.at[step % 2])
        move.start()
        d_up_moves.append(move)
    for move in d_up_moves[-2:]:
        move.wait()


    for index in range(count):
        for phase in range(4):
            sent(index, phase)
    for lead in leads:
        lead.wait_send()
    keep.wait()
    rest = small_all.at[pl.ds(0, total - 1)]
    pltpu.make_async_copy(rest, rest, misc_sem.at[0]).wait()

    @pl.when(holder)
    def _():
        part = turned_ref.at[:, pl.ds(0, tokens * (total - 1))]
        pltpu.make_async_copy(part, part, att_send).wait()
    for store in stores:
        store.wait()

    @pl.when(holder)
    def _():
        part = d_att_ref.at[pl.ds(0, UNITS - 1)]
        pltpu.make_async_copy(back_out, back_out, grad_recv).wait()
        pltpu.make_async_copy(part, part, grad_send).wait()

    @pl.when(jnp.logical_not(holder))
    def _():
        pltpu.make_async_copy(d_att_ref, d_att_ref, grad_send).wait()


def front(
    depth, w_qkv, w_attn_out, w_cross_q, w_cross_out, w_kv, w_up, w_down, own_gains, segments, valid, neigh, hidden, grads
):
    total = depth * 8
    rows = w_qkv.shape[0]
    down_rows = w_down.shape[0]
    micro, tokens, width = hidden.shape
    length = tokens * total
    third = down_rows // 3
    row_total = micro * tokens
    ff = w_up.shape[1]
    items = [
        (0, 0, 1, 0), (0, 1, 2, 1), (0, 2, 3, 0), (0, 3, 4, 1), (0, 4, 5, 0), (0, 5, 6, 1),
        (2, 0, 1, 0), (2, 1, 2, 1),
        (1, 0, 1, 0), (1, 1, 2, 1),
        (1, 2, 3, 0), (3, 0, 1, 1),
        (4, 0, third, 0), (4, third, 2 * third, 1),
        (4, 2 * third, down_rows, 0), (3, 1, 2, 1),
        (3, 2, 3, 0), (3, 3, 4, 1),
    ]
    count = len(items)
    low, high = jnp.bfloat16, jnp.float32
    spots = (depth, 2, 2, 2)
    qkv_shape = (6, *spots, rows, width // 2)
    out_shape = [
        jax.ShapeDtypeStruct(qkv_shape, low),
        jax.ShapeDtypeStruct((3, *spots, rows, width), low),
        jax.ShapeDtypeStruct((2, *spots, rows, width), low),
        jax.ShapeDtypeStruct((w_up.shape[1] // width, *spots, rows, width), low),
        jax.ShapeDtypeStruct((*spots, down_rows, width), low),
        jax.ShapeDtypeStruct((width, w_up.shape[1]), low),
        jax.ShapeDtypeStruct((3, HEAD_DIM, length), low),
        jax.ShapeDtypeStruct((HEAD_DIM, length), high),
        jax.ShapeDtypeStruct((row_total, ff), low),
        jax.ShapeDtypeStruct((2,) + neigh.shape, low),
        jax.ShapeDtypeStruct((8, width), high),
        jax.ShapeDtypeStruct((HEAD_DIM // 2, tokens), high),
        jax.ShapeDtypeStruct((HEAD_DIM // 2, tokens), high),
        jax.ShapeDtypeStruct((1, length), high),
        jax.ShapeDtypeStruct((1, length), jnp.int32),
        jax.ShapeDtypeStruct((UNITS, HEAD_DIM, tokens), low),
        jax.ShapeDtypeStruct((row_total, width), low),
        jax.ShapeDtypeStruct((row_total, width), high),
        jax.ShapeDtypeStruct((HEAD_DIM, length), low),
        jax.ShapeDtypeStruct((row_total, width), low),
        jax.ShapeDtypeStruct((row_total, width), low),
        jax.ShapeDtypeStruct((row_total, width), low),
        jax.ShapeDtypeStruct((row_total, width), low),
        jax.ShapeDtypeStruct((row_total, width), low),
        jax.ShapeDtypeStruct((row_total, width), low),
        jax.ShapeDtypeStruct((8, width), high),
    ]
    steps = row_total // SPAN * HEADS // 2
    dma = pltpu.SemaphoreType.DMA
    return pl.pallas_call(
        functools.partial(front_kernel, depth, items),
        out_shape=out_shape,
        in_specs=[VMEM] * 9 + [SMEM] + [VMEM] + [ANY] * 2,
        out_specs=[ANY] * 10 + [VMEM] * 16,
        scratch_shapes=[
            pltpu.VMEM(qkv_shape, low),
            pltpu.VMEM((total, 48, 128), low),
            pltpu.VMEM(hidden.shape, low),
            pltpu.VMEM(hidden.shape, low),
            pltpu.VMEM((micro, 64, width), low),
            pltpu.VMEM((micro, 64, width), low),
            pltpu.VMEM((micro * tokens, width), low),
            pltpu.VMEM((width, width // 2), high),
            pltpu.VMEM((UNITS, 3, HEAD_DIM, tokens), low),
            pltpu.VMEM((HEAD_DIM, length), low),
            pltpu.VMEM((total, tokens), high),
            pltpu.VMEM((2, *spots, rows, width), low),
            pltpu.VMEM((3, width, width), low),
            pltpu.VMEM((2, width, width), low),
            pltpu.VMEM((ff // width, width, width), low),
            pltpu.VMEM((ff, width), low),
            pltpu.VMEM((row_total, width), low),
            pltpu.VMEM((row_total, width), high),
            pltpu.VMEM((row_total, width), low),
            pltpu.VMEM((2,) + neigh.shape, low),
            pltpu.VMEM((steps, 2 * SPAN, NEIGHBOURS * NEIGH_LEN), high),
            pltpu.VMEM((row_total, width), high),
            pltpu.VMEM((row_total, width), high),
            pltpu.VMEM((row_total, width), low),
            pltpu.VMEM((width, row_total), low),
            pltpu.VMEM((2, width, width), low),
            dma((count,)), dma((count, 4)), dma((count, 4)), dma((2,)), dma((2,)), dma((2,)), dma((3,)), dma, dma,
            dma, dma, dma((3,)), dma((2,)), dma, dma, dma((4,)),
            pltpu.VMEM((3, HEAD_DIM, length), low),
            pltpu.VMEM((HEAD_DIM, length), high),
            pltpu.VMEM((row_total, ff), low),
            pltpu.VMEM((2,) + neigh.shape, low),
            pltpu.VMEM((UNITS, HEAD_DIM, tokens), low),
            pltpu.VMEM((row_total, ff), low),
            pltpu.VMEM((48, 128), low),
            pltpu.VMEM((row_total, 1), high),
        ],
        compiler_params=pltpu.CompilerParams(
            collective_id=0, has_side_effects=True, vmem_limit_bytes=62 * 2**20
        ),
        cost_estimate=pl.CostEstimate(flops=10**9, bytes_accessed=20 * 10**6, transcendentals=0),
    )(w_qkv, w_attn_out, w_cross_q, w_cross_out, w_kv, w_up, w_down, own_gains, segments, valid, neigh, hidden, grads)


LAST_PLAN = (2, 0, 0, 1, 0, 0, 1, 0, 0, 1)


def last_kernel(depth, items, *refs):
    count = len(items)
    unit_hbm, result_hbm, first_hbm = refs[:3]
    sources = refs[1:14] + refs[15:16]
    qkv_hbm = refs[14]
    gain_ref, cos_ref, sin_ref, d_gain_rest_ref, shifted_hbm, mixed_hbm, total_ref, start_ref = refs[16:24]
    (
        output_ref, grad_in_ref, grad_neigh_ref, out_qkv, out_att, out_cq, out_co, out_kv, out_down, gain_out,
    ) = refs[24:34]
    full, got_core, got_one, got_two, got_z = [refs[34 + k * count : 34 + (k + 1) * count] for k in range(5)]
    (
        back_ref, grad_ref, dq_ref, delta_ref, w_ref,
        sent_ref, tail_first, tail_result, raw_ref, n1t_ref, temp_ref, gain_mine, gain_got, gain_z,
        send_sem, recv_sem, unit_send, unit_recv, tail_send, tail_recv, gain_send, gain_recv, load_sem,
    ) = refs[34 + 5 * count : -14]
    held_refs = refs[-14:]
    (
        result_ref, first_ref, n2_ref, d_cq_ref, cm_ref, gc_ref, ga_ref, gy_ref, act_ref, d_pair_ref,
        att_ref, neigh_ref, kv_ref, hidden_ref,
    ) = held_refs
    loads = [
        pltpu.make_async_copy(source, target, load_sem.at[index])
        for index, (source, target) in enumerate(zip(sources, held_refs))
    ]
    unit_loads = [
        pltpu.make_async_copy(source, target, load_sem.at[14 + index])
        for index, (source, target) in enumerate(
            [(unit_hbm, back_ref), (shifted_hbm, grad_ref), (mixed_hbm, dq_ref)]
        )
    ]
    for index in (8, 7):
        loads[index].start()
    for load in unit_loads:
        load.start()
    for index in (11, 9, 10, 6, 2, 3, 4, 5, 12, 13, 1, 0):
        loads[index].start()
    arrived = set()

    def need(*indices):
        for index in indices:
            if index not in arrived:
                arrived.add(index)
                loads[index].wait()

    micro, tokens, width = hidden_ref.shape
    rows = micro * tokens
    total = depth * 8
    z, y, c, x = coords()
    me = lax.axis_index("blk") * 2 + lax.axis_index("head")
    mine, holder = unit_of(me, total)
    whole = slice(None)
    all_barrier(total, me)

    after = lax.rem(me + 1, total)
    after_at = (after // 2, lax.rem(after, 2))
    tails = []
    for index in range(micro):
        part = pl.ds(index * tokens + tokens - 64, 64)
        tails.append(
            remote(first_hbm.at[part], tail_first.at[index], tail_send.at[index], tail_recv.at[index], after_at)
        )
        tails.append(
            remote(
                result_hbm.at[part], tail_result.at[index],
                tail_send.at[micro + index], tail_recv.at[micro + index], after_at,
            )
        )

    def slot(device):
        return back_ref.at[:, :, pl.ds(pl.multiple_of(device * tokens, 128), tokens)]

    def open_units():
        fetch(0).start()
        fetch(1).start()
        for load in unit_loads:
            load.wait()

        @pl.when(holder)
        def _():
            delta_ref[...] = jnp.zeros_like(delta_ref)

            def turn(step, carry):
                part = pl.ds(pl.multiple_of(step * 16, 16), 16)
                grad = pltpu.roll(grad_ref[part, :].astype(jnp.float32), LEAD, 1)
                grad_ref[part, :] = grad.astype(jnp.bfloat16)
                delta_ref[...] += jnp.sum(grad * dq_ref[part, :], axis=0, keepdims=True)
                dq_ref[part, :] = jnp.zeros((16, dq_ref.shape[1]), jnp.float32)
                return carry

            lax.fori_loop(0, HEAD_DIM // 16, turn, 0)

    tiles = tokens * total // TILE
    reach = (TILE + DOC_MAX - 2) // TILE

    def attend(key_tile):
        @pl.when(holder)
        def _():
            columns = pl.ds(key_tile * TILE, TILE)
            key_t = back_ref[1, :, columns]
            keys, values = key_t.T, back_ref[2, :, columns].T

            def one_query(query_tile, state):
                d_key, d_value = state
                query_t = tile_at(back_ref, query_tile, 0)
                grad_t = row_at(grad_ref, query_tile)
                scores = dot_nn(keys, query_t) * (SCORE_SCALE * LOG2E)
                allowed = tile_mask(key_tile, query_tile, row_at(start_ref, query_tile))
                probs = jnp.where(allowed, jnp.exp2(scores - row_at(total_ref, query_tile)), 0.0)
                d_probs = dot_nn(values, grad_t)
                d_scores = (probs * (d_probs - row_at(delta_ref, query_tile))).astype(jnp.bfloat16)
                d_value = d_value + dot_nn(probs.astype(jnp.bfloat16), grad_t.T)
                d_key = d_key + dot_nn(d_scores, query_t.T)
                place_q = pl.ds(pl.multiple_of(query_tile * TILE, TILE), TILE)
                dq_ref[:, place_q] += dot_nn(key_t, d_scores)
                return d_key, d_value

            zeros = jnp.zeros((TILE, HEAD_DIM), jnp.float32)
            d_key, d_value = lax.fori_loop(
                key_tile, min(key_tile + reach + 1, tiles), one_query, (zeros, zeros)
            )
            back_ref[0, :, columns] = (dq_ref[:, columns] * SCORE_SCALE).astype(jnp.bfloat16)
            back_ref[1, :, columns] = (d_key * SCORE_SCALE).T.astype(jnp.bfloat16)
            back_ref[2, :, columns] = d_value.T.astype(jnp.bfloat16)

    def send_back():
        @pl.when(holder)
        def _():
            pltpu.make_async_copy(slot(me), sent_ref.at[mine], unit_recv).start()

            def send(step, carry):
                peer = lax.rem(me + step, total)
                remote(
                    slot(peer), sent_ref.at[mine], unit_send, unit_recv, (peer // 2, lax.rem(peer, 2))
                ).start()
                return carry

            lax.fori_loop(1, total, send, 0)


    slab = full[0].shape[-2]

    def spread(index, block):
        buffer = full[index]
        cols = buffer.shape[-1]

        def body(level, carry):
            for place_in in range(8):
                at = pl.multiple_of((level * 8 + place_in) * slab, 8)
                buffer[block, level, place_in // 4, (place_in // 2) % 2, place_in % 2] = temp_ref[
                    pl.ds(at, slab), :cols
                ].astype(jnp.bfloat16)
            return carry

        lax.fori_loop(0, depth, body, 0)

    down_index = [index for index, item in enumerate(items) if item[0] == "down"]

    def make_down():
        need(7, 8)

        def body(level, carry):
            cols = pl.ds(pl.multiple_of(level * width, width), width)
            temp_ref[...] = dot_tn(act_ref[:, cols], gy_ref[...])
            for place_in in range(8):
                for part, index in enumerate(down_index):
                    at = place_in * slab * len(down_index) + part * slab
                    full[index][0, level, place_in // 4, (place_in // 2) % 2, place_in % 2] = temp_ref[
                        pl.ds(at, slab), :
                    ].astype(jnp.bfloat16)
            return carry

        lax.fori_loop(0, depth, body, 0)

    def take_units():
        @pl.when(holder)
        def _():
            part = back_ref.at[:, :, pl.ds(0, tokens * (total - 1))]
            pltpu.make_async_copy(part, part, unit_send).wait()

        pltpu.make_async_copy(sent_ref, sent_ref, unit_recv).wait()
        need(13)
        half = HEAD_DIM // 2

        def body(head, carry):
            for index in range(micro):
                lanes = pl.ds(index * tokens, tokens)
                cosine, sine = cos_ref[...], sin_ref[...]
                for part in range(3):
                    value = sent_ref[index * HEADS + head, part].astype(jnp.float32)
                    at = pl.multiple_of(part * width + head * HEAD_DIM, HEAD_DIM)
                    if part < 2:
                        first_half, second_half = value[:half], value[half:]
                        value = jnp.concatenate(
                            [
                                first_half * cosine + second_half * sine,
                                second_half * cosine - first_half * sine,
                            ],
                            axis=0,
                        )
                    raw_ref[pl.ds(at, HEAD_DIM), lanes] = value.astype(jnp.bfloat16)
            return carry

        lax.fori_loop(0, HEADS, body, 0)
        for index in range(micro):
            normed = norm_parts(hidden_ref[index].astype(jnp.float32))[0] * gain_ref[0:1, :]
            n1t_ref[:, pl.ds(index * tokens, tokens)] = normed.astype(jnp.bfloat16).T

    def make(index):
        kind, which = items[index][:2]
        if kind == "down":
            if index == down_index[0]:
                make_down()
            return
        if kind == "kv":
            need(9, 11)
            temp_ref[...] = dot_tn(neigh_ref[...], d_pair_ref[which])
        elif kind == "att":
            need(6, 10)
            temp_ref[...] = dot_nn(att_ref[0], ga_ref[pl.ds(0, tokens), :])
            for step in range(1, micro):
                temp_ref[...] += dot_nn(att_ref[step], ga_ref[pl.ds(step * tokens, tokens), :])
        elif kind == "cq":
            need(2, 3)
            temp_ref[...] = dot_tn(n2_ref[...], d_cq_ref[...])
        elif kind == "co":
            need(4, 5)
            temp_ref[...] = dot_tn(cm_ref[...], gc_ref[...])
        else:
            if which == 0:
                take_units()
            for block in range(2):
                half = width // 2
                at = which * width + block * half
                temp_ref[:, :half] = dot_nt(n1t_ref[...], raw_ref[pl.ds(at, half), :])
                spread(index, block)
            return
        spread(index, 0)

    def core(index):
        return remote(
            full[index].at[whole, whole, whole, 1 - c], got_core[index],
            send_sem.at[index, 0], recv_sem.at[index, 0], place(z, y, 1 - c, x),
        )

    def one(index):
        if items[index][2] == 0:
            src, where = full[index].at[whole, whole, 1 - y, c], place(z, 1 - y, c, x)
        else:
            src, where = full[index].at[whole, whole, whole, c, 1 - x], place(z, y, c, 1 - x)
        return remote(src, got_one[index], send_sem.at[index, 1], recv_sem.at[index, 1], where)

    def two(index):
        if items[index][2] == 0:
            src, where = full[index].at[whole, whole, y, c, 1 - x], place(z, y, c, 1 - x)
        else:
            src, where = full[index].at[whole, whole, 1 - y, c, x], place(z, 1 - y, c, x)
        return remote(src, got_two[index], send_sem.at[index, 2], recv_sem.at[index, 2], where)

    def send_z(index):
        for step in range(1, depth):
            other = lax.rem(z + step, depth)
            remote(
                full[index].at[whole, other, y, c, x], got_z[index].at[z],
                send_sem.at[index, 3], recv_sem.at[index, 3], place(other, y, c, x),
            ).start()

    def add_into(target, source):
        target[...] = (target[...].astype(jnp.float32) + source[...].astype(jnp.float32)).astype(
            jnp.bfloat16
        )

    def each_level(index, body):
        blocks = full[index].shape[0]
        lax.fori_loop(
            0, blocks * depth, lambda step, carry: (body(step // depth, lax.rem(step, depth)), carry)[1], 0
        )

    def sum_core(index):
        def body(block, level):
            for row in range(2):
                for col in range(2):
                    add_into(
                        full[index].at[block, level, row, c, col], got_core[index].at[block, level, row, col]
                    )

        each_level(index, body)

    def sum_one(index):
        def body(block, level):
            for side in range(2):
                if items[index][2] == 0:
                    target = full[index].at[block, level, y, c, side]
                else:
                    target = full[index].at[block, level, side, c, x]
                add_into(target, got_one[index].at[block, level, side])

        each_level(index, body)

    def sum_two(index):
        each_level(
            index,
            lambda block, level: add_into(
                full[index].at[block, level, y, c, x], got_two[index].at[block, level]
            ),
        )

    def sum_z(index):
        kind, which = items[index][:2]
        for block in range(full[index].shape[0]):
            value = full[index][block, z, y, c, x].astype(jnp.float32)
            for step in range(1, depth):
                value = value + got_z[index][lax.rem(z + step, depth), block].astype(jnp.float32)
            if kind == "down":
                out_down[pl.ds(which * slab, slab), :] = value
            elif kind == "kv":
                out_kv[:, pl.ds(which * width, width)] = value
            elif kind == "qkv":
                out_qkv[:, pl.ds(which * width + block * (width // 2), width // 2)] = value
            else:
                {"att": out_att, "cq": out_cq, "co": out_co}[kind][...] = value

    def phase(index, number):
        if number == 0:
            make(index)
            core(index).start()
        elif number == 1:
            core(index).wait_recv()
            sum_core(index)
            one(index).start()
        elif number == 2:
            one(index).wait_recv()
            sum_one(index)
            two(index).start()
        elif number == 3:
            two(index).wait_recv()
            sum_two(index)
            send_z(index)
        else:
            landed = got_z[index].at[pl.ds(0, depth - 1)]
            pltpu.make_async_copy(landed, landed, recv_sem.at[index, 3]).wait()
            sum_z(index)

    def gain_copy(stage):
        where = (place(z, y, 1 - c, x), place(z, 1 - y, c, x), place(z, y, c, 1 - x))[stage]
        return remote(
            gain_mine.at[stage], gain_got.at[stage], gain_send.at[stage], gain_recv.at[stage], where
        )

    def gain_phase(number):
        if number == 0:
            gain_copy(0).start()
        elif number < 4:
            gain_copy(number - 1).wait_recv()
            gain_mine[number] = gain_mine[number - 1] + gain_got[number - 1]
            if number < 3:
                gain_copy(number).start()
            else:
                for step in range(1, depth):
                    other = lax.rem(z + step, depth)
                    remote(
                        gain_mine.at[3], gain_z.at[z], gain_send.at[3], gain_recv.at[3], place(other, y, c, x)
                    ).start()
        else:
            landed = gain_z.at[pl.ds(0, depth - 1)]
            pltpu.make_async_copy(landed, landed, gain_recv.at[3]).wait()
            value = gain_mine[3]
            for step in range(1, depth):
                value = value + gain_z[lax.rem(z + step, depth)]
            gain_out[...] = value

    def neighbours_part(block):
        need(9, 12)
        chunk = 256
        part = pl.ds(block * chunk, chunk)
        grad_neigh_ref[part, :] = (
            dot_nt(d_pair_ref[0, part, :], kv_ref[0]) + dot_nt(d_pair_ref[1, part, :], kv_ref[1])
        ).astype(jnp.bfloat16)

    def fetch(block):
        return pltpu.make_async_copy(qkv_hbm.at[block], w_ref.at[block % 2], load_sem.at[17 + block % 2])

    def input_part():
        half = width // 2
        need(0, 1, 13)
        blocks = qkv_hbm.shape[0]
        for block in range(blocks):
            fetch(block).wait()
            part = dot_nn(w_ref[block % 2], raw_ref[pl.ds(block * half, half), :])
            temp_ref[:, :rows] = part if block == 0 else temp_ref[:, :rows] + part
            if block + 2 < blocks:
                fetch(block + 2).start()
        for tail in tails:
            tail.wait()
        d_gain = jnp.zeros((1, width), jnp.float32)
        for index in range(micro):
            part = pl.ds(index * tokens, tokens)
            d_normed = temp_ref[:, part].T
            pulled, part_gain = norm_pull(hidden_ref[index].astype(jnp.float32), gain_ref[0:1, :], d_normed)
            d_gain = d_gain + part_gain
            joined = jnp.concatenate([tail_first[index], first_ref[part, :]], axis=0)
            home = pltpu.roll(joined, joined.shape[0] - 1, 0)[:tokens]
            grad_in_ref[part, :] = (home + pulled).astype(jnp.bfloat16)
            joined = jnp.concatenate(
                [tail_result[index].astype(jnp.float32), result_ref[part, :].astype(jnp.float32)], axis=0
            )
            output_ref[part, :] = pltpu.roll(joined, joined.shape[0] - 1, 0)[:tokens].astype(jnp.bfloat16)
        gain_mine[0] = jnp.concatenate([d_gain, d_gain_rest_ref[0:7, :]], axis=0)

    early = [index for index, item in enumerate(items) if item[0] != "qkv"]
    late = [index for index, item in enumerate(items) if item[0] == "qkv"]
    early_pairs = [early[at : at + 2] for at in range(0, len(early), 2)]
    late_pairs = [late[at : at + 2] for at in range(0, len(late), 2)]
    chunks = neigh_ref.shape[0] // 256

    def scatter_step(pairs, step):
        for number in range(4, -1, -1):
            if 0 <= step - number < len(pairs):
                for index in pairs[step - number]:
                    phase(index, number)

    done = {"tick": 0}

    def tick(number):
        for _ in range(number):
            scatter_step(early_pairs, done["tick"])
            done["tick"] += 1

    tick(1)
    for tail in tails:
        tail.start()
    tick(LAST_PLAN[0] - 1)
    open_units()
    for tile in range(tiles):
        attend(tile)
        if tile == tiles - 1:
            send_back()
        tick(LAST_PLAN[1 + tile])
    for block in range(chunks):
        neighbours_part(block)
        if block == 1:
            tick(LAST_PLAN[1 + tiles])
    last_pair = len(late_pairs) - 1
    for step in range(len(late_pairs) + 4):
        if done["tick"] < len(early_pairs) + 4:
            tick(1)
        scatter_step(late_pairs, step)
        if step == last_pair:
            input_part()
        if 0 <= step - last_pair <= 4:
            gain_phase(step - last_pair)
    for index in range(count):
        core(index).wait_send()
        one(index).wait_send()
        two(index).wait_send()
        gone = got_z[index].at[pl.ds(0, depth - 1)]
        pltpu.make_async_copy(gone, gone, send_sem.at[index, 3]).wait()
    for stage in range(3):
        gain_copy(stage).wait_send()
    gone = gain_z.at[pl.ds(0, depth - 1)]
    pltpu.make_async_copy(gone, gone, gain_send.at[3]).wait()


def last(depth, collective, ff, *args):
    hidden = args[15]
    micro, tokens, width = hidden.shape
    rows = micro * tokens
    total = depth * 8
    slab = width // total
    neigh_rows = args[12].shape[0]
    items = [
        ("down", 0, 0), ("down", 1, 1), ("down", 2, 0), ("down", 3, 1), ("kv", 0, 0), ("kv", 1, 1),
        ("att", 0, 0), ("cq", 0, 1), ("co", 0, 0), ("qkv", 0, 1), ("qkv", 1, 0), ("qkv", 2, 1),
    ]
    count = len(items)
    low, high = jnp.bfloat16, jnp.float32
    out_shape = [
        jax.ShapeDtypeStruct((rows, width), low),
        jax.ShapeDtypeStruct((rows, width), low),
        jax.ShapeDtypeStruct((neigh_rows, width), low),
        jax.ShapeDtypeStruct((slab, 3 * width), high),
        jax.ShapeDtypeStruct((slab, width), high),
        jax.ShapeDtypeStruct((slab, width), high),
        jax.ShapeDtypeStruct((slab, width), high),
        jax.ShapeDtypeStruct((slab, 2 * width), high),
        jax.ShapeDtypeStruct((ff // total, width), high),
        jax.ShapeDtypeStruct((8, width), high),
    ]
    full, core, one, two, along = [], [], [], [], []
    for kind, which, order in items:
        blocks, cols = (2, width // 2) if kind == "qkv" else (1, width)
        full.append(pltpu.VMEM((blocks, depth, 2, 2, 2, slab, cols), low))
        core.append(pltpu.VMEM((blocks, depth, 2, 2, slab, cols), low))
        one.append(pltpu.VMEM((blocks, depth, 2, slab, cols), low))
        two.append(pltpu.VMEM((blocks, depth, slab, cols), low))
        along.append(pltpu.VMEM((depth, blocks, slab, cols), low))
    dma = pltpu.SemaphoreType.DMA
    length = tokens * total
    scratch = full + core + one + two + along + [
        pltpu.VMEM((3, HEAD_DIM, length), low),
        pltpu.VMEM((HEAD_DIM, length), low),
        pltpu.VMEM((HEAD_DIM, length), high),
        pltpu.VMEM((1, length), high),
        pltpu.VMEM((2, width, width // 2), low),
        pltpu.VMEM((UNITS, 3, HEAD_DIM, tokens), low),
        pltpu.VMEM((micro, 64, width), high),
        pltpu.VMEM((micro, 64, width), low),
        pltpu.VMEM((3 * width, rows), low),
        pltpu.VMEM((width, rows), low),
        pltpu.VMEM((width, width), high),
        pltpu.VMEM((4, 8, width), high),
        pltpu.VMEM((3, 8, width), high),
        pltpu.VMEM((depth, 8, width), high),
        dma((count, 4)), dma((count, 4)), dma, dma, dma((2 * micro,)), dma((2 * micro,)), dma((4,)), dma((4,)),
        dma((19,)),
    ] + [pltpu.VMEM(a.shape, a.dtype) for a in args[1:14] + args[15:16]]
    return pl.pallas_call(
        functools.partial(last_kernel, depth, items),
        out_shape=out_shape,
        in_specs=[ANY] * 16 + [VMEM] * 4 + [ANY] * 2 + [VMEM] * 2,
        out_specs=[VMEM] * 10,
        scratch_shapes=scratch,
        compiler_params=pltpu.CompilerParams(
            collective_id=collective, has_side_effects=True, vmem_limit_bytes=62 * 2**20
        ),
        cost_estimate=pl.CostEstimate(flops=10**10, bytes_accessed=40 * 10**6, transcendentals=0),
    )(*args)


def finish_kernel(copies, *refs):
    for source, result in zip(refs[:copies], refs[copies:]):
        result[...] = source[...].astype(result.dtype)


def finish(arrays, low):
    arrays = [*arrays, low]
    copies = len(arrays)
    vmem = pl.BlockSpec(memory_space=pltpu.VMEM)
    return pl.pallas_call(
        functools.partial(finish_kernel, copies),
        out_shape=[jax.ShapeDtypeStruct(a.shape, a.dtype) for a in arrays[:-1]]
        + [jax.ShapeDtypeStruct(low.shape, jnp.float32)],
        in_specs=[vmem] * copies,
        out_specs=[vmem] * copies,
        compiler_params=pltpu.CompilerParams(vmem_limit_bytes=62 * 2**20),
    )(*arrays)


def layer_norm(values, norm_gain):
    centred = values - jnp.mean(values, axis=-1, keepdims=True)
    spread = jnp.mean(centred * centred, axis=-1, keepdims=True)
    return centred * lax.rsqrt(spread + 1e-05) * norm_gain


def norm_backward(values, norm_gain, grad_out):
    result, pullback = jax.vjp(layer_norm, values, norm_gain)
    return pullback(grad_out)


def outer(left, right):
    return jnp.einsum("td,te->de", left, right, preferred_element_type=jnp.float32)


def turn_heads(values, cosine, sine):
    first_half, second_half = values[:, :32], values[:, 32:]
    return jnp.concatenate(
        [first_half * cosine - second_half * sine, second_half * cosine + first_half * sine], axis=1
    )


def on_device(
    hidden_in,
    segment_ids,
    neighbour_valid,
    neighbours,
    out_grad,
    norm_attn,
    w_qkv,
    w_attn_out,
    norm_cross,
    w_cross_q,
    w_cross_kv,
    w_cross_out,
    norm_mlp,
    w_up,
    w_down,
):
    micro, tok_count, model_width = hidden_in.shape
    blk_count = lax.axis_size("blk")
    depth = blk_count // 4
    total = blk_count * 2
    length = tok_count * total
    row_count = micro * tok_count
    gain_rows = norm_attn.shape[0]
    span_count = tok_count // SPAN
    pair_rows = NEIGHBOURS * NEIGH_LEN
    device = lax.axis_index(AXES)

    in_kernel = gain_rows % 8 == 0
    token_index = device * tok_count + jnp.arange(tok_count, dtype=jnp.int32)
    shifted_index = token_index + LEAD
    used = jnp.where(
        shifted_index[None] < length, jnp.repeat(neighbour_valid, SPAN, axis=1).astype(jnp.float32), 0.0
    ).reshape(row_count, 1)
    neigh_rows = neighbours.reshape(micro * span_count * pair_rows, model_width)
    if in_kernel:
        own_gains = jnp.pad(
            jnp.stack([norm_attn, norm_cross, norm_mlp]).astype(jnp.float32), ((0, 125), (0, 128 - gain_rows))
        )
        (
            got_qkv, got_sq, got_kv, up_full, down_full, d_up, unit_qkv, mixed, activated, d_pairs,
            gains, cosine, sine, totals, first_row, attended_t,
            result_rows, d_first, unit_grad, normed_cross, d_cross_query, cross_mixed, d_second_low, d_first_low,
            grad_low, d_gain_rest,
        ) = front(
            depth, w_qkv, w_attn_out, w_cross_q, w_cross_out, w_cross_kv, w_up, w_down, own_gains, segment_ids,
            neighbour_valid, neigh_rows, hidden_in, out_grad,
        )
        attended_t = attended_t.reshape(micro, model_width, tok_count)
    else:
        up_full = lax.all_gather(w_up, AXES, axis=0, tiled=True)
        down_full = lax.all_gather(w_down, AXES, axis=0, tiled=True)
        up_full = up_full.reshape(model_width, -1, model_width).transpose(1, 0, 2)
        small = jnp.zeros((16, 128), jnp.bfloat16)
        for row, gain in enumerate((norm_attn, norm_cross, norm_mlp)):
            small = small.at[row, :gain_rows].set(gain)
        small = small.at[3 : 3 + micro, :tok_count].set(segment_ids.astype(jnp.bfloat16))
        got_qkv, got_sq, got_kv, got_small, lead_hid, lead_grad = gather_all(
            depth, w_qkv, w_attn_out, w_cross_q, w_cross_out, w_cross_kv, small, hidden_in, out_grad
        )
        gains = got_small[:, :3, :gain_rows].astype(jnp.float32).transpose(1, 0, 2).reshape(3, model_width)
        gain_attn = gains[0]
        seg_full = got_small[:, 3 : 3 + micro, :tok_count].transpose(1, 0, 2).reshape(micro, length)
        seg_full = seg_full.astype(jnp.int32)
    qkv_blocks = got_qkv.reshape(6, model_width, model_width // 2)
    squares = got_sq.reshape(3, model_width, model_width)
    kv_blocks = got_kv.reshape(2, model_width, model_width)


    unit, holder = unit_of(device, total)
    tile_index = jnp.arange(length // TILE, dtype=jnp.int32)
    if in_kernel:
        tile_first = first_row[0, ::TILE]
    else:
        seg_unit = lax.dynamic_index_in_dim(seg_full, unit // HEADS, 0, keepdims=False)
        seg_tiles = seg_unit.reshape(length // TILE, TILE)
        tile_first = jnp.sum((seg_unit[None] < seg_tiles[:, :1]).astype(jnp.int32), axis=-1)
        inside = jnp.sum((seg_tiles[:, None, :] < seg_tiles[:, :, None]).astype(jnp.int32), axis=-1)
        first_row = jnp.where(
            seg_tiles == seg_tiles[:, :1], tile_first[:, None], tile_index[:, None] * TILE + inside
        ).reshape(1, length)
    low = tile_first // TILE
    high = jnp.sum((low[None] <= tile_index[:, None]).astype(jnp.int32), axis=-1)
    low = jnp.where(holder, low, tile_index + 1)
    high = jnp.where(holder, high, 0)

    if not in_kernel:
        first_of = jnp.sum(
            (seg_full[:, None, :] < segment_ids[:, :, None]).astype(jnp.int32), axis=-1
        )
        local_pos = token_index[None] - first_of
        frequency = jnp.exp(
            jnp.arange(HEAD_DIM // 2, dtype=jnp.float32) * (-2.0 * math.log(10000.0) / HEAD_DIM)
        )
        angles = frequency[:, None, None] * local_pos.astype(jnp.float32)[None]
        cosine, sine = jnp.cos(angles), jnp.sin(angles)

        hidden = hidden_in.astype(jnp.float32)
        normed_attn = layer_norm(hidden, gain_attn).astype(jnp.bfloat16).reshape(row_count, model_width)
        raw = jnp.einsum("bde,td->bet", qkv_blocks, normed_attn, preferred_element_type=jnp.float32)
        raw = raw.reshape(3, HEADS, HEAD_DIM, micro, tok_count)
        rotated = jnp.stack(
            [turn_heads(raw[0], cosine, sine), turn_heads(raw[1], cosine, sine), raw[2]]
        ).astype(jnp.bfloat16)
        message = rotated.transpose(3, 1, 0, 2, 4).reshape(UNITS, 3, HEAD_DIM, tok_count)
        unit_qkv = to_units(total, message, 1)
        shifted, mixed, totals = attn_forward(low, first_row, unit_qkv)
        (attended_t,) = to_tokens(total, shifted[None], (), 2)
    attended_t = attended_t.reshape(micro, model_width, tok_count)

    if not in_kernel:
        (
            result_rows, d_first, d_attended_t, normed_cross, d_cross_query, cross_mixed, d_second_low, d_first_low,
            grad_low, activated, d_pairs, d_gain_rest, d_up,
        ) = middle(
            attended_t, hidden_in, lead_hid, out_grad, lead_grad, gains, used, squares, kv_blocks, neigh_rows,
            up_full, down_full,
        )
    up_low = lax.psum_scatter(d_up, AXES, scatter_dimension=0, tiled=True)
    if not in_kernel:
        down_share = lax.psum_scatter(
            outer(activated, grad_low).astype(jnp.bfloat16), AXES, scatter_dimension=0, tiled=True
        ).astype(jnp.float32)
    if not in_kernel:
        unit_grad = to_units(total, d_attended_t.reshape(UNITS, 1, HEAD_DIM, tok_count), 3)[0]
    if not in_kernel:
        unit_back = attn_backward(low, high, first_row, unit_qkv, unit_grad, mixed, totals)
    if in_kernel:
        (
            output, grad_in, grad_neighbours, s_qkv, s_att, s_cq, s_co, s_kv, s_down, s_gain,
        ) = last(
            depth, 5, w_up.shape[1],
            unit_qkv, result_rows, d_first, normed_cross, d_cross_query, cross_mixed, d_second_low, d_first_low,
            grad_low, activated, d_pairs, attended_t, neigh_rows, kv_blocks, qkv_blocks, hidden_in, gains,
            cosine, sine, d_gain_rest, unit_grad, mixed, totals, first_row,
        )
        own_gain = lax.dynamic_slice_in_dim(s_gain, device * gain_rows, gain_rows, 1)
        (
            output, grad_in, grad_neighbours, s_qkv, s_att, s_cq, s_co, s_kv, s_down, up_share,
        ) = finish(
            [
                output, grad_in, grad_neighbours, s_qkv, s_att, s_cq, s_co, s_kv, s_down,
            ],
            up_low,
        )
        return (
            output.reshape(hidden_in.shape), grad_in.reshape(hidden_in.shape),
            grad_neighbours.reshape(neighbours.shape),
            own_gain[0], s_qkv, s_att, own_gain[1], s_cq, s_kv, s_co, own_gain[2], up_share, s_down,
        )
    up_share = up_low.astype(jnp.float32)
    result_rows = result_rows.reshape(micro, tok_count, model_width)
    d_first = d_first.reshape(micro, tok_count, model_width)
    sent_t, tail_first, tail_result = to_tokens(
        total, unit_back, (d_first[:, tok_count - 64 :], result_rows[:, tok_count - 64 :]), 4
    )

    def unshift(rows, tail):
        return jnp.concatenate([tail[:, 1:], rows[:, : tok_count - LEAD]], axis=1)

    output = unshift(result_rows, tail_result)
    d_first_home = unshift(d_first, tail_first)
    sent_t = sent_t.reshape(micro, HEADS, 3, HEAD_DIM, tok_count).transpose(2, 1, 3, 0, 4)
    sent_t = sent_t.astype(jnp.float32)
    raw_t = jnp.stack(
        [turn_heads(sent_t[0], cosine, -sine), turn_heads(sent_t[1], cosine, -sine), sent_t[2]]
    ).astype(jnp.bfloat16).reshape(6, model_width // 2, row_count)
    d_normed_attn = jnp.einsum("bet,bde->td", raw_t, qkv_blocks, preferred_element_type=jnp.float32)
    d_hidden_in, d_gain_attn = norm_backward(
        hidden, gain_attn, d_normed_attn.reshape(micro, tok_count, model_width)
    )
    grad_in = (d_first_home + d_hidden_in).astype(jnp.bfloat16)

    d_keys, d_values = d_pairs[0], d_pairs[1]
    d_first_low = d_first_low.reshape(micro, tok_count, model_width)
    d_neigh = (
        jnp.einsum("te,de->td", d_keys, kv_blocks[0], preferred_element_type=jnp.float32)
        + jnp.einsum("te,de->td", d_values, kv_blocks[1], preferred_element_type=jnp.float32)
    ).astype(jnp.bfloat16)
    grad_neighbours = d_neigh.reshape(neighbours.shape)

    def blocks_of(array):
        return array.astype(jnp.bfloat16).reshape(
            array.shape[0], depth, 2, 2, 2, gain_rows, array.shape[-1]
        )

    d_qkv = jnp.einsum("td,bet->bde", normed_attn, raw_t, preferred_element_type=jnp.float32)
    d_sq = jnp.stack(
        [
            jnp.einsum("mdt,mte->de", attended_t, d_first_low, preferred_element_type=jnp.float32),
            outer(normed_cross, d_cross_query),
            outer(cross_mixed, d_second_low),
        ]
    )
    d_kv = jnp.stack([outer(neigh_rows, d_keys), outer(neigh_rows, d_values)])
    d_gains = jnp.stack([d_gain_attn, d_gain_rest[0], d_gain_rest[1]]).reshape(3, total, gain_rows)
    d_gains = jnp.zeros((total, 8, 128), jnp.float32).at[:, :3, :gain_rows].set(d_gains.transpose(1, 0, 2))
    s_qkv, s_sq, s_kv, s_gain = scatter_all(
        depth, blocks_of(d_qkv), blocks_of(d_sq), blocks_of(d_kv), d_gains, 6
    )
    return (
        output,
        grad_in,
        grad_neighbours,
        s_gain[0, :gain_rows],
        s_qkv.transpose(1, 0, 2).reshape(gain_rows, 3 * model_width),
        s_sq[0],
        s_gain[1, :gain_rows],
        s_sq[1],
        s_kv.transpose(1, 0, 2).reshape(gain_rows, 2 * model_width),
        s_sq[2],
        s_gain[2, :gain_rows],
        up_share,
        down_share,
    )


def solution(mesh):
    placed = (
        P(None, ("blk", "head"), None),
        P(None, ("blk", "head")),
        P(None, ("blk", "head")),
        P(None, ("blk", "head"), None, None, None),
        P(None, ("blk", "head"), None),
        P(("blk", "head")),
        P(("blk", "head"), None),
        P(("blk", "head"), None),
        P(("blk", "head")),
        P(("blk", "head"), None),
        P(("blk", "head"), None),
        P(("blk", "head"), None),
        P(("blk", "head")),
        P(("blk", "head"), None),
        P(("blk", "head"), None),
    )
    return jax.shard_map(
        on_device,
        mesh=mesh,
        in_specs=placed,
        out_specs=(
            P(None, ("blk", "head"), None),
            P(None, ("blk", "head"), None),
            P(None, ("blk", "head"), None, None, None),
            P(("blk", "head")),
            P(("blk", "head"), None),
            P(("blk", "head"), None),
            P(("blk", "head")),
            P(("blk", "head"), None),
            P(("blk", "head"), None),
            P(("blk", "head"), None),
            P(("blk", "head")),
            P(("blk", "head"), None),
            P(("blk", "head"), None),
        ),
        check_vma=False,
    )
```
